32 devices in a mesh: dp: 8 (over z, y), head: 4 (over x, core).
Axes of the slice: x: 2, y: 2, z: 4, core: 2. Of those that a mesh axis runs over, the one named last changes fastest.
Arguments:
- inputs: float32 [32, 512, 1024], P(('dp', 'head')), may hold values from -6 to 6
- memory: bfloat16 [32, 512, 1024], P('dp'), may hold values from -6 to 6
- compressed: bfloat16 [32, 512, 1024], P('dp'), may hold values from -6 to 6
- counts: int32 [32], P('dp'), may hold values from 128 to 512, as said below
- mem_lens: int32 [32], P('dp'), may hold values from 1 to 512
- cmem_lens: int32 [32], P('dp'), may hold values from 1 to 512
- norm_gain: bfloat16 [1024], P(('dp', 'head')), may hold values from 0.5 to 1.5
- w_query: bfloat16 [1024, 1024], P(None, 'head'), may hold values from -0.1875 to 0.1875
- w_key: bfloat16 [1024, 1024], P(None, 'head'), may hold values from -0.1875 to 0.1875
- w_value: bfloat16 [1024, 1024], P(None, 'head'), may hold values from -0.1875 to 0.1875
- w_output: bfloat16 [1024, 1024], P('head'), may hold values from -4 to 4
- ffn_gain: bfloat16 [1024], P(('dp', 'head')), may hold values from 0.5 to 1.5
- w_in: bfloat16 [1024, 4096], P(('dp', 'head')), may hold values from -0.1875 to 0.1875
- w_out: bfloat16 [4096, 1024], P(('dp', 'head')), may hold values from -0.09375 to 0.09375
- w_conv: bfloat16 [3072, 1024], P(('dp', 'head')), may hold values from -0.109375 to 0.109375
- out_grad: float32 [32, 512, 1024], P(('dp', 'head')), may hold values from -6 to 6
- comp_grad: float32 [32, 171, 1024], P(('dp', 'head')), may hold values from -6 to 6
Outputs:
- outputs: float32 [32, 512, 1024], P(('dp', 'head'))
- input_grad: float32 [32, 512, 1024], P(('dp', 'head'))
- new_compressed: float32 [32, 171, 1024], P(('dp', 'head'))
- grad_norm_gain: float32 [1024], P(('dp', 'head'))
- grad_query: float32 [1024, 1024], P(None, 'head')
- grad_key: float32 [1024, 1024], P(None, 'head')
- grad_value: float32 [1024, 1024], P(None, 'head')
- grad_output: float32 [1024, 1024], P('head')
- grad_ffn_gain: float32 [1024], P(('dp', 'head'))
- grad_w_in: float32 [1024, 4096], P(('dp', 'head'))
- grad_w_out: float32 [4096, 1024], P(('dp', 'head'))
- grad_w_conv: float32 [3072, 1024], P(('dp', 'head'))
The draws below stay inside these ranges and needn't reach their ends.
Inputs may be any that keep to these rules, and one draw needn't show every extreme that they name: `counts`: each stream holds 128, 256 or 512 true tokens. Among the 4 streams of each index of dp, one drawn from the seed has 512 true tokens, 512 valid memory rows and 512 valid compressed rows.
All inputs are finite; a program needn't handle non-finite values.
Results may differ from the reference program's by a relative error of at most 0.018.
Values may be sent and summed in bfloat16 or wider, within the bound.
A program may use at most 320 MiB of HBM per device.

```python
import jax
import jax.numpy as jnp
from jax import lax

D = 1024
H = 8
E = 128
FF = 4096
MEM = 512
CMEM = 512
SLOT = 512
GROUP = 4
STREAMS = 32
CNEW = 171


def full_stream(key):
    chosen = jax.random.randint(key, (STREAMS // GROUP, 1), 0, GROUP)
    return (jnp.arange(GROUP, dtype=jnp.int32)[None, :] == chosen).reshape(STREAMS)


def draw_counts(key, part):
    chosen = full_stream(key)
    key = jax.random.fold_in(key, 5)
    levels = jax.random.randint(key, (STREAMS,), 0, 3)
    picked = jnp.where(levels == 0, SLOT // 4, jnp.where(levels == 1, SLOT // 2, SLOT))
    return jnp.where(chosen, SLOT, picked).astype(jnp.int32)


def draw_mem_lens(key, part):
    chosen = full_stream(key)
    key = jax.random.fold_in(key, 6)
    lengths = jax.random.randint(key, (STREAMS,), 1, MEM + 1)
    return jnp.where(chosen, MEM, lengths).astype(jnp.int32)


def draw_cmem_lens(key, part):
    chosen = full_stream(key)
    key = jax.random.fold_in(key, 7)
    lengths = jax.random.randint(key, (STREAMS,), 1, CMEM + 1)
    return jnp.where(chosen, CMEM, lengths).astype(jnp.int32)


def level_of(rng, shape, split, smallest, top_value):
    factor_of, own = 1.0, jax.random.fold_in(rng, 6)
    for axis_at, blocks in split:
        draws = jnp.exp(jax.random.uniform(jax.random.fold_in(own, axis_at), (blocks,), jnp.float32, smallest / len(split), top_value / len(split)))
        factor_of = factor_of * jnp.repeat(draws, shape[axis_at] // blocks).reshape([-1 if axis == axis_at else 1 for axis in range(len(shape))])
    return factor_of


def scatter_about(key, dims, spread, bound, cuts=(), kind=jnp.bfloat16):
    gain = level_of(key, dims, cuts, -0.22, 0.18) if cuts else 1.0
    entries = jax.random.normal(key, dims, jnp.float32) * spread * gain
    return jnp.minimum(jnp.maximum(entries, -bound), bound).astype(kind)


def setup_inputs(seed: int = 0) -> dict:
    splits = jax.random.split(jax.random.key(seed), 18)
    inputs = scatter_about(splits[0], (STREAMS, SLOT, D), 1.0, 6.0, ((0, 32),), jnp.float32)
    memory = scatter_about(splits[1], (STREAMS, MEM, D), 1.0, 6.0, ((0, 8),))
    compressed = scatter_about(splits[2], (STREAMS, CMEM, D), 1.0, 6.0, ((0, 8),))
    counts = draw_counts(jax.random.fold_in(splits[17], 71), 0)
    mem_lens = draw_mem_lens(jax.random.fold_in(splits[17], 71), 0)
    cmem_lens = draw_cmem_lens(jax.random.fold_in(splits[17], 71), 0)
    norm_gain = jnp.clip(1.0 + 0.1 * jax.random.normal(splits[6], (D,), jnp.float32), 0.5, 1.5).astype(jnp.bfloat16)
    w_query = scatter_about(splits[7], (D, H * E), D ** -0.5, 0.1875, ((1, 4),))
    w_key = scatter_about(splits[8], (D, H * E), D ** -0.5, 0.1875, ((1, 4),))
    w_value = scatter_about(splits[9], (D, H * E), D ** -0.5, 0.1875, ((1, 4),))
    w_output = scatter_about(splits[10], (H * E, D), 2 ** -0.5, 4.0, ((0, 4),))
    ffn_gain = jnp.clip(1.0 + 0.1 * jax.random.normal(splits[11], (D,), jnp.float32), 0.5, 1.5).astype(jnp.bfloat16)
    w_in = scatter_about(splits[12], (D, FF), D ** -0.5, 0.1875, ((0, 32),))
    w_out = scatter_about(splits[13], (FF, D), FF ** -0.5, 0.09375, ((0, 32),))
    w_conv = scatter_about(splits[14], (3 * D, D), (3 * D) ** -0.5, 0.109375, ((0, 32),))
    out_grad = scatter_about(splits[15], (STREAMS, SLOT, D), 1.0, 6.0, ((0, 32),), jnp.float32)
    comp_grad = scatter_about(splits[16], (STREAMS, CNEW, D), 1.0, 6.0, ((0, 32),), jnp.float32)
    return {"inputs": inputs, "memory": memory, "compressed": compressed, "counts": counts, "mem_lens": mem_lens, "cmem_lens": cmem_lens, "norm_gain": norm_gain, "w_query": w_query, "w_key": w_key, "w_value": w_value, "w_output": w_output, "ffn_gain": ffn_gain, "w_in": w_in, "w_out": w_out, "w_conv": w_conv, "out_grad": out_grad, "comp_grad": comp_grad}


epsilon = 1e-05
masked_value = -1e+30

@jax.custom_vjp
def low(v):
    return lax.optimization_barrier(v.astype(jnp.bfloat16)).astype(jnp.float32)

@jax.custom_vjp
def low_back(v):
    return v

def low_keep(v):
    return (low(v), None)

def low_pass(kept, grad):
    return (grad,)

def back_keep(v):
    return (v, None)

def back_low(kept, grad):
    return (low(grad),)
low.defvjp(low_keep, low_pass)
low_back.defvjp(back_keep, back_low)

def layer_norm(values, gain_vec):
    row_mean = lax.optimization_barrier(jnp.mean(values, axis=-1, keepdims=True))
    centred = values - row_mean
    variance = lax.optimization_barrier(jnp.mean(centred * centred, axis=-1, keepdims=True))
    return centred * lax.rsqrt(variance + epsilon) * gain_vec

def key_mask(slot_len, cmem_size, mem_size, mem_len, cmem_len):
    key_pos = jnp.arange(cmem_size + mem_size + slot_len, dtype=jnp.int32)
    row_pos = jnp.arange(slot_len, dtype=jnp.int32)
    slot_pos = key_pos - cmem_size - mem_size
    in_slot = slot_pos[None, :] <= row_pos[:, None]
    in_memory = jnp.where(key_pos < cmem_size, key_pos < cmem_len, key_pos - cmem_size < mem_len)
    return jnp.where((key_pos < cmem_size + mem_size)[None, :], in_memory[None, :], in_slot)

def product(left, right):
    return jnp.dot(left, right, precision=lax.Precision.HIGHEST, preferred_element_type=jnp.float32)

def stream_forward(params, inputs, memory, compressed, true_count, mem_len, cmem_len):
    norm_gain, w_query, w_key, w_value, w_output, ffn_gain, w_in, w_out, w_conv = params
    slot_len = inputs.shape[0]
    normed = low(layer_norm(inputs, norm_gain))
    normed_mem = low(layer_norm(memory, norm_gain))
    normed_cmem = low(layer_norm(compressed, norm_gain))
    key_rows = jnp.concatenate([normed_cmem, normed_mem, normed], axis=0)
    key_total = key_rows.shape[0]
    head_count = w_query.shape[1] // E
    queries = low_back(low(product(normed, w_query))).reshape(slot_len, head_count, E)
    key_heads = low_back(low(product(key_rows, w_key))).reshape(key_total, head_count, E)
    value_heads = low_back(low(product(key_rows, w_value))).reshape(key_total, head_count, E)
    raw_scores = jnp.einsum('qhe,khe->hqk', queries, key_heads, precision=lax.Precision.HIGHEST) * E ** (-0.5)
    scores = low_back(raw_scores)
    key_valid = key_mask(slot_len, CMEM, MEM, mem_len, cmem_len)
    masked = jnp.where(key_valid[None], scores, masked_value)
    row_top = lax.optimization_barrier(jnp.max(masked, axis=-1, keepdims=True))
    exp_scores = jnp.exp(masked - row_top)
    attn_probs = low(exp_scores / lax.optimization_barrier(jnp.sum(exp_scores, axis=-1, keepdims=True)))
    head_mixed = jnp.einsum('hqk,khe->qhe', attn_probs, value_heads, precision=lax.Precision.HIGHEST)
    head_mixed = low_back(low(head_mixed.reshape(slot_len, head_count * E)))
    attention = low_back(product(head_mixed, w_output))
    row_pos = jnp.arange(slot_len, dtype=jnp.int32)
    row_live = (row_pos < true_count).astype(jnp.float32)[:, None]
    hidden = inputs + row_live * attention
    normed_two = low(layer_norm(hidden, ffn_gain))
    inner = low_back(product(normed_two, w_in))
    activated = low(jax.nn.gelu(inner))
    ffn_out = low_back(product(activated, w_out))
    outputs = hidden + row_live * ffn_out
    evict_live = ((row_pos < true_count) & (row_pos < mem_len)).astype(jnp.float32)[:, None]
    evicted = memory[:slot_len] * evict_live
    evicted = jnp.pad(evicted, ((0, 3 * CNEW - slot_len), (0, 0))).reshape(CNEW, 3 * memory.shape[1])
    new_compressed = low_back(product(evicted, w_conv))
    return (outputs, new_compressed)

def reference(inputs, memory, compressed, counts, mem_lens, cmem_lens, norm_gain, w_query, w_key, w_value, w_output, ffn_gain, w_in, w_out, w_conv, out_grad, comp_grad):
    params = tuple((weight.astype(jnp.float32) for weight in (norm_gain, w_query, w_key, w_value, w_output, ffn_gain, w_in, w_out, w_conv)))

    def one_stream(totals, stream_item):
        stream_in, stream_mem, stream_cmem, true_count, mem_len, cmem_len, grad_y, grad_new = stream_item
        mem_float = stream_mem.astype(jnp.float32)
        cmem_float = stream_cmem.astype(jnp.float32)

        def forward(weights, values):
            return stream_forward(weights, values, mem_float, cmem_float, true_count, mem_len, cmem_len)
        results, pull_back = jax.vjp(forward, params, stream_in)
        gradients, grad_in = pull_back((grad_y, grad_new))
        new_totals = tuple((total + grad for total, grad in zip(totals, gradients)))
        return (new_totals, (results[0], grad_in, results[1]))
    zero_grads = tuple((jnp.zeros(weight.shape, jnp.float32) for weight in params))
    totals, (outputs, input_grad, new_compressed) = lax.scan(one_stream, zero_grads, (inputs, memory, compressed, counts, mem_lens, cmem_lens, out_grad, comp_grad))
    return (outputs, input_grad, new_compressed, totals[0], totals[1], totals[2], totals[3], totals[4], totals[5], totals[6], totals[7], totals[8])
```

```python
import functools

import jax
import jax.numpy as jnp
from jax import lax
from jax.experimental import pallas as pl
from jax.experimental.pallas import tpu as pltpu
from jax.sharding import PartitionSpec as P

E = 128
BLOCK = 256
epsilon = 1e-05
masked_value = -1e30
score_scale = E ** (-0.5)
log2e = 1.4426950408889634
bf16 = jnp.bfloat16
f32 = jnp.float32
VMEM_BYTES = 30 * 2**20
MESH = pl.DeviceIdType.MESH


def dot(left, right):
    return jnp.dot(left, right, preferred_element_type=f32)


def dot_tn(left, right):
    return lax.dot_general(left, right, (((0,), (0,)), ((), ())), preferred_element_type=f32)


def dot_nt(left, right):
    return lax.dot_general(left, right, (((1,), (1,)), ((), ())), preferred_element_type=f32)


def layer_norm(values, gain_vec):
    row_mean = jnp.mean(values, axis=-1, keepdims=True)
    centred = values - row_mean
    variance = jnp.mean(centred * centred, axis=-1, keepdims=True)
    return centred * lax.rsqrt(variance + epsilon) * gain_vec


def vmem():
    return pl.BlockSpec(memory_space=pltpu.VMEM)


def anywhere():
    return pl.BlockSpec(memory_space=pl.ANY)


def opening_kernel(
    heads, dps, count_ref, w_in_ref, w_conv_ref, cot_ref, out_grad_ref, gains_ref, *refs
):
    weights, refs = refs[:4], refs[4:]
    in_out, conv_out, cot_out, gains_out, gf_out, gf_core = refs[:6]
    weights_core = refs[6:10]
    in_send, conv_send, cot_send, sems = refs[10:]
    head = lax.axis_index("head")
    dp = lax.axis_index("dp")

    def head_device(r):
        return (dp, jnp.bitwise_xor(head, r))

    def dp_device(r):
        return (lax.rem(dp + r, dps), head)

    barrier = pltpu.get_barrier_semaphore()
    for r in range(1, heads):
        pl.semaphore_signal(barrier, inc=1, device_id=head_device(r), device_id_type=MESH)
    for r in range(1, dps):
        pl.semaphore_signal(barrier, inc=1, device_id=dp_device(r), device_id_type=MESH)
    pl.semaphore_wait(barrier, heads + dps - 2)

    started = []

    def send(source, target, device):
        n = len(started)
        copy = pltpu.make_async_remote_copy(
            src_ref=source,
            dst_ref=target,
            send_sem=sems.at[0, n],
            recv_sem=sems.at[1, n],
            device_id=device,
            device_id_type=MESH,
        )
        copy.start()
        started.append(copy)
        return copy

    at = dp * heads + head
    gains_out[at] = gains_ref[...]
    gain_copies = [
        send(gains_out.at[at], gains_out.at[at], head_device(r)) for r in range(1, heads)
    ]
    for mine, other in zip(weights, weights_core):
        send(mine, other, head_device(1))
    columns = w_conv_ref.shape[1] // heads
    new_rows = cot_ref.shape[0]
    pad_rows = cot_send.shape[1]
    for r in range(heads):
        other = jnp.bitwise_xor(head, r)
        cut = pl.ds(pl.multiple_of(other * columns, columns), columns)
        conv_piece = w_conv_ref[:, cut]
        cot_piece = jnp.concatenate(
            [cot_ref[:, cut], jnp.zeros((pad_rows - new_rows, columns), f32)], axis=0
        ).astype(bf16)
        if r == 0:
            in_out[head] = w_in_ref[0]
            conv_out[head] = conv_piece
            cot_out[head] = cot_piece
        else:
            in_send[r - 1] = w_in_ref[r]
            conv_send[r - 1] = conv_piece
            cot_send[r - 1] = cot_piece
            send(in_send.at[r - 1], in_out.at[head], head_device(r))
            send(conv_send.at[r - 1], conv_out.at[head], head_device(r))
            send(cot_send.at[r - 1], cot_out.at[head], head_device(r))
    for copy in gain_copies:
        copy.wait_recv()
    block = gains_out.at[pl.ds(dp * heads, heads)]
    for r in range(1, dps):
        send(block, block, dp_device(r))
    row = lax.broadcasted_iota(jnp.int32, out_grad_ref.shape, 0)
    gf_out[...] = jnp.where(row < count_ref[0], out_grad_ref[...], 0.0).astype(bf16)
    send(gf_out, gf_core, head_device(1))
    for copy in started:
        copy.wait_send()
        if not any(copy is other for other in gain_copies):
            copy.wait_recv()


def opening(count, in_pieces, w_conv, comp_grad, out_grad, gains, weights):
    heads, dps = lax.axis_size("head"), lax.axis_size("dp")
    columns = w_conv.shape[1] // heads
    new_rows = comp_grad.shape[0]
    pad_rows = (new_rows + 15) // 16 * 16
    shape = jax.ShapeDtypeStruct
    in_all = shape(in_pieces.shape, bf16)
    conv_all = shape((heads, w_conv.shape[0], columns), bf16)
    cot_all = shape((heads, pad_rows, columns), bf16)
    grad = shape(out_grad.shape, bf16)
    copies = 5 + 4 * (heads - 1) + dps - 1
    return pl.pallas_call(
        functools.partial(opening_kernel, heads, dps),
        in_specs=[pl.BlockSpec(memory_space=pltpu.SMEM)] + [vmem()] * 5 + [anywhere()] * 4,
        out_specs=[vmem()] * 6 + [anywhere()] * 4,
        out_shape=[in_all, conv_all, cot_all, shape((dps * heads,) + gains.shape, f32), grad, grad]
        + [shape(w.shape, bf16) for w in weights],
        scratch_shapes=[
            pltpu.VMEM((heads - 1,) + in_all.shape[1:], bf16),
            pltpu.VMEM((heads - 1,) + conv_all.shape[1:], bf16),
            pltpu.VMEM((heads - 1,) + cot_all.shape[1:], bf16),
            pltpu.SemaphoreType.DMA((2, copies)),
        ],
        compiler_params=pltpu.CompilerParams(
            collective_id=0, has_side_effects=True, vmem_limit_bytes=VMEM_BYTES
        ),
        name="opening",
    )(count, in_pieces, w_conv, comp_grad, out_grad, gains, *weights)


def closing_kernel(heads, new_ref, in_ref, conv_ref, new_out, in_out, conv_out, *refs):
    new_got, in_got, conv_got, sems = refs
    head = lax.axis_index("head")
    dp = lax.axis_index("dp")

    def device(r):
        return (dp, jnp.bitwise_xor(head, r))

    barrier = pltpu.get_barrier_semaphore()
    for r in range(1, heads):
        pl.semaphore_signal(barrier, inc=1, device_id=device(r), device_id_type=MESH)
    pl.semaphore_wait(barrier, heads - 1)
    copies = []
    for n, (source, target) in enumerate(
        ((new_ref, new_got), (in_ref, in_got), (conv_ref, conv_got))
    ):
        for r in range(1, heads):
            copy = pltpu.make_async_remote_copy(
                src_ref=source.at[jnp.bitwise_xor(head, r)],
                dst_ref=target.at[head],
                send_sem=sems.at[0, n, r],
                recv_sem=sems.at[1, n, r],
                device_id=device(r),
                device_id_type=MESH,
            )
            copy.start()
            copies.append(copy)
        target[head] = source[head]
    for copy in copies:
        copy.wait()
    columns = conv_ref.shape[2]
    new_rows = new_out.shape[0]
    for h in range(heads):
        cut = slice(h * columns, (h + 1) * columns)
        new_out[:, cut] = new_got[h][:new_rows].astype(f32)
        conv_out[:, cut] = conv_got[h].astype(f32)
        in_out[h] = in_got[h].astype(f32)


def closing(new_cols, grad_in, grad_conv, new_rows):
    heads = lax.axis_size("head")
    columns = grad_conv.shape[2]
    shape = jax.ShapeDtypeStruct
    return pl.pallas_call(
        functools.partial(closing_kernel, heads),
        in_specs=[vmem()] * 3,
        out_specs=[vmem()] * 3,
        out_shape=[
            shape((new_rows, heads * columns), f32),
            shape(grad_in.shape, f32),
            shape((grad_conv.shape[1], heads * columns), f32),
        ],
        scratch_shapes=[
            pltpu.VMEM(new_cols.shape, bf16),
            pltpu.VMEM(grad_in.shape, bf16),
            pltpu.VMEM(grad_conv.shape, bf16),
            pltpu.SemaphoreType.DMA((2, 3, heads)),
        ],
        compiler_params=pltpu.CompilerParams(
            collective_id=1, has_side_effects=True, vmem_limit_bytes=VMEM_BYTES
        ),
        name="closing",
    )(new_cols, grad_in, grad_conv)


def project_first_kernel(
    which, cmem_ref, mem_ref, inputs_ref, gain_ref, wq0, wq1, wk0, wk1, wv0, wv1, rows_ref,
    q_ref, k_ref, v_ref,
):
    step = pl.program_id(0)
    third = pl.num_programs(0) // 3
    gain = gain_ref[...]
    half = wk0.shape[1]

    def keyed(values):
        normed = layer_norm(values, gain).astype(bf16)
        rows_ref[...] = normed
        k_ref[:, :half] = dot(normed, wk0[...]).astype(bf16)
        k_ref[:, half:] = dot(normed, wk1[...]).astype(bf16)
        v_ref[:, :half] = dot(normed, wv0[...]).astype(bf16)
        v_ref[:, half:] = dot(normed, wv1[...]).astype(bf16)
        return normed

    @pl.when(step < third)
    def _():
        keyed(cmem_ref[0].astype(f32))

    @pl.when((step >= third) & (step < 2 * third))
    def _():
        keyed(mem_ref[0].astype(f32))

    @pl.when(step >= 2 * third)
    def _():
        normed = keyed(inputs_ref[0])
        q_ref[:, :half] = dot(normed, wq0[...]).astype(bf16)
        q_ref[:, half:] = dot(normed, wq1[...]).astype(bf16)


def project_first(which, compressed, memory, inputs, gain, weights):
    slot_len, width = inputs.shape[1:]
    rows = 256
    third = slot_len // rows
    half = weights[0].shape[1]

    def at(first):
        return lambda g, s: (s[0], jnp.clip(g - first, 0, third - 1), 0)

    def slots(g, s):
        return (jnp.clip(g - 2 * third, 0, third - 1), 0)

    def same(g, s):
        return (0, 0)

    shape = jax.ShapeDtypeStruct
    keys = 3 * slot_len
    return pl.pallas_call(
        project_first_kernel,
        grid_spec=pltpu.PrefetchScalarGridSpec(
            num_scalar_prefetch=1,
            grid=(3 * third,),
            in_specs=[
                pl.BlockSpec((1, rows, width), at(0)),
                pl.BlockSpec((1, rows, width), at(third)),
                pl.BlockSpec((1, rows, width), lambda g, s: (0,) + slots(g, s)),
                pl.BlockSpec((1, width), same),
            ]
            + [pl.BlockSpec((width, half), same)] * 6,
            out_specs=[
                pl.BlockSpec((rows, width), lambda g, s: (g, 0)),
                pl.BlockSpec((rows, 2 * half), slots),
                pl.BlockSpec((rows, 2 * half), lambda g, s: (g, 0)),
                pl.BlockSpec((rows, 2 * half), lambda g, s: (g, 0)),
            ],
        ),
        out_shape=[
            shape((keys, width), bf16),
            shape((slot_len, 2 * half), bf16),
            shape((keys, 2 * half), bf16),
            shape((keys, 2 * half), bf16),
        ],
        compiler_params=pltpu.CompilerParams(vmem_limit_bytes=VMEM_BYTES),
        cost_estimate=pl.CostEstimate(
            flops=2 * (2 * keys + slot_len) * width * 2 * half,
            bytes_accessed=10 * slot_len * width * 2,
            transcendentals=0,
        ),
        name="project_first",
    )(which, compressed, memory, inputs, gain, *weights)


def project_second_kernel(rows_ref, wq0, wq1, wk0, wk1, wv0, wv1, q_ref, k_ref, v_ref):
    step = pl.program_id(0)
    third = pl.num_programs(0) // 3
    half = wk0.shape[1]
    normed = rows_ref[...]
    k_ref[:, :half] = dot(normed, wk0[...]).astype(bf16)
    k_ref[:, half:] = dot(normed, wk1[...]).astype(bf16)
    v_ref[:, :half] = dot(normed, wv0[...]).astype(bf16)
    v_ref[:, half:] = dot(normed, wv1[...]).astype(bf16)

    @pl.when(step >= 2 * third)
    def _():
        q_ref[:, :half] = dot(normed, wq0[...]).astype(bf16)
        q_ref[:, half:] = dot(normed, wq1[...]).astype(bf16)


def project_second(key_rows, weights):
    keys, width = key_rows.shape
    rows = 256
    steps = keys // rows
    third = steps // 3
    half = weights[0].shape[1]
    shape = jax.ShapeDtypeStruct

    def same(g):
        return (0, 0)

    return pl.pallas_call(
        project_second_kernel,
        grid=(steps,),
        in_specs=[pl.BlockSpec((rows, width), lambda g: (g, 0))]
        + [pl.BlockSpec((width, half), same)] * 6,
        out_specs=[
            pl.BlockSpec((rows, 2 * half), lambda g: (jnp.clip(g - 2 * third, 0, third - 1), 0)),
            pl.BlockSpec((rows, 2 * half), lambda g: (g, 0)),
            pl.BlockSpec((rows, 2 * half), lambda g: (g, 0)),
        ],
        out_shape=[
            shape((keys // 3, 2 * half), bf16),
            shape((keys, 2 * half), bf16),
            shape((keys, 2 * half), bf16),
        ],
        compiler_params=pltpu.CompilerParams(vmem_limit_bytes=VMEM_BYTES),
        cost_estimate=pl.CostEstimate(
            flops=2 * (2 * keys + keys // 3) * width * 2 * half,
            bytes_accessed=4 * keys * width,
            transcendentals=0,
        ),
        name="project_second",
    )(key_rows, *weights)


def masked_scores(kb, lens_ref, scores):
    rows = lax.broadcasted_iota(jnp.int32, scores.shape, 0)
    if kb < 4:
        limit = lens_ref[kb // 2] - (kb % 2) * BLOCK
        return jnp.where(rows < limit, scores, masked_value)
    columns = lax.broadcasted_iota(jnp.int32, scores.shape, 1)
    return jnp.where(rows <= columns, scores, masked_value)


def attend_forward_kernel(lens_ref, q_ref, k_ref, v_ref, mixed_ref, lse_ref, scores):
    slot_len = q_ref.shape[0]
    q_t = q_ref[...].T
    v_t = v_ref[...].T
    c = score_scale * log2e
    top = jnp.full((1, slot_len), masked_value, f32)
    for kb in range(6):
        first = BLOCK if kb == 5 else 0
        s = dot(k_ref[kb * BLOCK : (kb + 1) * BLOCK, :], q_t[:, first:])
        s = masked_scores(kb, lens_ref, s)
        scores[kb * BLOCK : (kb + 1) * BLOCK, first:] = s
        part = jnp.max(s, axis=0, keepdims=True)
        if first:
            top = jnp.concatenate([top[:, :first], jnp.maximum(top[:, first:], part)], axis=1)
        else:
            top = jnp.maximum(top, part)
    shift = top * c
    mixed = jnp.zeros((E, slot_len), f32)
    total = jnp.zeros((1, slot_len), f32)
    for kb in range(6):
        first = BLOCK if kb == 5 else 0
        p = jnp.exp2(scores[kb * BLOCK : (kb + 1) * BLOCK, first:] * c - shift[:, first:])
        part = jnp.sum(p, axis=0, keepdims=True)
        out = dot(v_t[:, kb * BLOCK : (kb + 1) * BLOCK], p.astype(bf16))
        if first:
            total = jnp.concatenate([total[:, :first], total[:, first:] + part], axis=1)
            mixed = jnp.concatenate([mixed[:, :first], mixed[:, first:] + out], axis=1)
        else:
            total = total + part
            mixed = mixed + out
    mixed_ref[...] = (mixed / total).T.astype(bf16)
    lse_ref[0] = shift + jnp.log2(total)


def attend_forward(lens, queries, key_heads, value_heads):
    slot_len, width = queries.shape
    keys = key_heads.shape[0]
    heads = width // E
    flops = 4 * heads * slot_len * keys * E
    column = lambda h: (0, h)
    return pl.pallas_call(
        attend_forward_kernel,
        grid=(heads,),
        in_specs=[
            pl.BlockSpec(memory_space=pltpu.SMEM),
            pl.BlockSpec((slot_len, E), column),
            pl.BlockSpec((keys, E), column),
            pl.BlockSpec((keys, E), column),
        ],
        out_specs=[
            pl.BlockSpec((slot_len, E), column),
            pl.BlockSpec((1, 1, slot_len), lambda h: (h, 0, 0)),
        ],
        out_shape=[
            jax.ShapeDtypeStruct((slot_len, width), bf16),
            jax.ShapeDtypeStruct((heads, 1, slot_len), f32),
        ],
        scratch_shapes=[pltpu.VMEM((keys, slot_len), f32)],
        compiler_params=pltpu.CompilerParams(vmem_limit_bytes=VMEM_BYTES),
        cost_estimate=pl.CostEstimate(
            flops=2 * flops, bytes_accessed=0, transcendentals=heads * slot_len * keys
        ),
        name="attend_forward",
    )(lens, queries, key_heads, value_heads)


def attend_backward_kernel(
    lens_ref, q_ref, k_ref, v_ref, lse_ref, g_ref, dq_ref, dkv_ref, probs, grads
):
    slot_len = q_ref.shape[0]
    c = score_scale * log2e
    q = q_ref[...]
    g = g_ref[...]
    q_t = q.T
    g_t = g.T
    k_t = k_ref[...].T
    lse = lse_ref[0]
    row_dot = jnp.zeros((1, slot_len), f32)
    for kb in range(6):
        first = BLOCK if kb == 5 else 0
        rows = slice(kb * BLOCK, (kb + 1) * BLOCK)
        s = masked_scores(kb, lens_ref, dot(k_ref[rows, :], q_t[:, first:]))
        p = jnp.exp2(s * c - lse[:, first:])
        gp = dot(v_ref[rows, :], g_t[:, first:])
        probs[rows, first:] = p
        grads[rows, first:] = gp
        part = jnp.sum(p * gp, axis=0, keepdims=True)
        dkv_ref[rows, E:] = dot(p.astype(bf16), g[first:]).astype(bf16)
        if first:
            row_dot = jnp.concatenate([row_dot[:, :first], row_dot[:, first:] + part], axis=1)
        else:
            row_dot = row_dot + part
    dq = jnp.zeros((E, slot_len), f32)
    for kb in range(6):
        first = BLOCK if kb == 5 else 0
        rows = slice(kb * BLOCK, (kb + 1) * BLOCK)
        ds = (probs[rows, first:] * (grads[rows, first:] - row_dot[:, first:])).astype(bf16)
        dkv_ref[rows, :E] = (dot(ds, q[first:]) * score_scale).astype(bf16)
        out = dot(k_t[:, rows], ds)
        if first:
            dq = jnp.concatenate([dq[:, :first], dq[:, first:] + out], axis=1)
        else:
            dq = dq + out
    dq_ref[...] = (dq * score_scale).T.astype(bf16)


def attend_backward(parity, lens, queries, key_heads, value_heads, lse, grad_mixed):
    slot_len, width = queries.shape
    keys = key_heads.shape[0]
    heads = width // E // 2
    flops = 10 * heads * slot_len * keys * E
    column = lambda h: (0, 2 * h + parity)
    return pl.pallas_call(
        attend_backward_kernel,
        grid=(heads,),
        in_specs=[
            pl.BlockSpec(memory_space=pltpu.SMEM),
            pl.BlockSpec((slot_len, E), column),
            pl.BlockSpec((keys, E), column),
            pl.BlockSpec((keys, E), column),
            pl.BlockSpec((1, 1, slot_len), lambda h: (2 * h + parity, 0, 0)),
            pl.BlockSpec((slot_len, E), column),
        ],
        out_specs=[
            pl.BlockSpec((slot_len, E), lambda h: (0, h)),
            pl.BlockSpec((keys, 2 * E), lambda h: (0, h)),
        ],
        out_shape=[
            jax.ShapeDtypeStruct((slot_len, heads * E), bf16),
            jax.ShapeDtypeStruct((keys, heads * 2 * E), bf16),
        ],
        scratch_shapes=[pltpu.VMEM((keys, slot_len), f32), pltpu.VMEM((keys, slot_len), f32)],
        compiler_params=pltpu.CompilerParams(vmem_limit_bytes=VMEM_BYTES),
        cost_estimate=pl.CostEstimate(
            flops=2 * flops, bytes_accessed=0, transcendentals=heads * slot_len * keys
        ),
        name="attend_backward",
    )(lens, queries, key_heads, value_heads, lse, grad_mixed)


def live_rows(count_ref, rows, width):
    at = lax.broadcasted_iota(jnp.int32, (rows, width), 0) + pl.program_id(0) * rows
    return at < count_ref[0]


def mix_out_kernel(
    count_ref, inputs_ref, near_ref, far_ref, wo0, wo1, wo2, wo3, gain_ref, hidden_ref, normed_ref
):
    half = wo0.shape[0]
    near, far = near_ref[...], far_ref[...]
    attention = (
        dot(near[:, :half], wo0[...])
        + dot(near[:, half:], wo1[...])
        + dot(far[:, :half], wo2[...])
        + dot(far[:, half:], wo3[...])
    )
    live = live_rows(count_ref, *inputs_ref.shape)
    hidden = inputs_ref[...] + jnp.where(live, attention, 0.0)
    hidden_ref[...] = hidden
    normed_ref[...] = layer_norm(hidden, gain_ref[...]).astype(bf16)


def mix_out(count, inputs, near, far, weights, gain):
    slot_len, width = inputs.shape
    rows = 256
    row = lambda g: (g, 0)
    same = lambda g: (0, 0)
    return pl.pallas_call(
        mix_out_kernel,
        grid=(slot_len // rows,),
        in_specs=[
            pl.BlockSpec(memory_space=pltpu.SMEM),
            pl.BlockSpec((rows, width), row),
            pl.BlockSpec((rows, near.shape[1]), row),
            pl.BlockSpec((rows, far.shape[1]), row),
        ]
        + [pl.BlockSpec(w.shape, same) for w in weights]
        + [pl.BlockSpec((1, width), same)],
        out_specs=[pl.BlockSpec((rows, width), row), pl.BlockSpec((rows, width), row)],
        out_shape=[
            jax.ShapeDtypeStruct((slot_len, width), f32),
            jax.ShapeDtypeStruct((slot_len, width), bf16),
        ],
        compiler_params=pltpu.CompilerParams(vmem_limit_bytes=VMEM_BYTES),
        cost_estimate=pl.CostEstimate(
            flops=2 * slot_len * width * width, bytes_accessed=14 * slot_len * width, transcendentals=0
        ),
        name="mix_out",
    )(count, inputs, near, far, *weights, gain)


def norm_input_grad(values, gain, grad):
    mean = jnp.mean(values, axis=-1, keepdims=True)
    centred = values - mean
    scale = lax.rsqrt(jnp.mean(centred * centred, axis=-1, keepdims=True) + epsilon)
    unit = centred * scale
    grad = grad * gain
    shift = jnp.mean(grad, axis=-1, keepdims=True)
    slope = jnp.mean(grad * unit, axis=-1, keepdims=True)
    return scale * (grad - shift - unit * slope)


def back_norm_kernel(
    count_ref, own_ref, core_ref, far_ref, hidden_ref, out_grad_ref, gain_ref, grad_ref, live_ref
):
    grad = own_ref[...] + core_ref[...].astype(f32) + far_ref[...].astype(f32)
    grad = out_grad_ref[...] + norm_input_grad(hidden_ref[...], gain_ref[...], grad)
    grad_ref[...] = grad
    live = live_rows(count_ref, *grad.shape)
    live_ref[...] = jnp.where(live, grad, 0.0).astype(bf16)


def back_norm(count, own, core, far, hidden, out_grad, gain):
    slot_len, width = hidden.shape
    rows = 128
    row = lambda g: (g, 0)
    block = pl.BlockSpec((rows, width), row)
    return pl.pallas_call(
        back_norm_kernel,
        grid=(slot_len // rows,),
        in_specs=[pl.BlockSpec(memory_space=pltpu.SMEM)]
        + [block] * 5
        + [pl.BlockSpec((1, width), lambda g: (0, 0))],
        out_specs=[block, block],
        out_shape=[
            jax.ShapeDtypeStruct((slot_len, width), f32),
            jax.ShapeDtypeStruct((slot_len, width), bf16),
        ],
        compiler_params=pltpu.CompilerParams(vmem_limit_bytes=VMEM_BYTES),
        cost_estimate=pl.CostEstimate(
            flops=20 * slot_len * width, bytes_accessed=22 * slot_len * width, transcendentals=0
        ),
        name="back_norm",
    )(count, own, core, far, hidden, out_grad, gain)


def grad_inputs_kernel(*refs):
    dq, dkv, refs = refs[:4], refs[4:8], refs[8:]
    wq, wk, wv, refs = refs[:4], refs[4:8], refs[8:12], refs[12:]
    inputs_ref, grad_hidden_ref, gain_ref, out_ref = refs
    grad = jnp.zeros(out_ref.shape, f32)
    for r in range(4):
        first, second = 2 * (r // 2), 2 * (r // 2) + 1
        q_cut = slice((r % 2) * E, (r % 2 + 1) * E)
        k_cut = slice((r % 2) * 2 * E, (r % 2) * 2 * E + E)
        v_cut = slice((r % 2) * 2 * E + E, (r % 2 + 1) * 2 * E)
        for pieces, cut, weight in ((dq, q_cut, wq), (dkv, k_cut, wk), (dkv, v_cut, wv)):
            both_heads = jnp.concatenate([pieces[first][:, cut], pieces[second][:, cut]], axis=1)
            grad = grad + dot_nt(both_heads, weight[r][...])
    out_ref[...] = grad_hidden_ref[...] + norm_input_grad(inputs_ref[...], gain_ref[...], grad)


def grad_inputs(dq, dkv, wq, wk, wv, inputs, grad_hidden, gain):
    slot_len, width = inputs.shape
    rows = 256
    row = lambda g: (g, 0)
    same = lambda g: (0, 0)
    skip = (dkv[0].shape[0] - slot_len) // rows
    block = pl.BlockSpec((rows, width), row)
    return pl.pallas_call(
        grad_inputs_kernel,
        grid=(slot_len // rows,),
        in_specs=[pl.BlockSpec((rows, d.shape[1]), row) for d in dq]
        + [pl.BlockSpec((rows, d.shape[1]), lambda g: (skip + g, 0)) for d in dkv]
        + [pl.BlockSpec(w.shape, same) for w in (*wq, *wk, *wv)]
        + [block, block, pl.BlockSpec((1, width), same)],
        out_specs=block,
        out_shape=jax.ShapeDtypeStruct((slot_len, width), f32),
        compiler_params=pltpu.CompilerParams(vmem_limit_bytes=VMEM_BYTES),
        cost_estimate=pl.CostEstimate(
            flops=6 * slot_len * width * width, bytes_accessed=20 * slot_len * width, transcendentals=0
        ),
        name="grad_inputs",
    )(*dq, *dkv, *wq, *wk, *wv, inputs, grad_hidden, gain)


def swap_head(value, mask):
    size = lax.axis_size("head")
    return lax.ppermute(value, "head", [(i, i ^ mask) for i in range(size)])


def swap_dp(value, mask):
    size = lax.axis_size("dp")
    return lax.ppermute(value, "dp", [(i, i ^ mask) for i in range(size)])


def has(index, mask):
    return (index & mask) != 0


def both(flag, own, other, axis):
    return jnp.stack([jnp.where(flag, other, own), jnp.where(flag, own, other)], axis=axis)


def meet(*values):
    flat, tree = jax.tree.flatten(values)
    return jax.tree.unflatten(tree, lax.optimization_barrier(flat))


def gather_step(value, masks, n):
    return (value, swap_dp(value, masks[n]))


def gather_settle(pair, masks, n):
    return both(has(lax.axis_index("dp"), masks[n]), *pair, n)


def gather_early(value, masks):
    for n in range(len(masks) - 3):
        value = gather_settle(gather_step(value, masks, n), masks, n)
    return gather_step(value, masks, len(masks) - 3)


def scatter_split(value, masks, n):
    flag = has(lax.axis_index("dp"), masks[n])
    low = lax.index_in_dim(value, 0, n, keepdims=False)
    high = lax.index_in_dim(value, 1, n, keepdims=False)
    return jnp.where(flag, high, low), jnp.where(flag, low, high)


def scatter_step(value, masks, n):
    kept, sent = scatter_split(value, masks, n)
    return (kept, swap_dp(sent, masks[n]))


def scatter_settle(pair):
    return (pair[0].astype(f32) + pair[1].astype(f32)).astype(bf16)


def scatter_late(value, masks):
    for n in reversed(range(1, len(masks) - 2)):
        value = scatter_settle(scatter_step(value, masks, n))
    return scatter_step(value, masks, 0)


def cut_bits(value, masks):
    return value.reshape((2,) * len(masks) + value.shape[1:])


def cut_in_kernel(in_ref, out_ref):
    heads, units = out_ref.shape[0], E
    head = lax.axis_index("head")
    for r in range(heads):
        other = jnp.bitwise_xor(head, r)
        for i in range(out_ref.shape[2] // units):
            source = pl.multiple_of((i * heads + other) * units, units)
            out_ref[r, :, i * units : (i + 1) * units] = in_ref[:, pl.ds(source, units)]


def cut_in(w_in, heads, dps):
    rows, units = w_in.shape[0], w_in.shape[1] // (heads * dps)
    if units == E:
        return pl.pallas_call(
            cut_in_kernel,
            in_specs=[vmem()],
            out_specs=vmem(),
            out_shape=jax.ShapeDtypeStruct((heads, rows, dps * units), bf16),
            name="cut_in",
        )(w_in)
    head = lax.axis_index("head")
    cut = w_in.reshape(rows, dps, heads, units)
    return jnp.stack(
        [
            lax.dynamic_index_in_dim(cut, head ^ r, 2, keepdims=False).reshape(rows, dps * units)
            for r in range(heads)
        ]
    )


def shards(
    inputs,
    memory,
    compressed,
    counts,
    mem_lens,
    cmem_lens,
    norm_gain,
    w_query,
    w_key,
    w_value,
    w_output,
    ffn_gain,
    w_in,
    w_out,
    w_conv,
    out_grad,
    comp_grad,
):
    slot_len, width = inputs.shape[1:]
    heads, dps = lax.axis_size("head"), lax.axis_size("dp")
    masks = [1 << b for b in reversed(range(dps.bit_length() - 1))]
    bits = len(masks)
    group = memory.shape[0]
    head_at, dp_at = lax.axis_index("head"), lax.axis_index("dp")
    head_width = w_query.shape[1]
    new_rows = comp_grad.shape[1]
    conv_cols = width // heads
    count = lax.dynamic_slice_in_dim(counts, head_at, 1)
    lens = lax.dynamic_index_in_dim(jnp.stack([cmem_lens, mem_lens]), head_at, 1, keepdims=False)

    gains = jnp.stack([norm_gain, ffn_gain]).astype(f32)
    opened = opening(
        count,
        cut_in(w_in, heads, dps),
        w_conv,
        comp_grad[0],
        out_grad[0],
        gains,
        (w_query, w_key, w_value, w_output),
    )
    in_rows, conv_rows, comp_cot, gains_all, grad_ffn, gf_core = opened[:6]
    wq, wk, wv, wo = ([own, got] for own, got in zip((w_query, w_key, w_value, w_output), opened[6:]))
    gains_all = gains_all.transpose(1, 0, 2).reshape(2, width)
    gain_one, gain_two = gains_all[0:1], gains_all[1:2]
    w_out_rows = w_out
    (in_rows, conv_rows, comp_cot, grad_ffn, gf_core, wq, wk, wv, wo, gain_one, gain_two, memory) = meet(
        in_rows, conv_rows, comp_cot, grad_ffn, gf_core, wq, wk, wv, wo, gain_one, gain_two, memory
    )

    wk_x = swap_head(wk[0], 2)
    in_step = gather_early(in_rows.reshape(-1, in_rows.shape[2]), masks)
    key_rows, q_near, k_near, v_near = project_first(
        head_at[None], compressed, memory, inputs, gain_one, (*wq, *wk, *wv)
    )
    (wk_x, in_step, key_rows, q_near, k_near, v_near, wv, w_out_rows) = meet(
        wk_x, in_step, key_rows, q_near, k_near, v_near, wv, w_out_rows
    )

    wv_x = swap_head(wv[0], 2)
    in_step = gather_step(gather_settle(in_step, masks, bits - 3), masks, bits - 2)
    mixed_near, lse_near = attend_forward(lens, q_near, k_near, v_near)
    (wv_x, in_step, mixed_near, lse_near, wq, wk_x, w_out_rows, memory, comp_cot) = meet(
        wv_x, in_step, mixed_near, lse_near, wq, wk_x, w_out_rows, memory, comp_cot
    )

    wq_x = swap_head(wq[0], 2)
    wk += [wk_x, swap_head(wk_x, 1)]
    wv += [wv_x, swap_head(wv_x, 1)]
    in_all = gather_settle(in_step, masks, bits - 2)
    in_low = swap_dp(in_all[0], masks[-1])
    out_step = gather_early(w_out_rows, masks)
    live = jnp.minimum(counts, mem_lens)
    pad_rows = comp_cot.shape[1]
    source = jnp.arange(memory.shape[1], dtype=jnp.int32)
    evicted, grad_conv = [], []
    for tap in range(3):
        picked = 3 * jnp.arange(pad_rows, dtype=jnp.int32) + tap
        pick = (
            (source[None, None, :] == picked[None, :, None])
            & (source[None, None, :] < live[:, None, None])
            & (source < slot_len)[None, None, :]
        ).astype(bf16)
        rows = jnp.einsum("gcr,grd->gcd", pick, memory, preferred_element_type=f32).astype(bf16)
        evicted.append(rows.reshape(group * pad_rows, width))
        grad_conv.append(
            dot_tn(evicted[tap], comp_cot.reshape(group * pad_rows, conv_cols)).astype(bf16)
        )
    (wq_x, wk, wv, in_all, in_low, out_step, evicted, grad_conv, wo) = meet(
        wq_x, wk, wv, in_all, in_low, out_step, evicted, grad_conv, wo
    )

    wo_x = swap_head(wo[0], 2)
    wq += [wq_x, swap_head(wq_x, 1)]
    in_high = swap_dp(in_all[1], masks[-1])
    out_step = gather_step(gather_settle(out_step, masks, bits - 3), masks, bits - 2)
    q_far, k_far, v_far = project_second(key_rows, (*wq[2:], *wk[2:], *wv[2:]))
    (wo_x, wq, in_high, out_step, q_far, k_far, v_far, grad_ffn, conv_rows) = meet(
        wo_x, wq, in_high, out_step, q_far, k_far, v_far, grad_ffn, conv_rows
    )

    gf_x = swap_head(grad_ffn, 2)
    wo += [wo_x, swap_head(wo_x, 1)]
    out_all = gather_settle(out_step, masks, bits - 2)
    out_low = swap_dp(out_all[0], masks[-1])
    conv_step = gather_early(conv_rows, masks)
    mixed_far, lse_far = attend_forward(lens, q_far, k_far, v_far)
    w_in_own = gather_settle((in_all, jnp.stack([in_low, in_high])), masks, bits - 1)
    w_in_own = w_in_own.reshape(width, -1)
    (wo, out_all, out_low, conv_step, mixed_far, lse_far, w_in_own) = meet(
        wo, out_all, out_low, conv_step, mixed_far, lse_far, w_in_own
    )

    out_high = swap_dp(out_all[1], masks[-1])
    conv_step = gather_step(gather_settle(conv_step, masks, bits - 3), masks, bits - 2)
    hidden, normed_two = mix_out(count, inputs[0], mixed_near, mixed_far, wo, gain_two)
    (gf_x, out_high, conv_step, hidden, normed_two) = meet(
        gf_x, out_high, conv_step, hidden, normed_two
    )

    n2_x = swap_head(normed_two, 2)
    n2_core = swap_head(normed_two, 1)
    gf_diag = swap_head(gf_x, 1)
    conv_all = gather_settle(conv_step, masks, bits - 2)
    conv_step = gather_step(conv_all, masks, bits - 1)
    w_out_own = gather_settle((out_all, jnp.stack([out_low, out_high])), masks, bits - 1)
    w_out_own = w_out_own.reshape(-1, width)

    def feed_forward(tokens, cot):
        inner = dot(tokens, w_in_own)
        activated = jax.nn.gelu(inner).astype(bf16)
        grad_act = dot_nt(cot, w_out_own)
        grad_inner = jax.vjp(jax.nn.gelu, inner)[1](grad_act)[0].astype(bf16)
        return activated, grad_inner, dot_nt(grad_inner, w_in_own)

    n2_near = jnp.concatenate([normed_two, n2_core])
    gf_near = jnp.concatenate([grad_ffn, gf_core])
    act_near, gi_near, gn_near = feed_forward(n2_near, gf_near)
    gn_own, gn_sent = gn_near[:slot_len], gn_near[slot_len:].astype(bf16)
    (n2_x, gf_diag, conv_step, act_near, gi_near, gn_own, gn_sent, grad_conv) = meet(
        n2_x, gf_diag, conv_step, act_near, gi_near, gn_own, gn_sent, grad_conv
    )

    n2_far = jnp.concatenate([n2_x, swap_head(n2_x, 1)])
    gf_far = jnp.concatenate([gf_x, gf_diag])
    gn_core = swap_head(gn_sent, 1)
    conv_own = gather_settle(conv_step, masks, bits - 1).reshape(-1, conv_cols)
    grad_conv = jnp.concatenate(grad_conv).reshape(dps, -1, conv_cols)
    conv_back = scatter_step(cut_bits(grad_conv, masks), masks, bits - 1)
    act_far, gi_far, gn_far = feed_forward(n2_far, gf_far)
    gn_far_core = swap_head(gn_far[slot_len:].astype(bf16), 1)
    gn_far = (gn_far[:slot_len] + gn_far_core.astype(f32)).astype(bf16)
    (n2_far, gf_far, gn_core, conv_own, conv_back, act_far, gi_far, gn_far) = meet(
        n2_far, gf_far, gn_core, conv_own, conv_back, act_far, gi_far, gn_far
    )

    gn_back = swap_head(gn_far, 2)
    conv_back = scatter_step(scatter_settle(conv_back), masks, bits - 2)
    out_far = dot(act_far, w_out_own)
    out_far_core = swap_head(out_far[slot_len:].astype(bf16), 1)
    out_far = (out_far[:slot_len] + out_far_core.astype(f32)).astype(bf16)
    grad_w_out = (dot_tn(act_near, gf_near) + dot_tn(act_far, gf_far)).astype(bf16)
    grad_w_in = (dot_tn(n2_near, gi_near) + dot_tn(n2_far, gi_far)).astype(bf16)
    out_near = dot(act_near, w_out_own)
    out_core = swap_head(out_near[slot_len:].astype(bf16), 1)
    out_own = out_near[:slot_len]
    conv_tap = conv_own.reshape(3, width, conv_cols)
    new_cols = sum(dot(evicted[tap], conv_tap[tap]) for tap in range(3)).astype(bf16)
    (gn_back, conv_back, out_far, grad_w_out, grad_w_in, out_own, out_core, new_cols) = meet(
        gn_back, conv_back, out_far, grad_w_out, grad_w_in, out_own, out_core, new_cols
    )

    out_back = swap_head(out_far, 2)
    w_out_back = scatter_step(
        cut_bits(grad_w_out.reshape(dps, -1, width), masks), masks, bits - 1
    )
    conv_back = scatter_late(scatter_settle(conv_back), masks)
    grad_hidden, grad_attention = back_norm(
        count, gn_own, gn_core, gn_back, hidden, out_grad[0], gain_two
    )
    gm_near = jnp.concatenate([dot_nt(grad_attention, w) for w in wo[:2]], axis=1).astype(bf16)
    gm_far = jnp.concatenate([dot_nt(grad_attention, w) for w in wo[2:]], axis=1).astype(bf16)
    go_near = dot_tn(mixed_near, grad_attention)
    go_far = dot_tn(mixed_far, grad_attention)
    dq, dkv = [None] * 4, [None] * 4
    dq[0], dkv[0] = attend_backward(0, lens, q_near, k_near, v_near, lse_near, gm_near)
    dq[2], dkv[2] = attend_backward(0, lens, q_far, k_far, v_far, lse_far, gm_far)
    go_core = swap_head(jnp.concatenate([go_near[head_width:], go_far[head_width:]]).astype(bf16), 1)
    go_near = go_near[:head_width] + go_core[:head_width].astype(f32)
    go_far = (go_far[:head_width] + go_core[head_width:].astype(f32)).astype(bf16)
    (out_back, w_out_back, conv_back, grad_hidden, gm_near, gm_far, go_near, go_far, dq, dkv, grad_w_in) = meet(
        out_back, w_out_back, conv_back, grad_hidden, gm_near, gm_far, go_near, go_far, dq, dkv, grad_w_in
    )

    def head_terms(half, parity):
        n = 2 * half + parity
        of_kv = dot_tn(key_rows, dkv[n])
        of_q = dot_tn(key_rows[key_rows.shape[0] - slot_len :], dq[n])
        return [
            jnp.concatenate(
                [of_kv[:, 2 * E * r : 2 * E * (r + 1)], of_q[:, E * r : E * (r + 1)]], axis=1
            )
            for r in range(2)
        ]

    def to_chip(own, sent):
        return own + swap_head(sent.astype(bf16), 1).astype(f32)

    go_back = swap_head(go_far, 2)
    w_in_back = scatter_step(
        cut_bits(grad_w_in.reshape(dps, -1, grad_w_in.shape[1]), masks), masks, bits - 1
    )
    w_out_back = scatter_step(scatter_settle(w_out_back), masks, bits - 2)
    grad_conv = scatter_settle(conv_back)
    a_far = to_chip(*head_terms(1, 0)).astype(bf16)
    a_near = to_chip(*head_terms(0, 0))
    dq[1], dkv[1] = attend_backward(1, lens, q_near, k_near, v_near, lse_near, gm_near)
    (go_back, w_in_back, w_out_back, grad_conv, a_far, a_near, dq, dkv) = meet(
        go_back, w_in_back, w_out_back, grad_conv, a_far, a_near, dq, dkv
    )

    a_back = swap_head(a_far, 2)
    w_out_back = scatter_late(scatter_settle(w_out_back), masks)
    w_in_back = scatter_step(scatter_settle(w_in_back), masks, bits - 2)
    go = (go_near + go_back.astype(f32)).astype(bf16)
    go_step = scatter_step(cut_bits(go.reshape(dps, -1, width), masks), masks, bits - 1)
    dq[3], dkv[3] = attend_backward(1, lens, q_far, k_far, v_far, lse_far, gm_far)
    b_far = to_chip(*head_terms(1, 1)).astype(bf16)
    (a_back, w_out_back, w_in_back, go_step, dq, dkv, b_far) = meet(
        a_back, w_out_back, w_in_back, go_step, dq, dkv, b_far
    )

    def by_rows(value):
        return cut_bits(value.reshape(dps, -1, value.shape[1]), masks)

    a_step = scatter_step(by_rows((a_near + a_back.astype(f32)).astype(bf16)), masks, bits - 1)
    b_back = swap_head(b_far, 2)
    grad_w_out = scatter_settle(w_out_back)
    w_in_back = scatter_late(scatter_settle(w_in_back), masks)
    go_step = scatter_step(scatter_settle(go_step), masks, bits - 2)
    b_near = to_chip(*head_terms(0, 1))
    (a_step, b_back, grad_w_out, w_in_back, go_step, b_near) = meet(
        a_step, b_back, grad_w_out, w_in_back, go_step, b_near
    )

    a_step = scatter_step(scatter_settle(a_step), masks, bits - 2)
    b_step = scatter_step(by_rows((b_near + b_back.astype(f32)).astype(bf16)), masks, bits - 1)
    go_step = scatter_late(scatter_settle(go_step), masks)
    grad_w_in = scatter_settle(w_in_back)
    input_grad = grad_inputs(dq, dkv, wq, wk, wv, inputs[0], grad_hidden, gain_one)
    (a_step, b_step, go_step, grad_w_in, input_grad, grad_w_out) = meet(
        a_step, b_step, go_step, grad_w_in, input_grad, grad_w_out
    )

    a_step = scatter_late(scatter_settle(a_step), masks)
    b_step = scatter_step(scatter_settle(b_step), masks, bits - 2)
    go_step = gather_early(scatter_settle(go_step), masks)
    new_compressed, grad_w_in, grad_conv = closing(
        new_cols.reshape(group, -1, conv_cols),
        grad_w_in.reshape(heads, w_in.shape[0], -1),
        grad_conv.reshape(heads, w_conv.shape[0], conv_cols),
        new_rows,
    )
    row_pos = jnp.arange(slot_len, dtype=jnp.int32)
    row_live = (row_pos < count).astype(f32)[:, None]
    outputs = hidden + row_live * (out_own + out_core.astype(f32) + out_back.astype(f32))
    (a_step, b_step, go_step, new_compressed, grad_w_in, grad_conv, outputs) = meet(
        a_step, b_step, go_step, new_compressed, grad_w_in, grad_conv, outputs
    )

    own_rows = width // dps

    def gain_part(rows, parity):
        cut = slice(parity * E, (parity + 1) * E)
        terms = 0.0
        for n, weight in enumerate((w_key, w_value, w_query)):
            own = lax.dynamic_slice_in_dim(weight, dp_at * own_rows, own_rows, 0)[:, cut]
            grad = rows[:, n * E : (n + 1) * E].astype(f32)
            terms = terms + jnp.sum(grad * own.astype(f32), axis=1)
        return terms

    a_rows = scatter_settle(a_step)
    a_step = gather_early(a_rows, masks)
    b_step = scatter_late(scatter_settle(b_step), masks)
    go_step = gather_step(gather_settle(go_step, masks, bits - 3), masks, bits - 2)
    grad_w_in = (
        grad_w_in.reshape(heads, w_in.shape[0], dps, -1).transpose(1, 2, 0, 3).reshape(w_in.shape)
    )
    own_gain_two = lax.dynamic_slice_in_dim(
        gain_two[0], (dp_at * heads + head_at) * w_in.shape[0], w_in.shape[0]
    )
    grad_gain_two = jnp.sum(grad_w_in * w_in.astype(f32), axis=1) / own_gain_two
    (a_step, b_step, go_step, a_rows, grad_w_in) = meet(a_step, b_step, go_step, a_rows, grad_w_in)

    b_rows = scatter_settle(b_step)
    b_step = gather_early(b_rows, masks)
    a_step = gather_step(gather_settle(a_step, masks, bits - 3), masks, bits - 2)
    go_step = gather_step(gather_settle(go_step, masks, bits - 2), masks, bits - 1)
    gain_terms = gain_part(a_rows, 0) + gain_part(b_rows, 1)
    gain_terms = gain_terms + swap_head(gain_terms, 1)
    gain_terms = gain_terms + swap_head(gain_terms, 2)
    grad_gain_one = lax.dynamic_slice_in_dim(
        gain_terms, head_at * norm_gain.shape[0], norm_gain.shape[0]
    ) / norm_gain.astype(f32)
    (a_step, b_step, go_step, grad_gain_one) = meet(a_step, b_step, go_step, grad_gain_one)

    a_step = gather_step(gather_settle(a_step, masks, bits - 2), masks, bits - 1)
    b_step = gather_step(gather_settle(b_step, masks, bits - 3), masks, bits - 2)
    grad_out = gather_settle(go_step, masks, bits - 1).reshape(w_output.shape).astype(f32)
    (a_step, b_step, grad_out) = meet(a_step, b_step, grad_out)

    b_step = gather_step(gather_settle(b_step, masks, bits - 2), masks, bits - 1)
    a_all = gather_settle(a_step, masks, bits - 1).reshape(width, -1).astype(f32)
    (b_step, a_all) = meet(b_step, a_all)
    b_all = gather_settle(b_step, masks, bits - 1).reshape(width, -1).astype(f32)
    grad_key, grad_value, grad_query = (
        jnp.concatenate([a_all[:, n * E : (n + 1) * E], b_all[:, n * E : (n + 1) * E]], axis=1)
        for n in range(3)
    )

    return (
        outputs[None],
        input_grad[None],
        new_compressed[None],
        grad_gain_one,
        grad_query,
        grad_key,
        grad_value,
        grad_out,
        grad_gain_two,
        grad_w_in,
        grad_w_out.reshape(w_out.shape).astype(f32),
        grad_conv,
    )


def solution(mesh):
    whole = P(("dp", "head"), None, None)
    rows = P(("dp", "head"), None)
    vector = P(("dp", "head"))
    columns = P(None, "head")
    placed = (
        whole,
        P("dp", None, None),
        P("dp", None, None),
        P("dp"),
        P("dp"),
        P("dp"),
        vector,
        columns,
        columns,
        columns,
        P("head", None),
        vector,
        rows,
        rows,
        rows,
        whole,
        whole,
    )
    return jax.shard_map(
        shards,
        mesh=mesh,
        in_specs=placed,
        out_specs=(
            whole,
            whole,
            whole,
            vector,
            columns,
            columns,
            columns,
            P("head", None),
            vector,
            rows,
            rows,
            rows,
        ),
        check_vma=False,
    )
```

```python
import functools

import jax
import jax.numpy as jnp
from jax import lax
from jax.experimental import pallas as pl
from jax.experimental.pallas import tpu as pltpu
from jax.sharding import PartitionSpec as P

E = 128
BLOCK = 256
epsilon = 1e-05
masked_value = -1e30
score_scale = E ** (-0.5)
log2e = 1.4426950408889634
bf16 = jnp.bfloat16
f32 = jnp.float32
VMEM_BYTES = 30 * 2**20
MESH = pl.DeviceIdType.MESH


def dot(left, right):
    return jnp.dot(left, right, preferred_element_type=f32)


def dot_tn(left, right):
    return lax.dot_general(left, right, (((0,), (0,)), ((), ())), preferred_element_type=f32)


def dot_nt(left, right):
    return lax.dot_general(left, right, (((1,), (1,)), ((), ())), preferred_element_type=f32)


def layer_norm(values, gain_vec):
    row_mean = jnp.mean(values, axis=-1, keepdims=True)
    centred = values - row_mean
    variance = jnp.mean(centred * centred, axis=-1, keepdims=True)
    return centred * lax.rsqrt(variance + epsilon) * gain_vec


def vmem():
    return pl.BlockSpec(memory_space=pltpu.VMEM)


def anywhere():
    return pl.BlockSpec(memory_space=pl.ANY)


def opening_kernel(
    heads, dps, count_ref, w_in_ref, w_conv_ref, cot_ref, out_grad_ref, gains_ref, *refs
):
    weights, refs = refs[:4], refs[4:]
    in_out, conv_out, cot_out, gains_out, gf_out, gf_core = refs[:6]
    weights_core = refs[6:10]
    in_send, conv_send, cot_send, sems = refs[10:]
    head = lax.axis_index("head")
    dp = lax.axis_index("dp")

    def head_device(r):
        return (dp, jnp.bitwise_xor(head, r))

    def dp_device(r):
        return (lax.rem(dp + r, dps), head)

    barrier = pltpu.get_barrier_semaphore()
    for r in range(1, heads):
        pl.semaphore_signal(barrier, inc=1, device_id=head_device(r), device_id_type=MESH)
    for r in range(1, dps):
        pl.semaphore_signal(barrier, inc=1, device_id=dp_device(r), device_id_type=MESH)
    pl.semaphore_wait(barrier, heads + dps - 2)

    started = []

    def send(source, target, device):
        n = len(started)
        copy = pltpu.make_async_remote_copy(
            src_ref=source,
            dst_ref=target,
            send_sem=sems.at[0, n],
            recv_sem=sems.at[1, n],
            device_id=device,
            device_id_type=MESH,
        )
        copy.start()
        started.append(copy)
        return copy

    at = dp * heads + head
    gains_out[at] = gains_ref[...]
    gain_copies = [
        send(gains_out.at[at], gains_out.at[at], head_device(r)) for r in range(1, heads)
    ]
    for mine, other in zip(weights, weights_core):
        send(mine, other, head_device(1))
    columns = w_conv_ref.shape[1] // heads
    new_rows = cot_ref.shape[0]
    pad_rows = cot_send.shape[1]
    for r in range(heads):
        other = jnp.bitwise_xor(head, r)
        cut = pl.ds(pl.multiple_of(other * columns, columns), columns)
        conv_piece = w_conv_ref[:, cut]
        cot_piece = jnp.concatenate(
            [cot_ref[:, cut], jnp.zeros((pad_rows - new_rows, columns), f32)], axis=0
        ).astype(bf16)
        if r == 0:
            in_out[head] = w_in_ref[0]
            conv_out[head] = conv_piece
            cot_out[head] = cot_piece
        else:
            in_send[r - 1] = w_in_ref[r]
            conv_send[r - 1] = conv_piece
            cot_send[r - 1] = cot_piece
            send(in_send.at[r - 1], in_out.at[head], head_device(r))
            send(conv_send.at[r - 1], conv_out.at[head], head_device(r))
            send(cot_send.at[r - 1], cot_out.at[head], head_device(r))
    for copy in gain_copies:
        copy.wait_recv()
    block = gains_out.at[pl.ds(dp * heads, heads)]
    for r in range(1, dps):
        send(block, block, dp_device(r))
    row = lax.broadcasted_iota(jnp.int32, out_grad_ref.shape, 0)
    gf_out[...] = jnp.where(row < count_ref[0], out_grad_ref[...], 0.0).astype(bf16)
    send(gf_out, gf_core, head_device(1))
    for copy in started:
        copy.wait_send()
        if not any(copy is other for other in gain_copies):
            copy.wait_recv()


def opening(count, in_pieces, w_conv, comp_grad, out_grad, gains, weights):
    heads, dps = lax.axis_size("head"), lax.axis_size("dp")
    columns = w_conv.shape[1] // heads
    new_rows = comp_grad.shape[0]
    pad_rows = (new_rows + 15) // 16 * 16
    shape = jax.ShapeDtypeStruct
    in_all = shape(in_pieces.shape, bf16)
    conv_all = shape((heads, w_conv.shape[0], columns), bf16)
    cot_all = shape((heads, pad_rows, columns), bf16)
    grad = shape(out_grad.shape, bf16)
    copies = 5 + 4 * (heads - 1) + dps - 1
    return pl.pallas_call(
        functools.partial(opening_kernel, heads, dps),
        in_specs=[pl.BlockSpec(memory_space=pltpu.SMEM)] + [vmem()] * 5 + [anywhere()] * 4,
        out_specs=[vmem()] * 6 + [anywhere()] * 4,
        out_shape=[in_all, conv_all, cot_all, shape((dps * heads,) + gains.shape, f32), grad, grad]
        + [shape(w.shape, bf16) for w in weights],
        scratch_shapes=[
            pltpu.VMEM((heads - 1,) + in_all.shape[1:], bf16),
            pltpu.VMEM((heads - 1,) + conv_all.shape[1:], bf16),
            pltpu.VMEM((heads - 1,) + cot_all.shape[1:], bf16),
            pltpu.SemaphoreType.DMA((2, copies)),
        ],
        compiler_params=pltpu.CompilerParams(
            collective_id=0, has_side_effects=True, vmem_limit_bytes=VMEM_BYTES
        ),
        name="opening",
    )(count, in_pieces, w_conv, comp_grad, out_grad, gains, *weights)


def project_first_kernel(
    which, cmem_ref, mem_ref, inputs_ref, gain_ref, wq0, wq1, wk0, wk1, wv0, wv1, rows_ref,
    q_ref, k_ref, v_ref,
):
    step = pl.program_id(0)
    third = pl.num_programs(0) // 3
    gain = gain_ref[...]
    half = wk0.shape[1]

    def keyed(values):
        normed = layer_norm(values, gain).astype(bf16)
        rows_ref[...] = normed
        k_ref[:, :half] = dot(normed, wk0[...]).astype(bf16)
        k_ref[:, half:] = dot(normed, wk1[...]).astype(bf16)
        v_ref[:, :half] = dot(normed, wv0[...]).astype(bf16)
        v_ref[:, half:] = dot(normed, wv1[...]).astype(bf16)
        return normed

    @pl.when(step < third)
    def _():
        keyed(cmem_ref[0].astype(f32))

    @pl.when((step >= third) & (step < 2 * third))
    def _():
        keyed(mem_ref[0].astype(f32))

    @pl.when(step >= 2 * third)
    def _():
        normed = keyed(inputs_ref[0])
        q_ref[:, :half] = dot(normed, wq0[...]).astype(bf16)
        q_ref[:, half:] = dot(normed, wq1[...]).astype(bf16)


def project_first(which, compressed, memory, inputs, gain, weights):
    slot_len, width = inputs.shape[1:]
    rows = 256
    third = slot_len // rows
    half = weights[0].shape[1]

    def at(first):
        return lambda g, s: (s[0], jnp.clip(g - first, 0, third - 1), 0)

    def slots(g, s):
        return (jnp.clip(g - 2 * third, 0, third - 1), 0)

    def same(g, s):
        return (0, 0)

    shape = jax.ShapeDtypeStruct
    keys = 3 * slot_len
    return pl.pallas_call(
        project_first_kernel,
        grid_spec=pltpu.PrefetchScalarGridSpec(
            num_scalar_prefetch=1,
            grid=(3 * third,),
            in_specs=[
                pl.BlockSpec((1, rows, width), at(0)),
                pl.BlockSpec((1, rows, width), at(third)),
                pl.BlockSpec((1, rows, width), lambda g, s: (0,) + slots(g, s)),
                pl.BlockSpec((1, width), same),
            ]
            + [pl.BlockSpec((width, half), same)] * 6,
            out_specs=[
                pl.BlockSpec((rows, width), lambda g, s: (g, 0)),
                pl.BlockSpec((rows, 2 * half), slots),
                pl.BlockSpec((rows, 2 * half), lambda g, s: (g, 0)),
                pl.BlockSpec((rows, 2 * half), lambda g, s: (g, 0)),
            ],
        ),
        out_shape=[
            shape((keys, width), bf16),
            shape((slot_len, 2 * half), bf16),
            shape((keys, 2 * half), bf16),
            shape((keys, 2 * half), bf16),
        ],
        compiler_params=pltpu.CompilerParams(vmem_limit_bytes=VMEM_BYTES),
        cost_estimate=pl.CostEstimate(
            flops=2 * (2 * keys + slot_len) * width * 2 * half,
            bytes_accessed=10 * slot_len * width * 2,
            transcendentals=0,
        ),
        name="project_first",
    )(which, compressed, memory, inputs, gain, *weights)


def project_second_kernel(rows_ref, wq0, wq1, wk0, wk1, wv0, wv1, q_ref, k_ref, v_ref):
    step = pl.program_id(0)
    third = pl.num_programs(0) // 3
    half = wk0.shape[1]
    normed = rows_ref[...]
    k_ref[:, :half] = dot(normed, wk0[...]).astype(bf16)
    k_ref[:, half:] = dot(normed, wk1[...]).astype(bf16)
    v_ref[:, :half] = dot(normed, wv0[...]).astype(bf16)
    v_ref[:, half:] = dot(normed, wv1[...]).astype(bf16)

    @pl.when(step >= 2 * third)
    def _():
        q_ref[:, :half] = dot(normed, wq0[...]).astype(bf16)
        q_ref[:, half:] = dot(normed, wq1[...]).astype(bf16)


def project_second(key_rows, weights):
    keys, width = key_rows.shape
    rows = 256
    steps = keys // rows
    third = steps // 3
    half = weights[0].shape[1]
    shape = jax.ShapeDtypeStruct

    def same(g):
        return (0, 0)

    return pl.pallas_call(
        project_second_kernel,
        grid=(steps,),
        in_specs=[pl.BlockSpec((rows, width), lambda g: (g, 0))]
        + [pl.BlockSpec((width, half), same)] * 6,
        out_specs=[
            pl.BlockSpec((rows, 2 * half), lambda g: (jnp.clip(g - 2 * third, 0, third - 1), 0)),
            pl.BlockSpec((rows, 2 * half), lambda g: (g, 0)),
            pl.BlockSpec((rows, 2 * half), lambda g: (g, 0)),
        ],
        out_shape=[
            shape((keys // 3, 2 * half), bf16),
            shape((keys, 2 * half), bf16),
            shape((keys, 2 * half), bf16),
        ],
        compiler_params=pltpu.CompilerParams(vmem_limit_bytes=VMEM_BYTES),
        cost_estimate=pl.CostEstimate(
            flops=2 * (2 * keys + keys // 3) * width * 2 * half,
            bytes_accessed=4 * keys * width,
            transcendentals=0,
        ),
        name="project_second",
    )(key_rows, *weights)


def masked_scores(kb, lens_ref, scores):
    rows = lax.broadcasted_iota(jnp.int32, scores.shape, 0)
    if kb < 4:
        limit = lens_ref[kb // 2] - (kb % 2) * BLOCK
        return jnp.where(rows < limit, scores, masked_value)
    columns = lax.broadcasted_iota(jnp.int32, scores.shape, 1)
    return jnp.where(rows <= columns, scores, masked_value)


def attend_forward_kernel(lens_ref, q_ref, k_ref, v_ref, mixed_ref, lse_ref, scores):
    slot_len = q_ref.shape[0]
    q_t = q_ref[...].T
    v_t = v_ref[...].T
    c = score_scale * log2e
    top = jnp.full((1, slot_len), masked_value, f32)
    for kb in range(6):
        first = BLOCK if kb == 5 else 0
        s = dot(k_ref[kb * BLOCK : (kb + 1) * BLOCK, :], q_t[:, first:])
        s = masked_scores(kb, lens_ref, s)
        scores[kb * BLOCK : (kb + 1) * BLOCK, first:] = s
        part = jnp.max(s, axis=0, keepdims=True)
        if first:
            top = jnp.concatenate([top[:, :first], jnp.maximum(top[:, first:], part)], axis=1)
        else:
            top = jnp.maximum(top, part)
    shift = top * c
    mixed = jnp.zeros((E, slot_len), f32)
    total = jnp.zeros((1, slot_len), f32)
    for kb in range(6):
        first = BLOCK if kb == 5 else 0
        p = jnp.exp2(scores[kb * BLOCK : (kb + 1) * BLOCK, first:] * c - shift[:, first:])
        part = jnp.sum(p, axis=0, keepdims=True)
        out = dot(v_t[:, kb * BLOCK : (kb + 1) * BLOCK], p.astype(bf16))
        if first:
            total = jnp.concatenate([total[:, :first], total[:, first:] + part], axis=1)
            mixed = jnp.concatenate([mixed[:, :first], mixed[:, first:] + out], axis=1)
        else:
            total = total + part
            mixed = mixed + out
    mixed_ref[...] = (mixed / total).T.astype(bf16)
    lse_ref[0] = shift + jnp.log2(total)


def attend_forward(lens, queries, key_heads, value_heads):
    slot_len, width = queries.shape
    keys = key_heads.shape[0]
    heads = width // E
    flops = 4 * heads * slot_len * keys * E
    column = lambda h: (0, h)
    return pl.pallas_call(
        attend_forward_kernel,
        grid=(heads,),
        in_specs=[
            pl.BlockSpec(memory_space=pltpu.SMEM),
            pl.BlockSpec((slot_len, E), column),
            pl.BlockSpec((keys, E), column),
            pl.BlockSpec((keys, E), column),
        ],
        out_specs=[
            pl.BlockSpec((slot_len, E), column),
            pl.BlockSpec((1, 1, slot_len), lambda h: (h, 0, 0)),
        ],
        out_shape=[
            jax.ShapeDtypeStruct((slot_len, width), bf16),
            jax.ShapeDtypeStruct((heads, 1, slot_len), f32),
        ],
        scratch_shapes=[pltpu.VMEM((keys, slot_len), f32)],
        compiler_params=pltpu.CompilerParams(vmem_limit_bytes=VMEM_BYTES),
        cost_estimate=pl.CostEstimate(
            flops=2 * flops, bytes_accessed=0, transcendentals=heads * slot_len * keys
        ),
        name="attend_forward",
    )(lens, queries, key_heads, value_heads)


def live_rows(count_ref, rows, width):
    at = lax.broadcasted_iota(jnp.int32, (rows, width), 0) + pl.program_id(0) * rows
    return at < count_ref[0]


def mix_out_kernel(
    count_ref, inputs_ref, near_ref, far_ref, wo0, wo1, wo2, wo3, gain_ref, hidden_ref, normed_ref
):
    half = wo0.shape[0]
    near, far = near_ref[...], far_ref[...]
    attention = (
        dot(near[:, :half], wo0[...])
        + dot(near[:, half:], wo1[...])
        + dot(far[:, :half], wo2[...])
        + dot(far[:, half:], wo3[...])
    )
    live = live_rows(count_ref, *inputs_ref.shape)
    hidden = inputs_ref[...] + jnp.where(live, attention, 0.0)
    hidden_ref[...] = hidden
    normed_ref[...] = layer_norm(hidden, gain_ref[...]).astype(bf16)


def mix_out(count, inputs, near, far, weights, gain):
    slot_len, width = inputs.shape
    rows = 256
    row = lambda g: (g, 0)
    same = lambda g: (0, 0)
    return pl.pallas_call(
        mix_out_kernel,
        grid=(slot_len // rows,),
        in_specs=[
            pl.BlockSpec(memory_space=pltpu.SMEM),
            pl.BlockSpec((rows, width), row),
            pl.BlockSpec((rows, near.shape[1]), row),
            pl.BlockSpec((rows, far.shape[1]), row),
        ]
        + [pl.BlockSpec(w.shape, same) for w in weights]
        + [pl.BlockSpec((1, width), same)],
        out_specs=[pl.BlockSpec((rows, width), row), pl.BlockSpec((rows, width), row)],
        out_shape=[
            jax.ShapeDtypeStruct((slot_len, width), f32),
            jax.ShapeDtypeStruct((slot_len, width), bf16),
        ],
        compiler_params=pltpu.CompilerParams(vmem_limit_bytes=VMEM_BYTES),
        cost_estimate=pl.CostEstimate(
            flops=2 * slot_len * width * width, bytes_accessed=14 * slot_len * width, transcendentals=0
        ),
        name="mix_out",
    )(count, inputs, near, far, *weights, gain)


def norm_input_grad(values, gain, grad):
    mean = jnp.mean(values, axis=-1, keepdims=True)
    centred = values - mean
    scale = lax.rsqrt(jnp.mean(centred * centred, axis=-1, keepdims=True) + epsilon)
    unit = centred * scale
    grad = grad * gain
    shift = jnp.mean(grad, axis=-1, keepdims=True)
    slope = jnp.mean(grad * unit, axis=-1, keepdims=True)
    return scale * (grad - shift - unit * slope)


def back_norm_kernel(
    count_ref, own_ref, core_ref, far_ref, hidden_ref, out_grad_ref, gain_ref, grad_ref, live_ref
):
    grad = own_ref[...] + core_ref[...].astype(f32) + far_ref[...].astype(f32)
    grad = out_grad_ref[...] + norm_input_grad(hidden_ref[...], gain_ref[...], grad)
    grad_ref[...] = grad
    live = live_rows(count_ref, *grad.shape)
    live_ref[...] = jnp.where(live, grad, 0.0).astype(bf16)


def back_norm(count, own, core, far, hidden, out_grad, gain):
    slot_len, width = hidden.shape
    rows = 128
    row = lambda g: (g, 0)
    block = pl.BlockSpec((rows, width), row)
    return pl.pallas_call(
        back_norm_kernel,
        grid=(slot_len // rows,),
        in_specs=[pl.BlockSpec(memory_space=pltpu.SMEM)]
        + [block] * 5
        + [pl.BlockSpec((1, width), lambda g: (0, 0))],
        out_specs=[block, block],
        out_shape=[
            jax.ShapeDtypeStruct((slot_len, width), f32),
            jax.ShapeDtypeStruct((slot_len, width), bf16),
        ],
        compiler_params=pltpu.CompilerParams(vmem_limit_bytes=VMEM_BYTES),
        cost_estimate=pl.CostEstimate(
            flops=20 * slot_len * width, bytes_accessed=22 * slot_len * width, transcendentals=0
        ),
        name="back_norm",
    )(count, own, core, far, hidden, out_grad, gain)


def backward_kernel(heads, masks, slot_len, keys, *refs):
    (lens_ref, q_near, k_near, v_near, gm_near, lse_near, q_far, k_far, v_far, gm_far, lse_far), refs = refs[:11], refs[11:]
    wq, wk, wv, refs = refs[:heads], refs[heads : 2 * heads], refs[2 * heads : 3 * heads], refs[3 * heads :]
    (gain_ref, go_near, go_far, out_part, new_ref, conv_ref, key_t_hbm, in_hbm, inputs_hbm, hidden_hbm), refs = refs[:10], refs[10:]
    (grad_out, sum_rows, input_grad_hbm, go_out, gain_out, in_got, new_got, conv_got), refs = refs[:8], refs[8:]
    (key_t, probs, grads, dkv, terms, own_terms, got_near, got_far, got_x), refs = refs[:9], refs[9:]
    bits = len(masks)
    in_kept, refs = refs[0], refs[1:]
    in_got_rs, refs = refs[:bits], refs[bits:]
    out_got_rs, refs = refs[: bits - 1], refs[bits - 1 :]
    go_core_near, go_core_far, go_x, refs = refs[0], refs[1], refs[2], refs[3:]
    go_rs, refs = refs[:bits], refs[bits:]
    sum_rs, refs = refs[:bits], refs[bits:]
    grad_normed, gain_terms, sems = refs
    head = lax.axis_index("head")
    dp = lax.axis_index("dp")
    flags = [jnp.where(jnp.bitwise_and(dp, mask) != 0, 1, 0) for mask in masks]

    def head_device(r):
        return (dp, jnp.bitwise_xor(head, r))

    def dp_device(n):
        return (jnp.bitwise_xor(dp, masks[n]), head)

    barrier = pltpu.get_barrier_semaphore()
    for r in range(1, heads):
        pl.semaphore_signal(barrier, inc=1, device_id=head_device(r), device_id_type=MESH)
    for n in range(bits):
        pl.semaphore_signal(barrier, inc=1, device_id=dp_device(n), device_id_type=MESH)
    pl.semaphore_wait(barrier, heads - 1 + bits)

    slots = {}

    def remote(name, source, target, device, part=0):
        if name not in slots:
            slots[name] = 2 * len(slots)
        at = slots[name] + part
        return pltpu.make_async_remote_copy(
            src_ref=source,
            dst_ref=target,
            send_sem=sems.at[0, at],
            recv_sem=sems.at[1, at],
            device_id=device,
            device_id_type=MESH,
        )

    def local(name, source, target):
        if name not in slots:
            slots[name] = 2 * len(slots)
        return pltpu.make_async_copy(source, target, sems.at[0, slots[name]])

    whole = slice(None)

    def rs_copy(name, held, got, n, part=0):
        return remote(
            f"{name}{n}", held.at[(whole,) * n + (1 - flags[n],)], got, dp_device(n), part
        )

    def rs_add(held, got, n):
        for at in range(2**n):
            index = tuple((at >> (n - 1 - b)) & 1 for b in range(n))
            mine = held[index + (flags[n],)]
            got[index] = (got[index].astype(f32) + mine.astype(f32)).astype(bf16)

    def ag_copy(name, block, n, part=0):
        region = block.at[(whole,) * n + tuple(flags[n:])]
        return remote(f"{name}{n}", region, region, dp_device(n), part)

    load_keys = local("load_keys", key_t_hbm, key_t)
    load_keys.start()
    in_y = remote("in_rs", in_hbm.at[(whole,) * (bits - 1) + (1 - flags[bits - 1],)], in_got_rs[bits - 1], dp_device(bits - 1))
    in_y.start()
    load_in = local("load_in", in_hbm.at[(whole,) * (bits - 1) + (flags[bits - 1],)], in_kept)
    load_in.start()
    out_z = rs_copy("out_rs", out_part, out_got_rs[bits - 2], bits - 2)
    out_z.start()
    rows_o = go_x.shape[0]
    go_core = [
        remote("go_near", go_near.at[pl.ds(rows_o, rows_o)], go_core_near, head_device(1)),
        remote("go_far", go_far.at[pl.ds(rows_o, rows_o)], go_core_far, head_device(1)),
    ]
    for copy in go_core:
        copy.start()
    closing = []
    for name, source, target in (("new", new_ref, new_got), ("conv", conv_ref, conv_got)):
        for r in range(1, heads):
            copy = remote(
                f"{name}_{r}",
                source.at[jnp.bitwise_xor(head, r)],
                target.at[head],
                head_device(r),
            )
            copy.start()
            closing.append(copy)
        target[head] = source[head]
    go_to_x = remote("go_x", go_core_far, go_x, head_device(2))
    grad_normed[...] = jnp.zeros(grad_normed.shape, f32)
    c = score_scale * log2e

    def core_copy(r, p):
        return remote(f"core_{r}", terms.at[r - 1], (got_near if r == 1 else got_far).at[p], head_device(1), p)

    def x_copy(p):
        return remote("x_terms", terms.at[1], got_x.at[p], head_device(2), p)

    def sum_y(p):
        return rs_copy("sum", own_terms.at[p], sum_rs[bits - 1].at[p], bits - 1, p)

    def sum_copy(p, n):
        return rs_copy("sum", sum_rs[n + 1].at[p], sum_rs[n].at[p], n, p)

    def sum_gather(p, n):
        return ag_copy("gather", sum_rows.at[p], n, p)

    def add_rows(target, source):
        for at in range(target.shape[0]):
            target[at] = (target[at].astype(f32) + source[at].astype(f32)).astype(bf16)

    def each_block(function):
        def step(at, carry):
            function(tuple(lax.rem(lax.div(at, 2 ** (bits - 1 - b)), 2) for b in range(bits)))
            return carry

        lax.fori_loop(0, 2**bits, step, 0)

    def add_whole(target, source):
        def one(index):
            target[index] = (target[index].astype(f32) + source[index].astype(f32)).astype(bf16)

        each_block(one)

    def attend(r, p):
        half_q, half_k, half_v, half_g, half_l = (
            (q_near, k_near, v_near, gm_near, lse_near)
            if r < 2
            else (q_far, k_far, v_far, gm_far, lse_far)
        )
        cut = pl.ds(pl.multiple_of((r % 2) * 2 * E + p * E, E), E)
        q = half_q[:, cut]
        g = half_g[:, cut]
        q_t = q.T
        g_t = g.T
        k_t = half_k[:, cut].T
        lse = half_l[(r % 2) * 2 + p]
        row_dot = jnp.zeros((1, slot_len), f32)
        for kb in range(6):
            first = BLOCK if kb == 5 else 0
            rows = slice(kb * BLOCK, (kb + 1) * BLOCK)
            s = masked_scores(kb, lens_ref, dot(half_k[rows, cut], q_t[:, first:]))
            pr = jnp.exp2(s * c - lse[:, first:])
            gp = dot(half_v[rows, cut], g_t[:, first:])
            probs[rows, first:] = pr
            grads[rows, first:] = gp
            part = jnp.sum(pr * gp, axis=0, keepdims=True)
            dkv[rows, E:] = dot(pr.astype(bf16), g[first:]).astype(bf16)
            if first:
                row_dot = jnp.concatenate([row_dot[:, :first], row_dot[:, first:] + part], axis=1)
            else:
                row_dot = row_dot + part
        dq = jnp.zeros((E, slot_len), f32)
        for kb in range(6):
            first = BLOCK if kb == 5 else 0
            rows = slice(kb * BLOCK, (kb + 1) * BLOCK)
            ds = (probs[rows, first:] * (grads[rows, first:] - row_dot[:, first:])).astype(bf16)
            dkv[rows, :E] = (dot(ds, q[first:]) * score_scale).astype(bf16)
            out = dot(k_t[:, rows], ds)
            if first:
                dq = jnp.concatenate([dq[:, :first], dq[:, first:] + out], axis=1)
            else:
                dq = dq + out
        return (dq * score_scale).T.astype(bf16)

    per_block = own_terms.shape[1 + bits]

    def weight_terms(dq, target):
        blocks = 2 ** (bits - 1)
        many = blocks * per_block

        def one(at, carry):
            rows = pl.ds(pl.multiple_of(at * many, many), many)
            of_kv = dot(key_t[rows, :], dkv[...]).astype(bf16)
            of_q = dot(key_t[rows, keys - slot_len :], dq).astype(bf16)
            for n in range(blocks):
                index = (at,) + tuple((n >> (bits - 2 - b)) & 1 for b in range(bits - 1))
                cut = slice(n * per_block, (n + 1) * per_block)
                target[index + (whole, slice(0, 2 * E))] = of_kv[cut]
                target[index + (whole, slice(2 * E, 3 * E))] = of_q[cut]
            return carry

        lax.fori_loop(0, 2, one, 0)

    def normed_terms(r, p, dq):
        cut = pl.ds(pl.multiple_of(p * E, E), E)
        dk = dkv[keys - slot_len :, :E]
        dv = dkv[keys - slot_len :, E:]
        columns = 256
        for n in range(grad_normed.shape[1] // columns):
            rows = slice(n * columns, (n + 1) * columns)
            grad_normed[:, rows] += (
                dot_nt(dq, wq[r][rows, cut])
                + dot_nt(dk, wk[r][rows, cut])
                + dot_nt(dv, wv[r][rows, cut])
            )

    def parity(p, carry):
        first = p == 0
        dq = attend(3, p)

        @pl.when(first)
        def _():
            load_keys.wait()

        @pl.when(p == 1)
        def _():
            core_copy(3, 0).wait_send()

        weight_terms(dq, terms.at[2])
        core_copy(3, p).start()
        normed_terms(3, p, dq)

        @pl.when(first)
        def _():
            for copy in go_core:
                copy.wait_recv()
            go_core_far[...] = (
                go_core_far[...].astype(f32) + go_far[:rows_o].astype(f32)
            ).astype(bf16)
            go_to_x.start()

        dq = attend(2, p)

        @pl.when(p == 1)
        def _():
            x_copy(0).wait_send()

        weight_terms(dq, terms.at[1])
        core_copy(3, p).wait_recv()
        add_whole(terms.at[1], got_far.at[p])
        x_copy(p).start()
        normed_terms(2, p, dq)

        @pl.when(first)
        def _():
            out_z.wait_recv()
            rs_add(out_part, out_got_rs[bits - 2], bits - 2)
            if bits > 2:
                rs_copy("out_rs", out_got_rs[bits - 2], out_got_rs[bits - 3], bits - 3).start()

        @pl.when(p == 1)
        def _():
            in_y.wait_recv()
            load_in.wait()
            held = in_got_rs[bits - 1]
            for at in range(2 ** (bits - 1)):
                index = tuple((at >> (bits - 2 - b)) & 1 for b in range(bits - 1))
                held[index] = (held[index].astype(f32) + in_kept[index].astype(f32)).astype(bf16)
            rs_copy("in_rs", held, in_got_rs[bits - 2], bits - 2).start()

        dq = attend(1, p)

        @pl.when(p == 1)
        def _():
            core_copy(1, 0).wait_send()

        weight_terms(dq, terms.at[0])
        core_copy(1, p).start()
        normed_terms(1, p, dq)

        @pl.when(p == 1)
        def _():
            x_copy(0).wait_recv()
            add_whole(own_terms.at[0], got_x.at[0])
            sum_y(0).start()

        dq = attend(0, p)
        weight_terms(dq, own_terms.at[p])
        core_copy(1, p).wait_recv()
        add_whole(own_terms.at[p], got_near.at[p])
        normed_terms(0, p, dq)

        @pl.when(first)
        def _():
            go_to_x.wait_recv()
            for at in range(2**bits):
                rows = slice(at * rows_o // 2**bits, (at + 1) * rows_o // 2**bits)
                index = tuple((at >> (bits - 1 - b)) & 1 for b in range(bits))
                go_out[index] = (
                    go_near[rows].astype(f32)
                    + go_core_near[rows].astype(f32)
                    + go_x[rows].astype(f32)
                ).astype(bf16)
            rs_copy("go_rs", go_out, go_rs[bits - 1], bits - 1).start()

        @pl.when(p == 1)
        def _():
            rs_copy("go_rs", go_out, go_rs[bits - 1], bits - 1).wait()
            rs_add(go_out, go_rs[bits - 1], bits - 1)
            rs_copy("go_rs", go_rs[bits - 1], go_rs[bits - 2], bits - 2).start()

        return carry

    lax.fori_loop(0, 2, parity, 0)

    loads = []
    wide = probs.shape[1]
    for name, source, target in (("inputs", inputs_hbm, probs), ("hidden", hidden_hbm, grads)):
        for n in range(2):
            copy = local(
                f"load_{name}{n}",
                source.at[:, pl.ds(n * wide, wide)],
                target.at[pl.ds(n * slot_len, slot_len)],
            )
            copy.start()
            loads.append(copy)
    in_last = rs_copy("in_rs", in_got_rs[bits - 1], in_got_rs[bits - 2], bits - 2)
    in_last.wait_recv()
    rs_add(in_got_rs[bits - 1], in_got_rs[bits - 2], bits - 2)

    def in_rest(n):
        copy = rs_copy("in_rs", in_got_rs[n + 1], in_got_rs[n], n)
        return copy

    for n in reversed(range(bits - 2)):
        in_rest(n).start()
        if n:
            in_rest(n).wait_recv()
            rs_add(in_got_rs[n + 1], in_got_rs[n], n)
    sum_y(0).wait_recv()
    rs_add(own_terms.at[0], sum_rs[bits - 1].at[0], bits - 1)
    sum_copy(0, bits - 2).start()

    for copy in loads:
        copy.wait()
    gain_row = gain_ref[...]

    def input_rows(at, carry):
        rows = pl.ds(pl.multiple_of(at * 128, 128), 128)
        lower = pl.ds(pl.multiple_of(slot_len + at * 128, 128), 128)
        values = jnp.concatenate([probs[rows], probs[lower]], axis=1)
        before = jnp.concatenate([grads[rows], grads[lower]], axis=1)
        grad_normed[rows] = before + norm_input_grad(values, gain_row, grad_normed[rows])
        return carry

    lax.fori_loop(0, slot_len // 128, input_rows, 0)
    store_grad = local("store_grad", grad_normed, input_grad_hbm)
    store_grad.start()

    x_copy(1).wait_recv()
    add_whole(own_terms.at[1], got_x.at[1])
    sum_y(1).start()

    rs_copy("go_rs", go_rs[bits - 1], go_rs[bits - 2], bits - 2).wait_recv()
    rs_add(go_rs[bits - 1], go_rs[bits - 2], bits - 2)
    for n in reversed(range(bits - 2)):
        rs_copy("go_rs", go_rs[n + 1], go_rs[n], n).start()
        if n:
            rs_copy("go_rs", go_rs[n + 1], go_rs[n], n).wait_recv()
            rs_add(go_rs[n + 1], go_rs[n], n)
    sum_copy(0, bits - 2).wait_recv()
    rs_add(sum_rs[bits - 1].at[0], sum_rs[bits - 2].at[0], bits - 2)
    for n in reversed(range(bits - 2)):
        sum_copy(0, n).start()
        if n:
            sum_copy(0, n).wait_recv()
            rs_add(sum_rs[n + 1].at[0], sum_rs[n].at[0], n)

    for n in reversed(range(bits - 2)):
        copy = rs_copy("out_rs", out_got_rs[n + 1], out_got_rs[n], n)
        if n != bits - 3:
            copy.start()
        copy.wait_recv()
        rs_add(out_got_rs[n + 1], out_got_rs[n], n)
    grad_out[...] = out_got_rs[0][...].astype(f32)
    in_rest(0).wait_recv()
    rs_add(in_got_rs[1], in_got_rs[0], 0)
    in_copies = []
    for r in range(1, heads):
        copy = remote(
            f"in_{r}", in_got_rs[0].at[jnp.bitwise_xor(head, r)], in_got.at[head], head_device(r)
        )
        copy.start()
        in_copies.append(copy)
    in_got[head] = in_got_rs[0][head]

    rs_copy("go_rs", go_rs[1], go_rs[0], 0).wait_recv()
    rs_add(go_rs[1], go_rs[0], 0)
    go_out[tuple(flags)] = go_rs[0][...]
    go_gather = [ag_copy("go_ag", go_out, n) for n in range(bits)]
    go_gather[0].start()

    def gain_part(p):
        rows = pl.ds(pl.multiple_of(dp * per_block, per_block), per_block)
        total = jnp.zeros((per_block, 1), f32)
        grad = sum_rs[0][p]
        for n, weight in enumerate((wk[0], wv[0], wq[0])):
            own = weight[rows, p * E : (p + 1) * E].astype(f32)
            total = total + jnp.sum(
                grad[:, n * E : (n + 1) * E].astype(f32) * own, axis=1, keepdims=True
            )
        return total

    sum_copy(0, 0).wait_recv()
    rs_add(sum_rs[1].at[0], sum_rs[0].at[0], 0)
    sum_rows[(0,) + tuple(flags)] = sum_rs[0][0]
    sum_gather(0, 0).start()
    sum_y(1).wait_recv()
    rs_add(own_terms.at[1], sum_rs[bits - 1].at[1], bits - 1)
    sum_copy(1, bits - 2).start()
    gain = gain_part(0)
    go_gather[0].wait_recv()
    if bits > 1:
        go_gather[1].start()
    sum_gather(0, 0).wait_recv()
    sum_gather(0, 1).start()
    for n in reversed(range(bits - 1)):
        sum_copy(1, n).wait_recv()
        rs_add(sum_rs[n + 1].at[1], sum_rs[n].at[1], n)
        if n:
            sum_copy(1, n - 1).start()
    sum_rows[(1,) + tuple(flags)] = sum_rs[0][1]
    sum_gather(1, 0).start()
    gain = gain + gain_part(1)
    gain_terms[head] = jnp.broadcast_to(gain, gain_terms.shape[1:])
    gain_copies = []
    for r in range(1, heads):
        copy = remote(f"gain_{r}", gain_terms.at[head], gain_terms.at[head], head_device(r))
        copy.start()
        gain_copies.append(copy)
    for n in range(1, bits):
        go_gather[n].wait_recv()
        if n + 1 < bits:
            go_gather[n + 1].start()
        sum_gather(0, n).wait_recv()
        if n + 1 < bits:
            sum_gather(0, n + 1).start()
        sum_gather(1, n - 1).wait_recv()
        sum_gather(1, n).start()
    for copy in gain_copies:
        copy.wait_recv()
    gain_out[...] = sum(gain_terms[h] for h in range(heads))
    for copy in closing + in_copies:
        copy.wait()
    sum_gather(1, bits - 1).wait_recv()
    store_grad.wait()

    in_y.wait_send()
    for copy in go_core + gain_copies + go_gather:
        copy.wait_send()
    go_to_x.wait_send()
    for p in range(2):
        sum_y(p).wait_send()
        for n in range(bits - 1):
            sum_copy(p, n).wait_send()
        for n in range(bits):
            sum_gather(p, n).wait_send()
    for r in (1, 3):
        core_copy(r, 1).wait_send()
    x_copy(1).wait_send()
    out_z.wait_send()
    for n in range(bits - 2):
        rs_copy("out_rs", out_got_rs[n + 1], out_got_rs[n], n).wait_send()
    in_last.wait_send()
    for n in range(bits - 2):
        in_rest(n).wait_send()
    for n in range(bits - 1):
        rs_copy("go_rs", go_rs[n + 1], go_rs[n], n).wait_send()


def backward(lens, near, far, wq, wk, wv, gain, go_near, go_far, out_part, new_cols, conv, key_t, grad_in, inputs, grad_hidden):
    heads, dps = lax.axis_size("head"), lax.axis_size("dp")
    masks = [1 << b for b in reversed(range(dps.bit_length() - 1))]
    bits = len(masks)
    slot_len, width = inputs.shape
    keys = key_t.shape[1]
    shape = jax.ShapeDtypeStruct
    twos = lambda n: (2,) * n
    in_block = grad_in.shape[bits:]
    out_block = out_part.shape[bits - 1 :]
    rows_o = go_near.shape[0] // 2
    go_block = (rows_o // dps, width)
    sum_block = (width // dps, 3 * E)
    copies = 60 + 16 * bits
    scratch = (
        [
            pltpu.VMEM((width, keys), bf16),
            pltpu.VMEM((keys, slot_len), f32),
            pltpu.VMEM((keys, slot_len), f32),
            pltpu.VMEM((keys, 2 * E), bf16),
            pltpu.VMEM((3,) + twos(bits) + sum_block, bf16),
            pltpu.VMEM((2,) + twos(bits) + sum_block, bf16),
            pltpu.VMEM((2,) + twos(bits) + sum_block, bf16),
            pltpu.VMEM((2,) + twos(bits) + sum_block, bf16),
            pltpu.VMEM((2,) + twos(bits) + sum_block, bf16),
            pltpu.VMEM(twos(bits - 1) + in_block, bf16),
        ]
        + [pltpu.VMEM(twos(n) + in_block, bf16) for n in range(bits)]
        + [pltpu.VMEM(twos(n) + out_block, bf16) for n in range(bits - 1)]
        + [pltpu.VMEM((rows_o, width), bf16)] * 3
        + [pltpu.VMEM(twos(n) + go_block, bf16) for n in range(bits)]
        + [pltpu.VMEM((2,) + twos(n) + sum_block, bf16) for n in range(bits)]
        + [
            pltpu.VMEM((slot_len, width), f32),
            pltpu.VMEM((heads, width // dps, E), f32),
            pltpu.SemaphoreType.DMA((2, copies)),
        ]
    )
    q_n, k_n, v_n, g_n, l_n = near
    q_f, k_f, v_f, g_f, l_f = far
    return pl.pallas_call(
        functools.partial(backward_kernel, heads, masks, slot_len, keys),
        in_specs=[pl.BlockSpec(memory_space=pltpu.SMEM)]
        + [vmem()] * (10 + 3 * heads + 6)
        + [anywhere()] * 4,
        out_specs=[vmem()] * 2 + [anywhere()] + [vmem()] * 5,
        out_shape=[
            shape(out_block, f32),
            shape((2,) + twos(bits) + sum_block, bf16),
            shape((slot_len, width), f32),
            shape(twos(bits) + go_block, bf16),
            shape((width // dps, E), f32),
            shape(in_block, bf16),
            shape(new_cols.shape, bf16),
            shape(conv.shape, bf16),
        ],
        scratch_shapes=scratch,
        compiler_params=pltpu.CompilerParams(
            collective_id=1, has_side_effects=True, vmem_limit_bytes=61 * 2**20
        ),
        cost_estimate=pl.CostEstimate(flops=60 * 10**9, bytes_accessed=0, transcendentals=0),
        name="backward",
    )(lens, q_n, k_n, v_n, g_n, l_n, q_f, k_f, v_f, g_f, l_f, *wq, *wk, *wv, gain, go_near, go_far, out_part, new_cols, conv, key_t, grad_in, inputs, grad_hidden)


def swap_head(value, mask):
    size = lax.axis_size("head")
    return lax.ppermute(value, "head", [(i, i ^ mask) for i in range(size)])


def swap_dp(value, mask):
    size = lax.axis_size("dp")
    return lax.ppermute(value, "dp", [(i, i ^ mask) for i in range(size)])


def has(index, mask):
    return (index & mask) != 0


def both(flag, own, other, axis):
    return jnp.stack([jnp.where(flag, other, own), jnp.where(flag, own, other)], axis=axis)


def meet(*values):
    flat, tree = jax.tree.flatten(values)
    return jax.tree.unflatten(tree, lax.optimization_barrier(flat))


def gather_step(value, masks, n):
    return (value, swap_dp(value, masks[n]))


def gather_settle(pair, masks, n):
    return both(has(lax.axis_index("dp"), masks[n]), *pair, n)


def gather_early(value, masks):
    for n in range(len(masks) - 3):
        value = gather_settle(gather_step(value, masks, n), masks, n)
    return gather_step(value, masks, len(masks) - 3)


def scatter_split(value, masks, n):
    flag = has(lax.axis_index("dp"), masks[n])
    low = lax.index_in_dim(value, 0, n, keepdims=False)
    high = lax.index_in_dim(value, 1, n, keepdims=False)
    return jnp.where(flag, high, low), jnp.where(flag, low, high)


def scatter_step(value, masks, n):
    kept, sent = scatter_split(value, masks, n)
    return (kept, swap_dp(sent, masks[n]))


def scatter_settle(pair):
    return (pair[0].astype(f32) + pair[1].astype(f32)).astype(bf16)


def scatter_late(value, masks):
    for n in reversed(range(1, len(masks) - 2)):
        value = scatter_settle(scatter_step(value, masks, n))
    return scatter_step(value, masks, 0)


def cut_bits(value, masks):
    return value.reshape((2,) * len(masks) + value.shape[1:])


def cut_in_kernel(in_ref, out_ref):
    heads, units = out_ref.shape[0], E
    head = lax.axis_index("head")
    for r in range(heads):
        other = jnp.bitwise_xor(head, r)
        for i in range(out_ref.shape[2] // units):
            source = pl.multiple_of((i * heads + other) * units, units)
            out_ref[r, :, i * units : (i + 1) * units] = in_ref[:, pl.ds(source, units)]


def cut_in(w_in, heads, dps):
    rows, units = w_in.shape[0], w_in.shape[1] // (heads * dps)
    if units == E:
        return pl.pallas_call(
            cut_in_kernel,
            in_specs=[vmem()],
            out_specs=vmem(),
            out_shape=jax.ShapeDtypeStruct((heads, rows, dps * units), bf16),
            name="cut_in",
        )(w_in)
    head = lax.axis_index("head")
    cut = w_in.reshape(rows, dps, heads, units)
    return jnp.stack(
        [
            lax.dynamic_index_in_dim(cut, head ^ r, 2, keepdims=False).reshape(rows, dps * units)
            for r in range(heads)
        ]
    )


def shards(
    inputs,
    memory,
    compressed,
    counts,
    mem_lens,
    cmem_lens,
    norm_gain,
    w_query,
    w_key,
    w_value,
    w_output,
    ffn_gain,
    w_in,
    w_out,
    w_conv,
    out_grad,
    comp_grad,
):
    slot_len, width = inputs.shape[1:]
    heads, dps = lax.axis_size("head"), lax.axis_size("dp")
    masks = [1 << b for b in reversed(range(dps.bit_length() - 1))]
    bits = len(masks)
    group = memory.shape[0]
    head_at, dp_at = lax.axis_index("head"), lax.axis_index("dp")
    head_width = w_query.shape[1]
    new_rows = comp_grad.shape[1]
    conv_cols = width // heads
    count = lax.dynamic_slice_in_dim(counts, head_at, 1)
    lens = lax.dynamic_index_in_dim(jnp.stack([cmem_lens, mem_lens]), head_at, 1, keepdims=False)

    gains = jnp.stack([norm_gain, ffn_gain]).astype(f32)
    opened = opening(
        count,
        cut_in(w_in, heads, dps),
        w_conv,
        comp_grad[0],
        out_grad[0],
        gains,
        (w_query, w_key, w_value, w_output),
    )
    in_rows, conv_rows, comp_cot, gains_all, grad_ffn, gf_core = opened[:6]
    wq, wk, wv, wo = ([own, got] for own, got in zip((w_query, w_key, w_value, w_output), opened[6:]))
    gains_all = gains_all.transpose(1, 0, 2).reshape(2, width)
    gain_one, gain_two = gains_all[0:1], gains_all[1:2]
    w_out_rows = w_out
    (in_rows, conv_rows, comp_cot, grad_ffn, gf_core, wq, wk, wv, wo, gain_one, gain_two, memory) = meet(
        in_rows, conv_rows, comp_cot, grad_ffn, gf_core, wq, wk, wv, wo, gain_one, gain_two, memory
    )

    wk_x = swap_head(wk[0], 2)
    in_step = gather_early(in_rows.reshape(-1, in_rows.shape[2]), masks)
    key_rows, q_near, k_near, v_near = project_first(
        head_at[None], compressed, memory, inputs, gain_one, (*wq, *wk, *wv)
    )
    (wk_x, in_step, key_rows, q_near, k_near, v_near, wv, w_out_rows) = meet(
        wk_x, in_step, key_rows, q_near, k_near, v_near, wv, w_out_rows
    )

    wv_x = swap_head(wv[0], 2)
    in_step = gather_step(gather_settle(in_step, masks, bits - 3), masks, bits - 2)
    mixed_near, lse_near = attend_forward(lens, q_near, k_near, v_near)
    (wv_x, in_step, mixed_near, lse_near, wq, wk_x, w_out_rows, memory, comp_cot) = meet(
        wv_x, in_step, mixed_near, lse_near, wq, wk_x, w_out_rows, memory, comp_cot
    )

    wq_x = swap_head(wq[0], 2)
    wk += [wk_x, swap_head(wk_x, 1)]
    wv += [wv_x, swap_head(wv_x, 1)]
    in_all = gather_settle(in_step, masks, bits - 2)
    in_low = swap_dp(in_all[0], masks[-1])
    out_step = gather_early(w_out_rows, masks)
    live = jnp.minimum(counts, mem_lens)
    pad_rows = comp_cot.shape[1]
    source = jnp.arange(memory.shape[1], dtype=jnp.int32)
    evicted, grad_conv = [], []
    for tap in range(3):
        picked = 3 * jnp.arange(pad_rows, dtype=jnp.int32) + tap
        pick = (
            (source[None, None, :] == picked[None, :, None])
            & (source[None, None, :] < live[:, None, None])
            & (source < slot_len)[None, None, :]
        ).astype(bf16)
        rows = jnp.einsum("gcr,grd->gcd", pick, memory, preferred_element_type=f32).astype(bf16)
        evicted.append(rows.reshape(group * pad_rows, width))
        grad_conv.append(
            dot_tn(evicted[tap], comp_cot.reshape(group * pad_rows, conv_cols)).astype(bf16)
        )
    (wq_x, wk, wv, in_all, in_low, out_step, evicted, grad_conv, wo) = meet(
        wq_x, wk, wv, in_all, in_low, out_step, evicted, grad_conv, wo
    )

    wo_x = swap_head(wo[0], 2)
    wq += [wq_x, swap_head(wq_x, 1)]
    in_high = swap_dp(in_all[1], masks[-1])
    out_step = gather_step(gather_settle(out_step, masks, bits - 3), masks, bits - 2)
    q_far, k_far, v_far = project_second(key_rows, (*wq[2:], *wk[2:], *wv[2:]))
    (wo_x, wq, in_high, out_step, q_far, k_far, v_far, grad_ffn, conv_rows) = meet(
        wo_x, wq, in_high, out_step, q_far, k_far, v_far, grad_ffn, conv_rows
    )

    gf_x = swap_head(grad_ffn, 2)
    wo += [wo_x, swap_head(wo_x, 1)]
    out_all = gather_settle(out_step, masks, bits - 2)
    out_low = swap_dp(out_all[0], masks[-1])
    conv_step = gather_early(conv_rows, masks)
    mixed_far, lse_far = attend_forward(lens, q_far, k_far, v_far)
    w_in_own = gather_settle((in_all, jnp.stack([in_low, in_high])), masks, bits - 1)
    w_in_own = w_in_own.reshape(width, -1)
    (wo, out_all, out_low, conv_step, mixed_far, lse_far, w_in_own) = meet(
        wo, out_all, out_low, conv_step, mixed_far, lse_far, w_in_own
    )

    out_high = swap_dp(out_all[1], masks[-1])
    conv_step = gather_step(gather_settle(conv_step, masks, bits - 3), masks, bits - 2)
    hidden, normed_two = mix_out(count, inputs[0], mixed_near, mixed_far, wo, gain_two)
    (gf_x, out_high, conv_step, hidden, normed_two) = meet(
        gf_x, out_high, conv_step, hidden, normed_two
    )

    n2_x = swap_head(normed_two, 2)
    n2_core = swap_head(normed_two, 1)
    gf_diag = swap_head(gf_x, 1)
    conv_all = gather_settle(conv_step, masks, bits - 2)
    conv_step = gather_step(conv_all, masks, bits - 1)
    w_out_own = gather_settle((out_all, jnp.stack([out_low, out_high])), masks, bits - 1)
    w_out_own = w_out_own.reshape(-1, width)

    def feed_forward(tokens, cot):
        inner = dot(tokens, w_in_own)
        activated = jax.nn.gelu(inner).astype(bf16)
        grad_act = dot_nt(cot, w_out_own)
        grad_inner = jax.vjp(jax.nn.gelu, inner)[1](grad_act)[0].astype(bf16)
        return activated, grad_inner, dot_nt(grad_inner, w_in_own)

    n2_near = jnp.concatenate([normed_two, n2_core])
    gf_near = jnp.concatenate([grad_ffn, gf_core])
    act_near, gi_near, gn_near = feed_forward(n2_near, gf_near)
    gn_own, gn_sent = gn_near[:slot_len], gn_near[slot_len:].astype(bf16)
    key_t = key_rows.T
    (n2_x, gf_diag, conv_step, act_near, gi_near, gn_own, gn_sent, grad_conv, key_t) = meet(
        n2_x, gf_diag, conv_step, act_near, gi_near, gn_own, gn_sent, grad_conv, key_t
    )

    n2_far = jnp.concatenate([n2_x, swap_head(n2_x, 1)])
    gf_far = jnp.concatenate([gf_x, gf_diag])
    gn_core = swap_head(gn_sent, 1)
    conv_own = gather_settle(conv_step, masks, bits - 1).reshape(-1, conv_cols)
    grad_conv = jnp.concatenate(grad_conv).reshape(dps, -1, conv_cols)
    conv_back = scatter_step(cut_bits(grad_conv, masks), masks, bits - 1)
    act_far, gi_far, gn_far = feed_forward(n2_far, gf_far)
    gn_far_core = swap_head(gn_far[slot_len:].astype(bf16), 1)
    gn_far = (gn_far[:slot_len] + gn_far_core.astype(f32)).astype(bf16)
    (n2_far, gf_far, gn_core, conv_own, conv_back, act_far, gi_far, gn_far) = meet(
        n2_far, gf_far, gn_core, conv_own, conv_back, act_far, gi_far, gn_far
    )

    gn_back = swap_head(gn_far, 2)
    conv_back = scatter_step(scatter_settle(conv_back), masks, bits - 2)
    out_far = dot(act_far, w_out_own)
    out_far_core = swap_head(out_far[slot_len:].astype(bf16), 1)
    out_far = (out_far[:slot_len] + out_far_core.astype(f32)).astype(bf16)
    grad_w_out = (dot_tn(act_near, gf_near) + dot_tn(act_far, gf_far)).astype(bf16)
    grad_w_in = (dot_tn(n2_near, gi_near) + dot_tn(n2_far, gi_far)).astype(bf16)
    out_near = dot(act_near, w_out_own)
    out_core = swap_head(out_near[slot_len:].astype(bf16), 1)
    out_own = out_near[:slot_len]
    conv_tap = conv_own.reshape(3, width, conv_cols)
    new_cols = sum(dot(evicted[tap], conv_tap[tap]) for tap in range(3)).astype(bf16)
    (gn_back, conv_back, out_far, grad_w_out, grad_w_in, out_own, out_core, new_cols) = meet(
        gn_back, conv_back, out_far, grad_w_out, grad_w_in, out_own, out_core, new_cols
    )

    out_back = swap_head(out_far, 2)
    w_out_back = scatter_step(
        cut_bits(grad_w_out.reshape(dps, -1, width), masks), masks, bits - 1
    )
    conv_back = scatter_late(scatter_settle(conv_back), masks)
    grad_hidden, grad_attention = back_norm(
        count, gn_own, gn_core, gn_back, hidden, out_grad[0], gain_two
    )
    gm_near = jnp.concatenate([dot_nt(grad_attention, w) for w in wo[:2]], axis=1).astype(bf16)
    gm_far = jnp.concatenate([dot_nt(grad_attention, w) for w in wo[2:]], axis=1).astype(bf16)
    go_near = dot_tn(mixed_near, grad_attention).astype(bf16)
    go_far = dot_tn(mixed_far, grad_attention).astype(bf16)
    (w_out_back, conv_back, grad_hidden, gm_near, gm_far, go_near, go_far, grad_w_in, new_cols) = meet(
        w_out_back, conv_back, grad_hidden, gm_near, gm_far, go_near, go_far, grad_w_in, new_cols
    )

    grad_w_out, sum_rows, input_grad, grad_out, gain_terms, grad_w_in, new_all, grad_conv = backward(
        lens,
        (q_near, k_near, v_near, gm_near, lse_near),
        (q_far, k_far, v_far, gm_far, lse_far),
        wq,
        wk,
        wv,
        gain_one,
        go_near,
        go_far,
        scatter_settle(w_out_back),
        new_cols.reshape(group, -1, conv_cols),
        scatter_settle(conv_back).reshape(heads, w_conv.shape[0], conv_cols),
        key_t,
        cut_bits(grad_w_in.reshape((dps, heads, w_in.shape[0], -1)), masks),
        inputs[0],
        grad_hidden,
    )
    row_pos = jnp.arange(slot_len, dtype=jnp.int32)
    row_live = (row_pos < count).astype(f32)[:, None]
    outputs = hidden + row_live * (out_own + out_core.astype(f32) + out_back.astype(f32))
    new_compressed = new_all.transpose(1, 0, 2).reshape(-1, width)[:new_rows].astype(f32)
    grad_conv = grad_conv.transpose(1, 0, 2).reshape(w_conv.shape).astype(f32)
    grad_w_in = (
        grad_w_in.reshape(heads, w_in.shape[0], dps, -1)
        .transpose(1, 2, 0, 3)
        .reshape(w_in.shape)
        .astype(f32)
    )
    own_gain_two = lax.dynamic_slice_in_dim(
        gain_two[0], (dp_at * heads + head_at) * w_in.shape[0], w_in.shape[0]
    )
    grad_gain_two = jnp.sum(grad_w_in * w_in.astype(f32), axis=1) / own_gain_two
    grad_gain_one = lax.dynamic_slice_in_dim(
        gain_terms[:, 0], head_at * norm_gain.shape[0], norm_gain.shape[0]
    ) / norm_gain.astype(f32)
    sums = sum_rows.reshape(2, width, 3 * E).astype(f32)
    grad_key, grad_value, grad_query = (
        jnp.concatenate([sums[0, :, n * E : (n + 1) * E], sums[1, :, n * E : (n + 1) * E]], axis=1)
        for n in range(3)
    )
    grad_out = grad_out.reshape(w_output.shape).astype(f32)

    return (
        outputs[None],
        input_grad[None],
        new_compressed[None],
        grad_gain_one,
        grad_query,
        grad_key,
        grad_value,
        grad_out,
        grad_gain_two,
        grad_w_in,
        grad_w_out.reshape(w_out.shape).astype(f32),
        grad_conv,
    )


def solution(mesh):
    whole = P(("dp", "head"), None, None)
    rows = P(("dp", "head"), None)
    vector = P(("dp", "head"))
    columns = P(None, "head")
    placed = (
        whole,
        P("dp", None, None),
        P("dp", None, None),
        P("dp"),
        P("dp"),
        P("dp"),
        vector,
        columns,
        columns,
        columns,
        P("head", None),
        vector,
        rows,
        rows,
        rows,
        whole,
        whole,
    )
    return jax.shard_map(
        shards,
        mesh=mesh,
        in_specs=placed,
        out_specs=(
            whole,
            whole,
            whole,
            vector,
            columns,
            columns,
            columns,
            P("head", None),
            vector,
            rows,
            rows,
            rows,
        ),
        check_vma=False,
    )
```

```python
import functools

import jax
import jax.numpy as jnp
from jax import lax
from jax.experimental import pallas as pl
from jax.experimental.pallas import tpu as pltpu
from jax.sharding import PartitionSpec as P

E = 128
BLOCK = 256
epsilon = 1e-05
masked_value = -1e30
score_scale = E ** (-0.5)
log2e = 1.4426950408889634
bf16 = jnp.bfloat16
f32 = jnp.float32
VMEM_BYTES = 30 * 2**20
MESH = pl.DeviceIdType.MESH


def dot(left, right):
    return jnp.dot(left, right, preferred_element_type=f32)


def dot_tn(left, right):
    return lax.dot_general(left, right, (((0,), (0,)), ((), ())), preferred_element_type=f32)


def dot_nt(left, right):
    return lax.dot_general(left, right, (((1,), (1,)), ((), ())), preferred_element_type=f32)


def layer_norm(values, gain_vec):
    row_mean = jnp.mean(values, axis=-1, keepdims=True)
    centred = values - row_mean
    variance = jnp.mean(centred * centred, axis=-1, keepdims=True)
    return centred * lax.rsqrt(variance + epsilon) * gain_vec


def vmem():
    return pl.BlockSpec(memory_space=pltpu.VMEM)


def anywhere():
    return pl.BlockSpec(memory_space=pl.ANY)


def masked_scores(kb, lens_ref, scores):
    rows = lax.broadcasted_iota(jnp.int32, scores.shape, 0)
    if kb < 4:
        limit = lens_ref[kb // 2] - (kb % 2) * BLOCK
        return jnp.where(rows < limit, scores, masked_value)
    columns = lax.broadcasted_iota(jnp.int32, scores.shape, 1)
    return jnp.where(rows <= columns, scores, masked_value)


STORED = 26


def forward_kernel(heads, dps, masks, group, slot_len, *refs):
    (count_ref, lens_ref, limits_ref), refs = refs[:3], refs[3:]
    (in_pieces, w_conv_ref, cot_ref, gains_ref, wq0, wk0, wv0, wo0), refs = refs[:8], refs[8:]
    (w_out_hbm, out_grad_hbm, inputs_hbm, memory_hbm, cmem_hbm), refs = refs[:5], refs[5:]
    (gain_row_out, lse_near, lse_far), refs = refs[:3], refs[3:]
    places, refs = refs[:STORED], refs[STORED:]
    (w_in_all, w_out_all, gf_rest), refs = refs[:3], refs[3:]
    kept, refs = refs[:STORED], refs[STORED:]
    (conv_out, gf_out, q_near, k_near, v_near, q_far, k_far, v_far, mixed_near, mixed_far), more = kept[:10], kept[10:]
    (key_t, hidden_out, normed_out), more = more[:3], more[3:]
    (wq1, wq2, wq3, wk1, wk2, wk3, wv1, wv2, wv3, wo1, wo2, wo3, conv_grad) = more
    gains_out, cot_out, key_rows, scores, inputs, out_grad, memory, cmem, spread, conv_send, cot_send, sems = refs
    bits = len(masks)
    width = inputs.shape[1]
    half = wk0.shape[1]
    head = lax.axis_index("head")
    dp = lax.axis_index("dp")
    flags = tuple(jnp.where(jnp.bitwise_and(dp, mask) != 0, 1, 0) for mask in masks)
    whole = slice(None)

    def head_device(r):
        return (dp, jnp.bitwise_xor(head, r))

    def dp_device(r):
        return (lax.rem(dp + r, dps), head)

    barrier = pltpu.get_barrier_semaphore()
    for r in range(1, heads):
        pl.semaphore_signal(barrier, inc=1, device_id=head_device(r), device_id_type=MESH)
    for r in range(1, dps):
        pl.semaphore_signal(barrier, inc=1, device_id=dp_device(r), device_id_type=MESH)

    slots = {}

    def slot(name):
        if name not in slots:
            slots[name] = len(slots)
        return slots[name]

    def remote(name, source, target, device):
        at = slot(name)
        return pltpu.make_async_remote_copy(
            src_ref=source,
            dst_ref=target,
            send_sem=sems.at[0, at],
            recv_sem=sems.at[1, at],
            device_id=device,
            device_id_type=MESH,
        )

    def local(name, source, target):
        return pltpu.make_async_copy(source, target, sems.at[0, slot(name)])

    loads = {}
    for name, source, target in [
        ("out_grad", out_grad_hbm, out_grad),
        ("cmem", cmem_hbm.at[head], cmem),
        ("memory", memory_hbm, memory),
        ("inputs", inputs_hbm, inputs),
        ("w_out", w_out_hbm, w_out_all.at[flags]),
        ("in_own", in_pieces.at[0], w_in_all.at[flags + (head,)]),
    ]:
        loads[name] = local(f"load_{name}", source, target)
        loads[name].start()
    sent, stored = [], []

    def store(*buffers):
        for buffer in buffers:
            at = [buffer is other for other in kept].index(True)
            copy = local(f"store_{at}", buffer, places[at])
            copy.start()
            stored.append(copy)

    def send(*args):
        copy = remote(*args)
        copy.start()
        sent.append(copy)
        return copy

    at = dp * heads + head
    short = gains_ref.shape[1]
    lane = lax.broadcasted_iota(jnp.int32, (short, E), 1)
    place = lax.broadcasted_iota(jnp.int32, (short, E), 0) + lax.rem(at * short, E)
    spot = jnp.where(lane == place, 1.0, 0.0).astype(bf16)
    gains_out[at] = dot(gains_ref[...].astype(bf16), spot)
    columns = conv_out.shape[2]
    pad_rows = cot_out.shape[1]
    new_rows = cot_ref.shape[0]
    pl.semaphore_wait(barrier, heads + dps - 2)

    gain_heads = [
        send(f"gain_{r}", gains_out.at[at], gains_out.at[at], head_device(r))
        for r in range(1, heads)
    ]
    in_rows = [
        send(f"in_{r}", in_pieces.at[r], w_in_all.at[flags + (head,)], head_device(r))
        for r in range(1, heads)
    ]
    core = [
        send(f"core_{n}", source, target, head_device(1))
        for n, (source, target) in enumerate(((wk0, wk1), (wv0, wv1), (wq0, wq1), (wo0, wo1)))
    ]
    x_k = send("x_k", wk0, wk2, head_device(2))
    rows_o = wo2.shape[bits]
    own_o = wo0.at[pl.ds(pl.multiple_of(dp * rows_o, rows_o), rows_o)]
    x_o = send("x_o", own_o, wo2.at[flags], head_device(2))

    dp_partners = [(jnp.bitwise_xor(dp, mask), head) for mask in masks]

    def gather(name, block, order, source=None):
        copies, index = [], list(flags)
        for n, bit in enumerate(order):
            part = block.at[tuple(index)]
            first = source if source is not None and n == 0 else part
            copies.append(remote(f"gather_{name}_{n}", first, part, dp_partners[bit]))
            index[bit] = whole
        return copies

    straight = list(range(bits))
    crossed = straight[:-2] + [bits - 1, bits - 2]
    gathers = {
        "out": gather("out", w_out_all, straight, w_out_hbm),
        "in": gather("in", w_in_all, crossed),
        "o": gather("o", wo2, straight),
    }
    gathers["out"][0].start()

    def advance(name, n):
        gathers[name][n].wait_recv()
        if n + 1 < bits:
            gathers[name][n + 1].start()

    small = []
    for r in range(heads):
        other = jnp.bitwise_xor(head, r)
        cut = pl.ds(pl.multiple_of(other * columns, columns), columns)
        conv_piece = w_conv_ref[:, cut]
        cot_piece = jnp.concatenate(
            [cot_ref[:, cut], jnp.zeros((pad_rows - new_rows, columns), f32)], axis=0
        ).astype(bf16)
        if r == 0:
            conv_out[head] = conv_piece
            cot_out[head] = cot_piece
        else:
            conv_send[r - 1] = conv_piece
            cot_send[r - 1] = cot_piece
            small.append(send(f"conv_{r}", conv_send.at[r - 1], conv_out.at[head], head_device(r)))
            small.append(send(f"cot_{r}", cot_send.at[r - 1], cot_out.at[head], head_device(r)))
    for copy in gain_heads:
        copy.wait_recv()
    block = gains_out.at[pl.ds(dp * heads, heads)]
    gain_dps = [send(f"gain_dp_{r}", block, block, dp_device(r)) for r in range(1, dps)]
    for copy in in_rows:
        copy.wait_recv()
    loads["in_own"].wait()
    gathers["in"][0].start()
    x_v = send("x_v", wv0, wv2, head_device(2))
    x_q = send("x_q", wq0, wq2, head_device(2))

    loads["out_grad"].wait()

    def cotangent(n, carry):
        rows = pl.ds(pl.multiple_of(n * 128, 128), 128)
        row = lax.broadcasted_iota(jnp.int32, (128, width), 0) + n * 128
        gf_out[rows] = jnp.where(row < count_ref[0], out_grad[rows], 0.0).astype(bf16)
        return carry

    lax.fori_loop(0, slot_len // 128, cotangent, 0)
    store(gf_out)
    gf_core = send("gf_core", gf_out, gf_rest.at[0], head_device(1))
    gf_x = send("gf_x", gf_out, gf_rest.at[1], head_device(2))
    for copy in gain_dps:
        copy.wait_recv()
    many = E // short
    tiles = [
        sum(gains_out[t * many + n] for n in range(many)) for t in range(dps * heads // many)
    ]
    gain_one = jnp.concatenate([tile[0:1] for tile in tiles], axis=1)
    gain_two = jnp.concatenate([tile[1:2] for tile in tiles], axis=1)
    gain_row_out[0:1] = gain_one
    gain_row_out[1:2] = gain_two
    for copy in core:
        copy.wait_recv()
    store(wk1, wv1, wq1, wo1)

    def project(normed, rows, weights, k_ref, v_ref):
        for n, (wk, wv) in enumerate(weights):
            cut = slice(n * half, (n + 1) * half)
            k_ref[rows, cut] = dot(normed, wk).astype(bf16)
            v_ref[rows, cut] = dot(normed, wv).astype(bf16)

    def near_rows(source, part):
        def one(n, carry):
            rows = pl.ds(pl.multiple_of(n * BLOCK, BLOCK), BLOCK)
            target = pl.ds(pl.multiple_of(part * slot_len + n * BLOCK, BLOCK), BLOCK)
            normed = layer_norm(source[rows].astype(f32), gain_one).astype(bf16)
            key_rows[target] = normed
            key_t[:, target] = normed.T
            project(normed, target, ((wk0[...], wv0[...]), (wk1[...], wv1[...])), k_near, v_near)
            if part == 2:
                q_near[rows, :half] = dot(normed, wq0[...]).astype(bf16)
                q_near[rows, half:] = dot(normed, wq1[...]).astype(bf16)
            return carry

        lax.fori_loop(0, slot_len // BLOCK, one, 0)

    loads["cmem"].wait()
    near_rows(cmem, 0)
    loads["w_out"].wait()
    advance("out", 0)
    loads["memory"].wait()
    near_rows(memory.at[head], 1)
    x_o.wait_recv()
    gathers["o"][0].start()
    loads["inputs"].wait()
    near_rows(inputs, 2)
    store(q_near, k_near, v_near, key_t)
    advance("in", 0)

    c = score_scale * log2e

    def attend(q_ref, k_ref, v_ref, mixed_ref, lse_ref, events):
        def one(h, carry):
            cut = pl.ds(pl.multiple_of(h * E, E), E)
            q_t = q_ref[:, cut].T
            v_t = v_ref[:, cut].T
            top = jnp.full((1, slot_len), masked_value, f32)
            for kb in range(6):
                first = BLOCK if kb == 5 else 0
                rows = slice(kb * BLOCK, (kb + 1) * BLOCK)
                s = masked_scores(kb, lens_ref, dot(k_ref[rows, cut], q_t[:, first:]))
                scores[rows, first:] = s
                part = jnp.max(s, axis=0, keepdims=True)
                if first:
                    top = jnp.concatenate([top[:, :first], jnp.maximum(top[:, first:], part)], axis=1)
                else:
                    top = jnp.maximum(top, part)
            shift = top * c
            mixed = jnp.zeros((E, slot_len), f32)
            total = jnp.zeros((1, slot_len), f32)
            for kb in range(6):
                first = BLOCK if kb == 5 else 0
                rows = slice(kb * BLOCK, (kb + 1) * BLOCK)
                p = jnp.exp2(scores[rows, first:] * c - shift[:, first:])
                part = jnp.sum(p, axis=0, keepdims=True)
                out = dot(v_t[:, rows], p.astype(bf16))
                if first:
                    total = jnp.concatenate([total[:, :first], total[:, first:] + part], axis=1)
                    mixed = jnp.concatenate([mixed[:, :first], mixed[:, first:] + out], axis=1)
                else:
                    total = total + part
                    mixed = mixed + out
            mixed_ref[:, cut] = (mixed / total).T.astype(bf16)
            lse_ref[h] = shift + jnp.log2(total)
            for when, event in events:
                pl.when(h == when)(event)
            return carry

        lax.fori_loop(0, q_ref.shape[1] // E, one, 0)

    attend(
        q_near,
        k_near,
        v_near,
        mixed_near,
        lse_near,
        [
            (1, lambda: advance("out", 1)),
            (2, lambda: advance("o", 0)),
        ],
    )

    for copy in small:
        copy.wait_recv()
    store(mixed_near, conv_out)
    taps = 3

    def spread_rows(g, carry):
        source_row = lax.broadcasted_iota(jnp.int32, (slot_len, pad_rows), 0)
        picked_row = lax.broadcasted_iota(jnp.int32, (slot_len, pad_rows), 1)
        kept = source_row < limits_ref[g]
        for tap in range(taps):
            pick = jnp.where(kept & (source_row == taps * picked_row + tap), 1.0, 0.0).astype(bf16)
            spread[g, :, tap * columns : (tap + 1) * columns] = dot(pick, cot_out[g]).astype(bf16)
        return carry

    lax.fori_loop(0, group, spread_rows, 0)
    x_k.wait_recv()
    fwd_k = send("fwd_k", wk2, wk3, head_device(1))

    def conv_rows(n, carry):
        rows = pl.ds(pl.multiple_of(n * BLOCK, BLOCK), BLOCK)
        total = sum(dot(memory[g, :, rows].T, spread[g]) for g in range(group)).astype(bf16)
        for tap in range(taps):
            conv_grad[tap, rows] = total[:, tap * columns : (tap + 1) * columns]
        return carry

    lax.fori_loop(0, width // BLOCK, conv_rows, 0)
    advance("in", 1)
    x_v.wait_recv()
    fwd_v = send("fwd_v", wv2, wv3, head_device(1))
    store(conv_grad)
    advance("o", 1)
    x_q.wait_recv()
    fwd_q = send("fwd_q", wq2, wq3, head_device(1))
    for copy in (fwd_k, fwd_v):
        copy.wait_recv()
    store(wk2, wk3, wv2, wv3)

    def far_rows(n, carry):
        rows = pl.ds(pl.multiple_of(n * BLOCK, BLOCK), BLOCK)
        project(key_rows[rows], rows, ((wk2[...], wv2[...]), (wk3[...], wv3[...])), k_far, v_far)
        return carry

    lax.fori_loop(0, key_rows.shape[0] // BLOCK, far_rows, 0)
    fwd_q.wait_recv()
    store(wq2, wq3)
    for n in range(slot_len // BLOCK):
        rows = slice(n * BLOCK, (n + 1) * BLOCK)
        normed = key_rows[2 * slot_len + n * BLOCK : 2 * slot_len + (n + 1) * BLOCK]
        q_far[rows, :half] = dot(normed, wq2[...]).astype(bf16)
        q_far[rows, half:] = dot(normed, wq3[...]).astype(bf16)
    store(q_far, k_far, v_far)
    for n in range(2, bits):
        advance("o", n)
    fwd_o = send("fwd_o", wo2, wo3, head_device(1))
    attend(q_far, k_far, v_far, mixed_far, lse_far, [])
    store(mixed_far)
    fwd_o.wait_recv()
    store(wo2, wo3)

    def mix(n, carry):
        rows = pl.ds(pl.multiple_of(n * 128, 128), 128)
        near, far = mixed_near[rows], mixed_far[rows]
        attention = (
            dot(near[:, :half], wo0[...])
            + dot(near[:, half:], wo1[...])
            + dot(far[:, :half], wo2[...].reshape(half, width))
            + dot(far[:, half:], wo3[...].reshape(half, width))
        )
        row = lax.broadcasted_iota(jnp.int32, (128, width), 0) + n * 128
        hidden = inputs[rows] + jnp.where(row < count_ref[0], attention, 0.0)
        hidden_out[rows] = hidden
        normed_out[rows] = layer_norm(hidden, gain_two).astype(bf16)
        return carry

    lax.fori_loop(0, slot_len // 128, mix, 0)
    store(hidden_out, normed_out)
    gf_x.wait_recv()
    gf_diag = send("gf_diag", gf_rest.at[1], gf_rest.at[2], head_device(1))
    gf_core.wait_recv()
    gf_diag.wait_recv()
    for n in range(2, bits):
        advance("in", n)
        advance("out", n)
    for copy in stored:
        copy.wait()
    for copy in sent:
        copy.wait_send()
    for copies in gathers.values():
        for copy in copies:
            copy.wait_send()


def forward(count, lens, limits, in_pieces, w_conv, comp_grad, gains, weights, w_out, out_grad, inputs, memory, compressed):
    heads, dps = lax.axis_size("head"), lax.axis_size("dp")
    masks = [1 << b for b in reversed(range(dps.bit_length() - 1))]
    twos = (2,) * len(masks)
    slot_len, width = inputs.shape
    group, keys = memory.shape[0], 3 * slot_len
    wq, wk, wv, wo = weights
    half = wk.shape[1]
    columns = width // heads
    new_rows = comp_grad.shape[0]
    pad_rows = (new_rows + 15) // 16 * 16
    shape = jax.ShapeDtypeStruct
    wide = 2 * half
    conv_all = (heads, w_conv.shape[0], columns)
    cot_all = (heads, pad_rows, columns)
    o_cut = twos + (half // dps, width)
    outs = [
        shape((2, width), f32),
        shape((wide // E, 1, slot_len), f32),
        shape((wide // E, 1, slot_len), f32),
    ]
    kept = [
        shape(conv_all, bf16),
        shape((slot_len, width), bf16),
        shape((slot_len, wide), bf16),
        shape((keys, wide), bf16),
        shape((keys, wide), bf16),
        shape((slot_len, wide), bf16),
        shape((keys, wide), bf16),
        shape((keys, wide), bf16),
        shape((slot_len, wide), bf16),
        shape((slot_len, wide), bf16),
        shape((width, keys), bf16),
        shape((slot_len, width), f32),
        shape((slot_len, width), bf16),
        *[shape(wq.shape, bf16)] * 3,
        *[shape(wk.shape, bf16)] * 3,
        *[shape(wv.shape, bf16)] * 3,
        shape(wo.shape, bf16),
        shape(o_cut, bf16),
        shape(o_cut, bf16),
        shape((3, width, columns), bf16),
    ]
    far_outs = [
        shape(twos + in_pieces.shape, bf16),
        shape(twos + w_out.shape, bf16),
        shape((heads - 1, slot_len, width), bf16),
    ]
    smem = pl.BlockSpec(memory_space=pltpu.SMEM)
    return pl.pallas_call(
        functools.partial(forward_kernel, heads, dps, masks, group, slot_len),
        in_specs=[smem] * 3 + [vmem()] * 8 + [anywhere()] * 5,
        out_specs=[vmem()] * len(outs) + [anywhere()] * (len(kept) + len(far_outs)),
        out_shape=outs + kept + far_outs,
        scratch_shapes=[pltpu.VMEM(k.shape, k.dtype) for k in kept]
        + [
            pltpu.VMEM((dps * heads, 8, E), f32),
            pltpu.VMEM(cot_all, bf16),
            pltpu.VMEM((keys, width), bf16),
            pltpu.VMEM((keys, slot_len), f32),
            pltpu.VMEM((slot_len, width), f32),
            pltpu.VMEM((slot_len, width), f32),
            pltpu.VMEM(memory.shape, bf16),
            pltpu.VMEM((slot_len, width), bf16),
            pltpu.VMEM((group, slot_len, 3 * columns), bf16),
            pltpu.VMEM((heads - 1,) + conv_all[1:], bf16),
            pltpu.VMEM((heads - 1,) + cot_all[1:], bf16),
            pltpu.SemaphoreType.DMA((2, 30 + STORED + 6 * heads + dps + 4 * len(masks))),
        ],
        compiler_params=pltpu.CompilerParams(
            collective_id=0, has_side_effects=True, vmem_limit_bytes=61 * 2**20
        ),
        cost_estimate=pl.CostEstimate(flops=40 * 10**9, bytes_accessed=0, transcendentals=0),
        name="forward",
    )(count, lens, limits, in_pieces, w_conv, comp_grad, gains, *weights, w_out, out_grad, inputs, memory, compressed)


def live_rows(count_ref, rows, width):
    at = lax.broadcasted_iota(jnp.int32, (rows, width), 0) + pl.program_id(0) * rows
    return at < count_ref[0]


def norm_input_grad(values, gain, grad):
    mean = jnp.mean(values, axis=-1, keepdims=True)
    centred = values - mean
    scale = lax.rsqrt(jnp.mean(centred * centred, axis=-1, keepdims=True) + epsilon)
    unit = centred * scale
    grad = grad * gain
    shift = jnp.mean(grad, axis=-1, keepdims=True)
    slope = jnp.mean(grad * unit, axis=-1, keepdims=True)
    return scale * (grad - shift - unit * slope)


def back_norm_kernel(
    count_ref, own_ref, core_ref, far_ref, hidden_ref, out_grad_ref, gain_ref, grad_ref, live_ref
):
    grad = own_ref[...] + core_ref[...].astype(f32) + far_ref[...].astype(f32)
    grad = out_grad_ref[...] + norm_input_grad(hidden_ref[...], gain_ref[...], grad)
    grad_ref[...] = grad
    live = live_rows(count_ref, *grad.shape)
    live_ref[...] = jnp.where(live, grad, 0.0).astype(bf16)


def back_norm(count, own, core, far, hidden, out_grad, gain):
    slot_len, width = hidden.shape
    rows = 128
    row = lambda g: (g, 0)
    block = pl.BlockSpec((rows, width), row)
    return pl.pallas_call(
        back_norm_kernel,
        grid=(slot_len // rows,),
        in_specs=[pl.BlockSpec(memory_space=pltpu.SMEM)]
        + [block] * 5
        + [pl.BlockSpec((1, width), lambda g: (0, 0))],
        out_specs=[block, block],
        out_shape=[
            jax.ShapeDtypeStruct((slot_len, width), f32),
            jax.ShapeDtypeStruct((slot_len, width), bf16),
        ],
        compiler_params=pltpu.CompilerParams(vmem_limit_bytes=VMEM_BYTES),
        cost_estimate=pl.CostEstimate(
            flops=20 * slot_len * width, bytes_accessed=22 * slot_len * width, transcendentals=0
        ),
        name="back_norm",
    )(count, own, core, far, hidden, out_grad, gain)


def backward_kernel(heads, masks, slot_len, keys, *refs):
    (lens_ref, lse_near, lse_far), refs = refs[:3], refs[3:]
    loaded = 8 + 3 * heads
    sources, refs = refs[:loaded], refs[loaded:]
    (gain_ref, go_near, go_far, out_part, new_ref, conv_ref, key_t_hbm, in_hbm, inputs_hbm, hidden_hbm), refs = refs[:10], refs[10:]
    (grad_out, sum_rows, input_grad_hbm, go_out, gain_out, in_got, new_got, conv_got), refs = refs[:8], refs[8:]
    held, refs = refs[:loaded], refs[loaded:]
    (q_near, k_near, v_near, gm_near, q_far, k_far, v_far, gm_far), more = held[:8], held[8:]
    wq, wk, wv = more[:heads], more[heads : 2 * heads], more[2 * heads :]
    (key_t, probs, grads, dkv, terms, own_terms, got_near, got_far, got_x), refs = refs[:9], refs[9:]
    bits = len(masks)
    in_kept, refs = refs[0], refs[1:]
    in_got_rs, refs = refs[:bits], refs[bits:]
    out_got_rs, refs = refs[: bits - 1], refs[bits - 1 :]
    go_core_near, go_core_far, go_x, refs = refs[0], refs[1], refs[2], refs[3:]
    go_rs, refs = refs[:bits], refs[bits:]
    sum_rs, refs = refs[:bits], refs[bits:]
    grad_normed, gain_terms, sems = refs
    head = lax.axis_index("head")
    dp = lax.axis_index("dp")
    flags = [jnp.where(jnp.bitwise_and(dp, mask) != 0, 1, 0) for mask in masks]

    def head_device(r):
        return (dp, jnp.bitwise_xor(head, r))

    def dp_device(n):
        return (jnp.bitwise_xor(dp, masks[n]), head)

    barrier = pltpu.get_barrier_semaphore()
    for r in range(1, heads):
        pl.semaphore_signal(barrier, inc=1, device_id=head_device(r), device_id_type=MESH)
    for n in range(bits):
        pl.semaphore_signal(barrier, inc=1, device_id=dp_device(n), device_id_type=MESH)
    pl.semaphore_wait(barrier, heads - 1 + bits)

    slots = {}

    def remote(name, source, target, device, part=0):
        if name not in slots:
            slots[name] = 2 * len(slots)
        at = slots[name] + part
        return pltpu.make_async_remote_copy(
            src_ref=source,
            dst_ref=target,
            send_sem=sems.at[0, at],
            recv_sem=sems.at[1, at],
            device_id=device,
            device_id_type=MESH,
        )

    def local(name, source, target):
        if name not in slots:
            slots[name] = 2 * len(slots)
        return pltpu.make_async_copy(source, target, sems.at[0, slots[name]])

    whole = slice(None)

    def rs_copy(name, held, got, n, part=0):
        return remote(
            f"{name}{n}", held.at[(whole,) * n + (1 - flags[n],)], got, dp_device(n), part
        )

    def rs_add(held, got, n):
        for at in range(2**n):
            index = tuple((at >> (n - 1 - b)) & 1 for b in range(n))
            mine = held[index + (flags[n],)]
            got[index] = (got[index].astype(f32) + mine.astype(f32)).astype(bf16)

    def ag_copy(name, block, n, part=0):
        region = block.at[(whole,) * n + tuple(flags[n:])]
        return remote(f"{name}{n}", region, region, dp_device(n), part)

    fetches = [local(f"fetch_{n}", source, target) for n, (source, target) in enumerate(zip(sources, held))]
    for n in (4, 5, 6, 7):
        fetches[n].start()
    load_keys = local("load_keys", key_t_hbm, key_t)
    load_keys.start()
    for n in range(loaded):
        if n not in (4, 5, 6, 7):
            fetches[n].start()
    in_y = remote("in_rs", in_hbm.at[(whole,) * (bits - 1) + (1 - flags[bits - 1],)], in_got_rs[bits - 1], dp_device(bits - 1))
    in_y.start()
    load_in = local("load_in", in_hbm.at[(whole,) * (bits - 1) + (flags[bits - 1],)], in_kept)
    load_in.start()
    out_z = rs_copy("out_rs", out_part, out_got_rs[bits - 2], bits - 2)
    out_z.start()
    rows_o = go_x.shape[0]
    go_core = [
        remote("go_near", go_near.at[pl.ds(rows_o, rows_o)], go_core_near, head_device(1)),
        remote("go_far", go_far.at[pl.ds(rows_o, rows_o)], go_core_far, head_device(1)),
    ]
    for copy in go_core:
        copy.start()
    closing = []
    for name, source, target in (("new", new_ref, new_got), ("conv", conv_ref, conv_got)):
        for r in range(1, heads):
            copy = remote(
                f"{name}_{r}",
                source.at[jnp.bitwise_xor(head, r)],
                target.at[head],
                head_device(r),
            )
            copy.start()
            closing.append(copy)
        target[head] = source[head]
    go_to_x = remote("go_x", go_core_far, go_x, head_device(2))
    grad_normed[...] = jnp.zeros(grad_normed.shape, f32)
    c = score_scale * log2e

    def core_copy(r, p):
        return remote(f"core_{r}", terms.at[r - 1], (got_near if r == 1 else got_far).at[p], head_device(1), p)

    def x_copy(p):
        return remote("x_terms", terms.at[1], got_x.at[p], head_device(2), p)

    def sum_y(p):
        return rs_copy("sum", own_terms.at[p], sum_rs[bits - 1].at[p], bits - 1, p)

    def sum_copy(p, n):
        return rs_copy("sum", sum_rs[n + 1].at[p], sum_rs[n].at[p], n, p)

    def sum_gather(p, n):
        return ag_copy("gather", sum_rows.at[p], n, p)

    def add_rows(target, source):
        for at in range(target.shape[0]):
            target[at] = (target[at].astype(f32) + source[at].astype(f32)).astype(bf16)

    def each_block(function):
        def step(at, carry):
            function(tuple(lax.rem(lax.div(at, 2 ** (bits - 1 - b)), 2) for b in range(bits)))
            return carry

        lax.fori_loop(0, 2**bits, step, 0)

    def add_whole(target, source):
        def one(index):
            target[index] = (target[index].astype(f32) + source[index].astype(f32)).astype(bf16)

        each_block(one)

    def attend(r, p):
        half_q, half_k, half_v, half_g, half_l = (
            (q_near, k_near, v_near, gm_near, lse_near)
            if r < 2
            else (q_far, k_far, v_far, gm_far, lse_far)
        )
        cut = pl.ds(pl.multiple_of((r % 2) * 2 * E + p * E, E), E)
        q = half_q[:, cut]
        g = half_g[:, cut]
        q_t = q.T
        g_t = g.T
        k_t = half_k[:, cut].T
        lse = half_l[(r % 2) * 2 + p]
        row_dot = jnp.zeros((1, slot_len), f32)
        for kb in range(6):
            first = BLOCK if kb == 5 else 0
            rows = slice(kb * BLOCK, (kb + 1) * BLOCK)
            s = masked_scores(kb, lens_ref, dot(half_k[rows, cut], q_t[:, first:]))
            pr = jnp.exp2(s * c - lse[:, first:])
            gp = dot(half_v[rows, cut], g_t[:, first:])
            probs[rows, first:] = pr
            grads[rows, first:] = gp
            part = jnp.sum(pr * gp, axis=0, keepdims=True)
            dkv[rows, E:] = dot(pr.astype(bf16), g[first:]).astype(bf16)
            if first:
                row_dot = jnp.concatenate([row_dot[:, :first], row_dot[:, first:] + part], axis=1)
            else:
                row_dot = row_dot + part
        dq = jnp.zeros((E, slot_len), f32)
        for kb in range(6):
            first = BLOCK if kb == 5 else 0
            rows = slice(kb * BLOCK, (kb + 1) * BLOCK)
            ds = (probs[rows, first:] * (grads[rows, first:] - row_dot[:, first:])).astype(bf16)
            dkv[rows, :E] = (dot(ds, q[first:]) * score_scale).astype(bf16)
            out = dot(k_t[:, rows], ds)
            if first:
                dq = jnp.concatenate([dq[:, :first], dq[:, first:] + out], axis=1)
            else:
                dq = dq + out
        return (dq * score_scale).T.astype(bf16)

    per_block = own_terms.shape[1 + bits]

    def weight_terms(dq, target):
        blocks = 2 ** (bits - 1)
        many = blocks * per_block

        def one(at, carry):
            rows = pl.ds(pl.multiple_of(at * many, many), many)
            of_kv = dot(key_t[rows, :], dkv[...]).astype(bf16)
            of_q = dot(key_t[rows, keys - slot_len :], dq).astype(bf16)
            for n in range(blocks):
                index = (at,) + tuple((n >> (bits - 2 - b)) & 1 for b in range(bits - 1))
                cut = slice(n * per_block, (n + 1) * per_block)
                target[index + (whole, slice(0, 2 * E))] = of_kv[cut]
                target[index + (whole, slice(2 * E, 3 * E))] = of_q[cut]
            return carry

        lax.fori_loop(0, 2, one, 0)

    def normed_terms(r, p, dq):
        cut = pl.ds(pl.multiple_of(p * E, E), E)
        dk = dkv[keys - slot_len :, :E]
        dv = dkv[keys - slot_len :, E:]
        columns = 256
        for n in range(grad_normed.shape[1] // columns):
            rows = slice(n * columns, (n + 1) * columns)
            grad_normed[:, rows] += (
                dot_nt(dq, wq[r][rows, cut])
                + dot_nt(dk, wk[r][rows, cut])
                + dot_nt(dv, wv[r][rows, cut])
            )

    def parity(p, carry):
        first = p == 0
        dq = attend(3, p)

        @pl.when(first)
        def _():
            load_keys.wait()
            for n in range(loaded):
                if n not in (4, 5, 6, 7):
                    fetches[n].wait()

        @pl.when(p == 1)
        def _():
            core_copy(3, 0).wait_send()

        weight_terms(dq, terms.at[2])
        core_copy(3, p).start()
        normed_terms(3, p, dq)

        @pl.when(first)
        def _():
            for copy in go_core:
                copy.wait_recv()
            go_core_far[...] = (
                go_core_far[...].astype(f32) + go_far[:rows_o].astype(f32)
            ).astype(bf16)
            go_to_x.start()

        dq = attend(2, p)

        @pl.when(p == 1)
        def _():
            x_copy(0).wait_send()

        weight_terms(dq, terms.at[1])
        core_copy(3, p).wait_recv()
        add_whole(terms.at[1], got_far.at[p])
        x_copy(p).start()
        normed_terms(2, p, dq)

        @pl.when(first)
        def _():
            out_z.wait_recv()
            rs_add(out_part, out_got_rs[bits - 2], bits - 2)
            if bits > 2:
                rs_copy("out_rs", out_got_rs[bits - 2], out_got_rs[bits - 3], bits - 3).start()

        @pl.when(p == 1)
        def _():
            in_y.wait_recv()
            load_in.wait()
            held = in_got_rs[bits - 1]
            for at in range(2 ** (bits - 1)):
                index = tuple((at >> (bits - 2 - b)) & 1 for b in range(bits - 1))
                held[index] = (held[index].astype(f32) + in_kept[index].astype(f32)).astype(bf16)
            rs_copy("in_rs", held, in_got_rs[bits - 2], bits - 2).start()

        dq = attend(1, p)

        @pl.when(p == 1)
        def _():
            core_copy(1, 0).wait_send()

        weight_terms(dq, terms.at[0])
        core_copy(1, p).start()
        normed_terms(1, p, dq)

        @pl.when(p == 1)
        def _():
            x_copy(0).wait_recv()
            add_whole(own_terms.at[0], got_x.at[0])
            sum_y(0).start()

        dq = attend(0, p)
        weight_terms(dq, own_terms.at[p])
        core_copy(1, p).wait_recv()
        add_whole(own_terms.at[p], got_near.at[p])
        normed_terms(0, p, dq)

        @pl.when(first)
        def _():
            go_to_x.wait_recv()
            for at in range(2**bits):
                rows = slice(at * rows_o // 2**bits, (at + 1) * rows_o // 2**bits)
                index = tuple((at >> (bits - 1 - b)) & 1 for b in range(bits))
                go_out[index] = (
                    go_near[rows].astype(f32)
                    + go_core_near[rows].astype(f32)
                    + go_x[rows].astype(f32)
                ).astype(bf16)
            rs_copy("go_rs", go_out, go_rs[bits - 1], bits - 1).start()

        @pl.when(p == 1)
        def _():
            rs_copy("go_rs", go_out, go_rs[bits - 1], bits - 1).wait()
            rs_add(go_out, go_rs[bits - 1], bits - 1)
            rs_copy("go_rs", go_rs[bits - 1], go_rs[bits - 2], bits - 2).start()

        return carry

    for n in (4, 5, 6, 7):
        fetches[n].wait()
    lax.fori_loop(0, 2, parity, 0)

    loads = []
    wide = probs.shape[1]
    for name, source, target in (("inputs", inputs_hbm, probs), ("hidden", hidden_hbm, grads)):
        for n in range(2):
            copy = local(
                f"load_{name}{n}",
                source.at[:, pl.ds(n * wide, wide)],
                target.at[pl.ds(n * slot_len, slot_len)],
            )
            copy.start()
            loads.append(copy)
    in_last = rs_copy("in_rs", in_got_rs[bits - 1], in_got_rs[bits - 2], bits - 2)
    in_last.wait_recv()
    rs_add(in_got_rs[bits - 1], in_got_rs[bits - 2], bits - 2)

    def in_rest(n):
        copy = rs_copy("in_rs", in_got_rs[n + 1], in_got_rs[n], n)
        return copy

    for n in reversed(range(bits - 2)):
        in_rest(n).start()
        if n:
            in_rest(n).wait_recv()
            rs_add(in_got_rs[n + 1], in_got_rs[n], n)
    sum_y(0).wait_recv()
    rs_add(own_terms.at[0], sum_rs[bits - 1].at[0], bits - 1)
    sum_copy(0, bits - 2).start()

    for copy in loads:
        copy.wait()
    gain_row = gain_ref[...]

    def input_rows(at, carry):
        rows = pl.ds(pl.multiple_of(at * 128, 128), 128)
        lower = pl.ds(pl.multiple_of(slot_len + at * 128, 128), 128)
        values = jnp.concatenate([probs[rows], probs[lower]], axis=1)
        before = jnp.concatenate([grads[rows], grads[lower]], axis=1)
        grad_normed[rows] = before + norm_input_grad(values, gain_row, grad_normed[rows])
        return carry

    lax.fori_loop(0, slot_len // 128, input_rows, 0)
    store_grad = local("store_grad", grad_normed, input_grad_hbm)
    store_grad.start()

    x_copy(1).wait_recv()
    add_whole(own_terms.at[1], got_x.at[1])
    sum_y(1).start()

    rs_copy("go_rs", go_rs[bits - 1], go_rs[bits - 2], bits - 2).wait_recv()
    rs_add(go_rs[bits - 1], go_rs[bits - 2], bits - 2)
    for n in reversed(range(bits - 2)):
        rs_copy("go_rs", go_rs[n + 1], go_rs[n], n).start()
        if n:
            rs_copy("go_rs", go_rs[n + 1], go_rs[n], n).wait_recv()
            rs_add(go_rs[n + 1], go_rs[n], n)
    sum_copy(0, bits - 2).wait_recv()
    rs_add(sum_rs[bits - 1].at[0], sum_rs[bits - 2].at[0], bits - 2)
    for n in reversed(range(bits - 2)):
        sum_copy(0, n).start()
        if n:
            sum_copy(0, n).wait_recv()
            rs_add(sum_rs[n + 1].at[0], sum_rs[n].at[0], n)

    for n in reversed(range(bits - 2)):
        copy = rs_copy("out_rs", out_got_rs[n + 1], out_got_rs[n], n)
        if n != bits - 3:
            copy.start()
        copy.wait_recv()
        rs_add(out_got_rs[n + 1], out_got_rs[n], n)
    grad_out[...] = out_got_rs[0][...].astype(f32)
    in_rest(0).wait_recv()
    rs_add(in_got_rs[1], in_got_rs[0], 0)
    in_copies = []
    for r in range(1, heads):
        copy = remote(
            f"in_{r}", in_got_rs[0].at[jnp.bitwise_xor(head, r)], in_got.at[head], head_device(r)
        )
        copy.start()
        in_copies.append(copy)
    in_got[head] = in_got_rs[0][head]

    rs_copy("go_rs", go_rs[1], go_rs[0], 0).wait_recv()
    rs_add(go_rs[1], go_rs[0], 0)
    go_out[tuple(flags)] = go_rs[0][...]
    go_gather = [ag_copy("go_ag", go_out, n) for n in range(bits)]
    go_gather[0].start()

    def gain_part(p):
        rows = pl.ds(pl.multiple_of(dp * per_block, per_block), per_block)
        total = jnp.zeros((per_block, 1), f32)
        grad = sum_rs[0][p]
        for n, weight in enumerate((wk[0], wv[0], wq[0])):
            own = weight[rows, p * E : (p + 1) * E].astype(f32)
            total = total + jnp.sum(
                grad[:, n * E : (n + 1) * E].astype(f32) * own, axis=1, keepdims=True
            )
        return total

    sum_copy(0, 0).wait_recv()
    rs_add(sum_rs[1].at[0], sum_rs[0].at[0], 0)
    sum_rows[(0,) + tuple(flags)] = sum_rs[0][0]
    sum_gather(0, 0).start()
    sum_y(1).wait_recv()
    rs_add(own_terms.at[1], sum_rs[bits - 1].at[1], bits - 1)
    sum_copy(1, bits - 2).start()
    gain = gain_part(0)
    go_gather[0].wait_recv()
    if bits > 1:
        go_gather[1].start()
    sum_gather(0, 0).wait_recv()
    sum_gather(0, 1).start()
    for n in reversed(range(bits - 1)):
        sum_copy(1, n).wait_recv()
        rs_add(sum_rs[n + 1].at[1], sum_rs[n].at[1], n)
        if n:
            sum_copy(1, n - 1).start()
    sum_rows[(1,) + tuple(flags)] = sum_rs[0][1]
    sum_gather(1, 0).start()
    gain = gain + gain_part(1)
    gain_terms[head] = jnp.broadcast_to(gain, gain_terms.shape[1:])
    gain_copies = []
    for r in range(1, heads):
        copy = remote(f"gain_{r}", gain_terms.at[head], gain_terms.at[head], head_device(r))
        copy.start()
        gain_copies.append(copy)
    for n in range(1, bits):
        go_gather[n].wait_recv()
        if n + 1 < bits:
            go_gather[n + 1].start()
        sum_gather(0, n).wait_recv()
        if n + 1 < bits:
            sum_gather(0, n + 1).start()
        sum_gather(1, n - 1).wait_recv()
        sum_gather(1, n).start()
    for copy in gain_copies:
        copy.wait_recv()
    gain_out[...] = sum(gain_terms[h] for h in range(heads))
    for copy in closing + in_copies:
        copy.wait()
    sum_gather(1, bits - 1).wait_recv()
    store_grad.wait()

    in_y.wait_send()
    for copy in go_core + gain_copies + go_gather:
        copy.wait_send()
    go_to_x.wait_send()
    for p in range(2):
        sum_y(p).wait_send()
        for n in range(bits - 1):
            sum_copy(p, n).wait_send()
        for n in range(bits):
            sum_gather(p, n).wait_send()
    for r in (1, 3):
        core_copy(r, 1).wait_send()
    x_copy(1).wait_send()
    out_z.wait_send()
    for n in range(bits - 2):
        rs_copy("out_rs", out_got_rs[n + 1], out_got_rs[n], n).wait_send()
    in_last.wait_send()
    for n in range(bits - 2):
        in_rest(n).wait_send()
    for n in range(bits - 1):
        rs_copy("go_rs", go_rs[n + 1], go_rs[n], n).wait_send()


def backward(lens, near, far, wq, wk, wv, gain, go_near, go_far, out_part, new_cols, conv, key_t, grad_in, inputs, grad_hidden):
    heads, dps = lax.axis_size("head"), lax.axis_size("dp")
    masks = [1 << b for b in reversed(range(dps.bit_length() - 1))]
    bits = len(masks)
    slot_len, width = inputs.shape
    keys = key_t.shape[1]
    shape = jax.ShapeDtypeStruct
    twos = lambda n: (2,) * n
    in_block = grad_in.shape[bits:]
    out_block = out_part.shape[bits - 1 :]
    rows_o = go_near.shape[0] // 2
    go_block = (rows_o // dps, width)
    sum_block = (width // dps, 3 * E)
    copies = 60 + 16 * bits + 2 * (8 + 3 * heads)
    q_n, k_n, v_n, g_n, l_n = near
    q_f, k_f, v_f, g_f, l_f = far
    loaded = (q_n, k_n, v_n, g_n, q_f, k_f, v_f, g_f, *wq, *wk, *wv)
    scratch = (
        [pltpu.VMEM(value.shape, value.dtype) for value in loaded]
        + [
            pltpu.VMEM((width, keys), bf16),
            pltpu.VMEM((keys, slot_len), f32),
            pltpu.VMEM((keys, slot_len), f32),
            pltpu.VMEM((keys, 2 * E), bf16),
            pltpu.VMEM((3,) + twos(bits) + sum_block, bf16),
            pltpu.VMEM((2,) + twos(bits) + sum_block, bf16),
            pltpu.VMEM((2,) + twos(bits) + sum_block, bf16),
            pltpu.VMEM((2,) + twos(bits) + sum_block, bf16),
            pltpu.VMEM((2,) + twos(bits) + sum_block, bf16),
            pltpu.VMEM(twos(bits - 1) + in_block, bf16),
        ]
        + [pltpu.VMEM(twos(n) + in_block, bf16) for n in range(bits)]
        + [pltpu.VMEM(twos(n) + out_block, bf16) for n in range(bits - 1)]
        + [pltpu.VMEM((rows_o, width), bf16)] * 3
        + [pltpu.VMEM(twos(n) + go_block, bf16) for n in range(bits)]
        + [pltpu.VMEM((2,) + twos(n) + sum_block, bf16) for n in range(bits)]
        + [
            pltpu.VMEM((slot_len, width), f32),
            pltpu.VMEM((heads, width // dps, E), f32),
            pltpu.SemaphoreType.DMA((2, copies)),
        ]
    )
    return pl.pallas_call(
        functools.partial(backward_kernel, heads, masks, slot_len, keys),
        in_specs=[pl.BlockSpec(memory_space=pltpu.SMEM)]
        + [vmem()] * 2
        + [anywhere()] * len(loaded)
        + [vmem()] * 6
        + [anywhere()] * 4,
        out_specs=[vmem()] * 2 + [anywhere()] + [vmem()] * 5,
        out_shape=[
            shape(out_block, f32),
            shape((2,) + twos(bits) + sum_block, bf16),
            shape((slot_len, width), f32),
            shape(twos(bits) + go_block, bf16),
            shape((width // dps, E), f32),
            shape(in_block, bf16),
            shape(new_cols.shape, bf16),
            shape(conv.shape, bf16),
        ],
        scratch_shapes=scratch,
        compiler_params=pltpu.CompilerParams(
            collective_id=1, has_side_effects=True, vmem_limit_bytes=61 * 2**20
        ),
        cost_estimate=pl.CostEstimate(flops=60 * 10**9, bytes_accessed=0, transcendentals=0),
        name="backward",
    )(lens, l_n, l_f, *loaded, gain, go_near, go_far, out_part, new_cols, conv, key_t, grad_in, inputs, grad_hidden)


def swap_head(value, mask):
    size = lax.axis_size("head")
    return lax.ppermute(value, "head", [(i, i ^ mask) for i in range(size)])


def swap_dp(value, mask):
    size = lax.axis_size("dp")
    return lax.ppermute(value, "dp", [(i, i ^ mask) for i in range(size)])


def has(index, mask):
    return (index & mask) != 0


def both(flag, own, other, axis):
    return jnp.stack([jnp.where(flag, other, own), jnp.where(flag, own, other)], axis=axis)


def meet(*values):
    flat, tree = jax.tree.flatten(values)
    return jax.tree.unflatten(tree, lax.optimization_barrier(flat))


def gather_step(value, masks, n):
    return (value, swap_dp(value, masks[n]))


def gather_settle(pair, masks, n):
    return both(has(lax.axis_index("dp"), masks[n]), *pair, n)


def gather_early(value, masks):
    for n in range(len(masks) - 3):
        value = gather_settle(gather_step(value, masks, n), masks, n)
    return gather_step(value, masks, len(masks) - 3)


def scatter_split(value, masks, n):
    flag = has(lax.axis_index("dp"), masks[n])
    low = lax.index_in_dim(value, 0, n, keepdims=False)
    high = lax.index_in_dim(value, 1, n, keepdims=False)
    return jnp.where(flag, high, low), jnp.where(flag, low, high)


def scatter_step(value, masks, n):
    kept, sent = scatter_split(value, masks, n)
    return (kept, swap_dp(sent, masks[n]))


def scatter_settle(pair):
    return (pair[0].astype(f32) + pair[1].astype(f32)).astype(bf16)


def scatter_late(value, masks):
    for n in reversed(range(1, len(masks) - 2)):
        value = scatter_settle(scatter_step(value, masks, n))
    return scatter_step(value, masks, 0)


def cut_bits(value, masks):
    return value.reshape((2,) * len(masks) + value.shape[1:])


def cut_in_kernel(in_ref, out_ref):
    heads, units = out_ref.shape[0], E
    head = lax.axis_index("head")
    for r in range(heads):
        other = jnp.bitwise_xor(head, r)
        for i in range(out_ref.shape[2] // units):
            source = pl.multiple_of((i * heads + other) * units, units)
            out_ref[r, :, i * units : (i + 1) * units] = in_ref[:, pl.ds(source, units)]


def cut_in(w_in, heads, dps):
    rows, units = w_in.shape[0], w_in.shape[1] // (heads * dps)
    if units == E:
        return pl.pallas_call(
            cut_in_kernel,
            in_specs=[vmem()],
            out_specs=vmem(),
            out_shape=jax.ShapeDtypeStruct((heads, rows, dps * units), bf16),
            name="cut_in",
        )(w_in)
    head = lax.axis_index("head")
    cut = w_in.reshape(rows, dps, heads, units)
    return jnp.stack(
        [
            lax.dynamic_index_in_dim(cut, head ^ r, 2, keepdims=False).reshape(rows, dps * units)
            for r in range(heads)
        ]
    )


def unpack(values, counts):
    parts, at = [], 0
    for count in counts:
        parts.append(values[at : at + count])
        at += count
    return parts


def shards(
    inputs,
    memory,
    compressed,
    counts,
    mem_lens,
    cmem_lens,
    norm_gain,
    w_query,
    w_key,
    w_value,
    w_output,
    ffn_gain,
    w_in,
    w_out,
    w_conv,
    out_grad,
    comp_grad,
):
    slot_len, width = inputs.shape[1:]
    heads, dps = lax.axis_size("head"), lax.axis_size("dp")
    masks = [1 << b for b in reversed(range(dps.bit_length() - 1))]
    bits = len(masks)
    group = memory.shape[0]
    head_at, dp_at = lax.axis_index("head"), lax.axis_index("dp")
    head_width = w_query.shape[1]
    new_rows = comp_grad.shape[1]
    conv_cols = width // heads
    count = lax.dynamic_slice_in_dim(counts, head_at, 1)
    lens = lax.dynamic_index_in_dim(jnp.stack([cmem_lens, mem_lens]), head_at, 1, keepdims=False)

    gains = jnp.pad(jnp.stack([norm_gain, ffn_gain]).astype(f32), ((0, 6), (0, 0)))
    limits = jnp.minimum(counts, mem_lens)
    (
        (gain_rows, lse_near, lse_far),
        (conv_rows, grad_ffn, q_near, k_near, v_near, q_far, k_far, v_far, mixed_near, mixed_far),
        (key_t, hidden, normed_two),
        weights,
        (grad_conv, w_in_own, w_out_own, gf_rest),
    ) = unpack(
        forward(
            count,
            lens,
            limits,
            cut_in(w_in, heads, dps),
            w_conv,
            comp_grad[0],
            gains,
            (w_query, w_key, w_value, w_output),
            w_out,
            out_grad[0],
            inputs[0],
            memory,
            compressed,
        ),
        (3, 10, 3, 12, 4),
    )
    gain_one, gain_two = gain_rows[0:1], gain_rows[1:2]
    wq, wk, wv, wo = (
        [own] + [w.reshape(own.shape) for w in weights[3 * n : 3 * n + 3]]
        for n, own in enumerate((w_query, w_key, w_value, w_output))
    )
    w_in_own = w_in_own.reshape(width, -1)
    w_out_own = w_out_own.reshape(-1, width)
    gf_core, gf_x, gf_diag = (gf_rest[n] for n in range(3))
    pad_rows = (new_rows + 15) // 16 * 16

    n2_x = swap_head(normed_two, 2)
    n2_core = swap_head(normed_two, 1)
    conv_step = gather_early(conv_rows, masks)

    def feed_forward(tokens, cot):
        inner = dot(tokens, w_in_own)
        activated = jax.nn.gelu(inner).astype(bf16)
        grad_act = dot_nt(cot, w_out_own)
        grad_inner = jax.vjp(jax.nn.gelu, inner)[1](grad_act)[0].astype(bf16)
        return activated, grad_inner, dot_nt(grad_inner, w_in_own)

    n2_near = jnp.concatenate([normed_two, n2_core])
    gf_near = jnp.concatenate([grad_ffn, gf_core])
    act_near, gi_near, gn_near = feed_forward(n2_near, gf_near)
    gn_own, gn_sent = gn_near[:slot_len], gn_near[slot_len:].astype(bf16)
    (n2_x, conv_step, act_near, gi_near, gn_own, gn_sent, grad_conv) = meet(
        n2_x, conv_step, act_near, gi_near, gn_own, gn_sent, grad_conv
    )

    n2_far = jnp.concatenate([n2_x, swap_head(n2_x, 1)])
    gf_far = jnp.concatenate([gf_x, gf_diag])
    gn_core = swap_head(gn_sent, 1)
    conv_step = gather_step(gather_settle(conv_step, masks, bits - 3), masks, bits - 2)
    grad_conv = grad_conv.reshape(dps, -1, conv_cols)
    conv_back = scatter_step(cut_bits(grad_conv, masks), masks, bits - 1)
    act_far, gi_far, gn_far = feed_forward(n2_far, gf_far)
    gn_far_core = swap_head(gn_far[slot_len:].astype(bf16), 1)
    gn_far = (gn_far[:slot_len] + gn_far_core.astype(f32)).astype(bf16)
    (n2_far, gf_far, gn_core, conv_step, act_far, gi_far, gn_far) = meet(
        n2_far, gf_far, gn_core, conv_step, act_far, gi_far, gn_far
    )

    gn_back = swap_head(gn_far, 2)
    conv_step = gather_step(gather_settle(conv_step, masks, bits - 2), masks, bits - 1)
    out_far = dot(act_far, w_out_own)
    out_far_core = swap_head(out_far[slot_len:].astype(bf16), 1)
    out_far = (out_far[:slot_len] + out_far_core.astype(f32)).astype(bf16)
    grad_w_out = (dot_tn(act_near, gf_near) + dot_tn(act_far, gf_far)).astype(bf16)
    grad_w_in = (dot_tn(n2_near, gi_near) + dot_tn(n2_far, gi_far)).astype(bf16)
    out_near = dot(act_near, w_out_own)
    out_core = swap_head(out_near[slot_len:].astype(bf16), 1)
    out_own = out_near[:slot_len]
    (gn_back, conv_back, conv_step, out_far, grad_w_out, grad_w_in, out_own, out_core, memory) = meet(
        gn_back, conv_back, conv_step, out_far, grad_w_out, grad_w_in, out_own, out_core, memory
    )

    out_back = swap_head(out_far, 2)
    w_out_back = scatter_step(
        cut_bits(grad_w_out.reshape(dps, -1, width), masks), masks, bits - 1
    )
    conv_back = scatter_step(scatter_settle(conv_back), masks, bits - 2)
    conv_tap = gather_settle(conv_step, masks, bits - 1).reshape(3, width, conv_cols)
    source = jnp.arange(memory.shape[1], dtype=jnp.int32)
    new_cols = 0.0
    for tap in range(3):
        picked = 3 * jnp.arange(pad_rows, dtype=jnp.int32) + tap
        pick = (
            (source[None, None, :] == picked[None, :, None])
            & (source[None, None, :] < limits[:, None, None])
        ).astype(bf16)
        rows = jnp.einsum("gcr,grd->gcd", pick, memory, preferred_element_type=f32).astype(bf16)
        new_cols = new_cols + dot(rows.reshape(group * pad_rows, width), conv_tap[tap])
    new_cols = new_cols.astype(bf16)
    grad_hidden, grad_attention = back_norm(
        count, gn_own, gn_core, gn_back, hidden, out_grad[0], gain_two
    )
    gm_near = jnp.concatenate([dot_nt(grad_attention, w) for w in wo[:2]], axis=1).astype(bf16)
    gm_far = jnp.concatenate([dot_nt(grad_attention, w) for w in wo[2:]], axis=1).astype(bf16)
    go_near = dot_tn(mixed_near, grad_attention).astype(bf16)
    go_far = dot_tn(mixed_far, grad_attention).astype(bf16)
    (w_out_back, conv_back, grad_hidden, gm_near, gm_far, go_near, go_far, grad_w_in, new_cols) = meet(
        w_out_back, conv_back, grad_hidden, gm_near, gm_far, go_near, go_far, grad_w_in, new_cols
    )

    conv_back = scatter_late(scatter_settle(conv_back), masks)

    grad_w_out, sum_rows, input_grad, grad_out, gain_terms, grad_w_in, new_all, grad_conv = backward(
        lens,
        (q_near, k_near, v_near, gm_near, lse_near),
        (q_far, k_far, v_far, gm_far, lse_far),
        wq,
        wk,
        wv,
        gain_one,
        go_near,
        go_far,
        scatter_settle(w_out_back),
        new_cols.reshape(group, -1, conv_cols),
        scatter_settle(conv_back).reshape(heads, w_conv.shape[0], conv_cols),
        key_t,
        cut_bits(grad_w_in.reshape((dps, heads, w_in.shape[0], -1)), masks),
        inputs[0],
        grad_hidden,
    )
    row_pos = jnp.arange(slot_len, dtype=jnp.int32)
    row_live = (row_pos < count).astype(f32)[:, None]
    outputs = hidden + row_live * (out_own + out_core.astype(f32) + out_back.astype(f32))
    new_compressed = new_all.transpose(1, 0, 2).reshape(-1, width)[:new_rows].astype(f32)
    grad_conv = grad_conv.transpose(1, 0, 2).reshape(w_conv.shape).astype(f32)
    grad_w_in = (
        grad_w_in.reshape(heads, w_in.shape[0], dps, -1)
        .transpose(1, 2, 0, 3)
        .reshape(w_in.shape)
        .astype(f32)
    )
    own_gain_two = lax.dynamic_slice_in_dim(
        gain_two[0], (dp_at * heads + head_at) * w_in.shape[0], w_in.shape[0]
    )
    grad_gain_two = jnp.sum(grad_w_in * w_in.astype(f32), axis=1) / own_gain_two
    grad_gain_one = lax.dynamic_slice_in_dim(
        gain_terms[:, 0], head_at * norm_gain.shape[0], norm_gain.shape[0]
    ) / norm_gain.astype(f32)
    sums = sum_rows.reshape(2, width, 3 * E).astype(f32)
    grad_key, grad_value, grad_query = (
        jnp.concatenate([sums[0, :, n * E : (n + 1) * E], sums[1, :, n * E : (n + 1) * E]], axis=1)
        for n in range(3)
    )
    grad_out = grad_out.reshape(w_output.shape).astype(f32)

    return (
        outputs[None],
        input_grad[None],
        new_compressed[None],
        grad_gain_one,
        grad_query,
        grad_key,
        grad_value,
        grad_out,
        grad_gain_two,
        grad_w_in,
        grad_w_out.reshape(w_out.shape).astype(f32),
        grad_conv,
    )


def solution(mesh):
    whole = P(("dp", "head"), None, None)
    rows = P(("dp", "head"), None)
    vector = P(("dp", "head"))
    columns = P(None, "head")
    placed = (
        whole,
        P("dp", None, None),
        P("dp", None, None),
        P("dp"),
        P("dp"),
        P("dp"),
        vector,
        columns,
        columns,
        columns,
        P("head", None),
        vector,
        rows,
        rows,
        rows,
        whole,
        whole,
    )
    return jax.shard_map(
        shards,
        mesh=mesh,
        in_specs=placed,
        out_specs=(
            whole,
            whole,
            whole,
            vector,
            columns,
            columns,
            columns,
            P("head", None),
            vector,
            rows,
            rows,
            rows,
        ),
        check_vma=False,
    )
```

```python
import functools

import jax
import jax.numpy as jnp
from jax import lax
from jax.experimental import pallas as pl
from jax.experimental.pallas import tpu as pltpu
from jax.sharding import PartitionSpec as P

E = 128
BLOCK = 256
epsilon = 1e-05
masked_value = -1e30
score_scale = E ** (-0.5)
log2e = 1.4426950408889634
bf16 = jnp.bfloat16
f32 = jnp.float32
VMEM_BYTES = 30 * 2**20
MESH = pl.DeviceIdType.MESH


def dot(left, right):
    return jnp.dot(left, right, preferred_element_type=f32)


def dot_tn(left, right):
    return lax.dot_general(left, right, (((0,), (0,)), ((), ())), preferred_element_type=f32)


def dot_nt(left, right):
    return lax.dot_general(left, right, (((1,), (1,)), ((), ())), preferred_element_type=f32)


def layer_norm(values, gain_vec):
    row_mean = jnp.mean(values, axis=-1, keepdims=True)
    centred = values - row_mean
    variance = jnp.mean(centred * centred, axis=-1, keepdims=True)
    return centred * lax.rsqrt(variance + epsilon) * gain_vec


def vmem():
    return pl.BlockSpec(memory_space=pltpu.VMEM)


def anywhere():
    return pl.BlockSpec(memory_space=pl.ANY)


def masked_scores(kb, lens_ref, scores):
    rows = lax.broadcasted_iota(jnp.int32, scores.shape, 0)
    if kb < 4:
        limit = lens_ref[kb // 2] - (kb % 2) * BLOCK
        return jnp.where(rows < limit, scores, masked_value)
    columns = lax.broadcasted_iota(jnp.int32, scores.shape, 1)
    return jnp.where(rows <= columns, scores, masked_value)


STORED = 26


def forward_kernel(heads, dps, masks, group, slot_len, *refs):
    (count_ref, lens_ref, limits_ref), refs = refs[:3], refs[3:]
    (in_pieces, w_conv_ref, cot_ref, gains_ref, wq0, wk0, wv0, wo0), refs = refs[:8], refs[8:]
    (w_out_hbm, out_grad_hbm, inputs_hbm, memory_hbm, cmem_hbm), refs = refs[:5], refs[5:]
    (gain_row_out, lse_near, lse_far), refs = refs[:3], refs[3:]
    places, refs = refs[:STORED], refs[STORED:]
    (w_in_all, w_out_all, gf_rest), refs = refs[:3], refs[3:]
    kept, refs = refs[:STORED], refs[STORED:]
    (conv_out, gf_out, q_near, k_near, v_near, q_far, k_far, v_far, mixed_near, mixed_far), more = kept[:10], kept[10:]
    (key_t, hidden_out, normed_out), more = more[:3], more[3:]
    (wq1, wq2, wq3, wk1, wk2, wk3, wv1, wv2, wv3, wo1, wo2, wo3, conv_grad) = more
    gains_out, cot_out, key_rows, scores, inputs, out_grad, memory, cmem, spread, conv_send, cot_send, sems = refs
    bits = len(masks)
    width = inputs.shape[1]
    half = wk0.shape[1]
    head = lax.axis_index("head")
    dp = lax.axis_index("dp")
    flags = tuple(jnp.where(jnp.bitwise_and(dp, mask) != 0, 1, 0) for mask in masks)
    whole = slice(None)

    def head_device(r):
        return (dp, jnp.bitwise_xor(head, r))

    def dp_device(r):
        return (lax.rem(dp + r, dps), head)

    barrier = pltpu.get_barrier_semaphore()
    for r in range(1, heads):
        pl.semaphore_signal(barrier, inc=1, device_id=head_device(r), device_id_type=MESH)
    for r in range(1, dps):
        pl.semaphore_signal(barrier, inc=1, device_id=dp_device(r), device_id_type=MESH)

    slots = {}

    def slot(name):
        if name not in slots:
            slots[name] = len(slots)
        return slots[name]

    def remote(name, source, target, device):
        at = slot(name)
        return pltpu.make_async_remote_copy(
            src_ref=source,
            dst_ref=target,
            send_sem=sems.at[0, at],
            recv_sem=sems.at[1, at],
            device_id=device,
            device_id_type=MESH,
        )

    def local(name, source, target):
        return pltpu.make_async_copy(source, target, sems.at[0, slot(name)])

    loads = {}
    for name, source, target in [
        ("out_grad", out_grad_hbm, out_grad),
        ("cmem", cmem_hbm.at[head], cmem),
        ("memory", memory_hbm, memory),
        ("inputs", inputs_hbm, inputs),
        ("w_out", w_out_hbm, w_out_all.at[flags]),
        ("in_own", in_pieces.at[0], w_in_all.at[flags + (head,)]),
    ]:
        loads[name] = local(f"load_{name}", source, target)
        loads[name].start()
    sent, stored = [], []

    def store(*buffers):
        for buffer in buffers:
            at = [buffer is other for other in kept].index(True)
            copy = local(f"store_{at}", buffer, places[at])
            copy.start()
            stored.append(copy)

    def send(*args):
        copy = remote(*args)
        copy.start()
        sent.append(copy)
        return copy

    at = dp * heads + head
    short = gains_ref.shape[1]
    lane = lax.broadcasted_iota(jnp.int32, (short, E), 1)
    place = lax.broadcasted_iota(jnp.int32, (short, E), 0) + lax.rem(at * short, E)
    spot = jnp.where(lane == place, 1.0, 0.0).astype(bf16)
    gains_out[at] = dot(gains_ref[...].astype(bf16), spot)
    columns = conv_out.shape[2]
    pad_rows = cot_out.shape[1]
    new_rows = cot_ref.shape[0]
    pl.semaphore_wait(barrier, heads + dps - 2)

    gain_heads = [
        send(f"gain_{r}", gains_out.at[at], gains_out.at[at], head_device(r))
        for r in range(1, heads)
    ]
    in_rows = [
        send(f"in_{r}", in_pieces.at[r], w_in_all.at[flags + (head,)], head_device(r))
        for r in range(1, heads)
    ]
    core = [
        send(f"core_{n}", source, target, head_device(1))
        for n, (source, target) in enumerate(((wk0, wk1), (wv0, wv1), (wq0, wq1), (wo0, wo1)))
    ]
    x_k = send("x_k", wk0, wk2, head_device(2))
    rows_o = wo2.shape[bits]
    own_o = wo0.at[pl.ds(pl.multiple_of(dp * rows_o, rows_o), rows_o)]
    x_o = send("x_o", own_o, wo2.at[flags], head_device(2))

    dp_partners = [(jnp.bitwise_xor(dp, mask), head) for mask in masks]

    def gather(name, block, order, source=None):
        copies, index = [], list(flags)
        for n, bit in enumerate(order):
            part = block.at[tuple(index)]
            first = source if source is not None and n == 0 else part
            copies.append(remote(f"gather_{name}_{n}", first, part, dp_partners[bit]))
            index[bit] = whole
        return copies

    straight = list(range(bits))
    crossed = straight[:-2] + [bits - 1, bits - 2]
    gathers = {
        "out": gather("out", w_out_all, straight, w_out_hbm),
        "in": gather("in", w_in_all, crossed),
        "o": gather("o", wo2, straight),
    }
    gathers["out"][0].start()

    def advance(name, n):
        gathers[name][n].wait_recv()
        if n + 1 < bits:
            gathers[name][n + 1].start()

    small = []
    for r in range(heads):
        other = jnp.bitwise_xor(head, r)
        cut = pl.ds(pl.multiple_of(other * columns, columns), columns)
        conv_piece = w_conv_ref[:, cut]
        cot_piece = jnp.concatenate(
            [cot_ref[:, cut], jnp.zeros((pad_rows - new_rows, columns), f32)], axis=0
        ).astype(bf16)
        if r == 0:
            conv_out[head] = conv_piece
            cot_out[head] = cot_piece
        else:
            conv_send[r - 1] = conv_piece
            cot_send[r - 1] = cot_piece
            small.append(send(f"conv_{r}", conv_send.at[r - 1], conv_out.at[head], head_device(r)))
            small.append(send(f"cot_{r}", cot_send.at[r - 1], cot_out.at[head], head_device(r)))
    for copy in gain_heads:
        copy.wait_recv()
    block = gains_out.at[pl.ds(dp * heads, heads)]
    gain_dps = [send(f"gain_dp_{r}", block, block, dp_device(r)) for r in range(1, dps)]
    for copy in in_rows:
        copy.wait_recv()
    loads["in_own"].wait()
    gathers["in"][0].start()
    x_v = send("x_v", wv0, wv2, head_device(2))
    x_q = send("x_q", wq0, wq2, head_device(2))

    loads["out_grad"].wait()

    def cotangent(n, carry):
        rows = pl.ds(pl.multiple_of(n * 128, 128), 128)
        row = lax.broadcasted_iota(jnp.int32, (128, width), 0) + n * 128
        gf_out[rows] = jnp.where(row < count_ref[0], out_grad[rows], 0.0).astype(bf16)
        return carry

    lax.fori_loop(0, slot_len // 128, cotangent, 0)
    store(gf_out)
    gf_core = send("gf_core", gf_out, gf_rest.at[0], head_device(1))
    gf_x = send("gf_x", gf_out, gf_rest.at[1], head_device(2))
    for copy in gain_dps:
        copy.wait_recv()
    many = E // short
    tiles = [
        sum(gains_out[t * many + n] for n in range(many)) for t in range(dps * heads // many)
    ]
    gain_one = jnp.concatenate([tile[0:1] for tile in tiles], axis=1)
    gain_two = jnp.concatenate([tile[1:2] for tile in tiles], axis=1)
    gain_row_out[0:1] = gain_one
    gain_row_out[1:2] = gain_two
    for copy in core:
        copy.wait_recv()
    store(wk1, wv1, wq1, wo1)

    def project(normed, rows, weights, k_ref, v_ref):
        for n, (wk, wv) in enumerate(weights):
            cut = slice(n * half, (n + 1) * half)
            k_ref[rows, cut] = dot(normed, wk).astype(bf16)
            v_ref[rows, cut] = dot(normed, wv).astype(bf16)

    def near_rows(source, part):
        def one(n, carry):
            rows = pl.ds(pl.multiple_of(n * BLOCK, BLOCK), BLOCK)
            target = pl.ds(pl.multiple_of(part * slot_len + n * BLOCK, BLOCK), BLOCK)
            normed = layer_norm(source[rows].astype(f32), gain_one).astype(bf16)
            key_rows[target] = normed
            key_t[:, target] = normed.T
            project(normed, target, ((wk0[...], wv0[...]), (wk1[...], wv1[...])), k_near, v_near)
            if part == 2:
                q_near[rows, :half] = dot(normed, wq0[...]).astype(bf16)
                q_near[rows, half:] = dot(normed, wq1[...]).astype(bf16)
            return carry

        lax.fori_loop(0, slot_len // BLOCK, one, 0)

    loads["cmem"].wait()
    near_rows(cmem, 0)
    loads["w_out"].wait()
    advance("out", 0)
    loads["memory"].wait()
    near_rows(memory.at[head], 1)
    x_o.wait_recv()
    gathers["o"][0].start()
    loads["inputs"].wait()
    near_rows(inputs, 2)
    store(q_near, k_near, v_near, key_t)
    advance("in", 0)

    c = score_scale * log2e

    def attend(q_ref, k_ref, v_ref, mixed_ref, lse_ref, events):
        def one(h, carry):
            cut = pl.ds(pl.multiple_of(h * E, E), E)
            q_t = q_ref[:, cut].T
            v_t = v_ref[:, cut].T
            top = jnp.full((1, slot_len), masked_value, f32)
            for kb in range(6):
                first = BLOCK if kb == 5 else 0
                rows = slice(kb * BLOCK, (kb + 1) * BLOCK)
                s = masked_scores(kb, lens_ref, dot(k_ref[rows, cut], q_t[:, first:]))
                scores[rows, first:] = s
                part = jnp.max(s, axis=0, keepdims=True)
                if first:
                    top = jnp.concatenate([top[:, :first], jnp.maximum(top[:, first:], part)], axis=1)
                else:
                    top = jnp.maximum(top, part)
            shift = top * c
            mixed = jnp.zeros((E, slot_len), f32)
            total = jnp.zeros((1, slot_len), f32)
            for kb in range(6):
                first = BLOCK if kb == 5 else 0
                rows = slice(kb * BLOCK, (kb + 1) * BLOCK)
                p = jnp.exp2(scores[rows, first:] * c - shift[:, first:])
                part = jnp.sum(p, axis=0, keepdims=True)
                out = dot(v_t[:, rows], p.astype(bf16))
                if first:
                    total = jnp.concatenate([total[:, :first], total[:, first:] + part], axis=1)
                    mixed = jnp.concatenate([mixed[:, :first], mixed[:, first:] + out], axis=1)
                else:
                    total = total + part
                    mixed = mixed + out
            mixed_ref[:, cut] = (mixed / total).T.astype(bf16)
            lse_ref[h] = shift + jnp.log2(total)
            for when, event in events:
                pl.when(h == when)(event)
            return carry

        lax.fori_loop(0, q_ref.shape[1] // E, one, 0)

    attend(
        q_near,
        k_near,
        v_near,
        mixed_near,
        lse_near,
        [
            (1, lambda: advance("out", 1)),
            (2, lambda: advance("o", 0)),
        ],
    )

    for copy in small:
        copy.wait_recv()
    store(mixed_near, conv_out)
    taps = 3

    def spread_rows(g, carry):
        source_row = lax.broadcasted_iota(jnp.int32, (slot_len, pad_rows), 0)
        picked_row = lax.broadcasted_iota(jnp.int32, (slot_len, pad_rows), 1)
        kept = source_row < limits_ref[g]
        for tap in range(taps):
            pick = jnp.where(kept & (source_row == taps * picked_row + tap), 1.0, 0.0).astype(bf16)
            spread[g, :, tap * columns : (tap + 1) * columns] = dot(pick, cot_out[g]).astype(bf16)
        return carry

    lax.fori_loop(0, group, spread_rows, 0)
    x_k.wait_recv()
    fwd_k = send("fwd_k", wk2, wk3, head_device(1))

    def conv_rows(n, carry):
        rows = pl.ds(pl.multiple_of(n * BLOCK, BLOCK), BLOCK)
        total = sum(dot(memory[g, :, rows].T, spread[g]) for g in range(group)).astype(bf16)
        for tap in range(taps):
            conv_grad[tap, rows] = total[:, tap * columns : (tap + 1) * columns]
        return carry

    lax.fori_loop(0, width // BLOCK, conv_rows, 0)
    advance("in", 1)
    x_v.wait_recv()
    fwd_v = send("fwd_v", wv2, wv3, head_device(1))
    store(conv_grad)
    advance("o", 1)
    x_q.wait_recv()
    fwd_q = send("fwd_q", wq2, wq3, head_device(1))
    for copy in (fwd_k, fwd_v):
        copy.wait_recv()
    store(wk2, wk3, wv2, wv3)

    def far_rows(n, carry):
        rows = pl.ds(pl.multiple_of(n * BLOCK, BLOCK), BLOCK)
        project(key_rows[rows], rows, ((wk2[...], wv2[...]), (wk3[...], wv3[...])), k_far, v_far)
        return carry

    lax.fori_loop(0, key_rows.shape[0] // BLOCK, far_rows, 0)
    fwd_q.wait_recv()
    store(wq2, wq3)
    for n in range(slot_len // BLOCK):
        rows = slice(n * BLOCK, (n + 1) * BLOCK)
        normed = key_rows[2 * slot_len + n * BLOCK : 2 * slot_len + (n + 1) * BLOCK]
        q_far[rows, :half] = dot(normed, wq2[...]).astype(bf16)
        q_far[rows, half:] = dot(normed, wq3[...]).astype(bf16)
    store(q_far, k_far, v_far)
    for n in range(2, bits):
        advance("o", n)
    fwd_o = send("fwd_o", wo2, wo3, head_device(1))
    attend(q_far, k_far, v_far, mixed_far, lse_far, [])
    store(mixed_far)
    fwd_o.wait_recv()
    store(wo2, wo3)

    def mix(n, carry):
        rows = pl.ds(pl.multiple_of(n * 128, 128), 128)
        near, far = mixed_near[rows], mixed_far[rows]
        attention = (
            dot(near[:, :half], wo0[...])
            + dot(near[:, half:], wo1[...])
            + dot(far[:, :half], wo2[...].reshape(half, width))
            + dot(far[:, half:], wo3[...].reshape(half, width))
        )
        row = lax.broadcasted_iota(jnp.int32, (128, width), 0) + n * 128
        hidden = inputs[rows] + jnp.where(row < count_ref[0], attention, 0.0)
        hidden_out[rows] = hidden
        normed_out[rows] = layer_norm(hidden, gain_two).astype(bf16)
        return carry

    lax.fori_loop(0, slot_len // 128, mix, 0)
    store(hidden_out, normed_out)
    gf_x.wait_recv()
    gf_diag = send("gf_diag", gf_rest.at[1], gf_rest.at[2], head_device(1))
    gf_core.wait_recv()
    gf_diag.wait_recv()
    for n in range(2, bits):
        advance("in", n)
        advance("out", n)
    for copy in stored:
        copy.wait()
    for copy in sent:
        copy.wait_send()
    for copies in gathers.values():
        for copy in copies:
            copy.wait_send()


def forward(count, lens, limits, in_pieces, w_conv, comp_grad, gains, weights, w_out, out_grad, inputs, memory, compressed):
    heads, dps = lax.axis_size("head"), lax.axis_size("dp")
    masks = [1 << b for b in reversed(range(dps.bit_length() - 1))]
    twos = (2,) * len(masks)
    slot_len, width = inputs.shape
    group, keys = memory.shape[0], 3 * slot_len
    wq, wk, wv, wo = weights
    half = wk.shape[1]
    columns = width // heads
    new_rows = comp_grad.shape[0]
    pad_rows = (new_rows + 15) // 16 * 16
    shape = jax.ShapeDtypeStruct
    wide = 2 * half
    conv_all = (heads, w_conv.shape[0], columns)
    cot_all = (heads, pad_rows, columns)
    o_cut = twos + (half // dps, width)
    outs = [
        shape((2, width), f32),
        shape((wide // E, 1, slot_len), f32),
        shape((wide // E, 1, slot_len), f32),
    ]
    kept = [
        shape(conv_all, bf16),
        shape((slot_len, width), bf16),
        shape((slot_len, wide), bf16),
        shape((keys, wide), bf16),
        shape((keys, wide), bf16),
        shape((slot_len, wide), bf16),
        shape((keys, wide), bf16),
        shape((keys, wide), bf16),
        shape((slot_len, wide), bf16),
        shape((slot_len, wide), bf16),
        shape((width, keys), bf16),
        shape((slot_len, width), f32),
        shape((slot_len, width), bf16),
        *[shape(wq.shape, bf16)] * 3,
        *[shape(wk.shape, bf16)] * 3,
        *[shape(wv.shape, bf16)] * 3,
        shape(wo.shape, bf16),
        shape(o_cut, bf16),
        shape(o_cut, bf16),
        shape((3, width, columns), bf16),
    ]
    far_outs = [
        shape(twos + in_pieces.shape, bf16),
        shape(twos + w_out.shape, bf16),
        shape((heads - 1, slot_len, width), bf16),
    ]
    smem = pl.BlockSpec(memory_space=pltpu.SMEM)
    return pl.pallas_call(
        functools.partial(forward_kernel, heads, dps, masks, group, slot_len),
        in_specs=[smem] * 3 + [vmem()] * 8 + [anywhere()] * 5,
        out_specs=[vmem()] * len(outs) + [anywhere()] * (len(kept) + len(far_outs)),
        out_shape=outs + kept + far_outs,
        scratch_shapes=[pltpu.VMEM(k.shape, k.dtype) for k in kept]
        + [
            pltpu.VMEM((dps * heads, 8, E), f32),
            pltpu.VMEM(cot_all, bf16),
            pltpu.VMEM((keys, width), bf16),
            pltpu.VMEM((keys, slot_len), f32),
            pltpu.VMEM((slot_len, width), f32),
            pltpu.VMEM((slot_len, width), f32),
            pltpu.VMEM(memory.shape, bf16),
            pltpu.VMEM((slot_len, width), bf16),
            pltpu.VMEM((group, slot_len, 3 * columns), bf16),
            pltpu.VMEM((heads - 1,) + conv_all[1:], bf16),
            pltpu.VMEM((heads - 1,) + cot_all[1:], bf16),
            pltpu.SemaphoreType.DMA((2, 30 + STORED + 6 * heads + dps + 4 * len(masks))),
        ],
        compiler_params=pltpu.CompilerParams(
            collective_id=0, has_side_effects=True, vmem_limit_bytes=61 * 2**20
        ),
        cost_estimate=pl.CostEstimate(flops=40 * 10**9, bytes_accessed=0, transcendentals=0),
        name="forward",
    )(count, lens, limits, in_pieces, w_conv, comp_grad, gains, *weights, w_out, out_grad, inputs, memory, compressed)


def norm_input_grad(values, gain, grad):
    mean = jnp.mean(values, axis=-1, keepdims=True)
    centred = values - mean
    scale = lax.rsqrt(jnp.mean(centred * centred, axis=-1, keepdims=True) + epsilon)
    unit = centred * scale
    grad = grad * gain
    shift = jnp.mean(grad, axis=-1, keepdims=True)
    slope = jnp.mean(grad * unit, axis=-1, keepdims=True)
    return scale * (grad - shift - unit * slope)


def gelu_parts(u):
    c = 0.7978845608028654
    cube = 0.044715 * u * u
    t = jnp.tanh(c * (u + cube * u))
    half = 0.5 * (1.0 + t)
    return u * half, half + 0.5 * u * (1.0 - t * t) * (c * (1.0 + 3.0 * cube))


def middle_kernel(heads, masks, group, *refs):
    (count_ref, limits_ref, gain_ref, conv_ref), refs = refs[:4], refs[4:]
    (n2_hbm, gf_hbm, gf_rest, w_in_hbm, w_out_hbm, conv_grad, memory_hbm), refs = refs[:7], refs[7:]
    (hidden_hbm, out_grad_hbm, mixed_near, mixed_far, wo0, wo1, wo2, wo3), refs = refs[:8], refs[8:]
    (conv_fin, new_cols, out_part), refs = refs[:3], refs[3:]
    (grad_hbm, gm_hbm, go_near, go_far, in_hbm, out_own_hbm, out_core_hbm, out_far_hbm), refs = refs[:8], refs[8:]
    (w_in, w_out, n2, gf, act, gi, gn_own, gn_part, gn_core, gn_diag, gn_x), refs = refs[:11], refs[11:]
    (out_own, out_send, out_diag, grad_out, grad_in, out_got, memory, out_grad, conv_all), refs = refs[:9], refs[9:]
    conv_kept, conv_got, sems = refs[0], refs[1:-1], refs[-1]
    bits = len(masks)
    slot_len, width = gn_own.shape
    head = lax.axis_index("head")
    dp = lax.axis_index("dp")
    flags = tuple(jnp.where(jnp.bitwise_and(dp, mask) != 0, 1, 0) for mask in masks)
    whole = slice(None)
    core = (dp, jnp.bitwise_xor(head, 1))
    chip = (dp, jnp.bitwise_xor(head, 2))
    partners = [(jnp.bitwise_xor(dp, mask), head) for mask in masks]

    barrier = pltpu.get_barrier_semaphore()
    for device in [core, chip] + partners:
        pl.semaphore_signal(barrier, inc=1, device_id=device, device_id_type=MESH)

    slots = {}

    def slot(name):
        if name not in slots:
            slots[name] = len(slots)
        return slots[name]

    sent, stored = [], []

    def remote(name, source, target, device):
        at = slot(name)
        copy = pltpu.make_async_remote_copy(
            src_ref=source,
            dst_ref=target,
            send_sem=sems.at[0, at],
            recv_sem=sems.at[1, at],
            device_id=device,
            device_id_type=MESH,
        )
        sent.append(copy)
        return copy

    def send(*args):
        copy = remote(*args)
        copy.start()
        return copy

    def local(name, source, target):
        copy = pltpu.make_async_copy(source, target, sems.at[0, slot(name)])
        copy.start()
        return copy

    def store(name, source, target):
        stored.append(local(name, source, target))

    load = {
        "n2": local("load_n2", n2_hbm, n2.at[0]),
        "w_in": local("load_w_in", w_in_hbm, w_in),
        "gf": local("load_gf", gf_hbm, gf.at[0]),
        "w_out": local("load_w_out", w_out_hbm, w_out),
        "gf_core": local("load_gf_core", gf_rest.at[0], gf.at[1]),
        "gf_far": local("load_gf_far", gf_rest.at[pl.ds(1, 2)], gf.at[pl.ds(2, 2)]),
        "conv": local(
            "load_conv", conv_grad.at[(whole,) * (bits - 1) + (flags[-1],)], conv_kept
        ),
        "out_grad": local("load_out_grad", out_grad_hbm, out_grad),
    }
    conv_all[flags] = conv_ref[...]
    pl.semaphore_wait(barrier, 2 + bits)

    n2_core = send("n2_core", n2_hbm, n2.at[1], core)
    halves = [pl.ds(h * (slot_len // 2), slot_len // 2) for h in range(2)]
    n2_x = [send(f"n2_x{h}", n2_hbm.at[halves[h]], n2.at[2, halves[h]], chip) for h in range(2)]
    n2_diag = [remote(f"n2_diag{h}", n2.at[2, halves[h]], n2.at[3, halves[h]], core) for h in range(2)]

    order = list(range(bits - 2)) + [bits - 1, bits - 2]
    index, gathers = list(flags), []
    for n, bit in enumerate(order):
        part = conv_all.at[tuple(index)]
        gathers.append(remote(f"conv_{n}", part, part, partners[bit]))
        index[bit] = whole
    sums = [
        remote(
            f"conv_sum{n}",
            (conv_grad if n == bits - 1 else conv_got[n + 1]).at[(whole,) * n + (1 - flags[n],)],
            conv_got[n],
            partners[n],
        )
        for n in range(bits)
    ]
    gathers[0].start()
    sums[bits - 1].start()

    def add_sum(n):
        sums[n].wait_recv()
        for at in range(2**n):
            spot = tuple((at >> (n - 1 - b)) & 1 for b in range(n))
            mine = conv_kept[spot] if n == bits - 1 else conv_got[n + 1][spot + (flags[n],)]
            conv_got[n][spot] = (conv_got[n][spot].astype(f32) + mine.astype(f32)).astype(bf16)
        if n:
            sums[n - 1].start()

    def next_gather(n):
        gathers[n].wait_recv()
        if n + 1 < bits:
            gathers[n + 1].start()

    rows_of = slot_len // 2
    units = w_in.shape[1]
    chunk = 512

    def tokens(s, half):
        rows = pl.ds(pl.multiple_of(half * rows_of, rows_of), rows_of)
        for n in range(units // chunk):
            cut = slice(n * chunk, (n + 1) * chunk)
            inner = dot(n2[s, rows], w_in[:, cut])
            value, slope = gelu_parts(inner)
            act[s, rows, cut] = value.astype(bf16)
            gi[s, rows, cut] = (dot_nt(gf[s, rows], w_out[cut, :]) * slope).astype(bf16)
        return rows, dot_nt(gi[s, rows], w_in[...])

    for name in ("n2", "w_in", "gf", "w_out", "gf_core"):
        load[name].wait()
    n2_core.wait_recv()

    def near(n, carry):
        s = lax.div(n, 2)
        rows, grad = tokens(s, lax.rem(n, 2))

        @pl.when(s == 0)
        def _():
            gn_own[rows] = grad

        @pl.when(s == 1)
        def _():
            gn_part[0, rows] = grad.astype(bf16)

        return carry

    lax.fori_loop(0, 4, near, 0)
    core_sent = send("gn_core", gn_part.at[0], gn_core, core)

    def terms(lhs, rhs, target, first, again):
        many = width // 4

        def one(n, carry):
            cut = pl.ds(pl.multiple_of(n * many, many), many)
            left = jnp.concatenate([lhs[first, :, cut].T, lhs[first + 1, :, cut].T], axis=1)
            total = dot(left, rhs[first : first + 2].reshape(2 * slot_len, rhs.shape[2]))
            block = target.shape[bits]
            per = many // block
            low = per.bit_length() - 1
            for m in range(per):
                spot = tuple(
                    lax.rem(lax.div(n, 2 ** (bits - low - 1 - b)), 2) for b in range(bits - low)
                ) + tuple((m >> (low - 1 - b)) & 1 for b in range(low))
                value = total[m * block : (m + 1) * block]
                if again:
                    value = value + target[spot].astype(f32)
                target[spot] = value.astype(bf16)
            return carry

        lax.fori_loop(0, 4, one, 0)

    def outward(n, carry):
        s = lax.div(n, 2)
        rows = pl.ds(pl.multiple_of(lax.rem(n, 2) * rows_of, rows_of), rows_of)
        value = dot(act[s, rows], w_out[...])

        @pl.when(s == 0)
        def _():
            out_own[rows] = value

        @pl.when(s > 0)
        def _():
            out_send[lax.max(s - 1, 0), rows] = value.astype(bf16)

        return carry

    n2_x[0].wait_recv()
    n2_diag[0].start()
    lax.fori_loop(0, 4, outward, 0)
    store("out_own", out_own, out_own_hbm)
    out_core = send("out_core", out_send.at[0], out_core_hbm, core)
    next_gather(0)
    load["gf_far"].wait()
    n2_diag[0].wait_recv()

    def far(half):
        def one(n, carry):
            rows, grad = tokens(2 + n, half)
            gn_part[1 + n, rows] = grad.astype(bf16)
            return carry

        lax.fori_loop(0, 2, one, 0)
        return send(f"gn_diag{half}", gn_part.at[2, halves[half]], gn_diag.at[halves[half]], core)

    def far_sum(half, copy):
        copy.wait_recv()
        rows = halves[half]
        gn_part[1, rows] = (gn_part[1, rows].astype(f32) + gn_diag[rows].astype(f32)).astype(bf16)
        return send(f"gn_x{half}", gn_part.at[1, rows], gn_x.at[rows], chip)

    diag_sent = far(0)
    terms(act, gf, grad_out, 0, False)
    gn_back = [far_sum(0, diag_sent)]
    load["conv"].wait()
    add_sum(bits - 1)
    terms(n2, gi, grad_in, 0, False)
    n2_x[1].wait_recv()
    n2_diag[1].start()
    next_gather(1)
    n2_diag[1].wait_recv()
    diag_sent = far(1)
    terms(act, gf, grad_out, 2, True)
    gn_back.append(far_sum(1, diag_sent))
    out_y = send(
        "out_sum", grad_out.at[(whole,) * (bits - 1) + (1 - flags[-1],)], out_got, partners[-1]
    )
    if bits > 1:
        add_sum(bits - 2)
    terms(n2, gi, grad_in, 2, True)
    store("grad_in", grad_in, in_hbm)
    lax.fori_loop(4, 8, outward, 0)
    out_back = send("out_diag", out_send.at[2], out_diag, core)
    for n in range(2, bits):
        next_gather(n)
    for n in reversed(range(bits - 2)):
        add_sum(n)
    conv_fin[...] = conv_got[0][...].reshape(conv_fin.shape)

    near_wide, far_wide = mixed_near.shape[1], mixed_far.shape[1]
    half_rows = wo0.shape[0]
    late = [
        local("load_mixed_near", mixed_near, act.at[0, :, pl.ds(0, near_wide)]),
        local("load_mixed_far", mixed_far, act.at[0, :, pl.ds(near_wide, far_wide)]),
    ] + [
        local(f"load_wo{r}", w, act.at[1 + r // 2, pl.ds((r % 2) * half_rows, half_rows)])
        for r, w in enumerate((wo0, wo1, wo2, wo3))
    ]
    stored[0].wait()
    hidden_load = local("load_hidden", hidden_hbm, out_own)

    pad_rows, columns = new_cols.shape[1], new_cols.shape[2]
    taps = 3

    def stream(g, carry):
        copy = local("load_memory", memory_hbm.at[g], memory)
        kernel = conv_all[...].reshape(taps * width, columns)
        source_row = lax.broadcasted_iota(jnp.int32, (pad_rows, slot_len), 1)
        picked_row = lax.broadcasted_iota(jnp.int32, (pad_rows, slot_len), 0)
        kept = source_row < limits_ref[g]
        copy.wait()
        total = jnp.zeros((pad_rows, columns), f32)
        for tap in range(taps):
            pick = jnp.where(kept & (source_row == taps * picked_row + tap), 1.0, 0.0).astype(bf16)
            rows = dot(pick, memory[0:slot_len]).astype(bf16)
            total = total + dot(rows, kernel[tap * width : (tap + 1) * width])
        new_cols[g] = total.astype(bf16)
        return carry

    lax.fori_loop(0, group, stream, 0)
    out_back.wait_recv()
    for h in range(2):
        rows = halves[h]
        out_diag[rows] = (out_diag[rows].astype(f32) + out_send[1, rows].astype(f32)).astype(bf16)
    store("out_far", out_diag, out_far_hbm)

    for copy in [hidden_load, load["out_grad"]] + late:
        copy.wait()
    for copy in gn_back:
        copy.wait_recv()
    core_sent.wait_recv()
    gain = gain_ref[1:2]

    def back(n, carry):
        rows = pl.ds(pl.multiple_of(n * 128, 128), 128)
        grad = gn_own[rows] + gn_core[rows].astype(f32) + gn_x[rows].astype(f32)
        grad = out_grad[rows] + norm_input_grad(out_own[rows], gain, grad)
        gn_own[rows] = grad
        row = lax.broadcasted_iota(jnp.int32, (128, width), 0) + n * 128
        gi[0, rows] = jnp.where(row < count_ref[0], grad, 0.0).astype(bf16)
        return carry

    lax.fori_loop(0, slot_len // 128, back, 0)
    store("grad_hidden", gn_own, grad_hbm)
    weights = act[1:3].reshape(2 * slot_len, width)
    for h in range(2):
        gi[1, halves[h]] = dot_nt(gi[0, halves[h]], weights).astype(bf16)
    store("gm", gi.at[1], gm_hbm)
    for n, target in enumerate((go_near, go_far)):
        cut = slice(n * near_wide, (n + 1) * near_wide)
        gi[2 + n] = dot(act[0, :, cut].T, gi[0]).astype(bf16)
        store(f"go{n}", gi.at[2 + n], target)
    out_y.wait_recv()
    for at in range(2 ** (bits - 1)):
        spot = tuple((at >> (bits - 2 - b)) & 1 for b in range(bits - 1))
        out_part[spot] = (
            out_got[spot].astype(f32) + grad_out[spot + (flags[-1],)].astype(f32)
        ).astype(bf16)
    out_core.wait_recv()
    for copy in stored[1:]:
        copy.wait()
    for copy in sent:
        copy.wait_send()


def middle(count, limits, gains, conv_rows, normed, grad_ffn, gf_rest, w_in, w_out, conv_grad, memory, hidden, out_grad, mixed_near, mixed_far, wo):
    heads, dps = lax.axis_size("head"), lax.axis_size("dp")
    masks = [1 << b for b in reversed(range(dps.bit_length() - 1))]
    bits = len(masks)
    twos = lambda n: (2,) * n
    slot_len, width = hidden.shape
    units = w_in.shape[1]
    columns = conv_rows.shape[2]
    new_rows = (slot_len + 2) // 3
    pad_rows = (new_rows + 15) // 16 * 16
    shape = jax.ShapeDtypeStruct
    stream = (slot_len, width)
    conv_block = conv_grad.shape[bits:]
    in_block = (width // dps, units)
    out_block = (units // dps, width)
    smem = pl.BlockSpec(memory_space=pltpu.SMEM)
    buffers = [
        (w_in.shape, bf16),
        (w_out.shape, bf16),
        ((4,) + stream, bf16),
        ((4,) + stream, bf16),
        ((4, slot_len, units), bf16),
        ((4, slot_len, units), bf16),
        (stream, f32),
        ((3,) + stream, bf16),
        (stream, bf16),
        (stream, bf16),
        (stream, bf16),
        (stream, f32),
        ((3,) + stream, bf16),
        (stream, bf16),
        (twos(bits) + out_block, bf16),
        (twos(bits) + in_block, bf16),
        (twos(bits - 1) + out_block, bf16),
        (memory.shape[1:], bf16),
        (stream, f32),
        (twos(bits) + conv_rows.shape, bf16),
        (twos(bits - 1) + conv_block, bf16),
    ] + [(twos(n) + conv_block, bf16) for n in range(bits)]
    return pl.pallas_call(
        functools.partial(middle_kernel, heads, masks, memory.shape[0]),
        in_specs=[smem] * 2 + [vmem()] * 2 + [anywhere()] * 15,
        out_specs=[vmem()] * 3 + [anywhere()] * 8,
        out_shape=[
            shape(conv_rows.shape, bf16),
            shape((memory.shape[0], pad_rows, columns), bf16),
            shape(twos(bits - 1) + out_block, bf16),
            shape(stream, f32),
            shape((slot_len, 4 * wo[0].shape[0]), bf16),
            shape((mixed_near.shape[1], width), bf16),
            shape((mixed_far.shape[1], width), bf16),
            shape(twos(bits) + in_block, bf16),
            shape(stream, f32),
            shape(stream, bf16),
            shape(stream, bf16),
        ],
        scratch_shapes=[pltpu.VMEM(*b) for b in buffers]
        + [pltpu.SemaphoreType.DMA((2, 48 + 3 * bits))],
        compiler_params=pltpu.CompilerParams(
            collective_id=2, has_side_effects=True, vmem_limit_bytes=61 * 2**20
        ),
        cost_estimate=pl.CostEstimate(flops=30 * 10**9, bytes_accessed=0, transcendentals=0),
        name="middle",
    )(count, limits, gains, conv_rows, normed, grad_ffn, gf_rest, w_in, w_out, conv_grad, memory, hidden, out_grad, mixed_near, mixed_far, *wo)


def backward_kernel(heads, masks, slot_len, keys, *refs):
    (lens_ref, lse_near, lse_far), refs = refs[:3], refs[3:]
    loaded = 8 + 3 * heads
    sources, refs = refs[:loaded], refs[loaded:]
    (gain_ref, go_near, go_far, out_part, new_ref, conv_ref, key_t_hbm, in_hbm, inputs_hbm, hidden_hbm), refs = refs[:10], refs[10:]
    (grad_out, sum_rows, input_grad_hbm, go_out, gain_out, in_got, new_got, conv_got), refs = refs[:8], refs[8:]
    held, refs = refs[:loaded], refs[loaded:]
    (q_near, k_near, v_near, gm_near, q_far, k_far, v_far, gm_far), more = held[:8], held[8:]
    wq, wk, wv = more[:heads], more[heads : 2 * heads], more[2 * heads :]
    (key_t, probs, grads, dkv, terms, own_terms, got_near, got_far, got_x), refs = refs[:9], refs[9:]
    bits = len(masks)
    in_kept, refs = refs[0], refs[1:]
    in_got_rs, refs = refs[:bits], refs[bits:]
    out_got_rs, refs = refs[: bits - 1], refs[bits - 1 :]
    go_core_near, go_core_far, go_x, refs = refs[0], refs[1], refs[2], refs[3:]
    go_rs, refs = refs[:bits], refs[bits:]
    sum_rs, refs = refs[:bits], refs[bits:]
    grad_normed, gain_terms, sems = refs
    head = lax.axis_index("head")
    dp = lax.axis_index("dp")
    flags = [jnp.where(jnp.bitwise_and(dp, mask) != 0, 1, 0) for mask in masks]

    def head_device(r):
        return (dp, jnp.bitwise_xor(head, r))

    def dp_device(n):
        return (jnp.bitwise_xor(dp, masks[n]), head)

    barrier = pltpu.get_barrier_semaphore()
    for r in range(1, heads):
        pl.semaphore_signal(barrier, inc=1, device_id=head_device(r), device_id_type=MESH)
    for n in range(bits):
        pl.semaphore_signal(barrier, inc=1, device_id=dp_device(n), device_id_type=MESH)
    pl.semaphore_wait(barrier, heads - 1 + bits)

    slots = {}

    def remote(name, source, target, device, part=0):
        if name not in slots:
            slots[name] = 2 * len(slots)
        at = slots[name] + part
        return pltpu.make_async_remote_copy(
            src_ref=source,
            dst_ref=target,
            send_sem=sems.at[0, at],
            recv_sem=sems.at[1, at],
            device_id=device,
            device_id_type=MESH,
        )

    def local(name, source, target):
        if name not in slots:
            slots[name] = 2 * len(slots)
        return pltpu.make_async_copy(source, target, sems.at[0, slots[name]])

    whole = slice(None)

    def rs_copy(name, held, got, n, part=0):
        return remote(
            f"{name}{n}", held.at[(whole,) * n + (1 - flags[n],)], got, dp_device(n), part
        )

    def rs_add(held, got, n):
        for at in range(2**n):
            index = tuple((at >> (n - 1 - b)) & 1 for b in range(n))
            mine = held[index + (flags[n],)]
            got[index] = (got[index].astype(f32) + mine.astype(f32)).astype(bf16)

    def ag_copy(name, block, n, part=0):
        region = block.at[(whole,) * n + tuple(flags[n:])]
        return remote(f"{name}{n}", region, region, dp_device(n), part)

    fetches = []
    for n, (source, target) in enumerate(zip(sources, held)):
        if n in (3, 7):
            wide = target.shape[1]
            source = source.at[:, pl.ds((n // 4) * wide, wide)]
        fetches.append(local(f"fetch_{n}", source, target))
    for n in (4, 5, 6, 7):
        fetches[n].start()
    load_keys = local("load_keys", key_t_hbm, key_t)
    load_keys.start()
    for n in range(loaded):
        if n not in (4, 5, 6, 7):
            fetches[n].start()
    in_y = remote("in_rs", in_hbm.at[(whole,) * (bits - 1) + (1 - flags[bits - 1],)], in_got_rs[bits - 1], dp_device(bits - 1))
    in_y.start()
    load_in = local("load_in", in_hbm.at[(whole,) * (bits - 1) + (flags[bits - 1],)], in_kept)
    load_in.start()
    out_z = rs_copy("out_rs", out_part, out_got_rs[bits - 2], bits - 2)
    out_z.start()
    rows_o = go_x.shape[0]
    go_core = [
        remote("go_near", go_near.at[pl.ds(rows_o, rows_o)], go_core_near, head_device(1)),
        remote("go_far", go_far.at[pl.ds(rows_o, rows_o)], go_core_far, head_device(1)),
    ]
    for copy in go_core:
        copy.start()
    closing = []
    for name, source, target in (("new", new_ref, new_got), ("conv", conv_ref, conv_got)):
        for r in range(1, heads):
            copy = remote(
                f"{name}_{r}",
                source.at[jnp.bitwise_xor(head, r)],
                target.at[head],
                head_device(r),
            )
            copy.start()
            closing.append(copy)
        target[head] = source[head]
    go_to_x = remote("go_x", go_core_far, go_x, head_device(2))
    grad_normed[...] = jnp.zeros(grad_normed.shape, f32)
    c = score_scale * log2e

    def core_copy(r, p):
        return remote(f"core_{r}", terms.at[r - 1], (got_near if r == 1 else got_far).at[p], head_device(1), p)

    def x_copy(p):
        return remote("x_terms", terms.at[1], got_x.at[p], head_device(2), p)

    def sum_y(p):
        return rs_copy("sum", own_terms.at[p], sum_rs[bits - 1].at[p], bits - 1, p)

    def sum_copy(p, n):
        return rs_copy("sum", sum_rs[n + 1].at[p], sum_rs[n].at[p], n, p)

    def sum_gather(p, n):
        return ag_copy("gather", sum_rows.at[p], n, p)

    def add_rows(target, source):
        for at in range(target.shape[0]):
            target[at] = (target[at].astype(f32) + source[at].astype(f32)).astype(bf16)

    def each_block(function):
        def step(at, carry):
            function(tuple(lax.rem(lax.div(at, 2 ** (bits - 1 - b)), 2) for b in range(bits)))
            return carry

        lax.fori_loop(0, 2**bits, step, 0)

    def add_whole(target, source):
        def one(index):
            target[index] = (target[index].astype(f32) + source[index].astype(f32)).astype(bf16)

        each_block(one)

    def attend(r, p):
        half_q, half_k, half_v, half_g, half_l = (
            (q_near, k_near, v_near, gm_near, lse_near)
            if r < 2
            else (q_far, k_far, v_far, gm_far, lse_far)
        )
        cut = pl.ds(pl.multiple_of((r % 2) * 2 * E + p * E, E), E)
        q = half_q[:, cut]
        g = half_g[:, cut]
        q_t = q.T
        g_t = g.T
        k_t = half_k[:, cut].T
        lse = half_l[(r % 2) * 2 + p]
        row_dot = jnp.zeros((1, slot_len), f32)
        for kb in range(6):
            first = BLOCK if kb == 5 else 0
            rows = slice(kb * BLOCK, (kb + 1) * BLOCK)
            s = masked_scores(kb, lens_ref, dot(half_k[rows, cut], q_t[:, first:]))
            pr = jnp.exp2(s * c - lse[:, first:])
            gp = dot(half_v[rows, cut], g_t[:, first:])
            probs[rows, first:] = pr
            grads[rows, first:] = gp
            part = jnp.sum(pr * gp, axis=0, keepdims=True)
            dkv[rows, E:] = dot(pr.astype(bf16), g[first:]).astype(bf16)
            if first:
                row_dot = jnp.concatenate([row_dot[:, :first], row_dot[:, first:] + part], axis=1)
            else:
                row_dot = row_dot + part
        dq = jnp.zeros((E, slot_len), f32)
        for kb in range(6):
            first = BLOCK if kb == 5 else 0
            rows = slice(kb * BLOCK, (kb + 1) * BLOCK)
            ds = (probs[rows, first:] * (grads[rows, first:] - row_dot[:, first:])).astype(bf16)
            dkv[rows, :E] = (dot(ds, q[first:]) * score_scale).astype(bf16)
            out = dot(k_t[:, rows], ds)
            if first:
                dq = jnp.concatenate([dq[:, :first], dq[:, first:] + out], axis=1)
            else:
                dq = dq + out
        return (dq * score_scale).T.astype(bf16)

    per_block = own_terms.shape[1 + bits]

    def weight_terms(dq, target):
        blocks = 2 ** (bits - 1)
        many = blocks * per_block

        def one(at, carry):
            rows = pl.ds(pl.multiple_of(at * many, many), many)
            of_kv = dot(key_t[rows, :], dkv[...]).astype(bf16)
            of_q = dot(key_t[rows, keys - slot_len :], dq).astype(bf16)
            for n in range(blocks):
                index = (at,) + tuple((n >> (bits - 2 - b)) & 1 for b in range(bits - 1))
                cut = slice(n * per_block, (n + 1) * per_block)
                target[index + (whole, slice(0, 2 * E))] = of_kv[cut]
                target[index + (whole, slice(2 * E, 3 * E))] = of_q[cut]
            return carry

        lax.fori_loop(0, 2, one, 0)

    def normed_terms(r, p, dq):
        cut = pl.ds(pl.multiple_of(p * E, E), E)
        dk = dkv[keys - slot_len :, :E]
        dv = dkv[keys - slot_len :, E:]
        columns = 256
        for n in range(grad_normed.shape[1] // columns):
            rows = slice(n * columns, (n + 1) * columns)
            grad_normed[:, rows] += (
                dot_nt(dq, wq[r][rows, cut])
                + dot_nt(dk, wk[r][rows, cut])
                + dot_nt(dv, wv[r][rows, cut])
            )

    def parity(p, carry):
        first = p == 0
        dq = attend(3, p)

        @pl.when(first)
        def _():
            load_keys.wait()
            for n in range(loaded):
                if n not in (4, 5, 6, 7):
                    fetches[n].wait()

        @pl.when(p == 1)
        def _():
            core_copy(3, 0).wait_send()

        weight_terms(dq, terms.at[2])
        core_copy(3, p).start()
        normed_terms(3, p, dq)

        @pl.when(first)
        def _():
            for copy in go_core:
                copy.wait_recv()
            go_core_far[...] = (
                go_core_far[...].astype(f32) + go_far[:rows_o].astype(f32)
            ).astype(bf16)
            go_to_x.start()

        dq = attend(2, p)

        @pl.when(p == 1)
        def _():
            x_copy(0).wait_send()

        weight_terms(dq, terms.at[1])
        core_copy(3, p).wait_recv()
        add_whole(terms.at[1], got_far.at[p])
        x_copy(p).start()
        normed_terms(2, p, dq)

        @pl.when(first)
        def _():
            out_z.wait_recv()
            rs_add(out_part, out_got_rs[bits - 2], bits - 2)
            if bits > 2:
                rs_copy("out_rs", out_got_rs[bits - 2], out_got_rs[bits - 3], bits - 3).start()

        @pl.when(p == 1)
        def _():
            in_y.wait_recv()
            load_in.wait()
            held = in_got_rs[bits - 1]
            for at in range(2 ** (bits - 1)):
                index = tuple((at >> (bits - 2 - b)) & 1 for b in range(bits - 1))
                held[index] = (held[index].astype(f32) + in_kept[index].astype(f32)).astype(bf16)
            rs_copy("in_rs", held, in_got_rs[bits - 2], bits - 2).start()

        dq = attend(1, p)

        @pl.when(p == 1)
        def _():
            core_copy(1, 0).wait_send()

        weight_terms(dq, terms.at[0])
        core_copy(1, p).start()
        normed_terms(1, p, dq)

        @pl.when(p == 1)
        def _():
            x_copy(0).wait_recv()
            add_whole(own_terms.at[0], got_x.at[0])
            sum_y(0).start()

        dq = attend(0, p)
        weight_terms(dq, own_terms.at[p])
        core_copy(1, p).wait_recv()
        add_whole(own_terms.at[p], got_near.at[p])
        normed_terms(0, p, dq)

        @pl.when(first)
        def _():
            go_to_x.wait_recv()
            for at in range(2**bits):
                rows = slice(at * rows_o // 2**bits, (at + 1) * rows_o // 2**bits)
                index = tuple((at >> (bits - 1 - b)) & 1 for b in range(bits))
                go_out[index] = (
                    go_near[rows].astype(f32)
                    + go_core_near[rows].astype(f32)
                    + go_x[rows].astype(f32)
                ).astype(bf16)
            rs_copy("go_rs", go_out, go_rs[bits - 1], bits - 1).start()

        @pl.when(p == 1)
        def _():
            rs_copy("go_rs", go_out, go_rs[bits - 1], bits - 1).wait()
            rs_add(go_out, go_rs[bits - 1], bits - 1)
            rs_copy("go_rs", go_rs[bits - 1], go_rs[bits - 2], bits - 2).start()

        return carry

    for n in (4, 5, 6, 7):
        fetches[n].wait()
    lax.fori_loop(0, 2, parity, 0)

    loads = []
    wide = probs.shape[1]
    for name, source, target in (("inputs", inputs_hbm, probs), ("hidden", hidden_hbm, grads)):
        for n in range(2):
            copy = local(
                f"load_{name}{n}",
                source.at[:, pl.ds(n * wide, wide)],
                target.at[pl.ds(n * slot_len, slot_len)],
            )
            copy.start()
            loads.append(copy)
    in_last = rs_copy("in_rs", in_got_rs[bits - 1], in_got_rs[bits - 2], bits - 2)
    in_last.wait_recv()
    rs_add(in_got_rs[bits - 1], in_got_rs[bits - 2], bits - 2)

    def in_rest(n):
        copy = rs_copy("in_rs", in_got_rs[n + 1], in_got_rs[n], n)
        return copy

    for n in reversed(range(bits - 2)):
        in_rest(n).start()
        if n:
            in_rest(n).wait_recv()
            rs_add(in_got_rs[n + 1], in_got_rs[n], n)
    sum_y(0).wait_recv()
    rs_add(own_terms.at[0], sum_rs[bits - 1].at[0], bits - 1)
    sum_copy(0, bits - 2).start()

    for copy in loads:
        copy.wait()
    gain_row = gain_ref[...]

    def input_rows(at, carry):
        rows = pl.ds(pl.multiple_of(at * 128, 128), 128)
        lower = pl.ds(pl.multiple_of(slot_len + at * 128, 128), 128)
        values = jnp.concatenate([probs[rows], probs[lower]], axis=1)
        before = jnp.concatenate([grads[rows], grads[lower]], axis=1)
        grad_normed[rows] = before + norm_input_grad(values, gain_row, grad_normed[rows])
        return carry

    lax.fori_loop(0, slot_len // 128, input_rows, 0)
    store_grad = local("store_grad", grad_normed, input_grad_hbm)
    store_grad.start()

    x_copy(1).wait_recv()
    add_whole(own_terms.at[1], got_x.at[1])
    sum_y(1).start()

    rs_copy("go_rs", go_rs[bits - 1], go_rs[bits - 2], bits - 2).wait_recv()
    rs_add(go_rs[bits - 1], go_rs[bits - 2], bits - 2)
    for n in reversed(range(bits - 2)):
        rs_copy("go_rs", go_rs[n + 1], go_rs[n], n).start()
        if n:
            rs_copy("go_rs", go_rs[n + 1], go_rs[n], n).wait_recv()
            rs_add(go_rs[n + 1], go_rs[n], n)
    sum_copy(0, bits - 2).wait_recv()
    rs_add(sum_rs[bits - 1].at[0], sum_rs[bits - 2].at[0], bits - 2)
    for n in reversed(range(bits - 2)):
        sum_copy(0, n).start()
        if n:
            sum_copy(0, n).wait_recv()
            rs_add(sum_rs[n + 1].at[0], sum_rs[n].at[0], n)

    for n in reversed(range(bits - 2)):
        copy = rs_copy("out_rs", out_got_rs[n + 1], out_got_rs[n], n)
        if n != bits - 3:
            copy.start()
        copy.wait_recv()
        rs_add(out_got_rs[n + 1], out_got_rs[n], n)
    grad_out[...] = out_got_rs[0][...].astype(f32)
    in_rest(0).wait_recv()
    rs_add(in_got_rs[1], in_got_rs[0], 0)
    in_copies = []
    for r in range(1, heads):
        copy = remote(
            f"in_{r}", in_got_rs[0].at[jnp.bitwise_xor(head, r)], in_got.at[head], head_device(r)
        )
        copy.start()
        in_copies.append(copy)
    in_got[head] = in_got_rs[0][head]

    rs_copy("go_rs", go_rs[1], go_rs[0], 0).wait_recv()
    rs_add(go_rs[1], go_rs[0], 0)
    go_out[tuple(flags)] = go_rs[0][...]
    go_gather = [ag_copy("go_ag", go_out, n) for n in range(bits)]
    go_gather[0].start()

    def gain_part(p):
        rows = pl.ds(pl.multiple_of(dp * per_block, per_block), per_block)
        total = jnp.zeros((per_block, 1), f32)
        grad = sum_rs[0][p]
        for n, weight in enumerate((wk[0], wv[0], wq[0])):
            own = weight[rows, p * E : (p + 1) * E].astype(f32)
            total = total + jnp.sum(
                grad[:, n * E : (n + 1) * E].astype(f32) * own, axis=1, keepdims=True
            )
        return total

    sum_copy(0, 0).wait_recv()
    rs_add(sum_rs[1].at[0], sum_rs[0].at[0], 0)
    sum_rows[(0,) + tuple(flags)] = sum_rs[0][0]
    sum_gather(0, 0).start()
    sum_y(1).wait_recv()
    rs_add(own_terms.at[1], sum_rs[bits - 1].at[1], bits - 1)
    sum_copy(1, bits - 2).start()
    gain = gain_part(0)
    go_gather[0].wait_recv()
    if bits > 1:
        go_gather[1].start()
    sum_gather(0, 0).wait_recv()
    sum_gather(0, 1).start()
    for n in reversed(range(bits - 1)):
        sum_copy(1, n).wait_recv()
        rs_add(sum_rs[n + 1].at[1], sum_rs[n].at[1], n)
        if n:
            sum_copy(1, n - 1).start()
    sum_rows[(1,) + tuple(flags)] = sum_rs[0][1]
    sum_gather(1, 0).start()
    gain = gain + gain_part(1)
    gain_terms[head] = jnp.broadcast_to(gain, gain_terms.shape[1:])
    gain_copies = []
    for r in range(1, heads):
        copy = remote(f"gain_{r}", gain_terms.at[head], gain_terms.at[head], head_device(r))
        copy.start()
        gain_copies.append(copy)
    for n in range(1, bits):
        go_gather[n].wait_recv()
        if n + 1 < bits:
            go_gather[n + 1].start()
        sum_gather(0, n).wait_recv()
        if n + 1 < bits:
            sum_gather(0, n + 1).start()
        sum_gather(1, n - 1).wait_recv()
        sum_gather(1, n).start()
    for copy in gain_copies:
        copy.wait_recv()
    gain_out[...] = sum(gain_terms[h] for h in range(heads))
    for copy in closing + in_copies:
        copy.wait()
    sum_gather(1, bits - 1).wait_recv()
    store_grad.wait()

    in_y.wait_send()
    for copy in go_core + gain_copies + go_gather:
        copy.wait_send()
    go_to_x.wait_send()
    for p in range(2):
        sum_y(p).wait_send()
        for n in range(bits - 1):
            sum_copy(p, n).wait_send()
        for n in range(bits):
            sum_gather(p, n).wait_send()
    for r in (1, 3):
        core_copy(r, 1).wait_send()
    x_copy(1).wait_send()
    out_z.wait_send()
    for n in range(bits - 2):
        rs_copy("out_rs", out_got_rs[n + 1], out_got_rs[n], n).wait_send()
    in_last.wait_send()
    for n in range(bits - 2):
        in_rest(n).wait_send()
    for n in range(bits - 1):
        rs_copy("go_rs", go_rs[n + 1], go_rs[n], n).wait_send()


def backward(lens, near, far, grad_mixed, wq, wk, wv, gain, go_near, go_far, out_part, new_cols, conv, key_t, grad_in, inputs, grad_hidden):
    heads, dps = lax.axis_size("head"), lax.axis_size("dp")
    masks = [1 << b for b in reversed(range(dps.bit_length() - 1))]
    bits = len(masks)
    slot_len, width = inputs.shape
    keys = key_t.shape[1]
    shape = jax.ShapeDtypeStruct
    twos = lambda n: (2,) * n
    in_block = grad_in.shape[bits:]
    out_block = out_part.shape[bits - 1 :]
    rows_o = go_near.shape[0] // 2
    go_block = (rows_o // dps, width)
    sum_block = (width // dps, 3 * E)
    copies = 60 + 16 * bits + 2 * (8 + 3 * heads)
    q_n, k_n, v_n, l_n = near
    q_f, k_f, v_f, l_f = far
    loaded = (q_n, k_n, v_n, grad_mixed, q_f, k_f, v_f, grad_mixed, *wq, *wk, *wv)
    held = (q_n, k_n, v_n, q_n, q_f, k_f, v_f, q_f, *wq, *wk, *wv)
    scratch = (
        [pltpu.VMEM(value.shape, value.dtype) for value in held]
        + [
            pltpu.VMEM((width, keys), bf16),
            pltpu.VMEM((keys, slot_len), f32),
            pltpu.VMEM((keys, slot_len), f32),
            pltpu.VMEM((keys, 2 * E), bf16),
            pltpu.VMEM((3,) + twos(bits) + sum_block, bf16),
            pltpu.VMEM((2,) + twos(bits) + sum_block, bf16),
            pltpu.VMEM((2,) + twos(bits) + sum_block, bf16),
            pltpu.VMEM((2,) + twos(bits) + sum_block, bf16),
            pltpu.VMEM((2,) + twos(bits) + sum_block, bf16),
            pltpu.VMEM(twos(bits - 1) + in_block, bf16),
        ]
        + [pltpu.VMEM(twos(n) + in_block, bf16) for n in range(bits)]
        + [pltpu.VMEM(twos(n) + out_block, bf16) for n in range(bits - 1)]
        + [pltpu.VMEM((rows_o, width), bf16)] * 3
        + [pltpu.VMEM(twos(n) + go_block, bf16) for n in range(bits)]
        + [pltpu.VMEM((2,) + twos(n) + sum_block, bf16) for n in range(bits)]
        + [
            pltpu.VMEM((slot_len, width), f32),
            pltpu.VMEM((heads, width // dps, E), f32),
            pltpu.SemaphoreType.DMA((2, copies)),
        ]
    )
    return pl.pallas_call(
        functools.partial(backward_kernel, heads, masks, slot_len, keys),
        in_specs=[pl.BlockSpec(memory_space=pltpu.SMEM)]
        + [vmem()] * 2
        + [anywhere()] * len(loaded)
        + [vmem()] * 6
        + [anywhere()] * 4,
        out_specs=[vmem()] * 2 + [anywhere()] + [vmem()] * 5,
        out_shape=[
            shape(out_block, f32),
            shape((2,) + twos(bits) + sum_block, bf16),
            shape((slot_len, width), f32),
            shape(twos(bits) + go_block, bf16),
            shape((width // dps, E), f32),
            shape(in_block, bf16),
            shape(new_cols.shape, bf16),
            shape(conv.shape, bf16),
        ],
        scratch_shapes=scratch,
        compiler_params=pltpu.CompilerParams(
            collective_id=1, has_side_effects=True, vmem_limit_bytes=61 * 2**20
        ),
        cost_estimate=pl.CostEstimate(flops=60 * 10**9, bytes_accessed=0, transcendentals=0),
        name="backward",
    )(lens, l_n, l_f, *loaded, gain, go_near, go_far, out_part, new_cols, conv, key_t, grad_in, inputs, grad_hidden)


def swap_head(value, mask):
    size = lax.axis_size("head")
    return lax.ppermute(value, "head", [(i, i ^ mask) for i in range(size)])


def cut_bits(value, masks):
    return value.reshape((2,) * len(masks) + value.shape[1:])


def cut_in_kernel(in_ref, out_ref):
    heads, units = out_ref.shape[0], E
    head = lax.axis_index("head")
    for r in range(heads):
        other = jnp.bitwise_xor(head, r)
        for i in range(out_ref.shape[2] // units):
            source = pl.multiple_of((i * heads + other) * units, units)
            out_ref[r, :, i * units : (i + 1) * units] = in_ref[:, pl.ds(source, units)]


def cut_in(w_in, heads, dps):
    rows, units = w_in.shape[0], w_in.shape[1] // (heads * dps)
    if units == E:
        return pl.pallas_call(
            cut_in_kernel,
            in_specs=[vmem()],
            out_specs=vmem(),
            out_shape=jax.ShapeDtypeStruct((heads, rows, dps * units), bf16),
            name="cut_in",
        )(w_in)
    head = lax.axis_index("head")
    cut = w_in.reshape(rows, dps, heads, units)
    return jnp.stack(
        [
            lax.dynamic_index_in_dim(cut, head ^ r, 2, keepdims=False).reshape(rows, dps * units)
            for r in range(heads)
        ]
    )


def unpack(values, counts):
    parts, at = [], 0
    for count in counts:
        parts.append(values[at : at + count])
        at += count
    return parts


def shards(
    inputs,
    memory,
    compressed,
    counts,
    mem_lens,
    cmem_lens,
    norm_gain,
    w_query,
    w_key,
    w_value,
    w_output,
    ffn_gain,
    w_in,
    w_out,
    w_conv,
    out_grad,
    comp_grad,
):
    slot_len, width = inputs.shape[1:]
    heads, dps = lax.axis_size("head"), lax.axis_size("dp")
    masks = [1 << b for b in reversed(range(dps.bit_length() - 1))]
    bits = len(masks)
    group = memory.shape[0]
    head_at, dp_at = lax.axis_index("head"), lax.axis_index("dp")
    head_width = w_query.shape[1]
    new_rows = comp_grad.shape[1]
    conv_cols = width // heads
    count = lax.dynamic_slice_in_dim(counts, head_at, 1)
    lens = lax.dynamic_index_in_dim(jnp.stack([cmem_lens, mem_lens]), head_at, 1, keepdims=False)

    gains = jnp.pad(jnp.stack([norm_gain, ffn_gain]).astype(f32), ((0, 6), (0, 0)))
    limits = jnp.minimum(counts, mem_lens)
    (
        (gain_rows, lse_near, lse_far),
        (conv_rows, grad_ffn, q_near, k_near, v_near, q_far, k_far, v_far, mixed_near, mixed_far),
        (key_t, hidden, normed_two),
        weights,
        (grad_conv, w_in_own, w_out_own, gf_rest),
    ) = unpack(
        forward(
            count,
            lens,
            limits,
            cut_in(w_in, heads, dps),
            w_conv,
            comp_grad[0],
            gains,
            (w_query, w_key, w_value, w_output),
            w_out,
            out_grad[0],
            inputs[0],
            memory,
            compressed,
        ),
        (3, 10, 3, 12, 4),
    )
    gain_one, gain_two = gain_rows[0:1], gain_rows[1:2]
    wq, wk, wv, wo = (
        [own] + [w.reshape(own.shape) for w in weights[3 * n : 3 * n + 3]]
        for n, own in enumerate((w_query, w_key, w_value, w_output))
    )
    w_in_own = w_in_own.reshape(width, -1)
    w_out_own = w_out_own.reshape(-1, width)
    gf_core, gf_x, gf_diag = (gf_rest[n] for n in range(3))
    pad_rows = (new_rows + 15) // 16 * 16

    (
        (grad_conv, new_cols, out_part, grad_hidden, grad_mixed, go_near, go_far, grad_w_in),
        (out_own, out_core, out_far),
    ) = unpack(
        middle(
            count,
            limits,
            gain_rows,
            conv_rows,
            normed_two,
            grad_ffn,
            gf_rest,
            w_in_own,
            w_out_own,
            cut_bits(grad_conv.reshape(dps, -1, conv_cols), masks),
            memory,
            hidden,
            out_grad[0],
            mixed_near,
            mixed_far,
            wo,
        ),
        (8, 3),
    )
    out_back = swap_head(out_far, 2)

    grad_w_out, sum_rows, input_grad, grad_out, gain_terms, grad_w_in, new_all, grad_conv = backward(
        lens,
        (q_near, k_near, v_near, lse_near),
        (q_far, k_far, v_far, lse_far),
        grad_mixed,
        wq,
        wk,
        wv,
        gain_one,
        go_near,
        go_far,
        out_part,
        new_cols,
        grad_conv,
        key_t,
        cut_bits(grad_w_in.reshape((dps, heads, w_in.shape[0], -1)), masks),
        inputs[0],
        grad_hidden,
    )
    row_pos = jnp.arange(slot_len, dtype=jnp.int32)
    row_live = (row_pos < count).astype(f32)[:, None]
    outputs = hidden + row_live * (out_own + out_core.astype(f32) + out_back.astype(f32))
    new_compressed = new_all.transpose(1, 0, 2).reshape(-1, width)[:new_rows].astype(f32)
    grad_conv = grad_conv.transpose(1, 0, 2).reshape(w_conv.shape).astype(f32)
    grad_w_in = (
        grad_w_in.reshape(heads, w_in.shape[0], dps, -1)
        .transpose(1, 2, 0, 3)
        .reshape(w_in.shape)
        .astype(f32)
    )
    own_gain_two = lax.dynamic_slice_in_dim(
        gain_two[0], (dp_at * heads + head_at) * w_in.shape[0], w_in.shape[0]
    )
    grad_gain_two = jnp.sum(grad_w_in * w_in.astype(f32), axis=1) / own_gain_two
    grad_gain_one = lax.dynamic_slice_in_dim(
        gain_terms[:, 0], head_at * norm_gain.shape[0], norm_gain.shape[0]
    ) / norm_gain.astype(f32)
    sums = sum_rows.reshape(2, width, 3 * E).astype(f32)
    grad_key, grad_value, grad_query = (
        jnp.concatenate([sums[0, :, n * E : (n + 1) * E], sums[1, :, n * E : (n + 1) * E]], axis=1)
        for n in range(3)
    )
    grad_out = grad_out.reshape(w_output.shape).astype(f32)

    return (
        outputs[None],
        input_grad[None],
        new_compressed[None],
        grad_gain_one,
        grad_query,
        grad_key,
        grad_value,
        grad_out,
        grad_gain_two,
        grad_w_in,
        grad_w_out.reshape(w_out.shape).astype(f32),
        grad_conv,
    )


def solution(mesh):
    whole = P(("dp", "head"), None, None)
    rows = P(("dp", "head"), None)
    vector = P(("dp", "head"))
    columns = P(None, "head")
    placed = (
        whole,
        P("dp", None, None),
        P("dp", None, None),
        P("dp"),
        P("dp"),
        P("dp"),
        vector,
        columns,
        columns,
        columns,
        P("head", None),
        vector,
        rows,
        rows,
        rows,
        whole,
        whole,
    )
    return jax.shard_map(
        shards,
        mesh=mesh,
        in_specs=placed,
        out_specs=(
            whole,
            whole,
            whole,
            vector,
            columns,
            columns,
            columns,
            P("head", None),
            vector,
            rows,
            rows,
            rows,
        ),
        check_vma=False,
    )
```

```python
import functools

import jax
import jax.numpy as jnp
from jax import lax
from jax.experimental import pallas as pl
from jax.experimental.pallas import tpu as pltpu
from jax.sharding import PartitionSpec as P

E = 128
BLOCK = 256
epsilon = 1e-05
masked_value = -1e30
score_scale = E ** (-0.5)
log2e = 1.4426950408889634
bf16 = jnp.bfloat16
f32 = jnp.float32
VMEM_BYTES = 30 * 2**20
MESH = pl.DeviceIdType.MESH


def dot(left, right):
    return jnp.dot(left, right, preferred_element_type=f32)


def dot_tn(left, right):
    return lax.dot_general(left, right, (((0,), (0,)), ((), ())), preferred_element_type=f32)


def dot_nt(left, right):
    return lax.dot_general(left, right, (((1,), (1,)), ((), ())), preferred_element_type=f32)


def layer_norm(values, gain_vec):
    row_mean = jnp.mean(values, axis=-1, keepdims=True)
    centred = values - row_mean
    variance = jnp.mean(centred * centred, axis=-1, keepdims=True)
    return centred * lax.rsqrt(variance + epsilon) * gain_vec


def vmem():
    return pl.BlockSpec(memory_space=pltpu.VMEM)


def anywhere():
    return pl.BlockSpec(memory_space=pl.ANY)


def masked_scores(kb, lens, scores):
    rows = lax.broadcasted_iota(jnp.int32, scores.shape, 0)
    if kb < 4:
        limit = lens[kb // 2] - (kb % 2) * BLOCK
        return jnp.where(rows < limit, scores, masked_value)
    columns = lax.broadcasted_iota(jnp.int32, scores.shape, 1)
    return jnp.where(rows <= columns, scores, masked_value)


STORED = 26


def forward_kernel(heads, dps, masks, group, slot_len, *refs):
    (counts_ref, mem_ref, cmem_ref), refs = refs[:3], refs[3:]
    (in_ref, w_conv_ref, cot_ref, gains_ref, wq0, wk0, wv0, wo0), refs = refs[:8], refs[8:]
    (w_out_hbm, out_grad_hbm, inputs_hbm, memory_hbm, cmem_hbm), refs = refs[:5], refs[5:]
    (gain_row_out, lse_near, lse_far), refs = refs[:3], refs[3:]
    places, refs = refs[:STORED], refs[STORED:]
    (w_in_all, w_out_all, gf_rest), refs = refs[:3], refs[3:]
    kept, refs = refs[:STORED], refs[STORED:]
    (conv_out, gf_out, q_near, k_near, v_near, q_far, k_far, v_far, mixed_near, mixed_far), more = kept[:10], kept[10:]
    (key_t, hidden_out, normed_out), more = more[:3], more[3:]
    (wq1, wq2, wq3, wk1, wk2, wk3, wv1, wv2, wv3, wo1, wo2, wo3, conv_grad) = more
    gains_out, cot_out, key_rows, scores, inputs, out_grad, memory, cmem, spread, conv_send, cot_send, in_pieces, sems = refs
    bits = len(masks)
    width = inputs.shape[1]
    half = wk0.shape[1]
    head = lax.axis_index("head")
    dp = lax.axis_index("dp")
    count = counts_ref[head]
    lens = (cmem_ref[head], mem_ref[head])
    flags = tuple(jnp.where(jnp.bitwise_and(dp, mask) != 0, 1, 0) for mask in masks)
    whole = slice(None)

    def head_device(r):
        return (dp, jnp.bitwise_xor(head, r))

    def dp_device(r):
        return (lax.rem(dp + r, dps), head)

    barrier = pltpu.get_barrier_semaphore()
    for r in range(1, heads):
        pl.semaphore_signal(barrier, inc=1, device_id=head_device(r), device_id_type=MESH)
    for r in range(1, dps):
        pl.semaphore_signal(barrier, inc=1, device_id=dp_device(r), device_id_type=MESH)

    slots = {}

    def slot(name):
        if name not in slots:
            slots[name] = len(slots)
        return slots[name]

    def remote(name, source, target, device):
        at = slot(name)
        return pltpu.make_async_remote_copy(
            src_ref=source,
            dst_ref=target,
            send_sem=sems.at[0, at],
            recv_sem=sems.at[1, at],
            device_id=device,
            device_id_type=MESH,
        )

    def local(name, source, target):
        return pltpu.make_async_copy(source, target, sems.at[0, slot(name)])

    for r in range(heads):
        if len(in_ref.shape) == 3:
            in_pieces[r] = in_ref[r]
        else:
            other = jnp.bitwise_xor(head, r)
            for n in range(dps):
                cut = pl.ds(pl.multiple_of((n * heads + other) * E, E), E)
                in_pieces[r, :, n * E : (n + 1) * E] = in_ref[:, cut]

    loads = {}
    for name, source, target in [
        ("out_grad", out_grad_hbm, out_grad),
        ("cmem", cmem_hbm.at[head], cmem),
        ("memory", memory_hbm, memory),
        ("inputs", inputs_hbm, inputs),
        ("w_out", w_out_hbm, w_out_all.at[flags]),
        ("in_own", in_pieces.at[0], w_in_all.at[flags + (head,)]),
    ]:
        loads[name] = local(f"load_{name}", source, target)
        loads[name].start()
    sent, stored = [], []

    def store(*buffers):
        for buffer in buffers:
            at = [buffer is other for other in kept].index(True)
            copy = local(f"store_{at}", buffer, places[at])
            copy.start()
            stored.append(copy)

    def send(*args):
        copy = remote(*args)
        copy.start()
        sent.append(copy)
        return copy

    at = dp * heads + head
    short = gains_ref.shape[1]
    lane = lax.broadcasted_iota(jnp.int32, (short, E), 1)
    place = lax.broadcasted_iota(jnp.int32, (short, E), 0) + lax.rem(at * short, E)
    spot = jnp.where(lane == place, 1.0, 0.0).astype(bf16)
    gains_out[at] = dot(gains_ref[...].astype(bf16), spot)
    columns = conv_out.shape[2]
    pad_rows = cot_out.shape[1]
    new_rows = cot_ref.shape[0]
    pl.semaphore_wait(barrier, heads + dps - 2)

    gain_heads = [
        send(f"gain_{r}", gains_out.at[at], gains_out.at[at], head_device(r))
        for r in range(1, heads)
    ]
    in_rows = [
        send(f"in_{r}", in_pieces.at[r], w_in_all.at[flags + (head,)], head_device(r))
        for r in range(1, heads)
    ]
    core = [
        send(f"core_{n}", source, target, head_device(1))
        for n, (source, target) in enumerate(((wk0, wk1), (wv0, wv1), (wq0, wq1), (wo0, wo1)))
    ]
    x_k = send("x_k", wk0, wk2, head_device(2))
    rows_o = wo2.shape[bits]
    own_o = wo0.at[pl.ds(pl.multiple_of(dp * rows_o, rows_o), rows_o)]
    x_o = send("x_o", own_o, wo2.at[flags], head_device(2))

    dp_partners = [(jnp.bitwise_xor(dp, mask), head) for mask in masks]

    def gather(name, block, order, source=None):
        copies, index = [], list(flags)
        for n, bit in enumerate(order):
            part = block.at[tuple(index)]
            first = source if source is not None and n == 0 else part
            copies.append(remote(f"gather_{name}_{n}", first, part, dp_partners[bit]))
            index[bit] = whole
        return copies

    straight = list(range(bits))
    crossed = straight[:-2] + [bits - 1, bits - 2]
    gathers = {
        "out": gather("out", w_out_all, straight, w_out_hbm),
        "in": gather("in", w_in_all, crossed),
        "o": gather("o", wo2, straight),
    }
    gathers["out"][0].start()

    def advance(name, n):
        gathers[name][n].wait_recv()
        if n + 1 < bits:
            gathers[name][n + 1].start()

    small = []
    for r in range(heads):
        other = jnp.bitwise_xor(head, r)
        cut = pl.ds(pl.multiple_of(other * columns, columns), columns)
        conv_piece = w_conv_ref[:, cut]
        cot_piece = jnp.concatenate(
            [cot_ref[:, 0, cut], jnp.zeros((pad_rows - new_rows, columns), f32)], axis=0
        ).astype(bf16)
        if r == 0:
            conv_out[head] = conv_piece
            cot_out[head] = cot_piece
        else:
            conv_send[r - 1] = conv_piece
            cot_send[r - 1] = cot_piece
            small.append(send(f"conv_{r}", conv_send.at[r - 1], conv_out.at[head], head_device(r)))
            small.append(send(f"cot_{r}", cot_send.at[r - 1], cot_out.at[head], head_device(r)))
    for copy in gain_heads:
        copy.wait_recv()
    block = gains_out.at[pl.ds(dp * heads, heads)]
    gain_dps = [send(f"gain_dp_{r}", block, block, dp_device(r)) for r in range(1, dps)]
    for copy in in_rows:
        copy.wait_recv()
    loads["in_own"].wait()
    gathers["in"][0].start()
    x_v = send("x_v", wv0, wv2, head_device(2))
    x_q = send("x_q", wq0, wq2, head_device(2))

    loads["out_grad"].wait()

    def cotangent(n, carry):
        rows = pl.ds(pl.multiple_of(n * 128, 128), 128)
        row = lax.broadcasted_iota(jnp.int32, (128, width), 0) + n * 128
        gf_out[rows] = jnp.where(row < count, out_grad[rows], 0.0).astype(bf16)
        return carry

    lax.fori_loop(0, slot_len // 128, cotangent, 0)
    store(gf_out)
    gf_core = send("gf_core", gf_out, gf_rest.at[0], head_device(1))
    gf_x = send("gf_x", gf_out, gf_rest.at[1], head_device(2))
    for copy in gain_dps:
        copy.wait_recv()
    many = E // short
    tiles = [
        sum(gains_out[t * many + n] for n in range(many)) for t in range(dps * heads // many)
    ]
    gain_one = jnp.concatenate([tile[0:1] for tile in tiles], axis=1)
    gain_two = jnp.concatenate([tile[1:2] for tile in tiles], axis=1)
    gain_row_out[0:1] = gain_one
    gain_row_out[1:2] = gain_two
    for copy in core:
        copy.wait_recv()
    store(wk1, wv1, wq1, wo1)

    def project(normed, rows, weights, k_ref, v_ref):
        for n, (wk, wv) in enumerate(weights):
            cut = slice(n * half, (n + 1) * half)
            k_ref[rows, cut] = dot(normed, wk).astype(bf16)
            v_ref[rows, cut] = dot(normed, wv).astype(bf16)

    def near_rows(source, part):
        def one(n, carry):
            rows = pl.ds(pl.multiple_of(n * BLOCK, BLOCK), BLOCK)
            target = pl.ds(pl.multiple_of(part * slot_len + n * BLOCK, BLOCK), BLOCK)
            normed = layer_norm(source[rows].astype(f32), gain_one).astype(bf16)
            key_rows[target] = normed
            key_t[:, target] = normed.T
            project(normed, target, ((wk0[...], wv0[...]), (wk1[...], wv1[...])), k_near, v_near)
            if part == 2:
                q_near[rows, :half] = dot(normed, wq0[...]).astype(bf16)
                q_near[rows, half:] = dot(normed, wq1[...]).astype(bf16)
            return carry

        lax.fori_loop(0, slot_len // BLOCK, one, 0)

    loads["cmem"].wait()
    near_rows(cmem, 0)
    loads["w_out"].wait()
    advance("out", 0)
    loads["memory"].wait()
    near_rows(memory.at[head], 1)
    x_o.wait_recv()
    gathers["o"][0].start()
    loads["inputs"].wait()
    near_rows(inputs, 2)
    store(q_near, k_near, v_near, key_t)
    advance("in", 0)

    c = score_scale * log2e

    def attend(q_ref, k_ref, v_ref, mixed_ref, lse_ref, events):
        def one(h, carry):
            cut = pl.ds(pl.multiple_of(h * E, E), E)
            q_t = q_ref[:, cut].T
            v_t = v_ref[:, cut].T
            top = jnp.full((1, slot_len), masked_value, f32)
            for kb in range(6):
                first = BLOCK if kb == 5 else 0
                rows = slice(kb * BLOCK, (kb + 1) * BLOCK)
                s = masked_scores(kb, lens, dot(k_ref[rows, cut], q_t[:, first:]))
                scores[rows, first:] = s
                part = jnp.max(s, axis=0, keepdims=True)
                if first:
                    top = jnp.concatenate([top[:, :first], jnp.maximum(top[:, first:], part)], axis=1)
                else:
                    top = jnp.maximum(top, part)
            shift = top * c
            mixed = jnp.zeros((E, slot_len), f32)
            total = jnp.zeros((1, slot_len), f32)
            for kb in range(6):
                first = BLOCK if kb == 5 else 0
                rows = slice(kb * BLOCK, (kb + 1) * BLOCK)
                p = jnp.exp2(scores[rows, first:] * c - shift[:, first:])
                part = jnp.sum(p, axis=0, keepdims=True)
                out = dot(v_t[:, rows], p.astype(bf16))
                if first:
                    total = jnp.concatenate([total[:, :first], total[:, first:] + part], axis=1)
                    mixed = jnp.concatenate([mixed[:, :first], mixed[:, first:] + out], axis=1)
                else:
                    total = total + part
                    mixed = mixed + out
            mixed_ref[:, cut] = (mixed / total).T.astype(bf16)
            lse_ref[h] = shift + jnp.log2(total)
            for when, event in events:
                pl.when(h == when)(event)
            return carry

        lax.fori_loop(0, q_ref.shape[1] // E, one, 0)

    attend(
        q_near,
        k_near,
        v_near,
        mixed_near,
        lse_near,
        [
            (1, lambda: advance("out", 1)),
            (2, lambda: advance("o", 0)),
        ],
    )

    for copy in small:
        copy.wait_recv()
    store(mixed_near, conv_out)
    taps = 3

    def spread_rows(g, carry):
        source_row = lax.broadcasted_iota(jnp.int32, (slot_len, pad_rows), 0)
        picked_row = lax.broadcasted_iota(jnp.int32, (slot_len, pad_rows), 1)
        kept = source_row < lax.min(counts_ref[g], mem_ref[g])
        for tap in range(taps):
            pick = jnp.where(kept & (source_row == taps * picked_row + tap), 1.0, 0.0).astype(bf16)
            spread[g, :, tap * columns : (tap + 1) * columns] = dot(pick, cot_out[g]).astype(bf16)
        return carry

    lax.fori_loop(0, group, spread_rows, 0)
    x_k.wait_recv()
    fwd_k = send("fwd_k", wk2, wk3, head_device(1))

    def conv_rows(n, carry):
        rows = pl.ds(pl.multiple_of(n * BLOCK, BLOCK), BLOCK)
        total = sum(dot(memory[g, :, rows].T, spread[g]) for g in range(group)).astype(bf16)
        for tap in range(taps):
            conv_grad[tap, rows] = total[:, tap * columns : (tap + 1) * columns]
        return carry

    lax.fori_loop(0, width // BLOCK, conv_rows, 0)
    advance("in", 1)
    x_v.wait_recv()
    fwd_v = send("fwd_v", wv2, wv3, head_device(1))
    store(conv_grad)
    advance("o", 1)
    x_q.wait_recv()
    fwd_q = send("fwd_q", wq2, wq3, head_device(1))
    for copy in (fwd_k, fwd_v):
        copy.wait_recv()
    store(wk2, wk3, wv2, wv3)

    def far_rows(n, carry):
        rows = pl.ds(pl.multiple_of(n * BLOCK, BLOCK), BLOCK)
        project(key_rows[rows], rows, ((wk2[...], wv2[...]), (wk3[...], wv3[...])), k_far, v_far)
        return carry

    lax.fori_loop(0, key_rows.shape[0] // BLOCK, far_rows, 0)
    fwd_q.wait_recv()
    store(wq2, wq3)
    for n in range(slot_len // BLOCK):
        rows = slice(n * BLOCK, (n + 1) * BLOCK)
        normed = key_rows[2 * slot_len + n * BLOCK : 2 * slot_len + (n + 1) * BLOCK]
        q_far[rows, :half] = dot(normed, wq2[...]).astype(bf16)
        q_far[rows, half:] = dot(normed, wq3[...]).astype(bf16)
    store(q_far, k_far, v_far)
    for n in range(2, bits):
        advance("o", n)
    fwd_o = send("fwd_o", wo2, wo3, head_device(1))
    attend(q_far, k_far, v_far, mixed_far, lse_far, [])
    store(mixed_far)
    fwd_o.wait_recv()
    store(wo2, wo3)

    def mix(n, carry):
        rows = pl.ds(pl.multiple_of(n * 128, 128), 128)
        near, far = mixed_near[rows], mixed_far[rows]
        attention = (
            dot(near[:, :half], wo0[...])
            + dot(near[:, half:], wo1[...])
            + dot(far[:, :half], wo2[...].reshape(half, width))
            + dot(far[:, half:], wo3[...].reshape(half, width))
        )
        row = lax.broadcasted_iota(jnp.int32, (128, width), 0) + n * 128
        hidden = inputs[rows] + jnp.where(row < count, attention, 0.0)
        hidden_out[rows] = hidden
        normed_out[rows] = layer_norm(hidden, gain_two).astype(bf16)
        return carry

    lax.fori_loop(0, slot_len // 128, mix, 0)
    store(hidden_out, normed_out)
    gf_x.wait_recv()
    gf_diag = send("gf_diag", gf_rest.at[1], gf_rest.at[2], head_device(1))
    gf_core.wait_recv()
    gf_diag.wait_recv()
    for n in range(2, bits):
        advance("in", n)
        advance("out", n)
    for copy in stored:
        copy.wait()
    for copy in sent:
        copy.wait_send()
    for copies in gathers.values():
        for copy in copies:
            copy.wait_send()


def forward(counts, mem_lens, cmem_lens, w_in, w_conv, comp_grad, gains, weights, w_out, out_grad, inputs, memory, compressed):
    heads, dps = lax.axis_size("head"), lax.axis_size("dp")
    masks = [1 << b for b in reversed(range(dps.bit_length() - 1))]
    twos = (2,) * len(masks)
    slot_len, width = inputs.shape
    group, keys = memory.shape[0], 3 * slot_len
    wq, wk, wv, wo = weights
    in_pieces = (heads, w_in.shape[-2], w_out.shape[0] * dps)
    half = wk.shape[1]
    columns = width // heads
    new_rows = comp_grad.shape[0]
    pad_rows = (new_rows + 15) // 16 * 16
    shape = jax.ShapeDtypeStruct
    wide = 2 * half
    conv_all = (heads, w_conv.shape[0], columns)
    cot_all = (heads, pad_rows, columns)
    o_cut = twos + (half // dps, width)
    outs = [
        shape((2, width), f32),
        shape((wide // E, 1, slot_len), f32),
        shape((wide // E, 1, slot_len), f32),
    ]
    kept = [
        shape(conv_all, bf16),
        shape((slot_len, width), bf16),
        shape((slot_len, wide), bf16),
        shape((keys, wide), bf16),
        shape((keys, wide), bf16),
        shape((slot_len, wide), bf16),
        shape((keys, wide), bf16),
        shape((keys, wide), bf16),
        shape((slot_len, wide), bf16),
        shape((slot_len, wide), bf16),
        shape((width, keys), bf16),
        shape((slot_len, width), f32),
        shape((slot_len, width), bf16),
        *[shape(wq.shape, bf16)] * 3,
        *[shape(wk.shape, bf16)] * 3,
        *[shape(wv.shape, bf16)] * 3,
        shape(wo.shape, bf16),
        shape(o_cut, bf16),
        shape(o_cut, bf16),
        shape((3, width, columns), bf16),
    ]
    far_outs = [
        shape(twos + in_pieces, bf16),
        shape(twos + w_out.shape, bf16),
        shape((heads - 1, slot_len, width), bf16),
    ]
    smem = pl.BlockSpec(memory_space=pltpu.SMEM)
    return pl.pallas_call(
        functools.partial(forward_kernel, heads, dps, masks, group, slot_len),
        in_specs=[smem] * 3 + [vmem()] * 8 + [anywhere()] * 5,
        out_specs=[vmem()] * len(outs) + [anywhere()] * (len(kept) + len(far_outs)),
        out_shape=outs + kept + far_outs,
        scratch_shapes=[pltpu.VMEM(k.shape, k.dtype) for k in kept]
        + [
            pltpu.VMEM((dps * heads, 8, E), f32),
            pltpu.VMEM(cot_all, bf16),
            pltpu.VMEM((keys, width), bf16),
            pltpu.VMEM((keys, slot_len), f32),
            pltpu.VMEM((slot_len, width), f32),
            pltpu.VMEM((slot_len, width), f32),
            pltpu.VMEM(memory.shape, bf16),
            pltpu.VMEM((slot_len, width), bf16),
            pltpu.VMEM((group, slot_len, 3 * columns), bf16),
            pltpu.VMEM((heads - 1,) + conv_all[1:], bf16),
            pltpu.VMEM((heads - 1,) + cot_all[1:], bf16),
            pltpu.VMEM(in_pieces, bf16),
            pltpu.SemaphoreType.DMA((2, 30 + STORED + 6 * heads + dps + 4 * len(masks))),
        ],
        compiler_params=pltpu.CompilerParams(
            collective_id=0, has_side_effects=True, vmem_limit_bytes=61 * 2**20
        ),
        cost_estimate=pl.CostEstimate(flops=40 * 10**9, bytes_accessed=0, transcendentals=0),
        name="forward",
    )(counts, mem_lens, cmem_lens, w_in, w_conv, comp_grad, gains, *weights, w_out, out_grad, inputs, memory, compressed)


def norm_input_grad(values, gain, grad):
    mean = jnp.mean(values, axis=-1, keepdims=True)
    centred = values - mean
    scale = lax.rsqrt(jnp.mean(centred * centred, axis=-1, keepdims=True) + epsilon)
    unit = centred * scale
    grad = grad * gain
    shift = jnp.mean(grad, axis=-1, keepdims=True)
    slope = jnp.mean(grad * unit, axis=-1, keepdims=True)
    return scale * (grad - shift - unit * slope)


def gelu_parts(u):
    c = 0.7978845608028654
    cube = 0.044715 * u * u
    t = jnp.tanh(c * (u + cube * u))
    half = 0.5 * (1.0 + t)
    return u * half, half + 0.5 * u * (1.0 - t * t) * (c * (1.0 + 3.0 * cube))


def middle_kernel(heads, masks, group, *refs):
    (counts_ref, mem_ref, gain_ref, conv_ref), refs = refs[:4], refs[4:]
    (n2_hbm, gf_hbm, gf_rest, w_in_hbm, w_out_hbm, conv_grad, memory_hbm), refs = refs[:7], refs[7:]
    (hidden_hbm, out_grad_hbm, mixed_near, mixed_far, wo0, wo1, wo2, wo3), refs = refs[:8], refs[8:]
    (conv_fin, new_cols, out_part), refs = refs[:3], refs[3:]
    (grad_hbm, gm_hbm, go_near, go_far, in_hbm, out_own_hbm, out_core_hbm, out_far_hbm, out_x_hbm), refs = refs[:9], refs[9:]
    (w_in, w_out, n2, gf, act, gi, gn_own, gn_part, gn_core, gn_diag, gn_x), refs = refs[:11], refs[11:]
    (out_own, out_send, out_diag, grad_out, grad_in, out_got, memory, out_grad, conv_all), refs = refs[:9], refs[9:]
    conv_kept, conv_got, sems = refs[0], refs[1:-1], refs[-1]
    bits = len(masks)
    slot_len, width = gn_own.shape
    head = lax.axis_index("head")
    dp = lax.axis_index("dp")
    flags = tuple(jnp.where(jnp.bitwise_and(dp, mask) != 0, 1, 0) for mask in masks)
    whole = slice(None)
    core = (dp, jnp.bitwise_xor(head, 1))
    chip = (dp, jnp.bitwise_xor(head, 2))
    partners = [(jnp.bitwise_xor(dp, mask), head) for mask in masks]

    barrier = pltpu.get_barrier_semaphore()
    for device in [core, chip] + partners:
        pl.semaphore_signal(barrier, inc=1, device_id=device, device_id_type=MESH)

    slots = {}

    def slot(name):
        if name not in slots:
            slots[name] = len(slots)
        return slots[name]

    sent, stored = [], []

    def remote(name, source, target, device):
        at = slot(name)
        copy = pltpu.make_async_remote_copy(
            src_ref=source,
            dst_ref=target,
            send_sem=sems.at[0, at],
            recv_sem=sems.at[1, at],
            device_id=device,
            device_id_type=MESH,
        )
        sent.append(copy)
        return copy

    def send(*args):
        copy = remote(*args)
        copy.start()
        return copy

    def local(name, source, target):
        copy = pltpu.make_async_copy(source, target, sems.at[0, slot(name)])
        copy.start()
        return copy

    def store(name, source, target):
        stored.append(local(name, source, target))

    load = {
        "n2": local("load_n2", n2_hbm, n2.at[0]),
        "w_in": local("load_w_in", w_in_hbm, w_in),
        "gf": local("load_gf", gf_hbm, gf.at[0]),
        "w_out": local("load_w_out", w_out_hbm, w_out),
        "gf_core": local("load_gf_core", gf_rest.at[0], gf.at[1]),
        "gf_far": local("load_gf_far", gf_rest.at[pl.ds(1, 2)], gf.at[pl.ds(2, 2)]),
        "conv": local(
            "load_conv", conv_grad.at[(whole,) * (bits - 1) + (flags[-1],)], conv_kept
        ),
        "out_grad": local("load_out_grad", out_grad_hbm, out_grad),
    }
    conv_all[flags] = conv_ref[...]
    pl.semaphore_wait(barrier, 2 + bits)

    n2_core = send("n2_core", n2_hbm, n2.at[1], core)
    halves = [pl.ds(h * (slot_len // 2), slot_len // 2) for h in range(2)]
    n2_x = [send(f"n2_x{h}", n2_hbm.at[halves[h]], n2.at[2, halves[h]], chip) for h in range(2)]
    n2_diag = [remote(f"n2_diag{h}", n2.at[2, halves[h]], n2.at[3, halves[h]], core) for h in range(2)]

    order = list(range(bits - 2)) + [bits - 1, bits - 2]
    index, gathers = list(flags), []
    for n, bit in enumerate(order):
        part = conv_all.at[tuple(index)]
        gathers.append(remote(f"conv_{n}", part, part, partners[bit]))
        index[bit] = whole
    sums = [
        remote(
            f"conv_sum{n}",
            (conv_grad if n == bits - 1 else conv_got[n + 1]).at[(whole,) * n + (1 - flags[n],)],
            conv_got[n],
            partners[n],
        )
        for n in range(bits)
    ]
    gathers[0].start()
    sums[bits - 1].start()

    def add_sum(n):
        sums[n].wait_recv()
        for at in range(2**n):
            spot = tuple((at >> (n - 1 - b)) & 1 for b in range(n))
            mine = conv_kept[spot] if n == bits - 1 else conv_got[n + 1][spot + (flags[n],)]
            conv_got[n][spot] = (conv_got[n][spot].astype(f32) + mine.astype(f32)).astype(bf16)
        if n:
            sums[n - 1].start()

    def next_gather(n):
        gathers[n].wait_recv()
        if n + 1 < bits:
            gathers[n + 1].start()

    rows_of = slot_len // 2
    units = w_in.shape[1]
    chunk = 512

    def tokens(s, half):
        rows = pl.ds(pl.multiple_of(half * rows_of, rows_of), rows_of)
        for n in range(units // chunk):
            cut = slice(n * chunk, (n + 1) * chunk)
            inner = dot(n2[s, rows], w_in[:, cut])
            value, slope = gelu_parts(inner)
            act[s, rows, cut] = value.astype(bf16)
            gi[s, rows, cut] = (dot_nt(gf[s, rows], w_out[cut, :]) * slope).astype(bf16)
        return rows, dot_nt(gi[s, rows], w_in[...])

    for name in ("n2", "w_in", "gf", "w_out", "gf_core"):
        load[name].wait()
    n2_core.wait_recv()

    def near(n, carry):
        s = lax.div(n, 2)
        rows, grad = tokens(s, lax.rem(n, 2))

        @pl.when(s == 0)
        def _():
            gn_own[rows] = grad

        @pl.when(s == 1)
        def _():
            gn_part[0, rows] = grad.astype(bf16)

        return carry

    lax.fori_loop(0, 4, near, 0)
    core_sent = send("gn_core", gn_part.at[0], gn_core, core)

    def terms(lhs, rhs, target, first, again):
        many = width // 4

        def one(n, carry):
            cut = pl.ds(pl.multiple_of(n * many, many), many)
            left = jnp.concatenate([lhs[first, :, cut].T, lhs[first + 1, :, cut].T], axis=1)
            total = dot(left, rhs[first : first + 2].reshape(2 * slot_len, rhs.shape[2]))
            block = target.shape[bits]
            per = many // block
            low = per.bit_length() - 1
            for m in range(per):
                spot = tuple(
                    lax.rem(lax.div(n, 2 ** (bits - low - 1 - b)), 2) for b in range(bits - low)
                ) + tuple((m >> (low - 1 - b)) & 1 for b in range(low))
                value = total[m * block : (m + 1) * block]
                if again:
                    value = value + target[spot].astype(f32)
                target[spot] = value.astype(bf16)
            return carry

        lax.fori_loop(0, 4, one, 0)

    def outward(n, carry):
        s = lax.div(n, 2)
        rows = pl.ds(pl.multiple_of(lax.rem(n, 2) * rows_of, rows_of), rows_of)
        value = dot(act[s, rows], w_out[...])

        @pl.when(s == 0)
        def _():
            out_own[rows] = value

        @pl.when(s > 0)
        def _():
            out_send[lax.max(s - 1, 0), rows] = value.astype(bf16)

        return carry

    n2_x[0].wait_recv()
    n2_diag[0].start()
    lax.fori_loop(0, 4, outward, 0)
    store("out_own", out_own, out_own_hbm)
    out_core = send("out_core", out_send.at[0], out_core_hbm, core)
    next_gather(0)
    load["gf_far"].wait()
    n2_diag[0].wait_recv()

    def far(half):
        def one(n, carry):
            rows, grad = tokens(2 + n, half)
            gn_part[1 + n, rows] = grad.astype(bf16)
            return carry

        lax.fori_loop(0, 2, one, 0)
        return send(f"gn_diag{half}", gn_part.at[2, halves[half]], gn_diag.at[halves[half]], core)

    def far_sum(half, copy):
        copy.wait_recv()
        rows = halves[half]
        gn_part[1, rows] = (gn_part[1, rows].astype(f32) + gn_diag[rows].astype(f32)).astype(bf16)
        return send(f"gn_x{half}", gn_part.at[1, rows], gn_x.at[rows], chip)

    diag_sent = far(0)
    terms(act, gf, grad_out, 0, False)
    gn_back = [far_sum(0, diag_sent)]
    load["conv"].wait()
    add_sum(bits - 1)
    terms(n2, gi, grad_in, 0, False)
    n2_x[1].wait_recv()
    n2_diag[1].start()
    next_gather(1)
    n2_diag[1].wait_recv()
    diag_sent = far(1)
    lax.fori_loop(4, 8, outward, 0)
    out_back = send("out_diag", out_send.at[2], out_diag, core)
    gn_back.append(far_sum(1, diag_sent))
    terms(act, gf, grad_out, 2, True)
    out_y = send(
        "out_sum", grad_out.at[(whole,) * (bits - 1) + (1 - flags[-1],)], out_got, partners[-1]
    )
    if bits > 1:
        add_sum(bits - 2)
    out_back.wait_recv()
    for h in range(2):
        rows = halves[h]
        out_diag[rows] = (out_diag[rows].astype(f32) + out_send[1, rows].astype(f32)).astype(bf16)
    out_x = send("out_x", out_diag.at[halves[0]], out_x_hbm, chip)
    store("out_far", out_diag.at[halves[1]], out_far_hbm)
    terms(n2, gi, grad_in, 2, True)
    store("grad_in", grad_in, in_hbm)
    for n in range(2, bits):
        next_gather(n)
    for n in reversed(range(bits - 2)):
        add_sum(n)
    conv_fin[...] = conv_got[0][...].reshape(conv_fin.shape)

    near_wide, far_wide = mixed_near.shape[1], mixed_far.shape[1]
    half_rows = wo0.shape[0]
    late = [
        local("load_mixed_near", mixed_near, act.at[0, :, pl.ds(0, near_wide)]),
        local("load_mixed_far", mixed_far, act.at[0, :, pl.ds(near_wide, far_wide)]),
    ] + [
        local(f"load_wo{r}", w, act.at[1 + r // 2, pl.ds((r % 2) * half_rows, half_rows)])
        for r, w in enumerate((wo0, wo1, wo2, wo3))
    ]
    stored[0].wait()
    hidden_load = local("load_hidden", hidden_hbm, out_own)

    pad_rows, columns = new_cols.shape[1], new_cols.shape[2]
    taps = 3

    def stream(g, carry):
        copy = local("load_memory", memory_hbm.at[g], memory)
        kernel = conv_all[...].reshape(taps * width, columns)
        source_row = lax.broadcasted_iota(jnp.int32, (pad_rows, slot_len), 1)
        picked_row = lax.broadcasted_iota(jnp.int32, (pad_rows, slot_len), 0)
        kept = source_row < lax.min(counts_ref[g], mem_ref[g])
        copy.wait()
        total = jnp.zeros((pad_rows, columns), f32)
        for tap in range(taps):
            pick = jnp.where(kept & (source_row == taps * picked_row + tap), 1.0, 0.0).astype(bf16)
            rows = dot(pick, memory[0:slot_len]).astype(bf16)
            total = total + dot(rows, kernel[tap * width : (tap + 1) * width])
        new_cols[g] = total.astype(bf16)
        return carry

    lax.fori_loop(0, group, stream, 0)
    for copy in [hidden_load, load["out_grad"]] + late:
        copy.wait()
    for copy in gn_back:
        copy.wait_recv()
    core_sent.wait_recv()
    gain = gain_ref[1:2]

    def back(n, carry):
        rows = pl.ds(pl.multiple_of(n * 128, 128), 128)
        grad = gn_own[rows] + gn_core[rows].astype(f32) + gn_x[rows].astype(f32)
        grad = out_grad[rows] + norm_input_grad(out_own[rows], gain, grad)
        gn_own[rows] = grad
        row = lax.broadcasted_iota(jnp.int32, (128, width), 0) + n * 128
        gi[0, rows] = jnp.where(row < counts_ref[head], grad, 0.0).astype(bf16)
        return carry

    lax.fori_loop(0, slot_len // 128, back, 0)
    store("grad_hidden", gn_own, grad_hbm)
    weights = act[1:3].reshape(2 * slot_len, width)
    for h in range(2):
        gi[1, halves[h]] = dot_nt(gi[0, halves[h]], weights).astype(bf16)
    store("gm", gi.at[1], gm_hbm)
    for n, target in enumerate((go_near, go_far)):
        cut = slice(n * near_wide, (n + 1) * near_wide)
        gi[2 + n] = dot(act[0, :, cut].T, gi[0]).astype(bf16)
        store(f"go{n}", gi.at[2 + n], target)
    out_y.wait_recv()
    for at in range(2 ** (bits - 1)):
        spot = tuple((at >> (bits - 2 - b)) & 1 for b in range(bits - 1))
        out_part[spot] = (
            out_got[spot].astype(f32) + grad_out[spot + (flags[-1],)].astype(f32)
        ).astype(bf16)
    out_core.wait_recv()
    out_x.wait_recv()
    for copy in stored[1:]:
        copy.wait()
    for copy in sent:
        copy.wait_send()


def middle(counts, mem_lens, gains, conv_rows, normed, grad_ffn, gf_rest, w_in, w_out, conv_grad, memory, hidden, out_grad, mixed_near, mixed_far, wo):
    heads, dps = lax.axis_size("head"), lax.axis_size("dp")
    masks = [1 << b for b in reversed(range(dps.bit_length() - 1))]
    bits = len(masks)
    twos = lambda n: (2,) * n
    slot_len, width = hidden.shape
    units = w_in.shape[1]
    columns = conv_rows.shape[2]
    new_rows = (slot_len + 2) // 3
    pad_rows = (new_rows + 15) // 16 * 16
    shape = jax.ShapeDtypeStruct
    stream = (slot_len, width)
    conv_block = conv_grad.shape[bits:]
    in_block = (width // dps, units)
    out_block = (units // dps, width)
    smem = pl.BlockSpec(memory_space=pltpu.SMEM)
    buffers = [
        (w_in.shape, bf16),
        (w_out.shape, bf16),
        ((4,) + stream, bf16),
        ((4,) + stream, bf16),
        ((4, slot_len, units), bf16),
        ((4, slot_len, units), bf16),
        (stream, f32),
        ((3,) + stream, bf16),
        (stream, bf16),
        (stream, bf16),
        (stream, bf16),
        (stream, f32),
        ((3,) + stream, bf16),
        (stream, bf16),
        (twos(bits) + out_block, bf16),
        (twos(bits) + in_block, bf16),
        (twos(bits - 1) + out_block, bf16),
        (memory.shape[1:], bf16),
        (stream, f32),
        (twos(bits) + conv_rows.shape, bf16),
        (twos(bits - 1) + conv_block, bf16),
    ] + [(twos(n) + conv_block, bf16) for n in range(bits)]
    return pl.pallas_call(
        functools.partial(middle_kernel, heads, masks, memory.shape[0]),
        in_specs=[smem] * 2 + [vmem()] * 2 + [anywhere()] * 15,
        out_specs=[vmem()] * 3 + [anywhere()] * 9,
        out_shape=[
            shape(conv_rows.shape, bf16),
            shape((memory.shape[0], pad_rows, columns), bf16),
            shape(twos(bits - 1) + out_block, bf16),
            shape(stream, f32),
            shape((slot_len, 4 * wo[0].shape[0]), bf16),
            shape((mixed_near.shape[1], width), bf16),
            shape((mixed_far.shape[1], width), bf16),
            shape(twos(bits) + in_block, bf16),
            shape(stream, f32),
            shape(stream, bf16),
            shape((slot_len // 2, width), bf16),
            shape((slot_len // 2, width), bf16),
        ],
        scratch_shapes=[pltpu.VMEM(*b) for b in buffers]
        + [pltpu.SemaphoreType.DMA((2, 52 + 3 * bits))],
        compiler_params=pltpu.CompilerParams(
            collective_id=2, has_side_effects=True, vmem_limit_bytes=61 * 2**20
        ),
        cost_estimate=pl.CostEstimate(flops=30 * 10**9, bytes_accessed=0, transcendentals=0),
        name="middle",
    )(counts, mem_lens, gains, conv_rows, normed, grad_ffn, gf_rest, w_in, w_out, conv_grad, memory, hidden, out_grad, mixed_near, mixed_far, *wo)


def backward_kernel(heads, masks, slot_len, keys, *refs):
    (mem_ref, cmem_ref, lse_near, lse_far), refs = refs[:4], refs[4:]
    loaded = 8 + 3 * heads
    sources, refs = refs[:loaded], refs[loaded:]
    (gain_ref, go_near, go_far, out_part, new_ref, conv_ref, key_t_hbm, in_hbm, inputs_hbm, hidden_hbm), refs = refs[:10], refs[10:]
    (out_far_hbm,), refs = refs[:1], refs[1:]
    (grad_out, sum_rows, input_grad_hbm, go_out, gain_out, in_got, new_got, conv_got, out_x_hbm), refs = refs[:9], refs[9:]
    held, refs = refs[:loaded], refs[loaded:]
    (q_near, k_near, v_near, gm_near, q_far, k_far, v_far, gm_far), more = held[:8], held[8:]
    wq, wk, wv = more[:heads], more[heads : 2 * heads], more[2 * heads :]
    (key_t, probs, grads, dkv, terms, far_terms, own_terms, got_near, got_far, got_x), refs = refs[:10], refs[10:]
    bits = len(masks)
    in_kept, refs = refs[0], refs[1:]
    in_got_rs, refs = refs[:bits], refs[bits:]
    out_got_rs, refs = refs[: bits - 1], refs[bits - 1 :]
    go_core_near, go_core_far, go_x, refs = refs[0], refs[1], refs[2], refs[3:]
    (go_sum, go_y_got, go_z_got), refs = refs[:3], refs[3:]
    y_got, z_got, last_got, last_z_got, grad_normed, gain_terms, sems = refs
    head = lax.axis_index("head")
    dp = lax.axis_index("dp")
    lens = (cmem_ref[head], mem_ref[head])
    flags = [jnp.where(jnp.bitwise_and(dp, mask) != 0, 1, 0) for mask in masks]

    def head_device(r):
        return (dp, jnp.bitwise_xor(head, r))

    def dp_device(n):
        return (jnp.bitwise_xor(dp, masks[n]), head)

    barrier = pltpu.get_barrier_semaphore()
    for r in range(1, heads):
        pl.semaphore_signal(barrier, inc=1, device_id=head_device(r), device_id_type=MESH)
    ring = 2 ** (bits - 1)

    def z_device(k):
        return (jnp.bitwise_xor(dp, 2 * k), head)

    pl.semaphore_signal(barrier, inc=1, device_id=dp_device(bits - 1), device_id_type=MESH)
    for k in range(1, ring):
        pl.semaphore_signal(barrier, inc=1, device_id=z_device(k), device_id_type=MESH)
    pl.semaphore_wait(barrier, heads - 1 + ring)

    slots = {}

    def remote(name, source, target, device, part=0):
        if name not in slots:
            slots[name] = 2 * len(slots)
        at = slots[name] + part
        return pltpu.make_async_remote_copy(
            src_ref=source,
            dst_ref=target,
            send_sem=sems.at[0, at],
            recv_sem=sems.at[1, at],
            device_id=device,
            device_id_type=MESH,
        )

    def local(name, source, target):
        if name not in slots:
            slots[name] = 2 * len(slots)
        return pltpu.make_async_copy(source, target, sems.at[0, slots[name]])

    whole = slice(None)

    def rs_copy(name, held, got, n, part=0):
        return remote(
            f"{name}{n}", held.at[(whole,) * n + (1 - flags[n],)], got, dp_device(n), part
        )

    def rs_add(held, got, n):
        for at in range(2**n):
            index = tuple((at >> (n - 1 - b)) & 1 for b in range(n))
            mine = held[index + (flags[n],)]
            got[index] = (got[index].astype(f32) + mine.astype(f32)).astype(bf16)

    fetches = []
    for n, (source, target) in enumerate(zip(sources, held)):
        if n in (3, 7):
            wide = target.shape[1]
            source = source.at[:, pl.ds((n // 4) * wide, wide)]
        fetches.append(local(f"fetch_{n}", source, target))
    for n in (4, 5, 6, 7):
        fetches[n].start()
    load_keys = local("load_keys", key_t_hbm, key_t)
    load_keys.start()
    for n in range(loaded):
        if n not in (4, 5, 6, 7):
            fetches[n].start()
    in_y = remote("in_rs", in_hbm.at[(whole,) * (bits - 1) + (1 - flags[bits - 1],)], in_got_rs[bits - 1], dp_device(bits - 1))
    in_y.start()
    load_in = local("load_in", in_hbm.at[(whole,) * (bits - 1) + (flags[bits - 1],)], in_kept)
    load_in.start()
    out_z = rs_copy("out_rs", out_part, out_got_rs[bits - 2], bits - 2)
    out_z.start()
    rows_o = go_x.shape[0]
    go_core = [
        remote("go_near", go_near.at[pl.ds(rows_o, rows_o)], go_core_near, head_device(1)),
        remote("go_far", go_far.at[pl.ds(rows_o, rows_o)], go_core_far, head_device(1)),
    ]
    for copy in go_core:
        copy.start()
    closing = []
    for name, source, target in (("new", new_ref, new_got), ("conv", conv_ref, conv_got)):
        for r in range(1, heads):
            copy = remote(
                f"{name}_{r}",
                source.at[jnp.bitwise_xor(head, r)],
                target.at[head],
                head_device(r),
            )
            copy.start()
            closing.append(copy)
        target[head] = source[head]
    go_to_x = remote("go_x", go_core_far, go_x, head_device(2))
    out_x = remote("out_x", out_far_hbm, out_x_hbm, head_device(2))
    out_x.start()

    def in_step(n):
        return rs_copy("in_rs", in_got_rs[n + 1], in_got_rs[n], n)

    def out_step(n):
        return rs_copy("out_rs", out_got_rs[n + 1], out_got_rs[n], n)

    grad_normed[...] = jnp.zeros(grad_normed.shape, f32)
    c = score_scale * log2e

    def core_copy(r, p):
        return remote(f"core_{r}", terms.at[r // 2], (got_near if r == 1 else got_far).at[p], head_device(1), p)

    def x_copy(p):
        return remote("x_terms", far_terms.at[p], got_x.at[p], head_device(2), p)

    z_flags, y_flag = tuple(flags[:-1]), flags[-1]
    half_rows = own_terms.shape[1 + bits] // 2
    upper, lower = pl.ds(0, half_rows), pl.ds(half_rows, half_rows)

    def z_spot(k):
        return tuple(
            jnp.bitwise_xor(flag, (k >> (bits - 2 - b)) & 1) for b, flag in enumerate(z_flags)
        )

    all_z = (whole,) * (bits - 1)

    def plus(*values):
        return sum(value.astype(f32) for value in values).astype(bf16)

    def first_y():
        return remote("first_y", own_terms.at[(0,) + all_z + (1 - y_flag,)], y_got, dp_device(bits - 1))

    def first_z(k):
        return remote(f"first_z{k}", y_got.at[z_spot(k)], z_got.at[k], z_device(k))

    def first_back_z(k):
        spot = sum_rows.at[(0,) + tuple(flags)]
        return remote(f"first_back_z{k}", spot, spot, z_device(k))

    def first_back_y():
        spot = sum_rows.at[(0,) + all_z + (y_flag,)]
        return remote("first_back_y", spot, spot, dp_device(bits - 1))

    parts = (upper, lower)

    def last_y(h):
        source = own_terms.at[(1,) + all_z + (1 - y_flag, parts[h])]
        return remote(f"last_y{h}", source, last_got.at[h], dp_device(bits - 1))

    def last_z(h, k):
        return remote(
            f"last_z{h}_{k}", last_got.at[(h,) + z_spot(k)], last_z_got.at[k, h], z_device(k)
        )

    def last_back_z(h, k):
        spot = sum_rows.at[(1,) + tuple(flags) + (parts[h],)]
        return remote(f"last_back_z{h}_{k}", spot, spot, z_device(k))

    def last_back_y(h):
        spot = sum_rows.at[(1,) + all_z + (y_flag, parts[h])]
        return remote(f"last_back_y{h}", spot, spot, dp_device(bits - 1))

    def go_y():
        return remote("go_y", go_sum.at[all_z + (1 - y_flag,)], go_y_got, dp_device(bits - 1))

    def go_z(k):
        return remote(f"go_z{k}", go_y_got.at[z_spot(k)], go_z_got.at[k], z_device(k))

    def go_back_z(k):
        spot = go_out.at[tuple(flags)]
        return remote(f"go_back_z{k}", spot, spot, z_device(k))

    def go_back_y():
        spot = go_out.at[all_z + (y_flag,)]
        return remote("go_back_y", spot, spot, dp_device(bits - 1))

    def z_index(at):
        return tuple((at >> (bits - 2 - b)) & 1 for b in range(bits - 1))

    def each_block(function):
        def step(at, carry):
            function(tuple(lax.rem(lax.div(at, 2 ** (bits - 1 - b)), 2) for b in range(bits)))
            return carry

        lax.fori_loop(0, 2**bits, step, 0)

    def add_whole(target, source):
        def one(index):
            target[index] = (target[index].astype(f32) + source[index].astype(f32)).astype(bf16)

        each_block(one)

    def attend(r, p):
        half_q, half_k, half_v, half_g, half_l = (
            (q_near, k_near, v_near, gm_near, lse_near)
            if r < 2
            else (q_far, k_far, v_far, gm_far, lse_far)
        )
        cut = pl.ds(pl.multiple_of((r % 2) * 2 * E + p * E, E), E)
        q = half_q[:, cut]
        g = half_g[:, cut]
        q_t = q.T
        g_t = g.T
        k_t = half_k[:, cut].T
        lse = half_l[(r % 2) * 2 + p]
        row_dot = jnp.zeros((1, slot_len), f32)
        for kb in range(6):
            first = BLOCK if kb == 5 else 0
            rows = slice(kb * BLOCK, (kb + 1) * BLOCK)
            s = masked_scores(kb, lens, dot(half_k[rows, cut], q_t[:, first:]))
            pr = jnp.exp2(s * c - lse[:, first:])
            gp = dot(half_v[rows, cut], g_t[:, first:])
            probs[rows, first:] = pr
            grads[rows, first:] = gp
            part = jnp.sum(pr * gp, axis=0, keepdims=True)
            dkv[rows, E:] = dot(pr.astype(bf16), g[first:]).astype(bf16)
            if first:
                row_dot = jnp.concatenate([row_dot[:, :first], row_dot[:, first:] + part], axis=1)
            else:
                row_dot = row_dot + part
        dq = jnp.zeros((E, slot_len), f32)
        for kb in range(6):
            first = BLOCK if kb == 5 else 0
            rows = slice(kb * BLOCK, (kb + 1) * BLOCK)
            ds = (probs[rows, first:] * (grads[rows, first:] - row_dot[:, first:])).astype(bf16)
            dkv[rows, :E] = (dot(ds, q[first:]) * score_scale).astype(bf16)
            out = dot(k_t[:, rows], ds)
            if first:
                dq = jnp.concatenate([dq[:, :first], dq[:, first:] + out], axis=1)
            else:
                dq = dq + out
        return (dq * score_scale).T.astype(bf16)

    per_block = own_terms.shape[1 + bits]

    def weight_terms(dq, target):
        blocks = 2 ** (bits - 1)
        many = blocks * per_block

        def one(at, carry):
            rows = pl.ds(pl.multiple_of(at * many, many), many)
            of_kv = dot(key_t[rows, :], dkv[...]).astype(bf16)
            of_q = dot(key_t[rows, keys - slot_len :], dq).astype(bf16)
            for n in range(blocks):
                index = (at,) + tuple((n >> (bits - 2 - b)) & 1 for b in range(bits - 1))
                cut = slice(n * per_block, (n + 1) * per_block)
                target[index + (whole, slice(0, 2 * E))] = of_kv[cut]
                target[index + (whole, slice(2 * E, 3 * E))] = of_q[cut]
            return carry

        lax.fori_loop(0, 2, one, 0)

    def normed_terms(r, p, dq):
        cut = pl.ds(pl.multiple_of(p * E, E), E)
        dk = dkv[keys - slot_len :, :E]
        dv = dkv[keys - slot_len :, E:]
        columns = 256
        for n in range(grad_normed.shape[1] // columns):
            rows = slice(n * columns, (n + 1) * columns)
            grad_normed[:, rows] += (
                dot_nt(dq, wq[r][rows, cut])
                + dot_nt(dk, wk[r][rows, cut])
                + dot_nt(dv, wv[r][rows, cut])
            )

    def far_parity(p, carry):
        dq = attend(3, p)

        @pl.when(p == 0)
        def _():
            load_keys.wait()

        @pl.when(p == 1)
        def _():
            core_copy(3, 0).wait_send()

        weight_terms(dq, terms.at[1])
        core_copy(3, p).start()

        @pl.when(p == 0)
        def _():
            for n in range(loaded):
                if n not in (4, 5, 6, 7):
                    fetches[n].wait()
            for copy in go_core:
                copy.wait_recv()
            go_core_far[...] = plus(go_core_far[...], go_far[:rows_o])

        normed_terms(3, p, dq)


        dq = attend(2, p)

        weight_terms(dq, far_terms.at[p])
        core_copy(3, p).wait_recv()
        add_whole(far_terms.at[p], got_far.at[p])
        x_copy(p).start()
        normed_terms(2, p, dq)

        @pl.when(p == 0)
        def _():
            out_z.wait_recv()
            rs_add(out_part, out_got_rs[bits - 2], bits - 2)
            if bits > 2:
                out_step(bits - 3).start()

        @pl.when(p == 1)
        def _():
            in_y.wait_recv()
            load_in.wait()
            held = in_got_rs[bits - 1]
            for at in range(ring):
                index = z_index(at)
                held[index] = plus(held[index], in_kept[index])
            in_step(bits - 2).start()
            go_to_x.start()

        return carry

    def near_parity(p, carry):
        dq = attend(1, p)

        @pl.when(p == 1)
        def _():
            core_copy(1, 0).wait_send()

        weight_terms(dq, terms.at[0])
        core_copy(1, p).start()
        normed_terms(1, p, dq)

        @pl.when(p == 0)
        def _():
            for n in reversed(range(bits - 2)):
                out_step(n).wait_recv()
                rs_add(out_got_rs[n + 1], out_got_rs[n], n)
                if n:
                    out_step(n - 1).start()
            grad_out[...] = out_got_rs[0][...]

        dq = attend(0, p)
        weight_terms(dq, own_terms.at[p])
        core_copy(1, p).wait_recv()
        add_whole(own_terms.at[p], got_near.at[p])

        @pl.when(p == 0)
        def _():
            in_step(bits - 2).wait_recv()
            rs_add(in_got_rs[bits - 1], in_got_rs[bits - 2], bits - 2)
            for n in reversed(range(bits - 2)):
                in_step(n).start()
                if n:
                    in_step(n).wait_recv()
                    rs_add(in_got_rs[n + 1], in_got_rs[n], n)
            x_copy(0).wait_recv()
            add_whole(own_terms.at[0], got_x.at[0])
            first_y().start()

        normed_terms(0, p, dq)

        return carry

    for n in (4, 5, 6, 7):
        fetches[n].wait()
    lax.fori_loop(0, 2, far_parity, 0)
    lax.fori_loop(0, 2, near_parity, 0)

    wide = probs.shape[1]

    def half_loads(name, source, target):
        copies = []
        for n in range(2):
            copy = local(
                f"load_{name}{n}",
                source.at[:, pl.ds(n * wide, wide)],
                target.at[pl.ds(n * slot_len, slot_len)],
            )
            copy.start()
            copies.append(copy)
        return copies

    loads = half_loads("inputs", inputs_hbm, probs) + half_loads("hidden", hidden_hbm, grads)
    for copy in loads:
        copy.wait()
    gain_row = gain_ref[...]

    def input_rows(at, carry):
        rows = pl.ds(pl.multiple_of(at * 128, 128), 128)
        lower = pl.ds(pl.multiple_of(slot_len + at * 128, 128), 128)
        values = jnp.concatenate([probs[rows], probs[lower]], axis=1)
        before = jnp.concatenate([grads[rows], grads[lower]], axis=1)
        grad_normed[rows] = before + norm_input_grad(values, gain_row, grad_normed[rows])
        return carry

    lax.fori_loop(0, slot_len // 128, input_rows, 0)
    store_grad = local("store_grad", grad_normed, input_grad_hbm)
    store_grad.start()

    first_y().wait_recv()
    for at in range(ring):
        index = z_index(at)
        y_got[index] = plus(y_got[index], own_terms[(0,) + index + (y_flag,)])
    for k in range(1, ring):
        first_z(k).start()
    x_copy(1).wait_recv()
    add_whole(own_terms.at[1], got_x.at[1])
    last_y(0).start()
    last_y(1).start()
    in_step(0).wait_recv()
    rs_add(in_got_rs[1], in_got_rs[0], 0)
    in_copies = []
    for r in range(1, heads):
        copy = remote(
            f"in_{r}", in_got_rs[0].at[jnp.bitwise_xor(head, r)], in_got.at[head], head_device(r)
        )
        copy.start()
        in_copies.append(copy)
    in_got[head] = in_got_rs[0][head]
    for k in range(1, ring):
        first_z(k).wait_recv()
    sum_rows[(0,) + tuple(flags)] = plus(
        y_got[z_flags], *(z_got[k] for k in range(1, ring))
    )
    for k in range(1, ring):
        first_back_z(k).start()

    def gain_part(p):
        rows = pl.ds(pl.multiple_of(dp * per_block, per_block), per_block)
        total = jnp.zeros((per_block, 1), f32)
        grad = sum_rows[(p,) + tuple(flags)]
        for n, weight in enumerate((wk[0], wv[0], wq[0])):
            own = weight[rows, p * E : (p + 1) * E].astype(f32)
            total = total + jnp.sum(
                grad[:, n * E : (n + 1) * E].astype(f32) * own, axis=1, keepdims=True
            )
        return total

    def last_middle(h):
        last_y(h).wait_recv()
        for at in range(ring):
            index = z_index(at)
            last_got[(h,) + index] = plus(
                last_got[(h,) + index], own_terms[(1,) + index + (y_flag, parts[h])]
            )
        for k in range(1, ring):
            last_z(h, k).start()

    def last_top(h):
        for k in range(1, ring):
            last_z(h, k).wait_recv()
        sum_rows[(1,) + tuple(flags) + (parts[h],)] = plus(
            last_got[(h,) + z_flags], *(last_z_got[k, h] for k in range(1, ring))
        )
        for k in range(1, ring):
            last_back_z(h, k).start()

    gain = gain_part(0)
    last_middle(0)
    last_middle(1)
    go_to_x.wait_recv()
    for at in range(2**bits):
        rows = slice(at * rows_o // 2**bits, (at + 1) * rows_o // 2**bits)
        index = tuple((at >> (bits - 1 - b)) & 1 for b in range(bits))
        go_sum[index] = plus(go_near[rows], go_core_near[rows], go_x[rows])
    go_y().start()
    for k in range(1, ring):
        first_back_z(k).wait_recv()
    first_back_y().start()
    last_top(0)
    go_y().wait_recv()
    for at in range(ring):
        index = z_index(at)
        go_y_got[index] = plus(go_y_got[index], go_sum[index + (y_flag,)])
    for k in range(1, ring):
        go_z(k).start()
    last_top(1)
    gain = gain + gain_part(1)
    gain_terms[head] = jnp.broadcast_to(gain, gain_terms.shape[1:])
    gain_copies = []
    for r in range(1, heads):
        copy = remote(f"gain_{r}", gain_terms.at[head], gain_terms.at[head], head_device(r))
        copy.start()
        gain_copies.append(copy)
    for k in range(1, ring):
        last_back_z(0, k).wait_recv()
    last_back_y(0).start()
    for k in range(1, ring):
        go_z(k).wait_recv()
    go_out[tuple(flags)] = plus(go_y_got[z_flags], *(go_z_got[k] for k in range(1, ring)))
    for k in range(1, ring):
        go_back_z(k).start()
    for k in range(1, ring):
        last_back_z(1, k).wait_recv()
    last_back_y(1).start()
    for k in range(1, ring):
        go_back_z(k).wait_recv()
    go_back_y().start()

    store_grad.wait()
    out_x.wait_recv()
    for copy in gain_copies:
        copy.wait_recv()
    gain_out[...] = sum(gain_terms[h] for h in range(heads))
    for copy in closing + in_copies:
        copy.wait()
    go_back_y().wait_recv()
    first_back_y().wait_recv()
    for h in range(2):
        last_back_y(h).wait_recv()

    for copy in go_core + gain_copies:
        copy.wait_send()
    for copy in (in_y, out_z, go_to_x, out_x, core_copy(1, 1), core_copy(3, 1), x_copy(0), x_copy(1)):
        copy.wait_send()
    for copy in (first_y(), first_back_y(), go_y(), go_back_y()):
        copy.wait_send()
    for h in range(2):
        last_y(h).wait_send()
        last_back_y(h).wait_send()
    for k in range(1, ring):
        for copy in (first_z, first_back_z, go_z, go_back_z):
            copy(k).wait_send()
        for h in range(2):
            last_z(h, k).wait_send()
            last_back_z(h, k).wait_send()
    for n in range(bits - 1):
        in_step(n).wait_send()
    for n in range(bits - 2):
        out_step(n).wait_send()


def backward(mem_lens, cmem_lens, near, far, grad_mixed, wq, wk, wv, gain, go_near, go_far, out_part, new_cols, conv, key_t, grad_in, inputs, grad_hidden, out_far):
    heads, dps = lax.axis_size("head"), lax.axis_size("dp")
    masks = [1 << b for b in reversed(range(dps.bit_length() - 1))]
    bits = len(masks)
    slot_len, width = inputs.shape
    keys = key_t.shape[1]
    shape = jax.ShapeDtypeStruct
    twos = lambda n: (2,) * n
    in_block = grad_in.shape[bits:]
    out_block = out_part.shape[bits - 1 :]
    rows_o = go_near.shape[0] // 2
    go_block = (rows_o // dps, width)
    sum_block = (width // dps, 3 * E)
    half_block = (width // dps // 2, 3 * E)
    copies = 160 + 16 * bits + 2 * (8 + 3 * heads) + 12 * dps
    q_n, k_n, v_n, l_n = near
    q_f, k_f, v_f, l_f = far
    loaded = (q_n, k_n, v_n, grad_mixed, q_f, k_f, v_f, grad_mixed, *wq, *wk, *wv)
    held = (q_n, k_n, v_n, q_n, q_f, k_f, v_f, q_f, *wq, *wk, *wv)
    scratch = (
        [pltpu.VMEM(value.shape, value.dtype) for value in held]
        + [
            pltpu.VMEM((width, keys), bf16),
            pltpu.VMEM((keys, slot_len), f32),
            pltpu.VMEM((keys, slot_len), f32),
            pltpu.VMEM((keys, 2 * E), bf16),
            pltpu.VMEM((2,) + twos(bits) + sum_block, bf16),
            pltpu.VMEM((2,) + twos(bits) + sum_block, bf16),
            pltpu.VMEM((2,) + twos(bits) + sum_block, bf16),
            pltpu.VMEM((2,) + twos(bits) + sum_block, bf16),
            pltpu.VMEM((2,) + twos(bits) + sum_block, bf16),
            pltpu.VMEM((2,) + twos(bits) + sum_block, bf16),
            pltpu.VMEM(twos(bits - 1) + in_block, bf16),
        ]
        + [pltpu.VMEM(twos(n) + in_block, bf16) for n in range(bits)]
        + [pltpu.VMEM(twos(n) + out_block, bf16) for n in range(bits - 1)]
        + [pltpu.VMEM((rows_o, width), bf16)] * 3
        + [
            pltpu.VMEM(twos(bits) + go_block, bf16),
            pltpu.VMEM(twos(bits - 1) + go_block, bf16),
            pltpu.VMEM((dps // 2,) + go_block, bf16),
        ]
        + [
            pltpu.VMEM(twos(bits - 1) + sum_block, bf16),
            pltpu.VMEM((dps // 2,) + sum_block, bf16),
            pltpu.VMEM((2,) + twos(bits - 1) + half_block, bf16),
            pltpu.VMEM((dps // 2, 2) + half_block, bf16),
        ]
        + [
            pltpu.VMEM((slot_len, width), f32),
            pltpu.VMEM((heads, width // dps, E), f32),
            pltpu.SemaphoreType.DMA((2, copies)),
        ]
    )
    return pl.pallas_call(
        functools.partial(backward_kernel, heads, masks, slot_len, keys),
        in_specs=[pl.BlockSpec(memory_space=pltpu.SMEM)] * 2
        + [vmem()] * 2
        + [anywhere()] * len(loaded)
        + [vmem()] * 6
        + [anywhere()] * 5,
        out_specs=[vmem()] * 2 + [anywhere()] + [vmem()] * 5 + [anywhere()],
        out_shape=[
            shape(out_block, bf16),
            shape((2,) + twos(bits) + sum_block, bf16),
            shape((slot_len, width), f32),
            shape(twos(bits) + go_block, bf16),
            shape((width // dps, E), f32),
            shape(in_block, bf16),
            shape(new_cols.shape, bf16),
            shape(conv.shape, bf16),
            shape(out_far.shape, bf16),
        ],
        scratch_shapes=scratch,
        compiler_params=pltpu.CompilerParams(
            collective_id=1, has_side_effects=True, vmem_limit_bytes=61 * 2**20
        ),
        cost_estimate=pl.CostEstimate(flops=60 * 10**9, bytes_accessed=0, transcendentals=0),
        name="backward",
    )(mem_lens, cmem_lens, l_n, l_f, *loaded, gain, go_near, go_far, out_part, new_cols, conv, key_t, grad_in, inputs, grad_hidden, out_far)


def finish_kernel(
    counts_ref, hidden_ref, own_ref, core_ref, x0_ref, x1_ref, grad_ref, sums_ref, go_ref, out_ref,
    in_ref, new_ref, conv_ref, w_in_ref, outputs, input_grad, grad_q, grad_k, grad_v, grad_o,
    grad_out, grad_in, new, conv, gain
):
    step = pl.program_id(0)
    rows = hidden_ref.shape[0]
    live = lax.broadcasted_iota(jnp.int32, hidden_ref.shape, 0) + step * rows
    live = live < counts_ref[lax.axis_index("head")]

    def whole(x_ref):
        added = own_ref[...] + core_ref[...].astype(f32) + x_ref[...].astype(f32)
        outputs[...] = hidden_ref[...] + jnp.where(live, added, 0.0)

    @pl.when(step < 2)
    def _():
        whole(x0_ref)

    @pl.when(step >= 2)
    def _():
        whole(x1_ref)

    input_grad[...] = grad_ref[...]
    for p in range(2):
        for n, target in enumerate((grad_k, grad_v, grad_q)):
            target[:, p * E : (p + 1) * E] = sums_ref[p, :, n * E : (n + 1) * E].astype(f32)
    grad_o[...] = go_ref[...].astype(f32)

    @pl.when(step == 0)
    def _():
        grad_out[...] = out_ref[...].astype(f32)
        heads, columns = new_ref.shape[0], new_ref.shape[2]
        for h in range(heads):
            cut = slice(h * columns, (h + 1) * columns)
            new[:, 0, cut] = new_ref[h][: new.shape[0]].astype(f32)
            conv[:, cut] = conv_ref[h].astype(f32)
        total = jnp.zeros((in_ref.shape[1], 1), f32)
        for h in range(heads):
            for n in range(in_ref.shape[2] // E):
                value = in_ref[h, :, n * E : (n + 1) * E].astype(f32)
                cut = slice((n * heads + h) * E, (n * heads + h + 1) * E)
                grad_in[:, cut] = value
                total = total + jnp.sum(
                    value * w_in_ref[:, cut].astype(f32), axis=1, keepdims=True
                )
        gain[...] = jnp.broadcast_to(total, gain.shape)


def finish(counts, hidden, own, core, x0, x1, grad, sums, go, out, grad_in, new, conv, w_in, new_rows):
    slot_len, width = hidden.shape
    steps = 4
    heads = new.shape[0]
    shape = jax.ShapeDtypeStruct
    row = lambda g: (g, 0)
    by_rows = lambda value: pl.BlockSpec((value.shape[0] // steps, value.shape[1]), row)

    def same(value):
        return pl.BlockSpec(value.shape, lambda g: (0,) * len(value.shape))

    half = 2 * E
    outs = [
        shape(hidden.shape, f32),
        shape(hidden.shape, f32),
        *[shape((width, half), f32)] * 3,
        shape(go.shape, f32),
    ]
    fixed = [
        shape(out.shape, f32),
        shape(w_in.shape, f32),
        shape((new_rows, 1, width), f32),
        shape((conv.shape[1], width), f32),
        shape((w_in.shape[0], E), f32),
    ]
    piece = (slot_len // steps, width)
    return pl.pallas_call(
        finish_kernel,
        grid=(steps,),
        in_specs=[pl.BlockSpec(memory_space=pltpu.SMEM)]
        + [by_rows(v) for v in (hidden, own, core)]
        + [
            pl.BlockSpec(piece, lambda g: (jnp.minimum(g, 1), 0)),
            pl.BlockSpec(piece, lambda g: (jnp.maximum(g - 2, 0), 0)),
            by_rows(grad),
            pl.BlockSpec((2, width // steps, sums.shape[2]), lambda g: (0, g, 0)),
            by_rows(go),
        ]
        + [same(v) for v in (out, grad_in, new, conv, w_in)],
        out_specs=[by_rows(v) for v in outs] + [same(v) for v in fixed],
        out_shape=outs + fixed,
        compiler_params=pltpu.CompilerParams(vmem_limit_bytes=61 * 2**20),
        name="finish",
    )(counts, hidden, own, core, x0, x1, grad, sums, go, out, grad_in, new, conv, w_in)


def swap_head(value, mask):
    size = lax.axis_size("head")
    return lax.ppermute(value, "head", [(i, i ^ mask) for i in range(size)])


def cut_bits(value, masks):
    return value.reshape((2,) * len(masks) + value.shape[1:])


def cut_in_kernel(in_ref, out_ref):
    heads, units = out_ref.shape[0], E
    head = lax.axis_index("head")
    for r in range(heads):
        other = jnp.bitwise_xor(head, r)
        for i in range(out_ref.shape[2] // units):
            source = pl.multiple_of((i * heads + other) * units, units)
            out_ref[r, :, i * units : (i + 1) * units] = in_ref[:, pl.ds(source, units)]


def cut_in(w_in, heads, dps):
    rows, units = w_in.shape[0], w_in.shape[1] // (heads * dps)
    if units == E:
        return pl.pallas_call(
            cut_in_kernel,
            in_specs=[vmem()],
            out_specs=vmem(),
            out_shape=jax.ShapeDtypeStruct((heads, rows, dps * units), bf16),
            name="cut_in",
        )(w_in)
    head = lax.axis_index("head")
    cut = w_in.reshape(rows, dps, heads, units)
    return jnp.stack(
        [
            lax.dynamic_index_in_dim(cut, head ^ r, 2, keepdims=False).reshape(rows, dps * units)
            for r in range(heads)
        ]
    )


def unpack(values, counts):
    parts, at = [], 0
    for count in counts:
        parts.append(values[at : at + count])
        at += count
    return parts


def shards(
    inputs,
    memory,
    compressed,
    counts,
    mem_lens,
    cmem_lens,
    norm_gain,
    w_query,
    w_key,
    w_value,
    w_output,
    ffn_gain,
    w_in,
    w_out,
    w_conv,
    out_grad,
    comp_grad,
):
    slot_len, width = inputs.shape[1:]
    heads, dps = lax.axis_size("head"), lax.axis_size("dp")
    masks = [1 << b for b in reversed(range(dps.bit_length() - 1))]
    bits = len(masks)
    group = memory.shape[0]
    head_at, dp_at = lax.axis_index("head"), lax.axis_index("dp")
    head_width = w_query.shape[1]
    new_rows = comp_grad.shape[1]
    conv_cols = width // heads
    gains = jnp.pad(jnp.stack([norm_gain, ffn_gain]).astype(f32), ((0, 6), (0, 0)))
    units = w_in.shape[1] // (heads * dps)
    (
        (gain_rows, lse_near, lse_far),
        (conv_rows, grad_ffn, q_near, k_near, v_near, q_far, k_far, v_far, mixed_near, mixed_far),
        (key_t, hidden, normed_two),
        weights,
        (grad_conv, w_in_own, w_out_own, gf_rest),
    ) = unpack(
        forward(
            counts,
            mem_lens,
            cmem_lens,
            w_in if units == E else cut_in(w_in, heads, dps),
            w_conv,
            comp_grad.transpose(1, 0, 2),
            gains,
            (w_query, w_key, w_value, w_output),
            w_out,
            out_grad[0],
            inputs[0],
            memory,
            compressed,
        ),
        (3, 10, 3, 12, 4),
    )
    gain_one, gain_two = gain_rows[0:1], gain_rows[1:2]
    wq, wk, wv, wo = (
        [own] + [w.reshape(own.shape) for w in weights[3 * n : 3 * n + 3]]
        for n, own in enumerate((w_query, w_key, w_value, w_output))
    )
    w_in_own = w_in_own.reshape(width, -1)
    w_out_own = w_out_own.reshape(-1, width)
    gf_core, gf_x, gf_diag = (gf_rest[n] for n in range(3))
    pad_rows = (new_rows + 15) // 16 * 16

    (
        (grad_conv, new_cols, out_part, grad_hidden, grad_mixed, go_near, go_far, grad_w_in),
        (out_own, out_core, out_far, out_first),
    ) = unpack(
        middle(
            counts,
            mem_lens,
            gain_rows,
            conv_rows,
            normed_two,
            grad_ffn,
            gf_rest,
            w_in_own,
            w_out_own,
            cut_bits(grad_conv.reshape(dps, -1, conv_cols), masks),
            memory,
            hidden,
            out_grad[0],
            mixed_near,
            mixed_far,
            wo,
        ),
        (8, 4),
    )
    grad_w_out, sum_rows, input_grad, grad_out, gain_terms, grad_w_in, new_all, grad_conv, out_second = backward(
        mem_lens,
        cmem_lens,
        (q_near, k_near, v_near, lse_near),
        (q_far, k_far, v_far, lse_far),
        grad_mixed,
        wq,
        wk,
        wv,
        gain_one,
        go_near,
        go_far,
        out_part,
        new_cols,
        grad_conv,
        key_t,
        cut_bits(grad_w_in.reshape((dps, heads, w_in.shape[0], -1)), masks),
        inputs[0],
        grad_hidden,
        out_far,
    )
    in_source, in_weight = grad_w_in, w_in
    if units != E:
        in_source = (
            grad_w_in.reshape(heads, w_in.shape[0], dps, units)
            .transpose(1, 2, 0, 3)
            .reshape(w_in.shape[0], -1, heads, E)
            .transpose(2, 0, 1, 3)
            .reshape(grad_w_in.shape)
        )
    (
        outputs, input_grad, grad_query, grad_key, grad_value, grad_out, grad_w_out, grad_w_in,
        new_compressed, grad_conv, gain_sums,
    ) = finish(
        counts,
        hidden,
        out_own,
        out_core,
        out_first,
        out_second,
        input_grad,
        sum_rows.reshape(2, width, 3 * E),
        grad_out.reshape(w_output.shape),
        grad_w_out,
        in_source,
        new_all,
        grad_conv,
        w_in,
        new_rows,
    )
    own_gain_two = lax.dynamic_slice_in_dim(
        gain_two[0], (dp_at * heads + head_at) * w_in.shape[0], w_in.shape[0]
    )
    grad_gain_two = gain_sums[:, 0] / own_gain_two
    grad_gain_one = lax.dynamic_slice_in_dim(
        gain_terms[:, 0], head_at * norm_gain.shape[0], norm_gain.shape[0]
    ) / norm_gain.astype(f32)

    return (
        outputs[None],
        input_grad[None],
        new_compressed.transpose(1, 0, 2),
        grad_gain_one,
        grad_query,
        grad_key,
        grad_value,
        grad_out,
        grad_gain_two,
        grad_w_in,
        grad_w_out,
        grad_conv,
    )


def solution(mesh):
    whole = P(("dp", "head"), None, None)
    rows = P(("dp", "head"), None)
    vector = P(("dp", "head"))
    columns = P(None, "head")
    placed = (
        whole,
        P("dp", None, None),
        P("dp", None, None),
        P("dp"),
        P("dp"),
        P("dp"),
        vector,
        columns,
        columns,
        columns,
        P("head", None),
        vector,
        rows,
        rows,
        rows,
        whole,
        whole,
    )
    return jax.shard_map(
        shards,
        mesh=mesh,
        in_specs=placed,
        out_specs=(
            whole,
            whole,
            whole,
            vector,
            columns,
            columns,
            columns,
            P("head", None),
            vector,
            rows,
            rows,
            rows,
        ),
        check_vma=False,
    )
```

```python
import functools

import jax
import jax.numpy as jnp
from jax import lax
from jax.experimental import pallas as pl
from jax.experimental.pallas import tpu as pltpu
from jax.sharding import PartitionSpec as P

E = 128
BLOCK = 256
epsilon = 1e-05
masked_value = -1e30
score_scale = E ** (-0.5)
log2e = 1.4426950408889634
bf16 = jnp.bfloat16
f32 = jnp.float32
VMEM_BYTES = 30 * 2**20
MESH = pl.DeviceIdType.MESH


def dot(left, right):
    return jnp.dot(left, right, preferred_element_type=f32)


def dot_tn(left, right):
    return lax.dot_general(left, right, (((0,), (0,)), ((), ())), preferred_element_type=f32)


def dot_nt(left, right):
    return lax.dot_general(left, right, (((1,), (1,)), ((), ())), preferred_element_type=f32)


def layer_norm(values, gain_vec):
    row_mean = jnp.mean(values, axis=-1, keepdims=True)
    centred = values - row_mean
    variance = jnp.mean(centred * centred, axis=-1, keepdims=True)
    return centred * lax.rsqrt(variance + epsilon) * gain_vec


def vmem():
    return pl.BlockSpec(memory_space=pltpu.VMEM)


def anywhere():
    return pl.BlockSpec(memory_space=pl.ANY)


def masked_scores(kb, lens, scores):
    rows = lax.broadcasted_iota(jnp.int32, scores.shape, 0)
    if kb < 4:
        limit = lens[kb // 2] - (kb % 2) * BLOCK
        return jnp.where(rows < limit, scores, masked_value)
    columns = lax.broadcasted_iota(jnp.int32, scores.shape, 1)
    return jnp.where(rows <= columns, scores, masked_value)


STORED = 26


def forward_kernel(heads, dps, masks, group, slot_len, *refs):
    (counts_ref, mem_ref, cmem_ref), refs = refs[:3], refs[3:]
    (in_ref, w_conv_ref, cot_ref, gains_ref, wq0, wk0, wv0, wo0), refs = refs[:8], refs[8:]
    (w_out_hbm, out_grad_hbm, inputs_hbm, memory_hbm, cmem_hbm), refs = refs[:5], refs[5:]
    (gain_row_out, lse_near, lse_far), refs = refs[:3], refs[3:]
    places, refs = refs[:STORED], refs[STORED:]
    (w_in_all, w_out_all, gf_rest), refs = refs[:3], refs[3:]
    kept, refs = refs[:STORED], refs[STORED:]
    (conv_out, gf_out, q_near, k_near, v_near, q_far, k_far, v_far, mixed_near, mixed_far), more = kept[:10], kept[10:]
    (key_t, hidden_out, normed_out), more = more[:3], more[3:]
    (wq1, wq2, wq3, wk1, wk2, wk3, wv1, wv2, wv3, wo1, wo2, wo3, conv_grad) = more
    gains_out, cot_out, key_rows, scores, inputs, out_grad, memory, cmem, spread, conv_send, cot_send, in_pieces, sems = refs
    bits = len(masks)
    width = inputs.shape[1]
    half = wk0.shape[1]
    head = lax.axis_index("head")
    dp = lax.axis_index("dp")
    count = counts_ref[head]
    lens = (cmem_ref[head], mem_ref[head])
    flags = tuple(jnp.where(jnp.bitwise_and(dp, mask) != 0, 1, 0) for mask in masks)
    whole = slice(None)

    def head_device(r):
        return (dp, jnp.bitwise_xor(head, r))

    def dp_device(r):
        return (lax.rem(dp + r, dps), head)

    barrier = pltpu.get_barrier_semaphore()
    for r in range(1, heads):
        pl.semaphore_signal(barrier, inc=1, device_id=head_device(r), device_id_type=MESH)
    for r in range(1, dps):
        pl.semaphore_signal(barrier, inc=1, device_id=dp_device(r), device_id_type=MESH)

    slots = {}

    def slot(name):
        if name not in slots:
            slots[name] = len(slots)
        return slots[name]

    def remote(name, source, target, device):
        at = slot(name)
        return pltpu.make_async_remote_copy(
            src_ref=source,
            dst_ref=target,
            send_sem=sems.at[0, at],
            recv_sem=sems.at[1, at],
            device_id=device,
            device_id_type=MESH,
        )

    def local(name, source, target):
        return pltpu.make_async_copy(source, target, sems.at[0, slot(name)])

    for r in range(heads):
        if len(in_ref.shape) == 3:
            in_pieces[r] = in_ref[r]
        else:
            other = jnp.bitwise_xor(head, r)
            for n in range(dps):
                cut = pl.ds(pl.multiple_of((n * heads + other) * E, E), E)
                in_pieces[r, :, n * E : (n + 1) * E] = in_ref[:, cut]

    loads = {}
    for name, source, target in [
        ("out_grad", out_grad_hbm, out_grad),
        ("cmem", cmem_hbm.at[head], cmem),
        ("memory", memory_hbm, memory),
        ("inputs", inputs_hbm, inputs),
        ("w_out", w_out_hbm, w_out_all.at[flags]),
        ("in_own", in_pieces.at[0], w_in_all.at[flags + (head,)]),
    ]:
        loads[name] = local(f"load_{name}", source, target)
        loads[name].start()
    sent, stored = [], []

    def store(*buffers):
        for buffer in buffers:
            at = [buffer is other for other in kept].index(True)
            copy = local(f"store_{at}", buffer, places[at])
            copy.start()
            stored.append(copy)

    def send(*args):
        copy = remote(*args)
        copy.start()
        sent.append(copy)
        return copy

    at = dp * heads + head
    short = gains_ref.shape[1]
    lane = lax.broadcasted_iota(jnp.int32, (short, E), 1)
    place = lax.broadcasted_iota(jnp.int32, (short, E), 0) + lax.rem(at * short, E)
    spot = jnp.where(lane == place, 1.0, 0.0).astype(bf16)
    gains_out[at] = dot(gains_ref[...].astype(bf16), spot)
    columns = conv_out.shape[2]
    pad_rows = cot_out.shape[1]
    new_rows = cot_ref.shape[0]
    pl.semaphore_wait(barrier, heads + dps - 2)

    gain_heads = [
        send(f"gain_{r}", gains_out.at[at], gains_out.at[at], head_device(r))
        for r in range(1, heads)
    ]
    in_rows = [
        send(f"in_{r}", in_pieces.at[r], w_in_all.at[flags + (head,)], head_device(r))
        for r in range(1, heads)
    ]
    core = [
        send(f"core_{n}", source, target, head_device(1))
        for n, (source, target) in enumerate(((wk0, wk1), (wv0, wv1), (wq0, wq1), (wo0, wo1)))
    ]
    x_k = send("x_k", wk0, wk2, head_device(2))
    rows_o = wo2.shape[bits]
    own_o = wo0.at[pl.ds(pl.multiple_of(dp * rows_o, rows_o), rows_o)]
    x_o = send("x_o", own_o, wo2.at[flags], head_device(2))

    dp_partners = [(jnp.bitwise_xor(dp, mask), head) for mask in masks]

    def gather(name, block, order, source=None):
        copies, index = [], list(flags)
        for n, bit in enumerate(order):
            part = block.at[tuple(index)]
            first = source if source is not None and n == 0 else part
            copies.append(remote(f"gather_{name}_{n}", first, part, dp_partners[bit]))
            index[bit] = whole
        return copies

    straight = list(range(bits))
    crossed = straight[:-2] + [bits - 1, bits - 2]
    gathers = {
        "out": gather("out", w_out_all, straight, w_out_hbm),
        "in": gather("in", w_in_all, crossed),
        "o": gather("o", wo2, straight),
    }
    gathers["out"][0].start()

    def advance(name, n):
        gathers[name][n].wait_recv()
        if n + 1 < bits:
            gathers[name][n + 1].start()

    small = []
    for r in range(heads):
        other = jnp.bitwise_xor(head, r)
        cut = pl.ds(pl.multiple_of(other * columns, columns), columns)
        conv_piece = w_conv_ref[:, cut]
        cot_piece = jnp.concatenate(
            [cot_ref[:, 0, cut], jnp.zeros((pad_rows - new_rows, columns), f32)], axis=0
        ).astype(bf16)
        if r == 0:
            conv_out[head] = conv_piece
            cot_out[head] = cot_piece
        else:
            conv_send[r - 1] = conv_piece
            cot_send[r - 1] = cot_piece
            small.append(send(f"conv_{r}", conv_send.at[r - 1], conv_out.at[head], head_device(r)))
            small.append(send(f"cot_{r}", cot_send.at[r - 1], cot_out.at[head], head_device(r)))
    for copy in gain_heads:
        copy.wait_recv()
    block = gains_out.at[pl.ds(dp * heads, heads)]
    gain_dps = [send(f"gain_dp_{r}", block, block, dp_device(r)) for r in range(1, dps)]
    for copy in in_rows:
        copy.wait_recv()
    loads["in_own"].wait()
    gathers["in"][0].start()
    x_v = send("x_v", wv0, wv2, head_device(2))
    x_q = send("x_q", wq0, wq2, head_device(2))

    loads["out_grad"].wait()

    def cotangent(n, carry):
        rows = pl.ds(pl.multiple_of(n * 128, 128), 128)
        row = lax.broadcasted_iota(jnp.int32, (128, width), 0) + n * 128
        gf_out[rows] = jnp.where(row < count, out_grad[rows], 0.0).astype(bf16)
        return carry

    lax.fori_loop(0, slot_len // 128, cotangent, 0)
    store(gf_out)
    gf_core = send("gf_core", gf_out, gf_rest.at[0], head_device(1))
    gf_x = send("gf_x", gf_out, gf_rest.at[1], head_device(2))
    for copy in gain_dps:
        copy.wait_recv()
    many = E // short
    tiles = [
        sum(gains_out[t * many + n] for n in range(many)) for t in range(dps * heads // many)
    ]
    gain_one = jnp.concatenate([tile[0:1] for tile in tiles], axis=1)
    gain_two = jnp.concatenate([tile[1:2] for tile in tiles], axis=1)
    gain_row_out[0:1] = gain_one
    gain_row_out[1:2] = gain_two
    for copy in core:
        copy.wait_recv()
    store(wk1, wv1, wq1, wo1)

    def project(normed, rows, weights, k_ref, v_ref):
        for n, (wk, wv) in enumerate(weights):
            cut = slice(n * half, (n + 1) * half)
            k_ref[rows, cut] = dot(normed, wk).astype(bf16)
            v_ref[rows, cut] = dot(normed, wv).astype(bf16)

    def near_rows(source, part):
        def one(n, carry):
            rows = pl.ds(pl.multiple_of(n * BLOCK, BLOCK), BLOCK)
            target = pl.ds(pl.multiple_of(part * slot_len + n * BLOCK, BLOCK), BLOCK)
            normed = layer_norm(source[rows].astype(f32), gain_one).astype(bf16)
            key_rows[target] = normed
            key_t[:, target] = normed.T
            project(normed, target, ((wk0[...], wv0[...]), (wk1[...], wv1[...])), k_near, v_near)
            if part == 2:
                q_near[rows, :half] = dot(normed, wq0[...]).astype(bf16)
                q_near[rows, half:] = dot(normed, wq1[...]).astype(bf16)
            return carry

        lax.fori_loop(0, slot_len // BLOCK, one, 0)

    loads["cmem"].wait()
    near_rows(cmem, 0)
    loads["w_out"].wait()
    advance("out", 0)
    loads["memory"].wait()
    near_rows(memory.at[head], 1)
    x_o.wait_recv()
    gathers["o"][0].start()
    loads["inputs"].wait()
    near_rows(inputs, 2)
    store(q_near, k_near, v_near, key_t)
    advance("in", 0)

    c = score_scale * log2e

    def attend(q_ref, k_ref, v_ref, mixed_ref, lse_ref, events):
        def one(h, carry):
            cut = pl.ds(pl.multiple_of(h * E, E), E)
            q_t = q_ref[:, cut].T
            v_t = v_ref[:, cut].T
            top = jnp.full((1, slot_len), masked_value, f32)
            for kb in range(6):
                first = BLOCK if kb == 5 else 0
                rows = slice(kb * BLOCK, (kb + 1) * BLOCK)
                s = masked_scores(kb, lens, dot(k_ref[rows, cut], q_t[:, first:]))
                scores[rows, first:] = s
                part = jnp.max(s, axis=0, keepdims=True)
                if first:
                    top = jnp.concatenate([top[:, :first], jnp.maximum(top[:, first:], part)], axis=1)
                else:
                    top = jnp.maximum(top, part)
            shift = top * c
            mixed = jnp.zeros((E, slot_len), f32)
            total = jnp.zeros((1, slot_len), f32)
            for kb in range(6):
                first = BLOCK if kb == 5 else 0
                rows = slice(kb * BLOCK, (kb + 1) * BLOCK)
                p = jnp.exp2(scores[rows, first:] * c - shift[:, first:])
                part = jnp.sum(p, axis=0, keepdims=True)
                out = dot(v_t[:, rows], p.astype(bf16))
                if first:
                    total = jnp.concatenate([total[:, :first], total[:, first:] + part], axis=1)
                    mixed = jnp.concatenate([mixed[:, :first], mixed[:, first:] + out], axis=1)
                else:
                    total = total + part
                    mixed = mixed + out
            mixed_ref[:, cut] = (mixed / total).T.astype(bf16)
            lse_ref[h] = shift + jnp.log2(total)
            for when, event in events:
                pl.when(h == when)(event)
            return carry

        lax.fori_loop(0, q_ref.shape[1] // E, one, 0)

    attend(
        q_near,
        k_near,
        v_near,
        mixed_near,
        lse_near,
        [
            (1, lambda: advance("out", 1)),
            (2, lambda: advance("o", 0)),
        ],
    )

    for copy in small:
        copy.wait_recv()
    store(mixed_near, conv_out)
    taps = 3

    def spread_rows(g, carry):
        source_row = lax.broadcasted_iota(jnp.int32, (slot_len, pad_rows), 0)
        picked_row = lax.broadcasted_iota(jnp.int32, (slot_len, pad_rows), 1)
        kept = source_row < lax.min(counts_ref[g], mem_ref[g])
        for tap in range(taps):
            pick = jnp.where(kept & (source_row == taps * picked_row + tap), 1.0, 0.0).astype(bf16)
            spread[g, :, tap * columns : (tap + 1) * columns] = dot(pick, cot_out[g]).astype(bf16)
        return carry

    lax.fori_loop(0, group, spread_rows, 0)
    x_k.wait_recv()
    fwd_k = send("fwd_k", wk2, wk3, head_device(1))

    def conv_rows(n, carry):
        rows = pl.ds(pl.multiple_of(n * BLOCK, BLOCK), BLOCK)
        total = sum(dot(memory[g, :, rows].T, spread[g]) for g in range(group)).astype(bf16)
        for tap in range(taps):
            conv_grad[tap, rows] = total[:, tap * columns : (tap + 1) * columns]
        return carry

    lax.fori_loop(0, width // BLOCK, conv_rows, 0)
    advance("in", 1)
    x_v.wait_recv()
    fwd_v = send("fwd_v", wv2, wv3, head_device(1))
    store(conv_grad)
    advance("o", 1)
    x_q.wait_recv()
    fwd_q = send("fwd_q", wq2, wq3, head_device(1))
    for copy in (fwd_k, fwd_v):
        copy.wait_recv()
    store(wk2, wk3, wv2, wv3)

    def far_rows(n, carry):
        rows = pl.ds(pl.multiple_of(n * BLOCK, BLOCK), BLOCK)
        project(key_rows[rows], rows, ((wk2[...], wv2[...]), (wk3[...], wv3[...])), k_far, v_far)
        return carry

    lax.fori_loop(0, key_rows.shape[0] // BLOCK, far_rows, 0)
    fwd_q.wait_recv()
    store(wq2, wq3)
    for n in range(slot_len // BLOCK):
        rows = slice(n * BLOCK, (n + 1) * BLOCK)
        normed = key_rows[2 * slot_len + n * BLOCK : 2 * slot_len + (n + 1) * BLOCK]
        q_far[rows, :half] = dot(normed, wq2[...]).astype(bf16)
        q_far[rows, half:] = dot(normed, wq3[...]).astype(bf16)
    store(q_far, k_far, v_far)
    for n in range(2, bits):
        advance("o", n)
    fwd_o = send("fwd_o", wo2, wo3, head_device(1))
    attend(q_far, k_far, v_far, mixed_far, lse_far, [])
    store(mixed_far)
    fwd_o.wait_recv()
    store(wo2, wo3)

    def mix(n, carry):
        rows = pl.ds(pl.multiple_of(n * 128, 128), 128)
        near, far = mixed_near[rows], mixed_far[rows]
        attention = (
            dot(near[:, :half], wo0[...])
            + dot(near[:, half:], wo1[...])
            + dot(far[:, :half], wo2[...].reshape(half, width))
            + dot(far[:, half:], wo3[...].reshape(half, width))
        )
        row = lax.broadcasted_iota(jnp.int32, (128, width), 0) + n * 128
        hidden = inputs[rows] + jnp.where(row < count, attention, 0.0)
        hidden_out[rows] = hidden
        normed_out[rows] = layer_norm(hidden, gain_two).astype(bf16)
        return carry

    lax.fori_loop(0, slot_len // 128, mix, 0)
    store(hidden_out, normed_out)
    gf_x.wait_recv()
    gf_diag = send("gf_diag", gf_rest.at[1], gf_rest.at[2], head_device(1))
    gf_core.wait_recv()
    gf_diag.wait_recv()
    for n in range(2, bits):
        advance("in", n)
        advance("out", n)
    for copy in stored:
        copy.wait()
    for copy in sent:
        copy.wait_send()
    for copies in gathers.values():
        for copy in copies:
            copy.wait_send()


def forward(counts, mem_lens, cmem_lens, w_in, w_conv, comp_grad, gains, weights, w_out, out_grad, inputs, memory, compressed):
    heads, dps = lax.axis_size("head"), lax.axis_size("dp")
    masks = [1 << b for b in reversed(range(dps.bit_length() - 1))]
    twos = (2,) * len(masks)
    slot_len, width = inputs.shape
    group, keys = memory.shape[0], 3 * slot_len
    wq, wk, wv, wo = weights
    in_pieces = (heads, w_in.shape[-2], w_out.shape[0] * dps)
    half = wk.shape[1]
    columns = width // heads
    new_rows = comp_grad.shape[0]
    pad_rows = (new_rows + 15) // 16 * 16
    shape = jax.ShapeDtypeStruct
    wide = 2 * half
    conv_all = (heads, w_conv.shape[0], columns)
    cot_all = (heads, pad_rows, columns)
    o_cut = twos + (half // dps, width)
    outs = [
        shape((2, width), f32),
        shape((wide // E, 1, slot_len), f32),
        shape((wide // E, 1, slot_len), f32),
    ]
    kept = [
        shape(conv_all, bf16),
        shape((slot_len, width), bf16),
        shape((slot_len, wide), bf16),
        shape((keys, wide), bf16),
        shape((keys, wide), bf16),
        shape((slot_len, wide), bf16),
        shape((keys, wide), bf16),
        shape((keys, wide), bf16),
        shape((slot_len, wide), bf16),
        shape((slot_len, wide), bf16),
        shape((width, keys), bf16),
        shape((slot_len, width), f32),
        shape((slot_len, width), bf16),
        *[shape(wq.shape, bf16)] * 3,
        *[shape(wk.shape, bf16)] * 3,
        *[shape(wv.shape, bf16)] * 3,
        shape(wo.shape, bf16),
        shape(o_cut, bf16),
        shape(o_cut, bf16),
        shape((3, width, columns), bf16),
    ]
    far_outs = [
        shape(twos + in_pieces, bf16),
        shape(twos + w_out.shape, bf16),
        shape((heads - 1, slot_len, width), bf16),
    ]
    smem = pl.BlockSpec(memory_space=pltpu.SMEM)
    return pl.pallas_call(
        functools.partial(forward_kernel, heads, dps, masks, group, slot_len),
        in_specs=[smem] * 3 + [vmem()] * 8 + [anywhere()] * 5,
        out_specs=[vmem()] * len(outs) + [anywhere()] * (len(kept) + len(far_outs)),
        out_shape=outs + kept + far_outs,
        scratch_shapes=[pltpu.VMEM(k.shape, k.dtype) for k in kept]
        + [
            pltpu.VMEM((dps * heads, 8, E), f32),
            pltpu.VMEM(cot_all, bf16),
            pltpu.VMEM((keys, width), bf16),
            pltpu.VMEM((keys, slot_len), f32),
            pltpu.VMEM((slot_len, width), f32),
            pltpu.VMEM((slot_len, width), f32),
            pltpu.VMEM(memory.shape, bf16),
            pltpu.VMEM((slot_len, width), bf16),
            pltpu.VMEM((group, slot_len, 3 * columns), bf16),
            pltpu.VMEM((heads - 1,) + conv_all[1:], bf16),
            pltpu.VMEM((heads - 1,) + cot_all[1:], bf16),
            pltpu.VMEM(in_pieces, bf16),
            pltpu.SemaphoreType.DMA((2, 30 + STORED + 6 * heads + dps + 4 * len(masks))),
        ],
        compiler_params=pltpu.CompilerParams(
            collective_id=0, has_side_effects=True, vmem_limit_bytes=61 * 2**20
        ),
        cost_estimate=pl.CostEstimate(flops=40 * 10**9, bytes_accessed=0, transcendentals=0),
        name="forward",
    )(counts, mem_lens, cmem_lens, w_in, w_conv, comp_grad, gains, *weights, w_out, out_grad, inputs, memory, compressed)


def norm_input_grad(values, gain, grad):
    mean = jnp.mean(values, axis=-1, keepdims=True)
    centred = values - mean
    scale = lax.rsqrt(jnp.mean(centred * centred, axis=-1, keepdims=True) + epsilon)
    unit = centred * scale
    grad = grad * gain
    shift = jnp.mean(grad, axis=-1, keepdims=True)
    slope = jnp.mean(grad * unit, axis=-1, keepdims=True)
    return scale * (grad - shift - unit * slope)


def gelu_parts(u):
    c = 0.7978845608028654
    cube = 0.044715 * u * u
    t = jnp.tanh(c * (u + cube * u))
    half = 0.5 * (1.0 + t)
    return u * half, half + 0.5 * u * (1.0 - t * t) * (c * (1.0 + 3.0 * cube))


def middle_kernel(heads, masks, group, *refs):
    (counts_ref, mem_ref, gain_ref, conv_ref), refs = refs[:4], refs[4:]
    (n2_hbm, gf_hbm, gf_rest, w_in_hbm, w_out_hbm, conv_grad, memory_hbm), refs = refs[:7], refs[7:]
    (hidden_hbm, out_grad_hbm, mixed_near, mixed_far, wo0, wo1, wo2, wo3), refs = refs[:8], refs[8:]
    (conv_fin, new_cols, out_part), refs = refs[:3], refs[3:]
    (grad_hbm, gm_hbm, go_near, go_far, in_hbm, out_own_hbm, out_core_hbm, out_far_hbm, out_x_hbm), refs = refs[:9], refs[9:]
    (w_in, w_out, n2, gf, act, gi, gn_own, gn_part, gn_core, gn_diag, gn_x), refs = refs[:11], refs[11:]
    (out_own, out_send, out_diag, grad_out, grad_in, out_got, memory, out_grad, conv_all), refs = refs[:9], refs[9:]
    conv_kept, conv_got, sems = refs[0], refs[1:-1], refs[-1]
    bits = len(masks)
    slot_len, width = gn_own.shape
    head = lax.axis_index("head")
    dp = lax.axis_index("dp")
    flags = tuple(jnp.where(jnp.bitwise_and(dp, mask) != 0, 1, 0) for mask in masks)
    whole = slice(None)
    core = (dp, jnp.bitwise_xor(head, 1))
    chip = (dp, jnp.bitwise_xor(head, 2))
    partners = [(jnp.bitwise_xor(dp, mask), head) for mask in masks]

    barrier = pltpu.get_barrier_semaphore()
    for device in [core, chip] + partners:
        pl.semaphore_signal(barrier, inc=1, device_id=device, device_id_type=MESH)

    slots = {}

    def slot(name):
        if name not in slots:
            slots[name] = len(slots)
        return slots[name]

    sent, stored = [], []

    def remote(name, source, target, device):
        at = slot(name)
        copy = pltpu.make_async_remote_copy(
            src_ref=source,
            dst_ref=target,
            send_sem=sems.at[0, at],
            recv_sem=sems.at[1, at],
            device_id=device,
            device_id_type=MESH,
        )
        sent.append(copy)
        return copy

    def send(*args):
        copy = remote(*args)
        copy.start()
        return copy

    def local(name, source, target):
        copy = pltpu.make_async_copy(source, target, sems.at[0, slot(name)])
        copy.start()
        return copy

    def store(name, source, target):
        stored.append(local(name, source, target))

    load = {
        "n2": local("load_n2", n2_hbm, n2.at[0]),
        "w_in": local("load_w_in", w_in_hbm, w_in),
        "gf": local("load_gf", gf_hbm, gf.at[0]),
        "w_out": local("load_w_out", w_out_hbm, w_out),
        "gf_core": local("load_gf_core", gf_rest.at[0], gf.at[1]),
        "gf_far": local("load_gf_far", gf_rest.at[pl.ds(1, 2)], gf.at[pl.ds(2, 2)]),
        "conv": local(
            "load_conv", conv_grad.at[(whole,) * (bits - 1) + (flags[-1],)], conv_kept
        ),
        "out_grad": local("load_out_grad", out_grad_hbm, out_grad),
    }
    conv_all[flags] = conv_ref[...]
    pl.semaphore_wait(barrier, 2 + bits)

    n2_core = send("n2_core", n2_hbm, n2.at[1], core)
    halves = [pl.ds(h * (slot_len // 2), slot_len // 2) for h in range(2)]
    n2_x = [send(f"n2_x{h}", n2_hbm.at[halves[h]], n2.at[2, halves[h]], chip) for h in range(2)]
    n2_diag = [remote(f"n2_diag{h}", n2.at[2, halves[h]], n2.at[3, halves[h]], core) for h in range(2)]

    order = list(range(bits - 2)) + [bits - 1, bits - 2]
    index, gathers = list(flags), []
    for n, bit in enumerate(order):
        part = conv_all.at[tuple(index)]
        gathers.append(remote(f"conv_{n}", part, part, partners[bit]))
        index[bit] = whole
    sums = [
        remote(
            f"conv_sum{n}",
            (conv_grad if n == bits - 1 else conv_got[n + 1]).at[(whole,) * n + (1 - flags[n],)],
            conv_got[n],
            partners[n],
        )
        for n in range(bits)
    ]
    gathers[0].start()
    sums[bits - 1].start()

    def add_sum(n):
        sums[n].wait_recv()
        for at in range(2**n):
            spot = tuple((at >> (n - 1 - b)) & 1 for b in range(n))
            mine = conv_kept[spot] if n == bits - 1 else conv_got[n + 1][spot + (flags[n],)]
            conv_got[n][spot] = (conv_got[n][spot].astype(f32) + mine.astype(f32)).astype(bf16)
        if n:
            sums[n - 1].start()

    def next_gather(n):
        gathers[n].wait_recv()
        if n + 1 < bits:
            gathers[n + 1].start()

    rows_of = slot_len // 2
    units = w_in.shape[1]
    chunk = 512

    def tokens(s, half):
        rows = pl.ds(pl.multiple_of(half * rows_of, rows_of), rows_of)
        for n in range(units // chunk):
            cut = slice(n * chunk, (n + 1) * chunk)
            inner = dot(n2[s, rows], w_in[:, cut])
            value, slope = gelu_parts(inner)
            act[s, rows, cut] = value.astype(bf16)
            gi[s, rows, cut] = (dot_nt(gf[s, rows], w_out[cut, :]) * slope).astype(bf16)
        return rows, dot_nt(gi[s, rows], w_in[...])

    for name in ("n2", "w_in", "gf", "w_out", "gf_core"):
        load[name].wait()
    n2_core.wait_recv()

    def near(n, carry):
        s = lax.div(n, 2)
        rows, grad = tokens(s, lax.rem(n, 2))

        @pl.when(s == 0)
        def _():
            gn_own[rows] = grad

        @pl.when(s == 1)
        def _():
            gn_part[0, rows] = grad.astype(bf16)

        return carry

    lax.fori_loop(0, 4, near, 0)
    core_sent = send("gn_core", gn_part.at[0], gn_core, core)

    def terms(lhs, rhs, target, first, again):
        many = width // 4

        def one(n, carry):
            cut = pl.ds(pl.multiple_of(n * many, many), many)
            left = jnp.concatenate([lhs[first, :, cut].T, lhs[first + 1, :, cut].T], axis=1)
            total = dot(left, rhs[first : first + 2].reshape(2 * slot_len, rhs.shape[2]))
            block = target.shape[bits]
            per = many // block
            low = per.bit_length() - 1
            for m in range(per):
                spot = tuple(
                    lax.rem(lax.div(n, 2 ** (bits - low - 1 - b)), 2) for b in range(bits - low)
                ) + tuple((m >> (low - 1 - b)) & 1 for b in range(low))
                value = total[m * block : (m + 1) * block]
                if again:
                    value = value + target[spot].astype(f32)
                target[spot] = value.astype(bf16)
            return carry

        lax.fori_loop(0, 4, one, 0)

    def outward(n, carry):
        s = lax.div(n, 2)
        rows = pl.ds(pl.multiple_of(lax.rem(n, 2) * rows_of, rows_of), rows_of)
        value = dot(act[s, rows], w_out[...])

        @pl.when(s == 0)
        def _():
            out_own[rows] = value

        @pl.when(s > 0)
        def _():
            out_send[lax.max(s - 1, 0), rows] = value.astype(bf16)

        return carry

    n2_x[0].wait_recv()
    n2_diag[0].start()
    lax.fori_loop(0, 4, outward, 0)
    store("out_own", out_own, out_own_hbm)
    out_core = send("out_core", out_send.at[0], out_core_hbm, core)
    next_gather(0)
    load["gf_far"].wait()
    n2_diag[0].wait_recv()

    def far(half):
        def one(n, carry):
            rows, grad = tokens(2 + n, half)
            gn_part[1 + n, rows] = grad.astype(bf16)
            return carry

        lax.fori_loop(0, 2, one, 0)
        return send(f"gn_diag{half}", gn_part.at[2, halves[half]], gn_diag.at[halves[half]], core)

    def far_sum(half, copy):
        copy.wait_recv()
        rows = halves[half]
        gn_part[1, rows] = (gn_part[1, rows].astype(f32) + gn_diag[rows].astype(f32)).astype(bf16)
        return send(f"gn_x{half}", gn_part.at[1, rows], gn_x.at[rows], chip)

    diag_sent = far(0)
    terms(act, gf, grad_out, 0, False)
    gn_back = [far_sum(0, diag_sent)]
    load["conv"].wait()
    add_sum(bits - 1)
    terms(n2, gi, grad_in, 0, False)
    n2_x[1].wait_recv()
    n2_diag[1].start()
    next_gather(1)
    n2_diag[1].wait_recv()
    diag_sent = far(1)
    lax.fori_loop(4, 8, outward, 0)
    out_back = send("out_diag", out_send.at[2], out_diag, core)
    gn_back.append(far_sum(1, diag_sent))
    terms(act, gf, grad_out, 2, True)
    out_y = send(
        "out_sum", grad_out.at[(whole,) * (bits - 1) + (1 - flags[-1],)], out_got, partners[-1]
    )
    if bits > 1:
        add_sum(bits - 2)
    out_back.wait_recv()
    for h in range(2):
        rows = halves[h]
        out_diag[rows] = (out_diag[rows].astype(f32) + out_send[1, rows].astype(f32)).astype(bf16)
    out_x = send("out_x", out_diag.at[halves[0]], out_x_hbm, chip)
    store("out_far", out_diag.at[halves[1]], out_far_hbm)
    terms(n2, gi, grad_in, 2, True)
    store("grad_in", grad_in, in_hbm)
    for n in range(2, bits):
        next_gather(n)
    for n in reversed(range(bits - 2)):
        add_sum(n)
    conv_fin[...] = conv_got[0][...].reshape(conv_fin.shape)

    near_wide, far_wide = mixed_near.shape[1], mixed_far.shape[1]
    half_rows = wo0.shape[0]
    late = [
        local("load_mixed_near", mixed_near, act.at[0, :, pl.ds(0, near_wide)]),
        local("load_mixed_far", mixed_far, act.at[0, :, pl.ds(near_wide, far_wide)]),
    ] + [
        local(f"load_wo{r}", w, act.at[1 + r // 2, pl.ds((r % 2) * half_rows, half_rows)])
        for r, w in enumerate((wo0, wo1, wo2, wo3))
    ]
    stored[0].wait()
    hidden_load = local("load_hidden", hidden_hbm, out_own)

    pad_rows, columns = new_cols.shape[1], new_cols.shape[2]
    taps = 3

    def stream(g, carry):
        copy = local("load_memory", memory_hbm.at[g], memory)
        kernel = conv_all[...].reshape(taps * width, columns)
        source_row = lax.broadcasted_iota(jnp.int32, (pad_rows, slot_len), 1)
        picked_row = lax.broadcasted_iota(jnp.int32, (pad_rows, slot_len), 0)
        kept = source_row < lax.min(counts_ref[g], mem_ref[g])
        copy.wait()
        total = jnp.zeros((pad_rows, columns), f32)
        for tap in range(taps):
            pick = jnp.where(kept & (source_row == taps * picked_row + tap), 1.0, 0.0).astype(bf16)
            rows = dot(pick, memory[0:slot_len]).astype(bf16)
            total = total + dot(rows, kernel[tap * width : (tap + 1) * width])
        new_cols[g] = total.astype(bf16)
        return carry

    lax.fori_loop(0, group, stream, 0)
    for copy in [hidden_load, load["out_grad"]] + late:
        copy.wait()
    for copy in gn_back:
        copy.wait_recv()
    core_sent.wait_recv()
    gain = gain_ref[1:2]

    def back(n, carry):
        rows = pl.ds(pl.multiple_of(n * 128, 128), 128)
        grad = gn_own[rows] + gn_core[rows].astype(f32) + gn_x[rows].astype(f32)
        grad = out_grad[rows] + norm_input_grad(out_own[rows], gain, grad)
        gn_own[rows] = grad
        row = lax.broadcasted_iota(jnp.int32, (128, width), 0) + n * 128
        gi[0, rows] = jnp.where(row < counts_ref[head], grad, 0.0).astype(bf16)
        return carry

    lax.fori_loop(0, slot_len // 128, back, 0)
    store("grad_hidden", gn_own, grad_hbm)
    weights = act[1:3].reshape(2 * slot_len, width)
    for h in range(2):
        gi[1, halves[h]] = dot_nt(gi[0, halves[h]], weights).astype(bf16)
    store("gm", gi.at[1], gm_hbm)
    for n, target in enumerate((go_near, go_far)):
        cut = slice(n * near_wide, (n + 1) * near_wide)
        gi[2 + n] = dot(act[0, :, cut].T, gi[0]).astype(bf16)
        store(f"go{n}", gi.at[2 + n], target)
    out_y.wait_recv()
    for at in range(2 ** (bits - 1)):
        spot = tuple((at >> (bits - 2 - b)) & 1 for b in range(bits - 1))
        out_part[spot] = (
            out_got[spot].astype(f32) + grad_out[spot + (flags[-1],)].astype(f32)
        ).astype(bf16)
    out_core.wait_recv()
    out_x.wait_recv()
    for copy in stored[1:]:
        copy.wait()
    for copy in sent:
        copy.wait_send()


def middle(counts, mem_lens, gains, conv_rows, normed, grad_ffn, gf_rest, w_in, w_out, conv_grad, memory, hidden, out_grad, mixed_near, mixed_far, wo):
    heads, dps = lax.axis_size("head"), lax.axis_size("dp")
    masks = [1 << b for b in reversed(range(dps.bit_length() - 1))]
    bits = len(masks)
    twos = lambda n: (2,) * n
    slot_len, width = hidden.shape
    units = w_in.shape[1]
    columns = conv_rows.shape[2]
    new_rows = (slot_len + 2) // 3
    pad_rows = (new_rows + 15) // 16 * 16
    shape = jax.ShapeDtypeStruct
    stream = (slot_len, width)
    conv_block = conv_grad.shape[bits:]
    in_block = (width // dps, units)
    out_block = (units // dps, width)
    smem = pl.BlockSpec(memory_space=pltpu.SMEM)
    buffers = [
        (w_in.shape, bf16),
        (w_out.shape, bf16),
        ((4,) + stream, bf16),
        ((4,) + stream, bf16),
        ((4, slot_len, units), bf16),
        ((4, slot_len, units), bf16),
        (stream, f32),
        ((3,) + stream, bf16),
        (stream, bf16),
        (stream, bf16),
        (stream, bf16),
        (stream, f32),
        ((3,) + stream, bf16),
        (stream, bf16),
        (twos(bits) + out_block, bf16),
        (twos(bits) + in_block, bf16),
        (twos(bits - 1) + out_block, bf16),
        (memory.shape[1:], bf16),
        (stream, f32),
        (twos(bits) + conv_rows.shape, bf16),
        (twos(bits - 1) + conv_block, bf16),
    ] + [(twos(n) + conv_block, bf16) for n in range(bits)]
    return pl.pallas_call(
        functools.partial(middle_kernel, heads, masks, memory.shape[0]),
        in_specs=[smem] * 2 + [vmem()] * 2 + [anywhere()] * 15,
        out_specs=[vmem()] * 3 + [anywhere()] * 9,
        out_shape=[
            shape(conv_rows.shape, bf16),
            shape((memory.shape[0], pad_rows, columns), bf16),
            shape(twos(bits - 1) + out_block, bf16),
            shape(stream, f32),
            shape((slot_len, 4 * wo[0].shape[0]), bf16),
            shape((mixed_near.shape[1], width), bf16),
            shape((mixed_far.shape[1], width), bf16),
            shape(twos(bits) + in_block, bf16),
            shape(stream, f32),
            shape(stream, bf16),
            shape((slot_len // 2, width), bf16),
            shape((slot_len // 2, width), bf16),
        ],
        scratch_shapes=[pltpu.VMEM(*b) for b in buffers]
        + [pltpu.SemaphoreType.DMA((2, 52 + 3 * bits))],
        compiler_params=pltpu.CompilerParams(
            collective_id=2, has_side_effects=True, vmem_limit_bytes=61 * 2**20
        ),
        cost_estimate=pl.CostEstimate(flops=30 * 10**9, bytes_accessed=0, transcendentals=0),
        name="middle",
    )(counts, mem_lens, gains, conv_rows, normed, grad_ffn, gf_rest, w_in, w_out, conv_grad, memory, hidden, out_grad, mixed_near, mixed_far, *wo)


def backward_kernel(heads, masks, slot_len, keys, *refs):
    (mem_ref, cmem_ref, lse_near, lse_far), refs = refs[:4], refs[4:]
    loaded = 8 + 3 * heads
    sources, refs = refs[:loaded], refs[loaded:]
    (gain_ref, go_near, go_far, out_part, new_ref, conv_ref, key_t_hbm, in_hbm, inputs_hbm, hidden_hbm), refs = refs[:10], refs[10:]
    (out_far_hbm,), refs = refs[:1], refs[1:]
    (grad_out, sum_rows, input_grad_hbm, go_out, gain_out, in_got, new_got, conv_got, out_x_hbm), refs = refs[:9], refs[9:]
    held, refs = refs[:loaded], refs[loaded:]
    (q_near, k_near, v_near, gm_near, q_far, k_far, v_far, gm_far), more = held[:8], held[8:]
    wq, wk, wv = more[:heads], more[heads : 2 * heads], more[2 * heads :]
    (key_t, probs, grads, dkv, terms, far_terms, own_terms, got_near, got_far, got_x), refs = refs[:10], refs[10:]
    bits = len(masks)
    in_kept, refs = refs[0], refs[1:]
    in_got_rs, refs = refs[:bits], refs[bits:]
    out_got_rs, refs = refs[: bits - 1], refs[bits - 1 :]
    go_core_near, go_core_far, go_x, refs = refs[0], refs[1], refs[2], refs[3:]
    (go_sum, go_y_got, go_z_got), refs = refs[:3], refs[3:]
    y_got, z_got, last_got, last_z_got, grad_normed, gain_terms, sems = refs
    head = lax.axis_index("head")
    dp = lax.axis_index("dp")
    lens = (cmem_ref[head], mem_ref[head])
    flags = [jnp.where(jnp.bitwise_and(dp, mask) != 0, 1, 0) for mask in masks]

    def head_device(r):
        return (dp, jnp.bitwise_xor(head, r))

    def dp_device(n):
        return (jnp.bitwise_xor(dp, masks[n]), head)

    barrier = pltpu.get_barrier_semaphore()
    for r in range(1, heads):
        pl.semaphore_signal(barrier, inc=1, device_id=head_device(r), device_id_type=MESH)
    ring = 2 ** (bits - 1)

    def z_device(k):
        return (jnp.bitwise_xor(dp, 2 * k), head)

    pl.semaphore_signal(barrier, inc=1, device_id=dp_device(bits - 1), device_id_type=MESH)
    for k in range(1, ring):
        pl.semaphore_signal(barrier, inc=1, device_id=z_device(k), device_id_type=MESH)
    pl.semaphore_wait(barrier, heads - 1 + ring)

    slots = {}

    def remote(name, source, target, device, part=0):
        if name not in slots:
            slots[name] = 2 * len(slots)
        at = slots[name] + part
        return pltpu.make_async_remote_copy(
            src_ref=source,
            dst_ref=target,
            send_sem=sems.at[0, at],
            recv_sem=sems.at[1, at],
            device_id=device,
            device_id_type=MESH,
        )

    def local(name, source, target):
        if name not in slots:
            slots[name] = 2 * len(slots)
        return pltpu.make_async_copy(source, target, sems.at[0, slots[name]])

    whole = slice(None)

    def rs_copy(name, held, got, n, part=0):
        return remote(
            f"{name}{n}", held.at[(whole,) * n + (1 - flags[n],)], got, dp_device(n), part
        )

    def rs_add(held, got, n):
        for at in range(2**n):
            index = tuple((at >> (n - 1 - b)) & 1 for b in range(n))
            mine = held[index + (flags[n],)]
            got[index] = (got[index].astype(f32) + mine.astype(f32)).astype(bf16)

    fetches = []
    for n, (source, target) in enumerate(zip(sources, held)):
        if n in (3, 7):
            wide = target.shape[1]
            source = source.at[:, pl.ds((n // 4) * wide, wide)]
        fetches.append(local(f"fetch_{n}", source, target))
    for n in (4, 5, 6, 7):
        fetches[n].start()
    load_keys = local("load_keys", key_t_hbm, key_t)
    load_keys.start()
    for n in range(loaded):
        if n not in (4, 5, 6, 7):
            fetches[n].start()
    in_y = remote("in_rs", in_hbm.at[(whole,) * (bits - 1) + (1 - flags[bits - 1],)], in_got_rs[bits - 1], dp_device(bits - 1))
    in_y.start()
    load_in = local("load_in", in_hbm.at[(whole,) * (bits - 1) + (flags[bits - 1],)], in_kept)
    load_in.start()
    out_z = rs_copy("out_rs", out_part, out_got_rs[bits - 2], bits - 2)
    out_z.start()
    rows_o = go_x.shape[0]
    go_core = [
        remote("go_near", go_near.at[pl.ds(rows_o, rows_o)], go_core_near, head_device(1)),
        remote("go_far", go_far.at[pl.ds(rows_o, rows_o)], go_core_far, head_device(1)),
    ]
    for copy in go_core:
        copy.start()
    closing = []
    for name, source, target in (("new", new_ref, new_got), ("conv", conv_ref, conv_got)):
        for r in range(1, heads):
            copy = remote(
                f"{name}_{r}",
                source.at[jnp.bitwise_xor(head, r)],
                target.at[head],
                head_device(r),
            )
            copy.start()
            closing.append(copy)
        target[head] = source[head]
    go_to_x = remote("go_x", go_core_far, go_x, head_device(2))
    out_x = remote("out_x", out_far_hbm, out_x_hbm, head_device(2))

    def in_step(n):
        return rs_copy("in_rs", in_got_rs[n + 1], in_got_rs[n], n)

    def out_step(n):
        return rs_copy("out_rs", out_got_rs[n + 1], out_got_rs[n], n)

    grad_normed[...] = jnp.zeros(grad_normed.shape, f32)
    c = score_scale * log2e

    z_flags, y_flag = tuple(flags[:-1]), flags[-1]
    half_rows = own_terms.shape[1 + bits] // 2
    upper, lower = pl.ds(0, half_rows), pl.ds(half_rows, half_rows)

    parts = (upper, lower)

    def core_copy(r, p):
        return remote(f"core_{r}", terms.at[r // 2], (got_near if r == 1 else got_far).at[p], head_device(1), p)

    def x_copy(p, h=0):
        if p == 0:
            return remote("x_first", far_terms.at[0], got_x.at[0], head_device(2))
        spot = (1,) + (whole,) * bits + (parts[h],)
        return remote(f"x_last{h}", far_terms.at[spot], got_x.at[spot], head_device(2))

    def z_spot(k):
        return tuple(
            jnp.bitwise_xor(flag, (k >> (bits - 2 - b)) & 1) for b, flag in enumerate(z_flags)
        )

    all_z = (whole,) * (bits - 1)

    def plus(*values):
        return sum(value.astype(f32) for value in values).astype(bf16)

    def first_y():
        return remote("first_y", own_terms.at[(0,) + all_z + (1 - y_flag,)], y_got, dp_device(bits - 1))

    def first_z(k):
        return remote(f"first_z{k}", y_got.at[z_spot(k)], z_got.at[k], z_device(k))

    def first_back_z(k):
        spot = sum_rows.at[(0,) + tuple(flags)]
        return remote(f"first_back_z{k}", spot, spot, z_device(k))

    def first_back_y():
        spot = sum_rows.at[(0,) + all_z + (y_flag,)]
        return remote("first_back_y", spot, spot, dp_device(bits - 1))


    def last_y(h):
        source = own_terms.at[(1,) + all_z + (1 - y_flag, parts[h])]
        return remote(f"last_y{h}", source, last_got.at[h], dp_device(bits - 1))

    def last_z(h, k):
        return remote(
            f"last_z{h}_{k}", last_got.at[(h,) + z_spot(k)], last_z_got.at[k, h], z_device(k)
        )

    def last_back_z(h, k):
        spot = sum_rows.at[(1,) + tuple(flags) + (parts[h],)]
        return remote(f"last_back_z{h}_{k}", spot, spot, z_device(k))

    def last_back_y(h):
        spot = sum_rows.at[(1,) + all_z + (y_flag, parts[h])]
        return remote(f"last_back_y{h}", spot, spot, dp_device(bits - 1))

    def go_y():
        return remote("go_y", go_sum.at[all_z + (1 - y_flag,)], go_y_got, dp_device(bits - 1))

    def go_z(k):
        return remote(f"go_z{k}", go_y_got.at[z_spot(k)], go_z_got.at[k], z_device(k))

    def go_back_z(k):
        spot = go_out.at[tuple(flags)]
        return remote(f"go_back_z{k}", spot, spot, z_device(k))

    def go_back_y():
        spot = go_out.at[all_z + (y_flag,)]
        return remote("go_back_y", spot, spot, dp_device(bits - 1))

    def z_index(at):
        return tuple((at >> (bits - 2 - b)) & 1 for b in range(bits - 1))

    def each_block(function):
        def step(at, carry):
            function(tuple(lax.rem(lax.div(at, 2 ** (bits - 1 - b)), 2) for b in range(bits)))
            return carry

        lax.fori_loop(0, 2**bits, step, 0)

    def add_whole(target, source):
        def one(index):
            target[index] = (target[index].astype(f32) + source[index].astype(f32)).astype(bf16)

        each_block(one)

    def attend(r, p):
        half_q, half_k, half_v, half_g, half_l = (
            (q_near, k_near, v_near, gm_near, lse_near)
            if r < 2
            else (q_far, k_far, v_far, gm_far, lse_far)
        )
        cut = pl.ds(pl.multiple_of((r % 2) * 2 * E + p * E, E), E)
        q = half_q[:, cut]
        g = half_g[:, cut]
        q_t = q.T
        g_t = g.T
        k_t = half_k[:, cut].T
        lse = half_l[(r % 2) * 2 + p]
        row_dot = jnp.zeros((1, slot_len), f32)
        for kb in range(6):
            first = BLOCK if kb == 5 else 0
            rows = slice(kb * BLOCK, (kb + 1) * BLOCK)
            s = masked_scores(kb, lens, dot(half_k[rows, cut], q_t[:, first:]))
            pr = jnp.exp2(s * c - lse[:, first:])
            gp = dot(half_v[rows, cut], g_t[:, first:])
            probs[rows, first:] = pr
            grads[rows, first:] = gp
            part = jnp.sum(pr * gp, axis=0, keepdims=True)
            dkv[rows, E:] = dot(pr.astype(bf16), g[first:]).astype(bf16)
            if first:
                row_dot = jnp.concatenate([row_dot[:, :first], row_dot[:, first:] + part], axis=1)
            else:
                row_dot = row_dot + part
        dq = jnp.zeros((E, slot_len), f32)
        for kb in range(6):
            first = BLOCK if kb == 5 else 0
            rows = slice(kb * BLOCK, (kb + 1) * BLOCK)
            ds = (probs[rows, first:] * (grads[rows, first:] - row_dot[:, first:])).astype(bf16)
            dkv[rows, :E] = (dot(ds, q[first:]) * score_scale).astype(bf16)
            out = dot(k_t[:, rows], ds)
            if first:
                dq = jnp.concatenate([dq[:, :first], dq[:, first:] + out], axis=1)
            else:
                dq = dq + out
        return (dq * score_scale).T.astype(bf16)

    per_block = own_terms.shape[1 + bits]

    def weight_terms(dq, target):
        blocks = 2 ** (bits - 1)
        many = blocks * per_block

        def one(at, carry):
            rows = pl.ds(pl.multiple_of(at * many, many), many)
            of_kv = dot(key_t[rows, :], dkv[...]).astype(bf16)
            of_q = dot(key_t[rows, keys - slot_len :], dq).astype(bf16)
            for n in range(blocks):
                index = (at,) + tuple((n >> (bits - 2 - b)) & 1 for b in range(bits - 1))
                cut = slice(n * per_block, (n + 1) * per_block)
                target[index + (whole, slice(0, 2 * E))] = of_kv[cut]
                target[index + (whole, slice(2 * E, 3 * E))] = of_q[cut]
            return carry

        lax.fori_loop(0, 2, one, 0)

    def normed_terms(r, p, dq):
        cut = pl.ds(pl.multiple_of(p * E, E), E)
        dk = dkv[keys - slot_len :, :E]
        dv = dkv[keys - slot_len :, E:]
        columns = 256
        for n in range(grad_normed.shape[1] // columns):
            rows = slice(n * columns, (n + 1) * columns)
            grad_normed[:, rows] += (
                dot_nt(dq, wq[r][rows, cut])
                + dot_nt(dk, wk[r][rows, cut])
                + dot_nt(dv, wv[r][rows, cut])
            )

    def far_parity(p, carry):
        dq = attend(3, p)

        @pl.when(p == 0)
        def _():
            load_keys.wait()

        @pl.when(p == 1)
        def _():
            core_copy(3, 0).wait_send()

        weight_terms(dq, terms.at[1])
        core_copy(3, p).start()

        @pl.when(p == 0)
        def _():
            for n in range(loaded):
                if n not in (4, 5, 6, 7):
                    fetches[n].wait()

        normed_terms(3, p, dq)


        @pl.when(p == 1)
        def _():
            go_to_x.wait_recv()
            for at in range(2**bits):
                rows = slice(at * rows_o // 2**bits, (at + 1) * rows_o // 2**bits)
                index = tuple((at >> (bits - 1 - b)) & 1 for b in range(bits))
                go_sum[index] = plus(go_near[rows], go_core_near[rows], go_x[rows])
            go_y().start()

        dq = attend(2, p)

        weight_terms(dq, far_terms.at[p])
        core_copy(3, p).wait_recv()
        add_whole(far_terms.at[p], got_far.at[p])

        @pl.when(p == 0)
        def _():
            x_copy(0).start()

        @pl.when(p == 1)
        def _():
            x_copy(1, 0).start()
            x_copy(1, 1).start()

        normed_terms(2, p, dq)

        @pl.when(p == 0)
        def _():
            out_z.wait_recv()
            rs_add(out_part, out_got_rs[bits - 2], bits - 2)
            if bits > 2:
                out_step(bits - 3).start()

        @pl.when(p == 1)
        def _():
            in_y.wait_recv()
            load_in.wait()
            held = in_got_rs[bits - 1]
            for at in range(ring):
                index = z_index(at)
                held[index] = plus(held[index], in_kept[index])
            in_step(bits - 2).start()

        return carry

    def near_parity(p, carry):
        dq = attend(1, p)

        @pl.when(p == 1)
        def _():
            core_copy(1, 0).wait_send()

        weight_terms(dq, terms.at[0])
        core_copy(1, p).start()
        normed_terms(1, p, dq)

        @pl.when(p == 0)
        def _():
            for n in reversed(range(bits - 2)):
                out_step(n).wait_recv()
                rs_add(out_got_rs[n + 1], out_got_rs[n], n)
                if n:
                    out_step(n - 1).start()
            grad_out[...] = out_got_rs[0][...]

        @pl.when(p == 1)
        def _():
            pass

        dq = attend(0, p)

        @pl.when(p == 1)
        def _():
            for k in range(1, ring):
                go_z(k).wait_recv()
            go_out[tuple(flags)] = plus(go_y_got[z_flags], *(go_z_got[k] for k in range(1, ring)))
            for k in range(1, ring):
                go_back_z(k).start()

        weight_terms(dq, own_terms.at[p])
        core_copy(1, p).wait_recv()
        add_whole(own_terms.at[p], got_near.at[p])

        @pl.when(p == 0)
        def _():
            in_step(bits - 2).wait_recv()
            rs_add(in_got_rs[bits - 1], in_got_rs[bits - 2], bits - 2)
            for n in reversed(range(bits - 2)):
                in_step(n).start()
                if n:
                    in_step(n).wait_recv()
                    rs_add(in_got_rs[n + 1], in_got_rs[n], n)
            go_y().wait_recv()
            for at in range(ring):
                index = z_index(at)
                go_y_got[index] = plus(go_y_got[index], go_sum[index + (y_flag,)])
            for k in range(1, ring):
                go_z(k).start()
            x_copy(0).wait_recv()
            add_whole(own_terms.at[0], got_x.at[0])
            first_y().start()

        normed_terms(0, p, dq)

        return carry

    for copy in go_core:
        copy.wait_recv()
    go_core_far[...] = plus(go_core_far[...], go_far[:rows_o])
    go_to_x.start()
    for n in (4, 5, 6, 7):
        fetches[n].wait()
    lax.fori_loop(0, 2, far_parity, 0)
    lax.fori_loop(0, 2, near_parity, 0)

    wide = probs.shape[1]

    def half_loads(name, source, target):
        copies = []
        for n in range(2):
            copy = local(
                f"load_{name}{n}",
                source.at[:, pl.ds(n * wide, wide)],
                target.at[pl.ds(n * slot_len, slot_len)],
            )
            copy.start()
            copies.append(copy)
        return copies

    loads = half_loads("inputs", inputs_hbm, probs) + half_loads("hidden", hidden_hbm, grads)
    for copy in loads:
        copy.wait()
    gain_row = gain_ref[...]

    def input_rows(at, carry):
        rows = pl.ds(pl.multiple_of(at * 128, 128), 128)
        lower = pl.ds(pl.multiple_of(slot_len + at * 128, 128), 128)
        values = jnp.concatenate([probs[rows], probs[lower]], axis=1)
        before = jnp.concatenate([grads[rows], grads[lower]], axis=1)
        grad_normed[rows] = before + norm_input_grad(values, gain_row, grad_normed[rows])
        return carry

    lax.fori_loop(0, slot_len // 128, input_rows, 0)
    store_grad = local("store_grad", grad_normed, input_grad_hbm)
    store_grad.start()

    first_y().wait_recv()
    for at in range(ring):
        index = z_index(at)
        y_got[index] = plus(y_got[index], own_terms[(0,) + index + (y_flag,)])
    for k in range(1, ring):
        first_z(k).start()
    def last_bottom(h):
        x_copy(1, h).wait_recv()

        def add(index):
            spot = (1,) + index + (parts[h],)
            own_terms[spot] = plus(own_terms[spot], got_x[spot])

        each_block(add)
        last_y(h).start()

    last_bottom(0)
    for k in range(1, ring):
        go_back_z(k).wait_recv()
    go_back_y().start()
    last_bottom(1)
    out_x.start()
    in_step(0).wait_recv()
    rs_add(in_got_rs[1], in_got_rs[0], 0)
    in_copies = []
    for r in range(1, heads):
        copy = remote(
            f"in_{r}", in_got_rs[0].at[jnp.bitwise_xor(head, r)], in_got.at[head], head_device(r)
        )
        copy.start()
        in_copies.append(copy)
    in_got[head] = in_got_rs[0][head]
    def gain_part(p):
        rows = pl.ds(pl.multiple_of(dp * per_block, per_block), per_block)
        total = jnp.zeros((per_block, 1), f32)
        grad = sum_rows[(p,) + tuple(flags)]
        for n, weight in enumerate((wk[0], wv[0], wq[0])):
            own = weight[rows, p * E : (p + 1) * E].astype(f32)
            total = total + jnp.sum(
                grad[:, n * E : (n + 1) * E].astype(f32) * own, axis=1, keepdims=True
            )
        return total

    def last_middle(h):
        last_y(h).wait_recv()
        for at in range(ring):
            index = z_index(at)
            last_got[(h,) + index] = plus(
                last_got[(h,) + index], own_terms[(1,) + index + (y_flag, parts[h])]
            )
        for k in range(1, ring):
            last_z(h, k).start()

    def last_top(h):
        for k in range(1, ring):
            last_z(h, k).wait_recv()
        sum_rows[(1,) + tuple(flags) + (parts[h],)] = plus(
            last_got[(h,) + z_flags], *(last_z_got[k, h] for k in range(1, ring))
        )
        for k in range(1, ring):
            last_back_z(h, k).start()

    last_middle(0)
    for k in range(1, ring):
        first_z(k).wait_recv()
    sum_rows[(0,) + tuple(flags)] = plus(
        y_got[z_flags], *(z_got[k] for k in range(1, ring))
    )
    for k in range(1, ring):
        first_back_z(k).start()
    last_middle(1)
    gain = gain_part(0)
    for k in range(1, ring):
        first_back_z(k).wait_recv()
    first_back_y().start()
    last_top(0)
    last_top(1)
    gain = gain + gain_part(1)
    gain_terms[head] = jnp.broadcast_to(gain, gain_terms.shape[1:])
    gain_copies = []
    for r in range(1, heads):
        copy = remote(f"gain_{r}", gain_terms.at[head], gain_terms.at[head], head_device(r))
        copy.start()
        gain_copies.append(copy)
    for k in range(1, ring):
        last_back_z(0, k).wait_recv()
    last_back_y(0).start()
    for k in range(1, ring):
        last_back_z(1, k).wait_recv()
    last_back_y(1).start()

    store_grad.wait()
    out_x.wait_recv()
    for copy in gain_copies:
        copy.wait_recv()
    gain_out[...] = sum(gain_terms[h] for h in range(heads))
    for copy in closing + in_copies:
        copy.wait()
    go_back_y().wait_recv()
    first_back_y().wait_recv()
    for h in range(2):
        last_back_y(h).wait_recv()

    for copy in go_core + gain_copies:
        copy.wait_send()
    for copy in (in_y, out_z, go_to_x, out_x, core_copy(1, 1), core_copy(3, 1), x_copy(0), x_copy(1, 0), x_copy(1, 1)):
        copy.wait_send()
    for copy in (first_y(), first_back_y(), go_y(), go_back_y()):
        copy.wait_send()
    for h in range(2):
        last_y(h).wait_send()
        last_back_y(h).wait_send()
    for k in range(1, ring):
        for copy in (first_z, first_back_z, go_z, go_back_z):
            copy(k).wait_send()
        for h in range(2):
            last_z(h, k).wait_send()
            last_back_z(h, k).wait_send()
    for n in range(bits - 1):
        in_step(n).wait_send()
    for n in range(bits - 2):
        out_step(n).wait_send()


def backward(mem_lens, cmem_lens, near, far, grad_mixed, wq, wk, wv, gain, go_near, go_far, out_part, new_cols, conv, key_t, grad_in, inputs, grad_hidden, out_far):
    heads, dps = lax.axis_size("head"), lax.axis_size("dp")
    masks = [1 << b for b in reversed(range(dps.bit_length() - 1))]
    bits = len(masks)
    slot_len, width = inputs.shape
    keys = key_t.shape[1]
    shape = jax.ShapeDtypeStruct
    twos = lambda n: (2,) * n
    in_block = grad_in.shape[bits:]
    out_block = out_part.shape[bits - 1 :]
    rows_o = go_near.shape[0] // 2
    go_block = (rows_o // dps, width)
    sum_block = (width // dps, 3 * E)
    half_block = (width // dps // 2, 3 * E)
    copies = 160 + 16 * bits + 2 * (8 + 3 * heads) + 12 * dps
    q_n, k_n, v_n, l_n = near
    q_f, k_f, v_f, l_f = far
    loaded = (q_n, k_n, v_n, grad_mixed, q_f, k_f, v_f, grad_mixed, *wq, *wk, *wv)
    held = (q_n, k_n, v_n, q_n, q_f, k_f, v_f, q_f, *wq, *wk, *wv)
    scratch = (
        [pltpu.VMEM(value.shape, value.dtype) for value in held]
        + [
            pltpu.VMEM((width, keys), bf16),
            pltpu.VMEM((keys, slot_len), f32),
            pltpu.VMEM((keys, slot_len), f32),
            pltpu.VMEM((keys, 2 * E), bf16),
            pltpu.VMEM((2,) + twos(bits) + sum_block, bf16),
            pltpu.VMEM((2,) + twos(bits) + sum_block, bf16),
            pltpu.VMEM((2,) + twos(bits) + sum_block, bf16),
            pltpu.VMEM((2,) + twos(bits) + sum_block, bf16),
            pltpu.VMEM((2,) + twos(bits) + sum_block, bf16),
            pltpu.VMEM((2,) + twos(bits) + sum_block, bf16),
            pltpu.VMEM(twos(bits - 1) + in_block, bf16),
        ]
        + [pltpu.VMEM(twos(n) + in_block, bf16) for n in range(bits)]
        + [pltpu.VMEM(twos(n) + out_block, bf16) for n in range(bits - 1)]
        + [pltpu.VMEM((rows_o, width), bf16)] * 3
        + [
            pltpu.VMEM(twos(bits) + go_block, bf16),
            pltpu.VMEM(twos(bits - 1) + go_block, bf16),
            pltpu.VMEM((dps // 2,) + go_block, bf16),
        ]
        + [
            pltpu.VMEM(twos(bits - 1) + sum_block, bf16),
            pltpu.VMEM((dps // 2,) + sum_block, bf16),
            pltpu.VMEM((2,) + twos(bits - 1) + half_block, bf16),
            pltpu.VMEM((dps // 2, 2) + half_block, bf16),
        ]
        + [
            pltpu.VMEM((slot_len, width), f32),
            pltpu.VMEM((heads, width // dps, E), f32),
            pltpu.SemaphoreType.DMA((2, copies)),
        ]
    )
    return pl.pallas_call(
        functools.partial(backward_kernel, heads, masks, slot_len, keys),
        in_specs=[pl.BlockSpec(memory_space=pltpu.SMEM)] * 2
        + [vmem()] * 2
        + [anywhere()] * len(loaded)
        + [vmem()] * 6
        + [anywhere()] * 5,
        out_specs=[vmem()] * 2 + [anywhere()] + [vmem()] * 5 + [anywhere()],
        out_shape=[
            shape(out_block, bf16),
            shape((2,) + twos(bits) + sum_block, bf16),
            shape((slot_len, width), f32),
            shape(twos(bits) + go_block, bf16),
            shape((width // dps, E), f32),
            shape(in_block, bf16),
            shape(new_cols.shape, bf16),
            shape(conv.shape, bf16),
            shape(out_far.shape, bf16),
        ],
        scratch_shapes=scratch,
        compiler_params=pltpu.CompilerParams(
            collective_id=1, has_side_effects=True, vmem_limit_bytes=61 * 2**20
        ),
        cost_estimate=pl.CostEstimate(flops=60 * 10**9, bytes_accessed=0, transcendentals=0),
        name="backward",
    )(mem_lens, cmem_lens, l_n, l_f, *loaded, gain, go_near, go_far, out_part, new_cols, conv, key_t, grad_in, inputs, grad_hidden, out_far)


def finish_kernel(
    counts_ref, hidden_ref, own_ref, core_ref, x0_ref, x1_ref, grad_ref, sums_ref, go_ref, out_ref,
    in_ref, new_ref, conv_ref, w_in_ref, outputs, input_grad, grad_q, grad_k, grad_v, grad_o,
    grad_out, grad_in, new, conv, gain
):
    step = pl.program_id(0)
    rows = hidden_ref.shape[0]
    live = lax.broadcasted_iota(jnp.int32, hidden_ref.shape, 0) + step * rows
    live = live < counts_ref[lax.axis_index("head")]

    def whole(x_ref):
        added = own_ref[...] + core_ref[...].astype(f32) + x_ref[...].astype(f32)
        outputs[...] = hidden_ref[...] + jnp.where(live, added, 0.0)

    @pl.when(step < 2)
    def _():
        whole(x0_ref)

    @pl.when(step >= 2)
    def _():
        whole(x1_ref)

    input_grad[...] = grad_ref[...]
    for p in range(2):
        for n, target in enumerate((grad_k, grad_v, grad_q)):
            target[:, p * E : (p + 1) * E] = sums_ref[p, :, n * E : (n + 1) * E].astype(f32)
    grad_o[...] = go_ref[...].astype(f32)

    @pl.when(step == 0)
    def _():
        grad_out[...] = out_ref[...].astype(f32)
        heads, columns = new_ref.shape[0], new_ref.shape[2]
        for h in range(heads):
            cut = slice(h * columns, (h + 1) * columns)
            new[:, 0, cut] = new_ref[h][: new.shape[0]].astype(f32)
            conv[:, cut] = conv_ref[h].astype(f32)
        total = jnp.zeros((in_ref.shape[1], 1), f32)
        for h in range(heads):
            for n in range(in_ref.shape[2] // E):
                value = in_ref[h, :, n * E : (n + 1) * E].astype(f32)
                cut = slice((n * heads + h) * E, (n * heads + h + 1) * E)
                grad_in[:, cut] = value
                total = total + jnp.sum(
                    value * w_in_ref[:, cut].astype(f32), axis=1, keepdims=True
                )
        gain[...] = jnp.broadcast_to(total, gain.shape)


def finish(counts, hidden, own, core, x0, x1, grad, sums, go, out, grad_in, new, conv, w_in, new_rows):
    slot_len, width = hidden.shape
    steps = 4
    heads = new.shape[0]
    shape = jax.ShapeDtypeStruct
    row = lambda g: (g, 0)
    by_rows = lambda value: pl.BlockSpec((value.shape[0] // steps, value.shape[1]), row)

    def same(value):
        return pl.BlockSpec(value.shape, lambda g: (0,) * len(value.shape))

    half = 2 * E
    outs = [
        shape(hidden.shape, f32),
        shape(hidden.shape, f32),
        *[shape((width, half), f32)] * 3,
        shape(go.shape, f32),
    ]
    fixed = [
        shape(out.shape, f32),
        shape(w_in.shape, f32),
        shape((new_rows, 1, width), f32),
        shape((conv.shape[1], width), f32),
        shape((w_in.shape[0], E), f32),
    ]
    piece = (slot_len // steps, width)
    return pl.pallas_call(
        finish_kernel,
        grid=(steps,),
        in_specs=[pl.BlockSpec(memory_space=pltpu.SMEM)]
        + [by_rows(v) for v in (hidden, own, core)]
        + [
            pl.BlockSpec(piece, lambda g: (jnp.minimum(g, 1), 0)),
            pl.BlockSpec(piece, lambda g: (jnp.maximum(g - 2, 0), 0)),
            by_rows(grad),
            pl.BlockSpec((2, width // steps, sums.shape[2]), lambda g: (0, g, 0)),
            by_rows(go),
        ]
        + [same(v) for v in (out, grad_in, new, conv, w_in)],
        out_specs=[by_rows(v) for v in outs] + [same(v) for v in fixed],
        out_shape=outs + fixed,
        compiler_params=pltpu.CompilerParams(vmem_limit_bytes=61 * 2**20),
        name="finish",
    )(counts, hidden, own, core, x0, x1, grad, sums, go, out, grad_in, new, conv, w_in)


def swap_head(value, mask):
    size = lax.axis_size("head")
    return lax.ppermute(value, "head", [(i, i ^ mask) for i in range(size)])


def cut_bits(value, masks):
    return value.reshape((2,) * len(masks) + value.shape[1:])


def cut_in_kernel(in_ref, out_ref):
    heads, units = out_ref.shape[0], E
    head = lax.axis_index("head")
    for r in range(heads):
        other = jnp.bitwise_xor(head, r)
        for i in range(out_ref.shape[2] // units):
            source = pl.multiple_of((i * heads + other) * units, units)
            out_ref[r, :, i * units : (i + 1) * units] = in_ref[:, pl.ds(source, units)]


def cut_in(w_in, heads, dps):
    rows, units = w_in.shape[0], w_in.shape[1] // (heads * dps)
    if units == E:
        return pl.pallas_call(
            cut_in_kernel,
            in_specs=[vmem()],
            out_specs=vmem(),
            out_shape=jax.ShapeDtypeStruct((heads, rows, dps * units), bf16),
            name="cut_in",
        )(w_in)
    head = lax.axis_index("head")
    cut = w_in.reshape(rows, dps, heads, units)
    return jnp.stack(
        [
            lax.dynamic_index_in_dim(cut, head ^ r, 2, keepdims=False).reshape(rows, dps * units)
            for r in range(heads)
        ]
    )


def unpack(values, counts):
    parts, at = [], 0
    for count in counts:
        parts.append(values[at : at + count])
        at += count
    return parts


def shards(
    inputs,
    memory,
    compressed,
    counts,
    mem_lens,
    cmem_lens,
    norm_gain,
    w_query,
    w_key,
    w_value,
    w_output,
    ffn_gain,
    w_in,
    w_out,
    w_conv,
    out_grad,
    comp_grad,
):
    slot_len, width = inputs.shape[1:]
    heads, dps = lax.axis_size("head"), lax.axis_size("dp")
    masks = [1 << b for b in reversed(range(dps.bit_length() - 1))]
    bits = len(masks)
    group = memory.shape[0]
    head_at, dp_at = lax.axis_index("head"), lax.axis_index("dp")
    head_width = w_query.shape[1]
    new_rows = comp_grad.shape[1]
    conv_cols = width // heads
    gains = jnp.pad(jnp.stack([norm_gain, ffn_gain]).astype(f32), ((0, 6), (0, 0)))
    units = w_in.shape[1] // (heads * dps)
    (
        (gain_rows, lse_near, lse_far),
        (conv_rows, grad_ffn, q_near, k_near, v_near, q_far, k_far, v_far, mixed_near, mixed_far),
        (key_t, hidden, normed_two),
        weights,
        (grad_conv, w_in_own, w_out_own, gf_rest),
    ) = unpack(
        forward(
            counts,
            mem_lens,
            cmem_lens,
            w_in if units == E else cut_in(w_in, heads, dps),
            w_conv,
            comp_grad.transpose(1, 0, 2),
            gains,
            (w_query, w_key, w_value, w_output),
            w_out,
            out_grad[0],
            inputs[0],
            memory,
            compressed,
        ),
        (3, 10, 3, 12, 4),
    )
    gain_one, gain_two = gain_rows[0:1], gain_rows[1:2]
    wq, wk, wv, wo = (
        [own] + [w.reshape(own.shape) for w in weights[3 * n : 3 * n + 3]]
        for n, own in enumerate((w_query, w_key, w_value, w_output))
    )
    w_in_own = w_in_own.reshape(width, -1)
    w_out_own = w_out_own.reshape(-1, width)
    gf_core, gf_x, gf_diag = (gf_rest[n] for n in range(3))
    pad_rows = (new_rows + 15) // 16 * 16

    (
        (grad_conv, new_cols, out_part, grad_hidden, grad_mixed, go_near, go_far, grad_w_in),
        (out_own, out_core, out_far, out_first),
    ) = unpack(
        middle(
            counts,
            mem_lens,
            gain_rows,
            conv_rows,
            normed_two,
            grad_ffn,
            gf_rest,
            w_in_own,
            w_out_own,
            cut_bits(grad_conv.reshape(dps, -1, conv_cols), masks),
            memory,
            hidden,
            out_grad[0],
            mixed_near,
            mixed_far,
            wo,
        ),
        (8, 4),
    )
    grad_w_out, sum_rows, input_grad, grad_out, gain_terms, grad_w_in, new_all, grad_conv, out_second = backward(
        mem_lens,
        cmem_lens,
        (q_near, k_near, v_near, lse_near),
        (q_far, k_far, v_far, lse_far),
        grad_mixed,
        wq,
        wk,
        wv,
        gain_one,
        go_near,
        go_far,
        out_part,
        new_cols,
        grad_conv,
        key_t,
        cut_bits(grad_w_in.reshape((dps, heads, w_in.shape[0], -1)), masks),
        inputs[0],
        grad_hidden,
        out_far,
    )
    in_source, in_weight = grad_w_in, w_in
    if units != E:
        in_source = (
            grad_w_in.reshape(heads, w_in.shape[0], dps, units)
            .transpose(1, 2, 0, 3)
            .reshape(w_in.shape[0], -1, heads, E)
            .transpose(2, 0, 1, 3)
            .reshape(grad_w_in.shape)
        )
    (
        outputs, input_grad, grad_query, grad_key, grad_value, grad_out, grad_w_out, grad_w_in,
        new_compressed, grad_conv, gain_sums,
    ) = finish(
        counts,
        hidden,
        out_own,
        out_core,
        out_first,
        out_second,
        input_grad,
        sum_rows.reshape(2, width, 3 * E),
        grad_out.reshape(w_output.shape),
        grad_w_out,
        in_source,
        new_all,
        grad_conv,
        w_in,
        new_rows,
    )
    own_gain_two = lax.dynamic_slice_in_dim(
        gain_two[0], (dp_at * heads + head_at) * w_in.shape[0], w_in.shape[0]
    )
    grad_gain_two = gain_sums[:, 0] / own_gain_two
    grad_gain_one = lax.dynamic_slice_in_dim(
        gain_terms[:, 0], head_at * norm_gain.shape[0], norm_gain.shape[0]
    ) / norm_gain.astype(f32)

    return (
        outputs[None],
        input_grad[None],
        new_compressed.transpose(1, 0, 2),
        grad_gain_one,
        grad_query,
        grad_key,
        grad_value,
        grad_out,
        grad_gain_two,
        grad_w_in,
        grad_w_out,
        grad_conv,
    )


def solution(mesh):
    whole = P(("dp", "head"), None, None)
    rows = P(("dp", "head"), None)
    vector = P(("dp", "head"))
    columns = P(None, "head")
    placed = (
        whole,
        P("dp", None, None),
        P("dp", None, None),
        P("dp"),
        P("dp"),
        P("dp"),
        vector,
        columns,
        columns,
        columns,
        P("head", None),
        vector,
        rows,
        rows,
        rows,
        whole,
        whole,
    )
    return jax.shard_map(
        shards,
        mesh=mesh,
        in_specs=placed,
        out_specs=(
            whole,
            whole,
            whole,
            vector,
            columns,
            columns,
            columns,
            P("head", None),
            vector,
            rows,
            rows,
            rows,
        ),
        check_vma=False,
    )
```

```python
import functools

import jax
import jax.numpy as jnp
from jax import lax
from jax.experimental import pallas as pl
from jax.experimental.pallas import tpu as pltpu
from jax.sharding import PartitionSpec as P

E = 128
BLOCK = 256
epsilon = 1e-05
masked_value = -1e30
score_scale = E ** (-0.5)
log2e = 1.4426950408889634
bf16 = jnp.bfloat16
f32 = jnp.float32
VMEM_BYTES = 30 * 2**20
MESH = pl.DeviceIdType.MESH


def dot(left, right):
    return jnp.dot(left, right, preferred_element_type=f32)


def dot_tn(left, right):
    return lax.dot_general(left, right, (((0,), (0,)), ((), ())), preferred_element_type=f32)


def dot_nt(left, right):
    return lax.dot_general(left, right, (((1,), (1,)), ((), ())), preferred_element_type=f32)


def layer_norm(values, gain_vec):
    row_mean = jnp.mean(values, axis=-1, keepdims=True)
    centred = values - row_mean
    variance = jnp.mean(centred * centred, axis=-1, keepdims=True)
    return centred * lax.rsqrt(variance + epsilon) * gain_vec


def vmem():
    return pl.BlockSpec(memory_space=pltpu.VMEM)


def anywhere():
    return pl.BlockSpec(memory_space=pl.ANY)


def masked_scores(kb, lens, scores):
    rows = lax.broadcasted_iota(jnp.int32, scores.shape, 0)
    if kb < 4:
        limit = lens[kb // 2] - (kb % 2) * BLOCK
        return jnp.where(rows < limit, scores, masked_value)
    columns = lax.broadcasted_iota(jnp.int32, scores.shape, 1)
    return jnp.where(rows <= columns, scores, masked_value)


STORED = 26


def forward_kernel(heads, dps, masks, group, slot_len, *refs):
    (counts_ref, mem_ref, cmem_ref), refs = refs[:3], refs[3:]
    (in_ref, w_conv_ref, cot_ref, gains_ref, wq0, wk0, wv0, wo0), refs = refs[:8], refs[8:]
    (w_out_hbm, out_grad_hbm, inputs_hbm, memory_hbm, cmem_hbm), refs = refs[:5], refs[5:]
    (gain_row_out, lse_near, lse_far), refs = refs[:3], refs[3:]
    places, refs = refs[:STORED], refs[STORED:]
    (w_in_all, w_out_all, gf_rest), refs = refs[:3], refs[3:]
    kept, refs = refs[:STORED], refs[STORED:]
    (conv_out, gf_out, q_near, k_near, v_near, q_far, k_far, v_far, mixed_near, mixed_far), more = kept[:10], kept[10:]
    (key_t, hidden_out, normed_out), more = more[:3], more[3:]
    (wq1, wq2, wq3, wk1, wk2, wk3, wv1, wv2, wv3, wo1, wo2, wo3, conv_grad) = more
    gains_out, cot_out, key_rows, scores, inputs, out_grad, memory, cmem, spread, conv_send, cot_send, in_pieces, sems = refs
    bits = len(masks)
    width = inputs.shape[1]
    half = wk0.shape[1]
    head = lax.axis_index("head")
    dp = lax.axis_index("dp")
    count = counts_ref[head]
    lens = (cmem_ref[head], mem_ref[head])
    flags = tuple(jnp.where(jnp.bitwise_and(dp, mask) != 0, 1, 0) for mask in masks)
    whole = slice(None)

    def head_device(r):
        return (dp, jnp.bitwise_xor(head, r))

    def dp_device(r):
        return (lax.rem(dp + r, dps), head)

    barrier = pltpu.get_barrier_semaphore()
    for r in range(1, heads):
        pl.semaphore_signal(barrier, inc=1, device_id=head_device(r), device_id_type=MESH)
    for r in range(1, dps):
        pl.semaphore_signal(barrier, inc=1, device_id=dp_device(r), device_id_type=MESH)

    slots = {}

    def slot(name):
        if name not in slots:
            slots[name] = len(slots)
        return slots[name]

    def remote(name, source, target, device):
        at = slot(name)
        return pltpu.make_async_remote_copy(
            src_ref=source,
            dst_ref=target,
            send_sem=sems.at[0, at],
            recv_sem=sems.at[1, at],
            device_id=device,
            device_id_type=MESH,
        )

    def local(name, source, target):
        return pltpu.make_async_copy(source, target, sems.at[0, slot(name)])

    for r in range(heads):
        if len(in_ref.shape) == 3:
            in_pieces[r] = in_ref[r]
        else:
            other = jnp.bitwise_xor(head, r)
            for n in range(dps):
                cut = pl.ds(pl.multiple_of((n * heads + other) * E, E), E)
                in_pieces[r, :, n * E : (n + 1) * E] = in_ref[:, cut]

    loads = {}
    for name, source, target in [
        ("out_grad", out_grad_hbm, out_grad),
        ("cmem", cmem_hbm.at[head], cmem),
        ("memory", memory_hbm, memory),
        ("inputs", inputs_hbm, inputs),
        ("w_out", w_out_hbm, w_out_all.at[flags]),
        ("in_own", in_pieces.at[0], w_in_all.at[flags + (head,)]),
    ]:
        loads[name] = local(f"load_{name}", source, target)
        loads[name].start()
    sent, stored = [], []

    def store(*buffers):
        for buffer in buffers:
            at = [buffer is other for other in kept].index(True)
            copy = local(f"store_{at}", buffer, places[at])
            copy.start()
            stored.append(copy)

    def send(*args):
        copy = remote(*args)
        copy.start()
        sent.append(copy)
        return copy

    at = dp * heads + head
    short = gains_ref.shape[1]
    lane = lax.broadcasted_iota(jnp.int32, (short, E), 1)
    place = lax.broadcasted_iota(jnp.int32, (short, E), 0) + lax.rem(at * short, E)
    spot = jnp.where(lane == place, 1.0, 0.0).astype(bf16)
    gains_out[at] = dot(gains_ref[...].astype(bf16), spot)
    columns = conv_out.shape[2]
    pad_rows = cot_out.shape[1]
    new_rows = cot_ref.shape[0]
    pl.semaphore_wait(barrier, heads + dps - 2)

    gain_heads = [
        send(f"gain_{r}", gains_out.at[at], gains_out.at[at], head_device(r))
        for r in range(1, heads)
    ]
    in_rows = [
        send(f"in_{r}", in_pieces.at[r], w_in_all.at[flags + (head,)], head_device(r))
        for r in range(1, heads)
    ]
    core = [
        send(f"core_{n}", source, target, head_device(1))
        for n, (source, target) in enumerate(((wk0, wk1), (wv0, wv1), (wq0, wq1), (wo0, wo1)))
    ]
    x_k = send("x_k", wk0, wk2, head_device(2))
    rows_o = wo2.shape[bits]
    own_o = wo0.at[pl.ds(pl.multiple_of(dp * rows_o, rows_o), rows_o)]
    x_o = send("x_o", own_o, wo2.at[flags], head_device(2))

    dp_partners = [(jnp.bitwise_xor(dp, mask), head) for mask in masks]

    def gather(name, block, order, source=None):
        copies, index = [], list(flags)
        for n, bit in enumerate(order):
            part = block.at[tuple(index)]
            first = source if source is not None and n == 0 else part
            copies.append(remote(f"gather_{name}_{n}", first, part, dp_partners[bit]))
            index[bit] = whole
        return copies

    straight = list(range(bits))
    crossed = straight[:-2] + [bits - 1, bits - 2]
    gathers = {
        "out": gather("out", w_out_all, straight, w_out_hbm),
        "in": gather("in", w_in_all, crossed),
        "o": gather("o", wo2, straight),
    }
    gathers["out"][0].start()

    def advance(name, n):
        gathers[name][n].wait_recv()
        if n + 1 < bits:
            gathers[name][n + 1].start()

    small = []
    for r in range(heads):
        other = jnp.bitwise_xor(head, r)
        cut = pl.ds(pl.multiple_of(other * columns, columns), columns)
        conv_piece = w_conv_ref[:, cut]
        cot_piece = jnp.concatenate(
            [cot_ref[:, 0, cut], jnp.zeros((pad_rows - new_rows, columns), f32)], axis=0
        ).astype(bf16)
        if r == 0:
            conv_out[head] = conv_piece
            cot_out[head] = cot_piece
        else:
            conv_send[r - 1] = conv_piece
            cot_send[r - 1] = cot_piece
            small.append(send(f"conv_{r}", conv_send.at[r - 1], conv_out.at[head], head_device(r)))
            small.append(send(f"cot_{r}", cot_send.at[r - 1], cot_out.at[head], head_device(r)))
    for copy in gain_heads:
        copy.wait_recv()
    block = gains_out.at[pl.ds(dp * heads, heads)]
    gain_dps = [send(f"gain_dp_{r}", block, block, dp_device(r)) for r in range(1, dps)]
    for copy in in_rows:
        copy.wait_recv()
    loads["in_own"].wait()
    gathers["in"][0].start()
    x_v = send("x_v", wv0, wv2, head_device(2))
    x_q = send("x_q", wq0, wq2, head_device(2))

    loads["out_grad"].wait()

    def cotangent(n, carry):
        rows = pl.ds(pl.multiple_of(n * 128, 128), 128)
        row = lax.broadcasted_iota(jnp.int32, (128, width), 0) + n * 128
        gf_out[rows] = jnp.where(row < count, out_grad[rows], 0.0).astype(bf16)
        return carry

    lax.fori_loop(0, slot_len // 128, cotangent, 0)
    store(gf_out)
    gf_core = send("gf_core", gf_out, gf_rest.at[0], head_device(1))
    gf_x = send("gf_x", gf_out, gf_rest.at[1], head_device(2))
    for copy in gain_dps:
        copy.wait_recv()
    many = E // short
    tiles = [
        sum(gains_out[t * many + n] for n in range(many)) for t in range(dps * heads // many)
    ]
    gain_one = jnp.concatenate([tile[0:1] for tile in tiles], axis=1)
    gain_two = jnp.concatenate([tile[1:2] for tile in tiles], axis=1)
    gain_row_out[0:1] = gain_one
    gain_row_out[1:2] = gain_two
    for copy in core:
        copy.wait_recv()
    store(wk1, wv1, wq1, wo1)

    def project(normed, rows, weights, k_ref, v_ref):
        for n, (wk, wv) in enumerate(weights):
            cut = slice(n * half, (n + 1) * half)
            k_ref[rows, cut] = dot(normed, wk).astype(bf16)
            v_ref[rows, cut] = dot(normed, wv).astype(bf16)

    def near_rows(source, part):
        def one(n, carry):
            rows = pl.ds(pl.multiple_of(n * BLOCK, BLOCK), BLOCK)
            target = pl.ds(pl.multiple_of(part * slot_len + n * BLOCK, BLOCK), BLOCK)
            normed = layer_norm(source[rows].astype(f32), gain_one).astype(bf16)
            key_rows[target] = normed
            key_t[:, target] = normed.T
            project(normed, target, ((wk0[...], wv0[...]), (wk1[...], wv1[...])), k_near, v_near)
            if part == 2:
                q_near[rows, :half] = dot(normed, wq0[...]).astype(bf16)
                q_near[rows, half:] = dot(normed, wq1[...]).astype(bf16)
            return carry

        lax.fori_loop(0, slot_len // BLOCK, one, 0)

    loads["cmem"].wait()
    near_rows(cmem, 0)
    loads["w_out"].wait()
    advance("out", 0)
    loads["memory"].wait()
    near_rows(memory.at[head], 1)
    x_o.wait_recv()
    gathers["o"][0].start()
    loads["inputs"].wait()
    near_rows(inputs, 2)
    store(q_near, k_near, v_near, key_t)
    advance("in", 0)

    c = score_scale * log2e

    def attend(q_ref, k_ref, v_ref, mixed_ref, lse_ref, events):
        def one(h, carry):
            cut = pl.ds(pl.multiple_of(h * E, E), E)
            q_t = q_ref[:, cut].T
            v_t = v_ref[:, cut].T
            top = jnp.full((1, slot_len), masked_value, f32)
            for kb in range(6):
                first = BLOCK if kb == 5 else 0
                rows = slice(kb * BLOCK, (kb + 1) * BLOCK)
                s = masked_scores(kb, lens, dot(k_ref[rows, cut], q_t[:, first:]))
                scores[rows, first:] = s
                part = jnp.max(s, axis=0, keepdims=True)
                if first:
                    top = jnp.concatenate([top[:, :first], jnp.maximum(top[:, first:], part)], axis=1)
                else:
                    top = jnp.maximum(top, part)
            shift = top * c
            mixed = jnp.zeros((E, slot_len), f32)
            total = jnp.zeros((1, slot_len), f32)
            for kb in range(6):
                first = BLOCK if kb == 5 else 0
                rows = slice(kb * BLOCK, (kb + 1) * BLOCK)
                p = jnp.exp2(scores[rows, first:] * c - shift[:, first:])
                part = jnp.sum(p, axis=0, keepdims=True)
                out = dot(v_t[:, rows], p.astype(bf16))
                if first:
                    total = jnp.concatenate([total[:, :first], total[:, first:] + part], axis=1)
                    mixed = jnp.concatenate([mixed[:, :first], mixed[:, first:] + out], axis=1)
                else:
                    total = total + part
                    mixed = mixed + out
            mixed_ref[:, cut] = (mixed / total).T.astype(bf16)
            lse_ref[h] = shift + jnp.log2(total)
            for when, event in events:
                pl.when(h == when)(event)
            return carry

        lax.fori_loop(0, q_ref.shape[1] // E, one, 0)

    attend(
        q_near,
        k_near,
        v_near,
        mixed_near,
        lse_near,
        [
            (1, lambda: advance("out", 1)),
            (2, lambda: advance("o", 0)),
        ],
    )

    for copy in small:
        copy.wait_recv()
    store(mixed_near, conv_out)
    taps = 3

    def spread_rows(g, carry):
        source_row = lax.broadcasted_iota(jnp.int32, (slot_len, pad_rows), 0)
        picked_row = lax.broadcasted_iota(jnp.int32, (slot_len, pad_rows), 1)
        kept = source_row < lax.min(counts_ref[g], mem_ref[g])
        for tap in range(taps):
            pick = jnp.where(kept & (source_row == taps * picked_row + tap), 1.0, 0.0).astype(bf16)
            spread[g, :, tap * columns : (tap + 1) * columns] = dot(pick, cot_out[g]).astype(bf16)
        return carry

    lax.fori_loop(0, group, spread_rows, 0)
    x_k.wait_recv()
    fwd_k = send("fwd_k", wk2, wk3, head_device(1))

    def conv_rows(n, carry):
        rows = pl.ds(pl.multiple_of(n * BLOCK, BLOCK), BLOCK)
        total = sum(dot(memory[g, :, rows].T, spread[g]) for g in range(group)).astype(bf16)
        for tap in range(taps):
            conv_grad[tap, rows] = total[:, tap * columns : (tap + 1) * columns]
        return carry

    lax.fori_loop(0, width // BLOCK, conv_rows, 0)
    advance("in", 1)
    x_v.wait_recv()
    fwd_v = send("fwd_v", wv2, wv3, head_device(1))
    store(conv_grad)
    advance("o", 1)
    x_q.wait_recv()
    fwd_q = send("fwd_q", wq2, wq3, head_device(1))
    for copy in (fwd_k, fwd_v):
        copy.wait_recv()
    store(wk2, wk3, wv2, wv3)

    def far_rows(n, carry):
        rows = pl.ds(pl.multiple_of(n * BLOCK, BLOCK), BLOCK)
        project(key_rows[rows], rows, ((wk2[...], wv2[...]), (wk3[...], wv3[...])), k_far, v_far)
        return carry

    lax.fori_loop(0, key_rows.shape[0] // BLOCK, far_rows, 0)
    fwd_q.wait_recv()
    store(wq2, wq3)
    for n in range(slot_len // BLOCK):
        rows = slice(n * BLOCK, (n + 1) * BLOCK)
        normed = key_rows[2 * slot_len + n * BLOCK : 2 * slot_len + (n + 1) * BLOCK]
        q_far[rows, :half] = dot(normed, wq2[...]).astype(bf16)
        q_far[rows, half:] = dot(normed, wq3[...]).astype(bf16)
    store(q_far, k_far, v_far)
    for n in range(2, bits):
        advance("o", n)
    fwd_o = send("fwd_o", wo2, wo3, head_device(1))
    attend(q_far, k_far, v_far, mixed_far, lse_far, [])
    store(mixed_far)
    fwd_o.wait_recv()
    store(wo2, wo3)

    def mix(n, carry):
        rows = pl.ds(pl.multiple_of(n * 128, 128), 128)
        near, far = mixed_near[rows], mixed_far[rows]
        attention = (
            dot(near[:, :half], wo0[...])
            + dot(near[:, half:], wo1[...])
            + dot(far[:, :half], wo2[...].reshape(half, width))
            + dot(far[:, half:], wo3[...].reshape(half, width))
        )
        row = lax.broadcasted_iota(jnp.int32, (128, width), 0) + n * 128
        hidden = inputs[rows] + jnp.where(row < count, attention, 0.0)
        hidden_out[rows] = hidden
        normed_out[rows] = layer_norm(hidden, gain_two).astype(bf16)
        return carry

    lax.fori_loop(0, slot_len // 128, mix, 0)
    store(hidden_out, normed_out)
    gf_x.wait_recv()
    gf_diag = send("gf_diag", gf_rest.at[1], gf_rest.at[2], head_device(1))
    gf_core.wait_recv()
    gf_diag.wait_recv()
    for n in range(2, bits):
        advance("in", n)
        advance("out", n)
    for copy in stored:
        copy.wait()
    for copy in sent:
        copy.wait_send()
    for copies in gathers.values():
        for copy in copies:
            copy.wait_send()


def forward(counts, mem_lens, cmem_lens, w_in, w_conv, comp_grad, gains, weights, w_out, out_grad, inputs, memory, compressed):
    heads, dps = lax.axis_size("head"), lax.axis_size("dp")
    masks = [1 << b for b in reversed(range(dps.bit_length() - 1))]
    twos = (2,) * len(masks)
    slot_len, width = inputs.shape
    group, keys = memory.shape[0], 3 * slot_len
    wq, wk, wv, wo = weights
    in_pieces = (heads, w_in.shape[-2], w_out.shape[0] * dps)
    half = wk.shape[1]
    columns = width // heads
    new_rows = comp_grad.shape[0]
    pad_rows = (new_rows + 15) // 16 * 16
    shape = jax.ShapeDtypeStruct
    wide = 2 * half
    conv_all = (heads, w_conv.shape[0], columns)
    cot_all = (heads, pad_rows, columns)
    o_cut = twos + (half // dps, width)
    outs = [
        shape((2, width), f32),
        shape((wide // E, 1, slot_len), f32),
        shape((wide // E, 1, slot_len), f32),
    ]
    kept = [
        shape(conv_all, bf16),
        shape((slot_len, width), bf16),
        shape((slot_len, wide), bf16),
        shape((keys, wide), bf16),
        shape((keys, wide), bf16),
        shape((slot_len, wide), bf16),
        shape((keys, wide), bf16),
        shape((keys, wide), bf16),
        shape((slot_len, wide), bf16),
        shape((slot_len, wide), bf16),
        shape((width, keys), bf16),
        shape((slot_len, width), f32),
        shape((slot_len, width), bf16),
        *[shape(wq.shape, bf16)] * 3,
        *[shape(wk.shape, bf16)] * 3,
        *[shape(wv.shape, bf16)] * 3,
        shape(wo.shape, bf16),
        shape(o_cut, bf16),
        shape(o_cut, bf16),
        shape((3, width, columns), bf16),
    ]
    far_outs = [
        shape(twos + in_pieces, bf16),
        shape(twos + w_out.shape, bf16),
        shape((heads - 1, slot_len, width), bf16),
    ]
    smem = pl.BlockSpec(memory_space=pltpu.SMEM)
    return pl.pallas_call(
        functools.partial(forward_kernel, heads, dps, masks, group, slot_len),
        in_specs=[smem] * 3 + [vmem()] * 8 + [anywhere()] * 5,
        out_specs=[vmem()] * len(outs) + [anywhere()] * (len(kept) + len(far_outs)),
        out_shape=outs + kept + far_outs,
        scratch_shapes=[pltpu.VMEM(k.shape, k.dtype) for k in kept]
        + [
            pltpu.VMEM((dps * heads, 8, E), f32),
            pltpu.VMEM(cot_all, bf16),
            pltpu.VMEM((keys, width), bf16),
            pltpu.VMEM((keys, slot_len), f32),
            pltpu.VMEM((slot_len, width), f32),
            pltpu.VMEM((slot_len, width), f32),
            pltpu.VMEM(memory.shape, bf16),
            pltpu.VMEM((slot_len, width), bf16),
            pltpu.VMEM((group, slot_len, 3 * columns), bf16),
            pltpu.VMEM((heads - 1,) + conv_all[1:], bf16),
            pltpu.VMEM((heads - 1,) + cot_all[1:], bf16),
            pltpu.VMEM(in_pieces, bf16),
            pltpu.SemaphoreType.DMA((2, 30 + STORED + 6 * heads + dps + 4 * len(masks))),
        ],
        compiler_params=pltpu.CompilerParams(
            collective_id=0, has_side_effects=True, vmem_limit_bytes=61 * 2**20
        ),
        cost_estimate=pl.CostEstimate(flops=40 * 10**9, bytes_accessed=0, transcendentals=0),
        name="forward",
    )(counts, mem_lens, cmem_lens, w_in, w_conv, comp_grad, gains, *weights, w_out, out_grad, inputs, memory, compressed)


def norm_input_grad(values, gain, grad):
    mean = jnp.mean(values, axis=-1, keepdims=True)
    centred = values - mean
    scale = lax.rsqrt(jnp.mean(centred * centred, axis=-1, keepdims=True) + epsilon)
    unit = centred * scale
    grad = grad * gain
    shift = jnp.mean(grad, axis=-1, keepdims=True)
    slope = jnp.mean(grad * unit, axis=-1, keepdims=True)
    return scale * (grad - shift - unit * slope)


def gelu_parts(u):
    c = 0.7978845608028654
    cube = 0.044715 * u * u
    t = jnp.tanh(c * (u + cube * u))
    half = 0.5 * (1.0 + t)
    return u * half, half + 0.5 * u * (1.0 - t * t) * (c * (1.0 + 3.0 * cube))


def middle_kernel(heads, masks, group, *refs):
    (counts_ref, mem_ref, gain_ref, conv_ref), refs = refs[:4], refs[4:]
    (n2_hbm, gf_hbm, gf_rest, w_in_hbm, w_out_hbm, conv_grad, memory_hbm), refs = refs[:7], refs[7:]
    (hidden_hbm, out_grad_hbm, mixed_near, mixed_far, wo0, wo1, wo2, wo3), refs = refs[:8], refs[8:]
    (conv_fin, new_cols, out_part), refs = refs[:3], refs[3:]
    (grad_hbm, gm_hbm, go_near, go_far, in_hbm, out_own_hbm, out_core_hbm, out_far_hbm, out_x_hbm), refs = refs[:9], refs[9:]
    (w_in, w_out, n2, gf, act, gi, gn_own, gn_part, gn_core, gn_diag, gn_x), refs = refs[:11], refs[11:]
    (out_own, out_send, out_diag, grad_out, grad_in, out_got, memory, out_grad, conv_all), refs = refs[:9], refs[9:]
    conv_kept, conv_got, sems = refs[0], refs[1:-1], refs[-1]
    bits = len(masks)
    slot_len, width = gn_own.shape
    head = lax.axis_index("head")
    dp = lax.axis_index("dp")
    flags = tuple(jnp.where(jnp.bitwise_and(dp, mask) != 0, 1, 0) for mask in masks)
    whole = slice(None)
    core = (dp, jnp.bitwise_xor(head, 1))
    chip = (dp, jnp.bitwise_xor(head, 2))
    partners = [(jnp.bitwise_xor(dp, mask), head) for mask in masks]

    barrier = pltpu.get_barrier_semaphore()
    for device in [core, chip] + partners:
        pl.semaphore_signal(barrier, inc=1, device_id=device, device_id_type=MESH)

    slots = {}

    def slot(name):
        if name not in slots:
            slots[name] = len(slots)
        return slots[name]

    sent, stored = [], []

    def remote(name, source, target, device):
        at = slot(name)
        copy = pltpu.make_async_remote_copy(
            src_ref=source,
            dst_ref=target,
            send_sem=sems.at[0, at],
            recv_sem=sems.at[1, at],
            device_id=device,
            device_id_type=MESH,
        )
        sent.append(copy)
        return copy

    def send(*args):
        copy = remote(*args)
        copy.start()
        return copy

    def local(name, source, target):
        copy = pltpu.make_async_copy(source, target, sems.at[0, slot(name)])
        copy.start()
        return copy

    def store(name, source, target):
        stored.append(local(name, source, target))

    load = {
        "n2": local("load_n2", n2_hbm, n2.at[0]),
        "w_in": local("load_w_in", w_in_hbm, w_in),
        "gf": local("load_gf", gf_hbm, gf.at[0]),
        "w_out": local("load_w_out", w_out_hbm, w_out),
        "gf_core": local("load_gf_core", gf_rest.at[0], gf.at[1]),
        "gf_far": local("load_gf_far", gf_rest.at[pl.ds(1, 2)], gf.at[pl.ds(2, 2)]),
        "conv": local(
            "load_conv", conv_grad.at[(whole,) * (bits - 1) + (flags[-1],)], conv_kept
        ),
        "out_grad": local("load_out_grad", out_grad_hbm, out_grad),
    }
    conv_all[flags] = conv_ref[...]
    pl.semaphore_wait(barrier, 2 + bits)

    n2_core = send("n2_core", n2_hbm, n2.at[1], core)
    halves = [pl.ds(h * (slot_len // 2), slot_len // 2) for h in range(2)]
    n2_x = [send(f"n2_x{h}", n2_hbm.at[halves[h]], n2.at[2, halves[h]], chip) for h in range(2)]
    n2_diag = [remote(f"n2_diag{h}", n2.at[2, halves[h]], n2.at[3, halves[h]], core) for h in range(2)]

    order = list(range(bits - 2)) + [bits - 1, bits - 2]
    index, gathers = list(flags), []
    for n, bit in enumerate(order):
        part = conv_all.at[tuple(index)]
        gathers.append(remote(f"conv_{n}", part, part, partners[bit]))
        index[bit] = whole
    sums = [
        remote(
            f"conv_sum{n}",
            (conv_grad if n == bits - 1 else conv_got[n + 1]).at[(whole,) * n + (1 - flags[n],)],
            conv_got[n],
            partners[n],
        )
        for n in range(bits)
    ]
    gathers[0].start()
    sums[bits - 1].start()

    def add_sum(n):
        sums[n].wait_recv()
        for at in range(2**n):
            spot = tuple((at >> (n - 1 - b)) & 1 for b in range(n))
            mine = conv_kept[spot] if n == bits - 1 else conv_got[n + 1][spot + (flags[n],)]
            conv_got[n][spot] = (conv_got[n][spot].astype(f32) + mine.astype(f32)).astype(bf16)
        if n:
            sums[n - 1].start()

    def next_gather(n):
        gathers[n].wait_recv()
        if n + 1 < bits:
            gathers[n + 1].start()

    rows_of = slot_len // 2
    units = w_in.shape[1]
    chunk = 512

    def tokens(s, half):
        rows = pl.ds(pl.multiple_of(half * rows_of, rows_of), rows_of)
        for n in range(units // chunk):
            cut = slice(n * chunk, (n + 1) * chunk)
            inner = dot(n2[s, rows], w_in[:, cut])
            value, slope = gelu_parts(inner)
            act[s, rows, cut] = value.astype(bf16)
            gi[s, rows, cut] = (dot_nt(gf[s, rows], w_out[cut, :]) * slope).astype(bf16)
        return rows, dot_nt(gi[s, rows], w_in[...])

    for name in ("n2", "w_in", "gf", "w_out", "gf_core"):
        load[name].wait()
    n2_core.wait_recv()

    def near(n, carry):
        s = lax.div(n, 2)
        rows, grad = tokens(s, lax.rem(n, 2))

        @pl.when(s == 0)
        def _():
            gn_own[rows] = grad

        @pl.when(s == 1)
        def _():
            gn_part[0, rows] = grad.astype(bf16)

        return carry

    lax.fori_loop(0, 4, near, 0)
    core_sent = send("gn_core", gn_part.at[0], gn_core, core)

    def terms(lhs, rhs, target, first, again):
        many = width // 4

        def one(n, carry):
            cut = pl.ds(pl.multiple_of(n * many, many), many)
            left = jnp.concatenate([lhs[first, :, cut].T, lhs[first + 1, :, cut].T], axis=1)
            total = dot(left, rhs[first : first + 2].reshape(2 * slot_len, rhs.shape[2]))
            block = target.shape[bits]
            per = many // block
            low = per.bit_length() - 1
            for m in range(per):
                spot = tuple(
                    lax.rem(lax.div(n, 2 ** (bits - low - 1 - b)), 2) for b in range(bits - low)
                ) + tuple((m >> (low - 1 - b)) & 1 for b in range(low))
                value = total[m * block : (m + 1) * block]
                if again:
                    value = value + target[spot].astype(f32)
                target[spot] = value.astype(bf16)
            return carry

        lax.fori_loop(0, 4, one, 0)

    def outward(n, carry):
        s = lax.div(n, 2)
        rows = pl.ds(pl.multiple_of(lax.rem(n, 2) * rows_of, rows_of), rows_of)
        value = dot(act[s, rows], w_out[...])

        @pl.when(s == 0)
        def _():
            out_own[rows] = value

        @pl.when(s > 0)
        def _():
            out_send[lax.max(s - 1, 0), rows] = value.astype(bf16)

        return carry

    n2_x[0].wait_recv()
    n2_diag[0].start()
    lax.fori_loop(0, 4, outward, 0)
    store("out_own", out_own, out_own_hbm)
    out_core = send("out_core", out_send.at[0], out_core_hbm, core)
    next_gather(0)
    load["gf_far"].wait()
    n2_diag[0].wait_recv()

    def far(half):
        def one(n, carry):
            rows, grad = tokens(2 + n, half)
            gn_part[1 + n, rows] = grad.astype(bf16)
            return carry

        lax.fori_loop(0, 2, one, 0)
        return send(f"gn_diag{half}", gn_part.at[2, halves[half]], gn_diag.at[halves[half]], core)

    def far_sum(half, copy):
        copy.wait_recv()
        rows = halves[half]
        gn_part[1, rows] = (gn_part[1, rows].astype(f32) + gn_diag[rows].astype(f32)).astype(bf16)
        return send(f"gn_x{half}", gn_part.at[1, rows], gn_x.at[rows], chip)

    diag_sent = far(0)
    terms(act, gf, grad_out, 0, False)
    gn_back = [far_sum(0, diag_sent)]
    load["conv"].wait()
    add_sum(bits - 1)
    terms(n2, gi, grad_in, 0, False)
    n2_x[1].wait_recv()
    n2_diag[1].start()
    next_gather(1)
    n2_diag[1].wait_recv()
    diag_sent = far(1)
    lax.fori_loop(4, 8, outward, 0)
    out_back = send("out_diag", out_send.at[2], out_diag, core)
    gn_back.append(far_sum(1, diag_sent))
    terms(act, gf, grad_out, 2, True)
    out_y = send(
        "out_sum", grad_out.at[(whole,) * (bits - 1) + (1 - flags[-1],)], out_got, partners[-1]
    )
    if bits > 1:
        add_sum(bits - 2)
    out_back.wait_recv()
    for h in range(2):
        rows = halves[h]
        out_diag[rows] = (out_diag[rows].astype(f32) + out_send[1, rows].astype(f32)).astype(bf16)
    out_x = send("out_x", out_diag.at[halves[0]], out_x_hbm, chip)
    store("out_far", out_diag.at[halves[1]], out_far_hbm)
    terms(n2, gi, grad_in, 2, True)
    store("grad_in", grad_in, in_hbm)
    near_wide, far_wide = mixed_near.shape[1], mixed_far.shape[1]
    half_rows = wo0.shape[0]
    late = [
        local("load_mixed_near", mixed_near, act.at[0, :, pl.ds(0, near_wide)]),
        local("load_mixed_far", mixed_far, act.at[0, :, pl.ds(near_wide, far_wide)]),
    ] + [
        local(f"load_wo{r}", w, act.at[1 + r // 2, pl.ds((r % 2) * half_rows, half_rows)])
        for r, w in enumerate((wo0, wo1, wo2, wo3))
    ]
    stored[0].wait()
    hidden_load = local("load_hidden", hidden_hbm, out_own)

    for copy in [hidden_load, load["out_grad"]] + late:
        copy.wait()
    for copy in gn_back:
        copy.wait_recv()
    core_sent.wait_recv()
    gain = gain_ref[1:2]

    def back(n, carry):
        rows = pl.ds(pl.multiple_of(n * 128, 128), 128)
        grad = gn_own[rows] + gn_core[rows].astype(f32) + gn_x[rows].astype(f32)
        grad = out_grad[rows] + norm_input_grad(out_own[rows], gain, grad)
        gn_own[rows] = grad
        row = lax.broadcasted_iota(jnp.int32, (128, width), 0) + n * 128
        gi[0, rows] = jnp.where(row < counts_ref[head], grad, 0.0).astype(bf16)
        return carry

    lax.fori_loop(0, slot_len // 128, back, 0)
    store("grad_hidden", gn_own, grad_hbm)
    weights = act[1:3].reshape(2 * slot_len, width)
    for h in range(2):
        gi[1, halves[h]] = dot_nt(gi[0, halves[h]], weights).astype(bf16)
    store("gm", gi.at[1], gm_hbm)
    for n, target in enumerate((go_near, go_far)):
        cut = slice(n * near_wide, (n + 1) * near_wide)
        gi[2 + n] = dot(act[0, :, cut].T, gi[0]).astype(bf16)
        store(f"go{n}", gi.at[2 + n], target)
    for n in range(2, bits):
        next_gather(n)
    for n in reversed(range(bits - 2)):
        add_sum(n)
    conv_fin[...] = conv_got[0][...].reshape(conv_fin.shape)

    pad_rows, columns = new_cols.shape[1], new_cols.shape[2]
    taps = 3

    def stream(g, carry):
        copy = local("load_memory", memory_hbm.at[g], memory)
        kernel = conv_all[...].reshape(taps * width, columns)
        source_row = lax.broadcasted_iota(jnp.int32, (pad_rows, slot_len), 1)
        picked_row = lax.broadcasted_iota(jnp.int32, (pad_rows, slot_len), 0)
        kept = source_row < lax.min(counts_ref[g], mem_ref[g])
        copy.wait()
        total = jnp.zeros((pad_rows, columns), f32)
        for tap in range(taps):
            pick = jnp.where(kept & (source_row == taps * picked_row + tap), 1.0, 0.0).astype(bf16)
            rows = dot(pick, memory[0:slot_len]).astype(bf16)
            total = total + dot(rows, kernel[tap * width : (tap + 1) * width])
        new_cols[g] = total.astype(bf16)
        return carry

    lax.fori_loop(0, group, stream, 0)
    out_y.wait_recv()
    for at in range(2 ** (bits - 1)):
        spot = tuple((at >> (bits - 2 - b)) & 1 for b in range(bits - 1))
        out_part[spot] = (
            out_got[spot].astype(f32) + grad_out[spot + (flags[-1],)].astype(f32)
        ).astype(bf16)
    out_core.wait_recv()
    out_x.wait_recv()
    for copy in stored[1:]:
        copy.wait()
    for copy in sent:
        copy.wait_send()


def middle(counts, mem_lens, gains, conv_rows, normed, grad_ffn, gf_rest, w_in, w_out, conv_grad, memory, hidden, out_grad, mixed_near, mixed_far, wo):
    heads, dps = lax.axis_size("head"), lax.axis_size("dp")
    masks = [1 << b for b in reversed(range(dps.bit_length() - 1))]
    bits = len(masks)
    twos = lambda n: (2,) * n
    slot_len, width = hidden.shape
    units = w_in.shape[1]
    columns = conv_rows.shape[2]
    new_rows = (slot_len + 2) // 3
    pad_rows = (new_rows + 15) // 16 * 16
    shape = jax.ShapeDtypeStruct
    stream = (slot_len, width)
    conv_block = conv_grad.shape[bits:]
    in_block = (width // dps, units)
    out_block = (units // dps, width)
    smem = pl.BlockSpec(memory_space=pltpu.SMEM)
    buffers = [
        (w_in.shape, bf16),
        (w_out.shape, bf16),
        ((4,) + stream, bf16),
        ((4,) + stream, bf16),
        ((4, slot_len, units), bf16),
        ((4, slot_len, units), bf16),
        (stream, f32),
        ((3,) + stream, bf16),
        (stream, bf16),
        (stream, bf16),
        (stream, bf16),
        (stream, f32),
        ((3,) + stream, bf16),
        (stream, bf16),
        (twos(bits) + out_block, bf16),
        (twos(bits) + in_block, bf16),
        (twos(bits - 1) + out_block, bf16),
        (memory.shape[1:], bf16),
        (stream, f32),
        (twos(bits) + conv_rows.shape, bf16),
        (twos(bits - 1) + conv_block, bf16),
    ] + [(twos(n) + conv_block, bf16) for n in range(bits)]
    return pl.pallas_call(
        functools.partial(middle_kernel, heads, masks, memory.shape[0]),
        in_specs=[smem] * 2 + [vmem()] * 2 + [anywhere()] * 15,
        out_specs=[vmem()] * 3 + [anywhere()] * 9,
        out_shape=[
            shape(conv_rows.shape, bf16),
            shape((memory.shape[0], pad_rows, columns), bf16),
            shape(twos(bits - 1) + out_block, bf16),
            shape(stream, f32),
            shape((slot_len, 4 * wo[0].shape[0]), bf16),
            shape((mixed_near.shape[1], width), bf16),
            shape((mixed_far.shape[1], width), bf16),
            shape(twos(bits) + in_block, bf16),
            shape(stream, f32),
            shape(stream, bf16),
            shape((slot_len // 2, width), bf16),
            shape((slot_len // 2, width), bf16),
        ],
        scratch_shapes=[pltpu.VMEM(*b) for b in buffers]
        + [pltpu.SemaphoreType.DMA((2, 52 + 3 * bits))],
        compiler_params=pltpu.CompilerParams(
            collective_id=2, has_side_effects=True, vmem_limit_bytes=61 * 2**20
        ),
        cost_estimate=pl.CostEstimate(flops=30 * 10**9, bytes_accessed=0, transcendentals=0),
        name="middle",
    )(counts, mem_lens, gains, conv_rows, normed, grad_ffn, gf_rest, w_in, w_out, conv_grad, memory, hidden, out_grad, mixed_near, mixed_far, *wo)


def backward_kernel(heads, masks, slot_len, keys, *refs):
    (mem_ref, cmem_ref, lse_near, lse_far), refs = refs[:4], refs[4:]
    loaded = 8 + 3 * heads
    sources, refs = refs[:loaded], refs[loaded:]
    (gain_ref, go_near, go_far, out_part, new_ref, conv_ref, key_t_hbm, in_hbm, inputs_hbm, hidden_hbm), refs = refs[:10], refs[10:]
    (out_far_hbm,), refs = refs[:1], refs[1:]
    (grad_out, sum_rows, input_grad_hbm, go_out, gain_out, in_got, new_got, conv_got, out_x_hbm), refs = refs[:9], refs[9:]
    held, refs = refs[:loaded], refs[loaded:]
    (q_near, k_near, v_near, gm_near, q_far, k_far, v_far, gm_far), more = held[:8], held[8:]
    wq, wk, wv = more[:heads], more[heads : 2 * heads], more[2 * heads :]
    (key_t, probs, grads, dkv, terms, far_terms, own_terms, got_near, got_far, got_x), refs = refs[:10], refs[10:]
    bits = len(masks)
    in_kept, refs = refs[0], refs[1:]
    in_got_rs, refs = refs[:bits], refs[bits:]
    out_got_rs, refs = refs[: bits - 1], refs[bits - 1 :]
    go_core_near, go_core_far, go_x, refs = refs[0], refs[1], refs[2], refs[3:]
    (go_sum, go_y_got, go_z_got), refs = refs[:3], refs[3:]
    y_got, z_got, last_got, last_z_got, grad_normed, gain_terms, sems = refs
    head = lax.axis_index("head")
    dp = lax.axis_index("dp")
    lens = (cmem_ref[head], mem_ref[head])
    flags = [jnp.where(jnp.bitwise_and(dp, mask) != 0, 1, 0) for mask in masks]

    def head_device(r):
        return (dp, jnp.bitwise_xor(head, r))

    def dp_device(n):
        return (jnp.bitwise_xor(dp, masks[n]), head)

    barrier = pltpu.get_barrier_semaphore()
    for r in range(1, heads):
        pl.semaphore_signal(barrier, inc=1, device_id=head_device(r), device_id_type=MESH)
    ring = 2 ** (bits - 1)

    def z_device(k):
        return (jnp.bitwise_xor(dp, 2 * k), head)

    pl.semaphore_signal(barrier, inc=1, device_id=dp_device(bits - 1), device_id_type=MESH)
    for k in range(1, ring):
        pl.semaphore_signal(barrier, inc=1, device_id=z_device(k), device_id_type=MESH)
    pl.semaphore_wait(barrier, heads - 1 + ring)

    slots = {}

    def remote(name, source, target, device, part=0):
        if name not in slots:
            slots[name] = 2 * len(slots)
        at = slots[name] + part
        return pltpu.make_async_remote_copy(
            src_ref=source,
            dst_ref=target,
            send_sem=sems.at[0, at],
            recv_sem=sems.at[1, at],
            device_id=device,
            device_id_type=MESH,
        )

    def local(name, source, target):
        if name not in slots:
            slots[name] = 2 * len(slots)
        return pltpu.make_async_copy(source, target, sems.at[0, slots[name]])

    whole = slice(None)

    def rs_copy(name, held, got, n, part=0):
        return remote(
            f"{name}{n}", held.at[(whole,) * n + (1 - flags[n],)], got, dp_device(n), part
        )

    def rs_add(held, got, n):
        for at in range(2**n):
            index = tuple((at >> (n - 1 - b)) & 1 for b in range(n))
            mine = held[index + (flags[n],)]
            got[index] = (got[index].astype(f32) + mine.astype(f32)).astype(bf16)

    fetches = []
    for n, (source, target) in enumerate(zip(sources, held)):
        if n in (3, 7):
            wide = target.shape[1]
            source = source.at[:, pl.ds((n // 4) * wide, wide)]
        fetches.append(local(f"fetch_{n}", source, target))
    for n in (4, 5, 6, 7):
        fetches[n].start()
    load_keys = local("load_keys", key_t_hbm, key_t)
    load_keys.start()
    for n in range(loaded):
        if n not in (4, 5, 6, 7):
            fetches[n].start()
    in_y = remote("in_rs", in_hbm.at[(whole,) * (bits - 1) + (1 - flags[bits - 1],)], in_got_rs[bits - 1], dp_device(bits - 1))
    in_y.start()
    load_in = local("load_in", in_hbm.at[(whole,) * (bits - 1) + (flags[bits - 1],)], in_kept)
    load_in.start()
    out_z = rs_copy("out_rs", out_part, out_got_rs[bits - 2], bits - 2)
    out_z.start()
    rows_o = go_x.shape[0]
    go_core = [
        remote("go_near", go_near.at[pl.ds(rows_o, rows_o)], go_core_near, head_device(1)),
        remote("go_far", go_far.at[pl.ds(rows_o, rows_o)], go_core_far, head_device(1)),
    ]
    for copy in go_core:
        copy.start()
    closing = []
    for name, source, target in (("new", new_ref, new_got), ("conv", conv_ref, conv_got)):
        for r in range(1, heads):
            copy = remote(
                f"{name}_{r}",
                source.at[jnp.bitwise_xor(head, r)],
                target.at[head],
                head_device(r),
            )
            copy.start()
            closing.append(copy)
        target[head] = source[head]
    go_to_x = remote("go_x", go_core_far, go_x, head_device(2))
    out_x = remote("out_x", out_far_hbm, out_x_hbm, head_device(2))

    def in_step(n):
        return rs_copy("in_rs", in_got_rs[n + 1], in_got_rs[n], n)

    def out_step(n):
        return rs_copy("out_rs", out_got_rs[n + 1], out_got_rs[n], n)

    grad_normed[...] = jnp.zeros(grad_normed.shape, f32)
    c = score_scale * log2e

    z_flags, y_flag = tuple(flags[:-1]), flags[-1]
    half_rows = own_terms.shape[1 + bits] // 2
    upper, lower = pl.ds(0, half_rows), pl.ds(half_rows, half_rows)

    parts = (upper, lower)

    def core_copy(r, p):
        return remote(f"core_{r}", terms.at[r // 2], (got_near if r == 1 else got_far).at[p], head_device(1), p)

    def x_copy(p, h=0):
        if p == 0:
            return remote("x_first", far_terms.at[0], got_x.at[0], head_device(2))
        spot = (1,) + (whole,) * bits + (parts[h],)
        return remote(f"x_last{h}", far_terms.at[spot], got_x.at[spot], head_device(2))

    def z_spot(k):
        return tuple(
            jnp.bitwise_xor(flag, (k >> (bits - 2 - b)) & 1) for b, flag in enumerate(z_flags)
        )

    all_z = (whole,) * (bits - 1)

    def plus(*values):
        return sum(value.astype(f32) for value in values).astype(bf16)

    def first_y():
        return remote("first_y", own_terms.at[(0,) + all_z + (1 - y_flag,)], y_got, dp_device(bits - 1))

    def first_z(k):
        return remote(f"first_z{k}", y_got.at[z_spot(k)], z_got.at[k], z_device(k))

    def first_back_z(k):
        spot = sum_rows.at[(0,) + tuple(flags)]
        return remote(f"first_back_z{k}", spot, spot, z_device(k))

    def first_back_y():
        spot = sum_rows.at[(0,) + all_z + (y_flag,)]
        return remote("first_back_y", spot, spot, dp_device(bits - 1))


    def last_y(h):
        source = own_terms.at[(1,) + all_z + (1 - y_flag, parts[h])]
        return remote(f"last_y{h}", source, last_got.at[h], dp_device(bits - 1))

    def last_z(h, k):
        return remote(
            f"last_z{h}_{k}", last_got.at[(h,) + z_spot(k)], last_z_got.at[k, h], z_device(k)
        )

    def last_back_z(h, k):
        spot = sum_rows.at[(1,) + tuple(flags) + (parts[h],)]
        return remote(f"last_back_z{h}_{k}", spot, spot, z_device(k))

    def last_back_y(h):
        spot = sum_rows.at[(1,) + all_z + (y_flag, parts[h])]
        return remote(f"last_back_y{h}", spot, spot, dp_device(bits - 1))

    def go_y():
        return remote("go_y", go_sum.at[all_z + (1 - y_flag,)], go_y_got, dp_device(bits - 1))

    def go_z(k):
        return remote(f"go_z{k}", go_y_got.at[z_spot(k)], go_z_got.at[k], z_device(k))

    def go_back_z(k):
        spot = go_out.at[tuple(flags)]
        return remote(f"go_back_z{k}", spot, spot, z_device(k))

    def go_back_y():
        spot = go_out.at[all_z + (y_flag,)]
        return remote("go_back_y", spot, spot, dp_device(bits - 1))

    def z_index(at):
        return tuple((at >> (bits - 2 - b)) & 1 for b in range(bits - 1))

    def each_block(function):
        def step(at, carry):
            function(tuple(lax.rem(lax.div(at, 2 ** (bits - 1 - b)), 2) for b in range(bits)))
            return carry

        lax.fori_loop(0, 2**bits, step, 0)

    def add_whole(target, source):
        def one(index):
            target[index] = (target[index].astype(f32) + source[index].astype(f32)).astype(bf16)

        each_block(one)

    def attend(r, p):
        half_q, half_k, half_v, half_g, half_l = (
            (q_near, k_near, v_near, gm_near, lse_near)
            if r < 2
            else (q_far, k_far, v_far, gm_far, lse_far)
        )
        cut = pl.ds(pl.multiple_of((r % 2) * 2 * E + p * E, E), E)
        q = half_q[:, cut]
        g = half_g[:, cut]
        q_t = q.T
        g_t = g.T
        k_t = half_k[:, cut].T
        lse = half_l[(r % 2) * 2 + p]
        row_dot = jnp.zeros((1, slot_len), f32)
        for kb in range(6):
            first = BLOCK if kb == 5 else 0
            rows = slice(kb * BLOCK, (kb + 1) * BLOCK)
            s = masked_scores(kb, lens, dot(half_k[rows, cut], q_t[:, first:]))
            pr = jnp.exp2(s * c - lse[:, first:])
            gp = dot(half_v[rows, cut], g_t[:, first:])
            probs[rows, first:] = pr
            grads[rows, first:] = gp
            part = jnp.sum(pr * gp, axis=0, keepdims=True)
            dkv[rows, E:] = dot(pr.astype(bf16), g[first:]).astype(bf16)
            if first:
                row_dot = jnp.concatenate([row_dot[:, :first], row_dot[:, first:] + part], axis=1)
            else:
                row_dot = row_dot + part
        dq = jnp.zeros((E, slot_len), f32)
        for kb in range(6):
            first = BLOCK if kb == 5 else 0
            rows = slice(kb * BLOCK, (kb + 1) * BLOCK)
            ds = (probs[rows, first:] * (grads[rows, first:] - row_dot[:, first:])).astype(bf16)
            dkv[rows, :E] = (dot(ds, q[first:]) * score_scale).astype(bf16)
            out = dot(k_t[:, rows], ds)
            if first:
                dq = jnp.concatenate([dq[:, :first], dq[:, first:] + out], axis=1)
            else:
                dq = dq + out
        return (dq * score_scale).T.astype(bf16)

    per_block = own_terms.shape[1 + bits]

    def weight_terms(dq, target):
        blocks = 2 ** (bits - 1)
        many = blocks * per_block

        def one(at, carry):
            rows = pl.ds(pl.multiple_of(at * many, many), many)
            of_kv = dot(key_t[rows, :], dkv[...]).astype(bf16)
            of_q = dot(key_t[rows, keys - slot_len :], dq).astype(bf16)
            for n in range(blocks):
                index = (at,) + tuple((n >> (bits - 2 - b)) & 1 for b in range(bits - 1))
                cut = slice(n * per_block, (n + 1) * per_block)
                target[index + (whole, slice(0, 2 * E))] = of_kv[cut]
                target[index + (whole, slice(2 * E, 3 * E))] = of_q[cut]
            return carry

        lax.fori_loop(0, 2, one, 0)

    def normed_terms(r, p, dq):
        cut = pl.ds(pl.multiple_of(p * E, E), E)
        dk = dkv[keys - slot_len :, :E]
        dv = dkv[keys - slot_len :, E:]
        columns = 256
        for n in range(grad_normed.shape[1] // columns):
            rows = slice(n * columns, (n + 1) * columns)
            grad_normed[:, rows] += (
                dot_nt(dq, wq[r][rows, cut])
                + dot_nt(dk, wk[r][rows, cut])
                + dot_nt(dv, wv[r][rows, cut])
            )

    def far_parity(p, carry):
        dq = attend(3, p)

        @pl.when(p == 0)
        def _():
            load_keys.wait()

        @pl.when(p == 1)
        def _():
            core_copy(3, 0).wait_send()

        weight_terms(dq, terms.at[1])
        core_copy(3, p).start()

        @pl.when(p == 0)
        def _():
            for n in range(loaded):
                if n not in (4, 5, 6, 7):
                    fetches[n].wait()

        normed_terms(3, p, dq)


        @pl.when(p == 1)
        def _():
            go_to_x.wait_recv()
            for at in range(2**bits):
                rows = slice(at * rows_o // 2**bits, (at + 1) * rows_o // 2**bits)
                index = tuple((at >> (bits - 1 - b)) & 1 for b in range(bits))
                go_sum[index] = plus(go_near[rows], go_core_near[rows], go_x[rows])
            go_y().start()

        dq = attend(2, p)

        weight_terms(dq, far_terms.at[p])
        core_copy(3, p).wait_recv()
        add_whole(far_terms.at[p], got_far.at[p])

        @pl.when(p == 0)
        def _():
            x_copy(0).start()

        @pl.when(p == 1)
        def _():
            x_copy(1, 0).start()
            x_copy(1, 1).start()

        normed_terms(2, p, dq)

        @pl.when(p == 0)
        def _():
            out_z.wait_recv()
            rs_add(out_part, out_got_rs[bits - 2], bits - 2)
            if bits > 2:
                out_step(bits - 3).start()

        @pl.when(p == 1)
        def _():
            in_y.wait_recv()
            load_in.wait()
            held = in_got_rs[bits - 1]
            for at in range(ring):
                index = z_index(at)
                held[index] = plus(held[index], in_kept[index])
            in_step(bits - 2).start()

        return carry

    def near_parity(p, carry):
        dq = attend(1, p)

        @pl.when(p == 1)
        def _():
            core_copy(1, 0).wait_send()

        weight_terms(dq, terms.at[0])
        core_copy(1, p).start()
        normed_terms(1, p, dq)

        @pl.when(p == 0)
        def _():
            for n in reversed(range(bits - 2)):
                out_step(n).wait_recv()
                rs_add(out_got_rs[n + 1], out_got_rs[n], n)
                if n:
                    out_step(n - 1).start()
            grad_out[...] = out_got_rs[0][...]

        @pl.when(p == 1)
        def _():
            pass

        dq = attend(0, p)

        @pl.when(p == 1)
        def _():
            for k in range(1, ring):
                go_z(k).wait_recv()
            go_out[tuple(flags)] = plus(go_y_got[z_flags], *(go_z_got[k] for k in range(1, ring)))
            for k in range(1, ring):
                go_back_z(k).start()

        weight_terms(dq, own_terms.at[p])
        core_copy(1, p).wait_recv()
        add_whole(own_terms.at[p], got_near.at[p])

        @pl.when(p == 0)
        def _():
            in_step(bits - 2).wait_recv()
            rs_add(in_got_rs[bits - 1], in_got_rs[bits - 2], bits - 2)
            for n in reversed(range(bits - 2)):
                in_step(n).start()
                if n:
                    in_step(n).wait_recv()
                    rs_add(in_got_rs[n + 1], in_got_rs[n], n)
            go_y().wait_recv()
            for at in range(ring):
                index = z_index(at)
                go_y_got[index] = plus(go_y_got[index], go_sum[index + (y_flag,)])
            for k in range(1, ring):
                go_z(k).start()
            x_copy(0).wait_recv()
            add_whole(own_terms.at[0], got_x.at[0])
            first_y().start()

        normed_terms(0, p, dq)

        return carry

    for copy in go_core:
        copy.wait_recv()
    go_core_far[...] = plus(go_core_far[...], go_far[:rows_o])
    go_to_x.start()
    for n in (4, 5, 6, 7):
        fetches[n].wait()
    lax.fori_loop(0, 2, far_parity, 0)
    lax.fori_loop(0, 2, near_parity, 0)

    wide = probs.shape[1]

    def half_loads(name, source, target):
        copies = []
        for n in range(2):
            copy = local(
                f"load_{name}{n}",
                source.at[:, pl.ds(n * wide, wide)],
                target.at[pl.ds(n * slot_len, slot_len)],
            )
            copy.start()
            copies.append(copy)
        return copies

    loads = half_loads("inputs", inputs_hbm, probs) + half_loads("hidden", hidden_hbm, grads)
    for copy in loads:
        copy.wait()
    gain_row = gain_ref[...]

    def input_rows(at, carry):
        rows = pl.ds(pl.multiple_of(at * 128, 128), 128)
        lower = pl.ds(pl.multiple_of(slot_len + at * 128, 128), 128)
        values = jnp.concatenate([probs[rows], probs[lower]], axis=1)
        before = jnp.concatenate([grads[rows], grads[lower]], axis=1)
        grad_normed[rows] = before + norm_input_grad(values, gain_row, grad_normed[rows])
        return carry

    lax.fori_loop(0, slot_len // 128, input_rows, 0)
    store_grad = local("store_grad", grad_normed, input_grad_hbm)
    store_grad.start()

    first_y().wait_recv()
    for at in range(ring):
        index = z_index(at)
        y_got[index] = plus(y_got[index], own_terms[(0,) + index + (y_flag,)])
    for k in range(1, ring):
        first_z(k).start()
    def last_bottom(h):
        x_copy(1, h).wait_recv()

        def add(index):
            spot = (1,) + index + (parts[h],)
            own_terms[spot] = plus(own_terms[spot], got_x[spot])

        each_block(add)
        last_y(h).start()

    last_bottom(0)
    for k in range(1, ring):
        go_back_z(k).wait_recv()
    go_back_y().start()
    last_bottom(1)
    out_x.start()
    in_step(0).wait_recv()
    rs_add(in_got_rs[1], in_got_rs[0], 0)
    in_copies = []
    for r in range(1, heads):
        copy = remote(
            f"in_{r}", in_got_rs[0].at[jnp.bitwise_xor(head, r)], in_got.at[head], head_device(r)
        )
        copy.start()
        in_copies.append(copy)
    in_got[head] = in_got_rs[0][head]
    def gain_part(p):
        rows = pl.ds(pl.multiple_of(dp * per_block, per_block), per_block)
        total = jnp.zeros((per_block, 1), f32)
        grad = sum_rows[(p,) + tuple(flags)]
        for n, weight in enumerate((wk[0], wv[0], wq[0])):
            own = weight[rows, p * E : (p + 1) * E].astype(f32)
            total = total + jnp.sum(
                grad[:, n * E : (n + 1) * E].astype(f32) * own, axis=1, keepdims=True
            )
        return total

    def last_middle(h):
        last_y(h).wait_recv()
        for at in range(ring):
            index = z_index(at)
            last_got[(h,) + index] = plus(
                last_got[(h,) + index], own_terms[(1,) + index + (y_flag, parts[h])]
            )
        for k in range(1, ring):
            last_z(h, k).start()

    def last_top(h):
        for k in range(1, ring):
            last_z(h, k).wait_recv()
        sum_rows[(1,) + tuple(flags) + (parts[h],)] = plus(
            last_got[(h,) + z_flags], *(last_z_got[k, h] for k in range(1, ring))
        )
        for k in range(1, ring):
            last_back_z(h, k).start()

    last_middle(0)
    for k in range(1, ring):
        first_z(k).wait_recv()
    sum_rows[(0,) + tuple(flags)] = plus(
        y_got[z_flags], *(z_got[k] for k in range(1, ring))
    )
    for k in range(1, ring):
        first_back_z(k).start()
    last_middle(1)
    gain = gain_part(0)
    for k in range(1, ring):
        first_back_z(k).wait_recv()
    first_back_y().start()
    last_top(0)
    last_top(1)
    gain = gain + gain_part(1)
    gain_terms[head] = jnp.broadcast_to(gain, gain_terms.shape[1:])
    gain_copies = []
    for r in range(1, heads):
        copy = remote(f"gain_{r}", gain_terms.at[head], gain_terms.at[head], head_device(r))
        copy.start()
        gain_copies.append(copy)
    for k in range(1, ring):
        last_back_z(0, k).wait_recv()
    last_back_y(0).start()
    for k in range(1, ring):
        last_back_z(1, k).wait_recv()
    last_back_y(1).start()

    store_grad.wait()
    out_x.wait_recv()
    for copy in gain_copies:
        copy.wait_recv()
    gain_out[...] = sum(gain_terms[h] for h in range(heads))
    for copy in closing + in_copies:
        copy.wait()
    go_back_y().wait_recv()
    first_back_y().wait_recv()
    for h in range(2):
        last_back_y(h).wait_recv()

    for copy in go_core + gain_copies:
        copy.wait_send()
    for copy in (in_y, out_z, go_to_x, out_x, core_copy(1, 1), core_copy(3, 1), x_copy(0), x_copy(1, 0), x_copy(1, 1)):
        copy.wait_send()
    for copy in (first_y(), first_back_y(), go_y(), go_back_y()):
        copy.wait_send()
    for h in range(2):
        last_y(h).wait_send()
        last_back_y(h).wait_send()
    for k in range(1, ring):
        for copy in (first_z, first_back_z, go_z, go_back_z):
            copy(k).wait_send()
        for h in range(2):
            last_z(h, k).wait_send()
            last_back_z(h, k).wait_send()
    for n in range(bits - 1):
        in_step(n).wait_send()
    for n in range(bits - 2):
        out_step(n).wait_send()


def backward(mem_lens, cmem_lens, near, far, grad_mixed, wq, wk, wv, gain, go_near, go_far, out_part, new_cols, conv, key_t, grad_in, inputs, grad_hidden, out_far):
    heads, dps = lax.axis_size("head"), lax.axis_size("dp")
    masks = [1 << b for b in reversed(range(dps.bit_length() - 1))]
    bits = len(masks)
    slot_len, width = inputs.shape
    keys = key_t.shape[1]
    shape = jax.ShapeDtypeStruct
    twos = lambda n: (2,) * n
    in_block = grad_in.shape[bits:]
    out_block = out_part.shape[bits - 1 :]
    rows_o = go_near.shape[0] // 2
    go_block = (rows_o // dps, width)
    sum_block = (width // dps, 3 * E)
    half_block = (width // dps // 2, 3 * E)
    copies = 160 + 16 * bits + 2 * (8 + 3 * heads) + 12 * dps
    q_n, k_n, v_n, l_n = near
    q_f, k_f, v_f, l_f = far
    loaded = (q_n, k_n, v_n, grad_mixed, q_f, k_f, v_f, grad_mixed, *wq, *wk, *wv)
    held = (q_n, k_n, v_n, q_n, q_f, k_f, v_f, q_f, *wq, *wk, *wv)
    scratch = (
        [pltpu.VMEM(value.shape, value.dtype) for value in held]
        + [
            pltpu.VMEM((width, keys), bf16),
            pltpu.VMEM((keys, slot_len), f32),
            pltpu.VMEM((keys, slot_len), f32),
            pltpu.VMEM((keys, 2 * E), bf16),
            pltpu.VMEM((2,) + twos(bits) + sum_block, bf16),
            pltpu.VMEM((2,) + twos(bits) + sum_block, bf16),
            pltpu.VMEM((2,) + twos(bits) + sum_block, bf16),
            pltpu.VMEM((2,) + twos(bits) + sum_block, bf16),
            pltpu.VMEM((2,) + twos(bits) + sum_block, bf16),
            pltpu.VMEM((2,) + twos(bits) + sum_block, bf16),
            pltpu.VMEM(twos(bits - 1) + in_block, bf16),
        ]
        + [pltpu.VMEM(twos(n) + in_block, bf16) for n in range(bits)]
        + [pltpu.VMEM(twos(n) + out_block, bf16) for n in range(bits - 1)]
        + [pltpu.VMEM((rows_o, width), bf16)] * 3
        + [
            pltpu.VMEM(twos(bits) + go_block, bf16),
            pltpu.VMEM(twos(bits - 1) + go_block, bf16),
            pltpu.VMEM((dps // 2,) + go_block, bf16),
        ]
        + [
            pltpu.VMEM(twos(bits - 1) + sum_block, bf16),
            pltpu.VMEM((dps // 2,) + sum_block, bf16),
            pltpu.VMEM((2,) + twos(bits - 1) + half_block, bf16),
            pltpu.VMEM((dps // 2, 2) + half_block, bf16),
        ]
        + [
            pltpu.VMEM((slot_len, width), f32),
            pltpu.VMEM((heads, width // dps, E), f32),
            pltpu.SemaphoreType.DMA((2, copies)),
        ]
    )
    return pl.pallas_call(
        functools.partial(backward_kernel, heads, masks, slot_len, keys),
        in_specs=[pl.BlockSpec(memory_space=pltpu.SMEM)] * 2
        + [vmem()] * 2
        + [anywhere()] * len(loaded)
        + [vmem()] * 6
        + [anywhere()] * 5,
        out_specs=[vmem()] * 2 + [anywhere()] + [vmem()] * 5 + [anywhere()],
        out_shape=[
            shape(out_block, bf16),
            shape((2,) + twos(bits) + sum_block, bf16),
            shape((slot_len, width), f32),
            shape(twos(bits) + go_block, bf16),
            shape((width // dps, E), f32),
            shape(in_block, bf16),
            shape(new_cols.shape, bf16),
            shape(conv.shape, bf16),
            shape(out_far.shape, bf16),
        ],
        scratch_shapes=scratch,
        compiler_params=pltpu.CompilerParams(
            collective_id=1, has_side_effects=True, vmem_limit_bytes=61 * 2**20
        ),
        cost_estimate=pl.CostEstimate(flops=60 * 10**9, bytes_accessed=0, transcendentals=0),
        name="backward",
    )(mem_lens, cmem_lens, l_n, l_f, *loaded, gain, go_near, go_far, out_part, new_cols, conv, key_t, grad_in, inputs, grad_hidden, out_far)


def finish_kernel(
    counts_ref, hidden_ref, own_ref, core_ref, x0_ref, x1_ref, grad_ref, sums_ref, go_ref, out_ref,
    in_ref, new_ref, conv_ref, w_in_ref, outputs, input_grad, grad_q, grad_k, grad_v, grad_o,
    grad_out, grad_in, new, conv, gain
):
    step = pl.program_id(0)
    rows = hidden_ref.shape[0]
    live = lax.broadcasted_iota(jnp.int32, hidden_ref.shape, 0) + step * rows
    live = live < counts_ref[lax.axis_index("head")]

    def whole(x_ref):
        added = own_ref[...] + core_ref[...].astype(f32) + x_ref[...].astype(f32)
        outputs[...] = hidden_ref[...] + jnp.where(live, added, 0.0)

    @pl.when(step < 2)
    def _():
        whole(x0_ref)

    @pl.when(step >= 2)
    def _():
        whole(x1_ref)

    input_grad[...] = grad_ref[...]
    for p in range(2):
        for n, target in enumerate((grad_k, grad_v, grad_q)):
            target[:, p * E : (p + 1) * E] = sums_ref[p, :, n * E : (n + 1) * E].astype(f32)
    grad_o[...] = go_ref[...].astype(f32)

    @pl.when(step == 0)
    def _():
        grad_out[...] = out_ref[...].astype(f32)
        heads, columns = new_ref.shape[0], new_ref.shape[2]
        for h in range(heads):
            cut = slice(h * columns, (h + 1) * columns)
            new[:, 0, cut] = new_ref[h][: new.shape[0]].astype(f32)
            conv[:, cut] = conv_ref[h].astype(f32)
        total = jnp.zeros((in_ref.shape[1], 1), f32)
        for h in range(heads):
            for n in range(in_ref.shape[2] // E):
                value = in_ref[h, :, n * E : (n + 1) * E].astype(f32)
                cut = slice((n * heads + h) * E, (n * heads + h + 1) * E)
                grad_in[:, cut] = value
                total = total + jnp.sum(
                    value * w_in_ref[:, cut].astype(f32), axis=1, keepdims=True
                )
        gain[...] = jnp.broadcast_to(total, gain.shape)


def finish(counts, hidden, own, core, x0, x1, grad, sums, go, out, grad_in, new, conv, w_in, new_rows):
    slot_len, width = hidden.shape
    steps = 4
    heads = new.shape[0]
    shape = jax.ShapeDtypeStruct
    row = lambda g: (g, 0)
    by_rows = lambda value: pl.BlockSpec((value.shape[0] // steps, value.shape[1]), row)

    def same(value):
        return pl.BlockSpec(value.shape, lambda g: (0,) * len(value.shape))

    half = 2 * E
    outs = [
        shape(hidden.shape, f32),
        shape(hidden.shape, f32),
        *[shape((width, half), f32)] * 3,
        shape(go.shape, f32),
    ]
    fixed = [
        shape(out.shape, f32),
        shape(w_in.shape, f32),
        shape((new_rows, 1, width), f32),
        shape((conv.shape[1], width), f32),
        shape((w_in.shape[0], E), f32),
    ]
    piece = (slot_len // steps, width)
    return pl.pallas_call(
        finish_kernel,
        grid=(steps,),
        in_specs=[pl.BlockSpec(memory_space=pltpu.SMEM)]
        + [by_rows(v) for v in (hidden, own, core)]
        + [
            pl.BlockSpec(piece, lambda g: (jnp.minimum(g, 1), 0)),
            pl.BlockSpec(piece, lambda g: (jnp.maximum(g - 2, 0), 0)),
            by_rows(grad),
            pl.BlockSpec((2, width // steps, sums.shape[2]), lambda g: (0, g, 0)),
            by_rows(go),
        ]
        + [same(v) for v in (out, grad_in, new, conv, w_in)],
        out_specs=[by_rows(v) for v in outs] + [same(v) for v in fixed],
        out_shape=outs + fixed,
        compiler_params=pltpu.CompilerParams(vmem_limit_bytes=61 * 2**20),
        name="finish",
    )(counts, hidden, own, core, x0, x1, grad, sums, go, out, grad_in, new, conv, w_in)


def swap_head(value, mask):
    size = lax.axis_size("head")
    return lax.ppermute(value, "head", [(i, i ^ mask) for i in range(size)])


def cut_bits(value, masks):
    return value.reshape((2,) * len(masks) + value.shape[1:])


def cut_in_kernel(in_ref, out_ref):
    heads, units = out_ref.shape[0], E
    head = lax.axis_index("head")
    for r in range(heads):
        other = jnp.bitwise_xor(head, r)
        for i in range(out_ref.shape[2] // units):
            source = pl.multiple_of((i * heads + other) * units, units)
            out_ref[r, :, i * units : (i + 1) * units] = in_ref[:, pl.ds(source, units)]


def cut_in(w_in, heads, dps):
    rows, units = w_in.shape[0], w_in.shape[1] // (heads * dps)
    if units == E:
        return pl.pallas_call(
            cut_in_kernel,
            in_specs=[vmem()],
            out_specs=vmem(),
            out_shape=jax.ShapeDtypeStruct((heads, rows, dps * units), bf16),
            name="cut_in",
        )(w_in)
    head = lax.axis_index("head")
    cut = w_in.reshape(rows, dps, heads, units)
    return jnp.stack(
        [
            lax.dynamic_index_in_dim(cut, head ^ r, 2, keepdims=False).reshape(rows, dps * units)
            for r in range(heads)
        ]
    )


def unpack(values, counts):
    parts, at = [], 0
    for count in counts:
        parts.append(values[at : at + count])
        at += count
    return parts


def shards(
    inputs,
    memory,
    compressed,
    counts,
    mem_lens,
    cmem_lens,
    norm_gain,
    w_query,
    w_key,
    w_value,
    w_output,
    ffn_gain,
    w_in,
    w_out,
    w_conv,
    out_grad,
    comp_grad,
):
    slot_len, width = inputs.shape[1:]
    heads, dps = lax.axis_size("head"), lax.axis_size("dp")
    masks = [1 << b for b in reversed(range(dps.bit_length() - 1))]
    bits = len(masks)
    group = memory.shape[0]
    head_at, dp_at = lax.axis_index("head"), lax.axis_index("dp")
    head_width = w_query.shape[1]
    new_rows = comp_grad.shape[1]
    conv_cols = width // heads
    gains = jnp.pad(jnp.stack([norm_gain, ffn_gain]).astype(f32), ((0, 6), (0, 0)))
    units = w_in.shape[1] // (heads * dps)
    (
        (gain_rows, lse_near, lse_far),
        (conv_rows, grad_ffn, q_near, k_near, v_near, q_far, k_far, v_far, mixed_near, mixed_far),
        (key_t, hidden, normed_two),
        weights,
        (grad_conv, w_in_own, w_out_own, gf_rest),
    ) = unpack(
        forward(
            counts,
            mem_lens,
            cmem_lens,
            w_in if units == E else cut_in(w_in, heads, dps),
            w_conv,
            comp_grad.transpose(1, 0, 2),
            gains,
            (w_query, w_key, w_value, w_output),
            w_out,
            out_grad[0],
            inputs[0],
            memory,
            compressed,
        ),
        (3, 10, 3, 12, 4),
    )
    gain_one, gain_two = gain_rows[0:1], gain_rows[1:2]
    wq, wk, wv, wo = (
        [own] + [w.reshape(own.shape) for w in weights[3 * n : 3 * n + 3]]
        for n, own in enumerate((w_query, w_key, w_value, w_output))
    )
    w_in_own = w_in_own.reshape(width, -1)
    w_out_own = w_out_own.reshape(-1, width)
    gf_core, gf_x, gf_diag = (gf_rest[n] for n in range(3))
    pad_rows = (new_rows + 15) // 16 * 16

    (
        (grad_conv, new_cols, out_part, grad_hidden, grad_mixed, go_near, go_far, grad_w_in),
        (out_own, out_core, out_far, out_first),
    ) = unpack(
        middle(
            counts,
            mem_lens,
            gain_rows,
            conv_rows,
            normed_two,
            grad_ffn,
            gf_rest,
            w_in_own,
            w_out_own,
            cut_bits(grad_conv.reshape(dps, -1, conv_cols), masks),
            memory,
            hidden,
            out_grad[0],
            mixed_near,
            mixed_far,
            wo,
        ),
        (8, 4),
    )
    grad_w_out, sum_rows, input_grad, grad_out, gain_terms, grad_w_in, new_all, grad_conv, out_second = backward(
        mem_lens,
        cmem_lens,
        (q_near, k_near, v_near, lse_near),
        (q_far, k_far, v_far, lse_far),
        grad_mixed,
        wq,
        wk,
        wv,
        gain_one,
        go_near,
        go_far,
        out_part,
        new_cols,
        grad_conv,
        key_t,
        cut_bits(grad_w_in.reshape((dps, heads, w_in.shape[0], -1)), masks),
        inputs[0],
        grad_hidden,
        out_far,
    )
    in_source, in_weight = grad_w_in, w_in
    if units != E:
        in_source = (
            grad_w_in.reshape(heads, w_in.shape[0], dps, units)
            .transpose(1, 2, 0, 3)
            .reshape(w_in.shape[0], -1, heads, E)
            .transpose(2, 0, 1, 3)
            .reshape(grad_w_in.shape)
        )
    (
        outputs, input_grad, grad_query, grad_key, grad_value, grad_out, grad_w_out, grad_w_in,
        new_compressed, grad_conv, gain_sums,
    ) = finish(
        counts,
        hidden,
        out_own,
        out_core,
        out_first,
        out_second,
        input_grad,
        sum_rows.reshape(2, width, 3 * E),
        grad_out.reshape(w_output.shape),
        grad_w_out,
        in_source,
        new_all,
        grad_conv,
        w_in,
        new_rows,
    )
    own_gain_two = lax.dynamic_slice_in_dim(
        gain_two[0], (dp_at * heads + head_at) * w_in.shape[0], w_in.shape[0]
    )
    grad_gain_two = gain_sums[:, 0] / own_gain_two
    grad_gain_one = lax.dynamic_slice_in_dim(
        gain_terms[:, 0], head_at * norm_gain.shape[0], norm_gain.shape[0]
    ) / norm_gain.astype(f32)

    return (
        outputs[None],
        input_grad[None],
        new_compressed.transpose(1, 0, 2),
        grad_gain_one,
        grad_query,
        grad_key,
        grad_value,
        grad_out,
        grad_gain_two,
        grad_w_in,
        grad_w_out,
        grad_conv,
    )


def solution(mesh):
    whole = P(("dp", "head"), None, None)
    rows = P(("dp", "head"), None)
    vector = P(("dp", "head"))
    columns = P(None, "head")
    placed = (
        whole,
        P("dp", None, None),
        P("dp", None, None),
        P("dp"),
        P("dp"),
        P("dp"),
        vector,
        columns,
        columns,
        columns,
        P("head", None),
        vector,
        rows,
        rows,
        rows,
        whole,
        whole,
    )
    return jax.shard_map(
        shards,
        mesh=mesh,
        in_specs=placed,
        out_specs=(
            whole,
            whole,
            whole,
            vector,
            columns,
            columns,
            columns,
            P("head", None),
            vector,
            rows,
            rows,
            rows,
        ),
        check_vma=False,
    )
```

```python
import functools

import jax
import jax.numpy as jnp
from jax import lax
from jax.experimental import pallas as pl
from jax.experimental.pallas import tpu as pltpu
from jax.sharding import PartitionSpec as P

E = 128
BLOCK = 256
epsilon = 1e-05
masked_value = -1e30
score_scale = E ** (-0.5)
log2e = 1.4426950408889634
bf16 = jnp.bfloat16
f32 = jnp.float32
VMEM_BYTES = 30 * 2**20
MESH = pl.DeviceIdType.MESH


def dot(left, right):
    return jnp.dot(left, right, preferred_element_type=f32)


def dot_tn(left, right):
    return lax.dot_general(left, right, (((0,), (0,)), ((), ())), preferred_element_type=f32)


def dot_nt(left, right):
    return lax.dot_general(left, right, (((1,), (1,)), ((), ())), preferred_element_type=f32)


def layer_norm(values, gain_vec):
    row_mean = jnp.mean(values, axis=-1, keepdims=True)
    centred = values - row_mean
    variance = jnp.mean(centred * centred, axis=-1, keepdims=True)
    return centred * lax.rsqrt(variance + epsilon) * gain_vec


def vmem():
    return pl.BlockSpec(memory_space=pltpu.VMEM)


def anywhere():
    return pl.BlockSpec(memory_space=pl.ANY)


def masked_scores(kb, lens, scores):
    rows = lax.broadcasted_iota(jnp.int32, scores.shape, 0)
    if kb < 4:
        limit = lens[kb // 2] - (kb % 2) * BLOCK
        return jnp.where(rows < limit, scores, masked_value)
    columns = lax.broadcasted_iota(jnp.int32, scores.shape, 1)
    return jnp.where(rows <= columns, scores, masked_value)


STORED = 26


def forward_kernel(heads, dps, masks, group, slot_len, *refs):
    (counts_ref, mem_ref, cmem_ref), refs = refs[:3], refs[3:]
    (in_ref, w_conv_ref, cot_ref, gains_ref, wq0, wk0, wv0, wo0), refs = refs[:8], refs[8:]
    (w_out_hbm, out_grad_hbm, inputs_hbm, memory_hbm, cmem_hbm), refs = refs[:5], refs[5:]
    (gain_row_out, lse_near, lse_far), refs = refs[:3], refs[3:]
    places, refs = refs[:STORED], refs[STORED:]
    (w_in_all, w_out_all, gf_rest), refs = refs[:3], refs[3:]
    kept, refs = refs[:STORED], refs[STORED:]
    (conv_out, gf_out, q_near, k_near, v_near, q_far, k_far, v_far, mixed_near, mixed_far), more = kept[:10], kept[10:]
    (key_t, hidden_out, normed_out), more = more[:3], more[3:]
    (wq1, wq2, wq3, wk1, wk2, wk3, wv1, wv2, wv3, wo1, wo2, wo3, conv_grad) = more
    gains_out, cot_out, key_rows, scores, inputs, out_grad, memory, cmem, spread, conv_send, cot_send, in_pieces, sems = refs
    bits = len(masks)
    width = inputs.shape[1]
    half = wk0.shape[1]
    head = lax.axis_index("head")
    dp = lax.axis_index("dp")
    count = counts_ref[head]
    lens = (cmem_ref[head], mem_ref[head])
    flags = tuple(jnp.where(jnp.bitwise_and(dp, mask) != 0, 1, 0) for mask in masks)
    whole = slice(None)

    def head_device(r):
        return (dp, jnp.bitwise_xor(head, r))

    def dp_device(r):
        return (lax.rem(dp + r, dps), head)

    barrier = pltpu.get_barrier_semaphore()
    for r in range(1, heads):
        pl.semaphore_signal(barrier, inc=1, device_id=head_device(r), device_id_type=MESH)
    for r in range(1, dps):
        pl.semaphore_signal(barrier, inc=1, device_id=dp_device(r), device_id_type=MESH)

    slots = {}

    def slot(name):
        if name not in slots:
            slots[name] = len(slots)
        return slots[name]

    def remote(name, source, target, device):
        at = slot(name)
        return pltpu.make_async_remote_copy(
            src_ref=source,
            dst_ref=target,
            send_sem=sems.at[0, at],
            recv_sem=sems.at[1, at],
            device_id=device,
            device_id_type=MESH,
        )

    def local(name, source, target):
        return pltpu.make_async_copy(source, target, sems.at[0, slot(name)])

    for r in range(heads):
        if len(in_ref.shape) == 3:
            in_pieces[r] = in_ref[r]
        else:
            other = jnp.bitwise_xor(head, r)
            for n in range(dps):
                cut = pl.ds(pl.multiple_of((n * heads + other) * E, E), E)
                in_pieces[r, :, n * E : (n + 1) * E] = in_ref[:, cut]

    loads = {}
    for name, source, target in [
        ("out_grad", out_grad_hbm, out_grad),
        ("cmem", cmem_hbm.at[head], cmem),
        ("memory", memory_hbm, memory),
        ("inputs", inputs_hbm, inputs),
        ("w_out", w_out_hbm, w_out_all.at[flags]),
        ("in_own", in_pieces.at[0], w_in_all.at[flags + (head,)]),
    ]:
        loads[name] = local(f"load_{name}", source, target)
        loads[name].start()
    sent, stored = [], []

    def store(*buffers):
        for buffer in buffers:
            at = [buffer is other for other in kept].index(True)
            copy = local(f"store_{at}", buffer, places[at])
            copy.start()
            stored.append(copy)

    def send(*args):
        copy = remote(*args)
        copy.start()
        sent.append(copy)
        return copy

    at = dp * heads + head
    short = gains_ref.shape[1]
    lane = lax.broadcasted_iota(jnp.int32, (short, E), 1)
    place = lax.broadcasted_iota(jnp.int32, (short, E), 0) + lax.rem(at * short, E)
    spot = jnp.where(lane == place, 1.0, 0.0).astype(bf16)
    gains_out[at] = dot(gains_ref[...].astype(bf16), spot)
    columns = conv_out.shape[2]
    pad_rows = cot_out.shape[1]
    new_rows = cot_ref.shape[0]
    pl.semaphore_wait(barrier, heads + dps - 2)

    gain_heads = [
        send(f"gain_{r}", gains_out.at[at], gains_out.at[at], head_device(r))
        for r in range(1, heads)
    ]
    in_rows = [
        send(f"in_{r}", in_pieces.at[r], w_in_all.at[flags + (head,)], head_device(r))
        for r in range(1, heads)
    ]
    core = [
        send(f"core_{n}", source, target, head_device(1))
        for n, (source, target) in enumerate(((wk0, wk1), (wv0, wv1), (wq0, wq1), (wo0, wo1)))
    ]
    x_k = send("x_k", wk0, wk2, head_device(2))
    rows_o = wo2.shape[bits]
    own_o = wo0.at[pl.ds(pl.multiple_of(dp * rows_o, rows_o), rows_o)]
    x_o = send("x_o", own_o, wo2.at[flags], head_device(2))

    dp_partners = [(jnp.bitwise_xor(dp, mask), head) for mask in masks]

    def gather(name, block, order, source=None):
        copies, index = [], list(flags)
        for n, bit in enumerate(order):
            part = block.at[tuple(index)]
            first = source if source is not None and n == 0 else part
            copies.append(remote(f"gather_{name}_{n}", first, part, dp_partners[bit]))
            index[bit] = whole
        return copies

    straight = list(range(bits))
    crossed = straight[:-2] + [bits - 1, bits - 2]
    gathers = {
        "out": gather("out", w_out_all, straight, w_out_hbm),
        "in": gather("in", w_in_all, crossed),
        "o": gather("o", wo2, straight),
    }
    gathers["out"][0].start()

    def advance(name, n):
        gathers[name][n].wait_recv()
        if n + 1 < bits:
            gathers[name][n + 1].start()

    small = []
    for r in range(heads):
        other = jnp.bitwise_xor(head, r)
        cut = pl.ds(pl.multiple_of(other * columns, columns), columns)
        conv_piece = w_conv_ref[:, cut]
        cot_piece = jnp.concatenate(
            [cot_ref[:, 0, cut], jnp.zeros((pad_rows - new_rows, columns), f32)], axis=0
        ).astype(bf16)
        if r == 0:
            conv_out[head] = conv_piece
            cot_out[head] = cot_piece
        else:
            conv_send[r - 1] = conv_piece
            cot_send[r - 1] = cot_piece
            small.append(send(f"conv_{r}", conv_send.at[r - 1], conv_out.at[head], head_device(r)))
            small.append(send(f"cot_{r}", cot_send.at[r - 1], cot_out.at[head], head_device(r)))
    for copy in gain_heads:
        copy.wait_recv()
    block = gains_out.at[pl.ds(dp * heads, heads)]
    gain_dps = [send(f"gain_dp_{r}", block, block, dp_device(r)) for r in range(1, dps)]
    for copy in in_rows:
        copy.wait_recv()
    loads["in_own"].wait()
    gathers["in"][0].start()
    x_v = send("x_v", wv0, wv2, head_device(2))
    x_q = send("x_q", wq0, wq2, head_device(2))

    loads["out_grad"].wait()

    def cotangent(n, carry):
        rows = pl.ds(pl.multiple_of(n * 128, 128), 128)
        row = lax.broadcasted_iota(jnp.int32, (128, width), 0) + n * 128
        gf_out[rows] = jnp.where(row < count, out_grad[rows], 0.0).astype(bf16)
        return carry

    lax.fori_loop(0, slot_len // 128, cotangent, 0)
    store(gf_out)
    gf_core = send("gf_core", gf_out, gf_rest.at[0], head_device(1))
    gf_x = send("gf_x", gf_out, gf_rest.at[1], head_device(2))
    for copy in gain_dps:
        copy.wait_recv()
    many = E // short
    tiles = [
        sum(gains_out[t * many + n] for n in range(many)) for t in range(dps * heads // many)
    ]
    gain_one = jnp.concatenate([tile[0:1] for tile in tiles], axis=1)
    gain_two = jnp.concatenate([tile[1:2] for tile in tiles], axis=1)
    gain_row_out[0:1] = gain_one
    gain_row_out[1:2] = gain_two
    for copy in core:
        copy.wait_recv()
    store(wk1, wv1, wq1, wo1)

    def project(normed, rows, weights, k_ref, v_ref):
        for n, (wk, wv) in enumerate(weights):
            cut = slice(n * half, (n + 1) * half)
            k_ref[rows, cut] = dot(normed, wk).astype(bf16)
            v_ref[rows, cut] = dot(normed, wv).astype(bf16)

    def near_rows(source, part):
        def one(n, carry):
            rows = pl.ds(pl.multiple_of(n * BLOCK, BLOCK), BLOCK)
            target = pl.ds(pl.multiple_of(part * slot_len + n * BLOCK, BLOCK), BLOCK)
            normed = layer_norm(source[rows].astype(f32), gain_one).astype(bf16)
            key_rows[target] = normed
            key_t[:, target] = normed.T
            project(normed, target, ((wk0[...], wv0[...]), (wk1[...], wv1[...])), k_near, v_near)
            if part == 2:
                q_near[rows, :half] = dot(normed, wq0[...]).astype(bf16)
                q_near[rows, half:] = dot(normed, wq1[...]).astype(bf16)
            return carry

        lax.fori_loop(0, slot_len // BLOCK, one, 0)

    loads["cmem"].wait()
    near_rows(cmem, 0)
    loads["w_out"].wait()
    advance("out", 0)
    loads["memory"].wait()
    near_rows(memory.at[head], 1)
    x_o.wait_recv()
    gathers["o"][0].start()
    loads["inputs"].wait()
    near_rows(inputs, 2)
    store(q_near, k_near, v_near, key_t)
    advance("in", 0)

    c = score_scale * log2e

    def attend(q_ref, k_ref, v_ref, mixed_ref, lse_ref, events):
        def one(h, carry):
            cut = pl.ds(pl.multiple_of(h * E, E), E)
            q_t = q_ref[:, cut].T
            v_t = v_ref[:, cut].T
            top = jnp.full((1, slot_len), masked_value, f32)
            for kb in range(6):
                first = BLOCK if kb == 5 else 0
                rows = slice(kb * BLOCK, (kb + 1) * BLOCK)
                s = masked_scores(kb, lens, dot(k_ref[rows, cut], q_t[:, first:]))
                scores[rows, first:] = s
                part = jnp.max(s, axis=0, keepdims=True)
                if first:
                    top = jnp.concatenate([top[:, :first], jnp.maximum(top[:, first:], part)], axis=1)
                else:
                    top = jnp.maximum(top, part)
            shift = top * c
            mixed = jnp.zeros((E, slot_len), f32)
            total = jnp.zeros((1, slot_len), f32)
            for kb in range(6):
                first = BLOCK if kb == 5 else 0
                rows = slice(kb * BLOCK, (kb + 1) * BLOCK)
                p = jnp.exp2(scores[rows, first:] * c - shift[:, first:])
                part = jnp.sum(p, axis=0, keepdims=True)
                out = dot(v_t[:, rows], p.astype(bf16))
                if first:
                    total = jnp.concatenate([total[:, :first], total[:, first:] + part], axis=1)
                    mixed = jnp.concatenate([mixed[:, :first], mixed[:, first:] + out], axis=1)
                else:
                    total = total + part
                    mixed = mixed + out
            mixed_ref[:, cut] = (mixed / total).T.astype(bf16)
            lse_ref[h] = shift + jnp.log2(total)
            for when, event in events:
                pl.when(h == when)(event)
            return carry

        lax.fori_loop(0, q_ref.shape[1] // E, one, 0)

    attend(
        q_near,
        k_near,
        v_near,
        mixed_near,
        lse_near,
        [
            (1, lambda: advance("out", 1)),
            (2, lambda: advance("o", 0)),
        ],
    )

    for copy in small:
        copy.wait_recv()
    store(mixed_near, conv_out)
    taps = 3

    def spread_rows(g, carry):
        source_row = lax.broadcasted_iota(jnp.int32, (slot_len, pad_rows), 0)
        picked_row = lax.broadcasted_iota(jnp.int32, (slot_len, pad_rows), 1)
        kept = source_row < lax.min(counts_ref[g], mem_ref[g])
        for tap in range(taps):
            pick = jnp.where(kept & (source_row == taps * picked_row + tap), 1.0, 0.0).astype(bf16)
            spread[g, :, tap * columns : (tap + 1) * columns] = dot(pick, cot_out[g]).astype(bf16)
        return carry

    lax.fori_loop(0, group, spread_rows, 0)
    x_k.wait_recv()
    fwd_k = send("fwd_k", wk2, wk3, head_device(1))

    def conv_rows(n, carry):
        rows = pl.ds(pl.multiple_of(n * BLOCK, BLOCK), BLOCK)
        total = sum(dot(memory[g, :, rows].T, spread[g]) for g in range(group)).astype(bf16)
        for tap in range(taps):
            conv_grad[tap, rows] = total[:, tap * columns : (tap + 1) * columns]
        return carry

    lax.fori_loop(0, width // BLOCK, conv_rows, 0)
    advance("in", 1)
    x_v.wait_recv()
    fwd_v = send("fwd_v", wv2, wv3, head_device(1))
    store(conv_grad)
    advance("o", 1)
    x_q.wait_recv()
    fwd_q = send("fwd_q", wq2, wq3, head_device(1))
    for copy in (fwd_k, fwd_v):
        copy.wait_recv()
    store(wk2, wk3, wv2, wv3)

    def far_rows(n, carry):
        rows = pl.ds(pl.multiple_of(n * BLOCK, BLOCK), BLOCK)
        project(key_rows[rows], rows, ((wk2[...], wv2[...]), (wk3[...], wv3[...])), k_far, v_far)
        return carry

    lax.fori_loop(0, key_rows.shape[0] // BLOCK, far_rows, 0)
    fwd_q.wait_recv()
    store(wq2, wq3)
    for n in range(slot_len // BLOCK):
        rows = slice(n * BLOCK, (n + 1) * BLOCK)
        normed = key_rows[2 * slot_len + n * BLOCK : 2 * slot_len + (n + 1) * BLOCK]
        q_far[rows, :half] = dot(normed, wq2[...]).astype(bf16)
        q_far[rows, half:] = dot(normed, wq3[...]).astype(bf16)
    store(q_far, k_far, v_far)
    for n in range(2, bits):
        advance("o", n)
    fwd_o = send("fwd_o", wo2, wo3, head_device(1))
    attend(q_far, k_far, v_far, mixed_far, lse_far, [])
    store(mixed_far)
    fwd_o.wait_recv()
    store(wo2, wo3)

    def mix(n, carry):
        rows = pl.ds(pl.multiple_of(n * 128, 128), 128)
        near, far = mixed_near[rows], mixed_far[rows]
        attention = (
            dot(near[:, :half], wo0[...])
            + dot(near[:, half:], wo1[...])
            + dot(far[:, :half], wo2[...].reshape(half, width))
            + dot(far[:, half:], wo3[...].reshape(half, width))
        )
        row = lax.broadcasted_iota(jnp.int32, (128, width), 0) + n * 128
        hidden = inputs[rows] + jnp.where(row < count, attention, 0.0)
        hidden_out[rows] = hidden
        normed_out[rows] = layer_norm(hidden, gain_two).astype(bf16)
        return carry

    lax.fori_loop(0, slot_len // 128, mix, 0)
    store(hidden_out, normed_out)
    gf_x.wait_recv()
    gf_diag = send("gf_diag", gf_rest.at[1], gf_rest.at[2], head_device(1))
    gf_core.wait_recv()
    gf_diag.wait_recv()
    for n in range(2, bits):
        advance("in", n)
        advance("out", n)
    for copy in stored:
        copy.wait()
    for copy in sent:
        copy.wait_send()
    for copies in gathers.values():
        for copy in copies:
            copy.wait_send()


def forward(counts, mem_lens, cmem_lens, w_in, w_conv, comp_grad, gains, weights, w_out, out_grad, inputs, memory, compressed):
    heads, dps = lax.axis_size("head"), lax.axis_size("dp")
    masks = [1 << b for b in reversed(range(dps.bit_length() - 1))]
    twos = (2,) * len(masks)
    slot_len, width = inputs.shape
    group, keys = memory.shape[0], 3 * slot_len
    wq, wk, wv, wo = weights
    in_pieces = (heads, w_in.shape[-2], w_out.shape[0] * dps)
    half = wk.shape[1]
    columns = width // heads
    new_rows = comp_grad.shape[0]
    pad_rows = (new_rows + 15) // 16 * 16
    shape = jax.ShapeDtypeStruct
    wide = 2 * half
    conv_all = (heads, w_conv.shape[0], columns)
    cot_all = (heads, pad_rows, columns)
    o_cut = twos + (half // dps, width)
    outs = [
        shape((2, width), f32),
        shape((wide // E, 1, slot_len), f32),
        shape((wide // E, 1, slot_len), f32),
    ]
    kept = [
        shape(conv_all, bf16),
        shape((slot_len, width), bf16),
        shape((slot_len, wide), bf16),
        shape((keys, wide), bf16),
        shape((keys, wide), bf16),
        shape((slot_len, wide), bf16),
        shape((keys, wide), bf16),
        shape((keys, wide), bf16),
        shape((slot_len, wide), bf16),
        shape((slot_len, wide), bf16),
        shape((width, keys), bf16),
        shape((slot_len, width), f32),
        shape((slot_len, width), bf16),
        *[shape(wq.shape, bf16)] * 3,
        *[shape(wk.shape, bf16)] * 3,
        *[shape(wv.shape, bf16)] * 3,
        shape(wo.shape, bf16),
        shape(o_cut, bf16),
        shape(o_cut, bf16),
        shape((3, width, columns), bf16),
    ]
    far_outs = [
        shape(twos + in_pieces, bf16),
        shape(twos + w_out.shape, bf16),
        shape((heads - 1, slot_len, width), bf16),
    ]
    smem = pl.BlockSpec(memory_space=pltpu.SMEM)
    return pl.pallas_call(
        functools.partial(forward_kernel, heads, dps, masks, group, slot_len),
        in_specs=[smem] * 3 + [vmem()] * 8 + [anywhere()] * 5,
        out_specs=[vmem()] * len(outs) + [anywhere()] * (len(kept) + len(far_outs)),
        out_shape=outs + kept + far_outs,
        scratch_shapes=[pltpu.VMEM(k.shape, k.dtype) for k in kept]
        + [
            pltpu.VMEM((dps * heads, 8, E), f32),
            pltpu.VMEM(cot_all, bf16),
            pltpu.VMEM((keys, width), bf16),
            pltpu.VMEM((keys, slot_len), f32),
            pltpu.VMEM((slot_len, width), f32),
            pltpu.VMEM((slot_len, width), f32),
            pltpu.VMEM(memory.shape, bf16),
            pltpu.VMEM((slot_len, width), bf16),
            pltpu.VMEM((group, slot_len, 3 * columns), bf16),
            pltpu.VMEM((heads - 1,) + conv_all[1:], bf16),
            pltpu.VMEM((heads - 1,) + cot_all[1:], bf16),
            pltpu.VMEM(in_pieces, bf16),
            pltpu.SemaphoreType.DMA((2, 30 + STORED + 6 * heads + dps + 4 * len(masks))),
        ],
        compiler_params=pltpu.CompilerParams(
            collective_id=0, has_side_effects=True, vmem_limit_bytes=61 * 2**20
        ),
        cost_estimate=pl.CostEstimate(flops=40 * 10**9, bytes_accessed=0, transcendentals=0),
        name="forward",
    )(counts, mem_lens, cmem_lens, w_in, w_conv, comp_grad, gains, *weights, w_out, out_grad, inputs, memory, compressed)


def norm_input_grad(values, gain, grad):
    mean = jnp.mean(values, axis=-1, keepdims=True)
    centred = values - mean
    scale = lax.rsqrt(jnp.mean(centred * centred, axis=-1, keepdims=True) + epsilon)
    unit = centred * scale
    grad = grad * gain
    shift = jnp.mean(grad, axis=-1, keepdims=True)
    slope = jnp.mean(grad * unit, axis=-1, keepdims=True)
    return scale * (grad - shift - unit * slope)


def gelu_parts(u):
    c = 0.7978845608028654
    cube = 0.044715 * u * u
    t = jnp.tanh(c * (u + cube * u))
    half = 0.5 * (1.0 + t)
    return u * half, half + 0.5 * u * (1.0 - t * t) * (c * (1.0 + 3.0 * cube))


def middle_kernel(heads, masks, group, *refs):
    (counts_ref, mem_ref, gain_ref, conv_ref), refs = refs[:4], refs[4:]
    (n2_hbm, gf_hbm, gf_rest, w_in_hbm, w_out_hbm, conv_grad, memory_hbm), refs = refs[:7], refs[7:]
    (hidden_hbm, out_grad_hbm, mixed_near, mixed_far, wo0, wo1, wo2, wo3), refs = refs[:8], refs[8:]
    (conv_fin, new_cols, out_part), refs = refs[:3], refs[3:]
    (grad_hbm, gm_hbm, go_near, go_far, in_hbm, out_own_hbm, out_core_hbm, out_far_hbm, out_x_hbm), refs = refs[:9], refs[9:]
    (w_in, w_out, n2, gf, act, gi, gn_own, gn_part, gn_core, gn_diag, gn_x), refs = refs[:11], refs[11:]
    (out_own, out_send, out_diag, grad_out, grad_in, out_got, memory, out_grad, conv_all), refs = refs[:9], refs[9:]
    conv_kept, conv_got, sems = refs[0], refs[1:-1], refs[-1]
    bits = len(masks)
    slot_len, width = gn_own.shape
    head = lax.axis_index("head")
    dp = lax.axis_index("dp")
    flags = tuple(jnp.where(jnp.bitwise_and(dp, mask) != 0, 1, 0) for mask in masks)
    whole = slice(None)
    core = (dp, jnp.bitwise_xor(head, 1))
    chip = (dp, jnp.bitwise_xor(head, 2))
    partners = [(jnp.bitwise_xor(dp, mask), head) for mask in masks]

    barrier = pltpu.get_barrier_semaphore()
    for device in [core, chip] + partners:
        pl.semaphore_signal(barrier, inc=1, device_id=device, device_id_type=MESH)

    slots = {}

    def slot(name):
        if name not in slots:
            slots[name] = len(slots)
        return slots[name]

    sent, stored = [], []

    def remote(name, source, target, device):
        at = slot(name)
        copy = pltpu.make_async_remote_copy(
            src_ref=source,
            dst_ref=target,
            send_sem=sems.at[0, at],
            recv_sem=sems.at[1, at],
            device_id=device,
            device_id_type=MESH,
        )
        sent.append(copy)
        return copy

    def send(*args):
        copy = remote(*args)
        copy.start()
        return copy

    def local(name, source, target):
        copy = pltpu.make_async_copy(source, target, sems.at[0, slot(name)])
        copy.start()
        return copy

    def store(name, source, target):
        stored.append(local(name, source, target))

    load = {
        "n2": local("load_n2", n2_hbm, n2.at[0]),
        "w_in": local("load_w_in", w_in_hbm, w_in),
        "gf": local("load_gf", gf_hbm, gf.at[0]),
        "w_out": local("load_w_out", w_out_hbm, w_out),
        "gf_core": local("load_gf_core", gf_rest.at[0], gf.at[1]),
        "gf_far": local("load_gf_far", gf_rest.at[pl.ds(1, 2)], gf.at[pl.ds(2, 2)]),
        "conv": local(
            "load_conv", conv_grad.at[(whole,) * (bits - 1) + (flags[-1],)], conv_kept
        ),
        "out_grad": local("load_out_grad", out_grad_hbm, out_grad),
    }
    conv_all[flags] = conv_ref[...]
    pl.semaphore_wait(barrier, 2 + bits)

    n2_core = send("n2_core", n2_hbm, n2.at[1], core)
    halves = [pl.ds(h * (slot_len // 2), slot_len // 2) for h in range(2)]
    n2_x = [send(f"n2_x{h}", n2_hbm.at[halves[h]], n2.at[2, halves[h]], chip) for h in range(2)]
    n2_diag = [remote(f"n2_diag{h}", n2.at[2, halves[h]], n2.at[3, halves[h]], core) for h in range(2)]

    order = list(range(bits - 2)) + [bits - 1, bits - 2]
    index, gathers = list(flags), []
    for n, bit in enumerate(order):
        part = conv_all.at[tuple(index)]
        gathers.append(remote(f"conv_{n}", part, part, partners[bit]))
        index[bit] = whole
    sums = [
        remote(
            f"conv_sum{n}",
            (conv_grad if n == bits - 1 else conv_got[n + 1]).at[(whole,) * n + (1 - flags[n],)],
            conv_got[n],
            partners[n],
        )
        for n in range(bits)
    ]
    gathers[0].start()
    sums[bits - 1].start()

    def add_sum(n):
        sums[n].wait_recv()
        for at in range(2**n):
            spot = tuple((at >> (n - 1 - b)) & 1 for b in range(n))
            mine = conv_kept[spot] if n == bits - 1 else conv_got[n + 1][spot + (flags[n],)]
            conv_got[n][spot] = (conv_got[n][spot].astype(f32) + mine.astype(f32)).astype(bf16)
        if n:
            sums[n - 1].start()

    def next_gather(n):
        gathers[n].wait_recv()
        if n + 1 < bits:
            gathers[n + 1].start()

    rows_of = slot_len // 2
    units = w_in.shape[1]
    chunk = 512

    def tokens(s, half):
        rows = pl.ds(pl.multiple_of(half * rows_of, rows_of), rows_of)
        for n in range(units // chunk):
            cut = slice(n * chunk, (n + 1) * chunk)
            inner = dot(n2[s, rows], w_in[:, cut])
            value, slope = gelu_parts(inner)
            act[s, rows, cut] = value.astype(bf16)
            gi[s, rows, cut] = (dot_nt(gf[s, rows], w_out[cut, :]) * slope).astype(bf16)
        return rows, dot_nt(gi[s, rows], w_in[...])

    for name in ("n2", "w_in", "gf", "w_out", "gf_core"):
        load[name].wait()
    n2_core.wait_recv()

    def near(n, carry):
        s = lax.div(n, 2)
        rows, grad = tokens(s, lax.rem(n, 2))

        @pl.when(s == 0)
        def _():
            gn_own[rows] = grad

        @pl.when(s == 1)
        def _():
            gn_part[0, rows] = grad.astype(bf16)

        return carry

    lax.fori_loop(0, 4, near, 0)
    core_sent = send("gn_core", gn_part.at[0], gn_core, core)

    def terms(lhs, rhs, target, first, again):
        many = width // 4

        def one(n, carry):
            cut = pl.ds(pl.multiple_of(n * many, many), many)
            left = jnp.concatenate([lhs[first, :, cut].T, lhs[first + 1, :, cut].T], axis=1)
            total = dot(left, rhs[first : first + 2].reshape(2 * slot_len, rhs.shape[2]))
            block = target.shape[bits]
            per = many // block
            low = per.bit_length() - 1
            for m in range(per):
                spot = tuple(
                    lax.rem(lax.div(n, 2 ** (bits - low - 1 - b)), 2) for b in range(bits - low)
                ) + tuple((m >> (low - 1 - b)) & 1 for b in range(low))
                value = total[m * block : (m + 1) * block]
                if again:
                    value = value + target[spot].astype(f32)
                target[spot] = value.astype(bf16)
            return carry

        lax.fori_loop(0, 4, one, 0)

    def outward(n, carry):
        s = lax.div(n, 2)
        rows = pl.ds(pl.multiple_of(lax.rem(n, 2) * rows_of, rows_of), rows_of)
        value = dot(act[s, rows], w_out[...])

        @pl.when(s == 0)
        def _():
            out_own[rows] = value

        @pl.when(s > 0)
        def _():
            out_send[lax.max(s - 1, 0), rows] = value.astype(bf16)

        return carry

    n2_x[0].wait_recv()
    n2_diag[0].start()
    lax.fori_loop(0, 4, outward, 0)
    store("out_own", out_own, out_own_hbm)
    out_core = send("out_core", out_send.at[0], out_core_hbm, core)
    next_gather(0)
    load["gf_far"].wait()
    n2_diag[0].wait_recv()

    def far(half):
        def one(n, carry):
            rows, grad = tokens(2 + n, half)
            gn_part[1 + n, rows] = grad.astype(bf16)
            return carry

        lax.fori_loop(0, 2, one, 0)
        return send(f"gn_diag{half}", gn_part.at[2, halves[half]], gn_diag.at[halves[half]], core)

    def far_sum(half, copy):
        copy.wait_recv()
        rows = halves[half]
        gn_part[1, rows] = (gn_part[1, rows].astype(f32) + gn_diag[rows].astype(f32)).astype(bf16)
        return send(f"gn_x{half}", gn_part.at[1, rows], gn_x.at[rows], chip)

    diag_sent = far(0)
    terms(act, gf, grad_out, 0, False)
    gn_back = [far_sum(0, diag_sent)]
    load["conv"].wait()
    add_sum(bits - 1)
    terms(n2, gi, grad_in, 0, False)
    n2_x[1].wait_recv()
    n2_diag[1].start()
    next_gather(1)
    n2_diag[1].wait_recv()
    diag_sent = far(1)
    lax.fori_loop(4, 8, outward, 0)
    out_back = send("out_diag", out_send.at[2], out_diag, core)
    gn_back.append(far_sum(1, diag_sent))
    terms(act, gf, grad_out, 2, True)
    out_y = send(
        "out_sum", grad_out.at[(whole,) * (bits - 1) + (1 - flags[-1],)], out_got, partners[-1]
    )
    if bits > 1:
        add_sum(bits - 2)
    out_back.wait_recv()
    for h in range(2):
        rows = halves[h]
        out_diag[rows] = (out_diag[rows].astype(f32) + out_send[1, rows].astype(f32)).astype(bf16)
    out_x = send("out_x", out_diag.at[halves[0]], out_x_hbm, chip)
    store("out_far", out_diag.at[halves[1]], out_far_hbm)
    terms(n2, gi, grad_in, 2, True)
    store("grad_in", grad_in, in_hbm)
    near_wide, far_wide = mixed_near.shape[1], mixed_far.shape[1]
    half_rows = wo0.shape[0]
    late = [
        local("load_mixed_near", mixed_near, act.at[0, :, pl.ds(0, near_wide)]),
        local("load_mixed_far", mixed_far, act.at[0, :, pl.ds(near_wide, far_wide)]),
    ] + [
        local(f"load_wo{r}", w, act.at[1 + r // 2, pl.ds((r % 2) * half_rows, half_rows)])
        for r, w in enumerate((wo0, wo1, wo2, wo3))
    ]
    stored[0].wait()
    hidden_load = local("load_hidden", hidden_hbm, out_own)

    for copy in [hidden_load, load["out_grad"]] + late:
        copy.wait()
    for copy in gn_back:
        copy.wait_recv()
    core_sent.wait_recv()
    gain = gain_ref[1:2]

    def back(n, carry):
        rows = pl.ds(pl.multiple_of(n * 128, 128), 128)
        grad = gn_own[rows] + gn_core[rows].astype(f32) + gn_x[rows].astype(f32)
        grad = out_grad[rows] + norm_input_grad(out_own[rows], gain, grad)
        gn_own[rows] = grad
        row = lax.broadcasted_iota(jnp.int32, (128, width), 0) + n * 128
        gi[0, rows] = jnp.where(row < counts_ref[head], grad, 0.0).astype(bf16)
        return carry

    lax.fori_loop(0, slot_len // 128, back, 0)
    store("grad_hidden", gn_own, grad_hbm)
    weights = act[1:3].reshape(2 * slot_len, width)
    for h in range(2):
        gi[1, halves[h]] = dot_nt(gi[0, halves[h]], weights).astype(bf16)
    store("gm", gi.at[1], gm_hbm)
    for n, target in enumerate((go_near, go_far)):
        cut = slice(n * near_wide, (n + 1) * near_wide)
        gi[2 + n] = dot(act[0, :, cut].T, gi[0]).astype(bf16)
        store(f"go{n}", gi.at[2 + n], target)
    for n in range(2, bits):
        next_gather(n)
    for n in reversed(range(bits - 2)):
        add_sum(n)
    conv_fin[...] = conv_got[0][...].reshape(conv_fin.shape)

    pad_rows, columns = new_cols.shape[1], new_cols.shape[2]
    taps = 3

    def stream(g, carry):
        copy = local("load_memory", memory_hbm.at[g], memory)
        kernel = conv_all[...].reshape(taps * width, columns)
        source_row = lax.broadcasted_iota(jnp.int32, (pad_rows, slot_len), 1)
        picked_row = lax.broadcasted_iota(jnp.int32, (pad_rows, slot_len), 0)
        kept = source_row < lax.min(counts_ref[g], mem_ref[g])
        copy.wait()
        total = jnp.zeros((pad_rows, columns), f32)
        for tap in range(taps):
            pick = jnp.where(kept & (source_row == taps * picked_row + tap), 1.0, 0.0).astype(bf16)
            rows = dot(pick, memory[0:slot_len]).astype(bf16)
            total = total + dot(rows, kernel[tap * width : (tap + 1) * width])
        new_cols[g] = total.astype(bf16)
        return carry

    lax.fori_loop(0, group, stream, 0)
    out_y.wait_recv()
    for at in range(2 ** (bits - 1)):
        spot = tuple((at >> (bits - 2 - b)) & 1 for b in range(bits - 1))
        out_part[spot] = (
            out_got[spot].astype(f32) + grad_out[spot + (flags[-1],)].astype(f32)
        ).astype(bf16)
    out_core.wait_recv()
    out_x.wait_recv()
    for copy in stored[1:]:
        copy.wait()
    for copy in sent:
        copy.wait_send()


def middle(counts, mem_lens, gains, conv_rows, normed, grad_ffn, gf_rest, w_in, w_out, conv_grad, memory, hidden, out_grad, mixed_near, mixed_far, wo):
    heads, dps = lax.axis_size("head"), lax.axis_size("dp")
    masks = [1 << b for b in reversed(range(dps.bit_length() - 1))]
    bits = len(masks)
    twos = lambda n: (2,) * n
    slot_len, width = hidden.shape
    units = w_in.shape[1]
    columns = conv_rows.shape[2]
    new_rows = (slot_len + 2) // 3
    pad_rows = (new_rows + 15) // 16 * 16
    shape = jax.ShapeDtypeStruct
    stream = (slot_len, width)
    conv_block = conv_grad.shape[bits:]
    in_block = (width // dps, units)
    out_block = (units // dps, width)
    smem = pl.BlockSpec(memory_space=pltpu.SMEM)
    buffers = [
        (w_in.shape, bf16),
        (w_out.shape, bf16),
        ((4,) + stream, bf16),
        ((4,) + stream, bf16),
        ((4, slot_len, units), bf16),
        ((4, slot_len, units), bf16),
        (stream, f32),
        ((3,) + stream, bf16),
        (stream, bf16),
        (stream, bf16),
        (stream, bf16),
        (stream, f32),
        ((3,) + stream, bf16),
        (stream, bf16),
        (twos(bits) + out_block, bf16),
        (twos(bits) + in_block, bf16),
        (twos(bits - 1) + out_block, bf16),
        (memory.shape[1:], bf16),
        (stream, f32),
        (twos(bits) + conv_rows.shape, bf16),
        (twos(bits - 1) + conv_block, bf16),
    ] + [(twos(n) + conv_block, bf16) for n in range(bits)]
    return pl.pallas_call(
        functools.partial(middle_kernel, heads, masks, memory.shape[0]),
        in_specs=[smem] * 2 + [vmem()] * 2 + [anywhere()] * 15,
        out_specs=[vmem()] * 3 + [anywhere()] * 9,
        out_shape=[
            shape(conv_rows.shape, bf16),
            shape((memory.shape[0], pad_rows, columns), bf16),
            shape(twos(bits - 1) + out_block, bf16),
            shape(stream, f32),
            shape((slot_len, 4 * wo[0].shape[0]), bf16),
            shape((mixed_near.shape[1], width), bf16),
            shape((mixed_far.shape[1], width), bf16),
            shape(twos(bits) + in_block, bf16),
            shape(stream, f32),
            shape(stream, bf16),
            shape((slot_len // 2, width), bf16),
            shape((slot_len // 2, width), bf16),
        ],
        scratch_shapes=[pltpu.VMEM(*b) for b in buffers]
        + [pltpu.SemaphoreType.DMA((2, 52 + 3 * bits))],
        compiler_params=pltpu.CompilerParams(
            collective_id=2, has_side_effects=True, vmem_limit_bytes=61 * 2**20
        ),
        cost_estimate=pl.CostEstimate(flops=30 * 10**9, bytes_accessed=0, transcendentals=0),
        name="middle",
    )(counts, mem_lens, gains, conv_rows, normed, grad_ffn, gf_rest, w_in, w_out, conv_grad, memory, hidden, out_grad, mixed_near, mixed_far, *wo)


def backward_kernel(heads, masks, slot_len, keys, *refs):
    (mem_ref, cmem_ref, lse_near, lse_far), refs = refs[:4], refs[4:]
    loaded = 8 + 3 * heads
    sources, refs = refs[:loaded], refs[loaded:]
    (gain_ref, go_near, go_far, out_part, new_ref, conv_ref, key_t_hbm, in_hbm, inputs_hbm, hidden_hbm), refs = refs[:10], refs[10:]
    (out_far_hbm,), refs = refs[:1], refs[1:]
    (grad_out, sum_rows, input_grad_hbm, go_out, gain_out, in_got, new_got, conv_got, out_x_hbm), refs = refs[:9], refs[9:]
    held, refs = refs[:loaded], refs[loaded:]
    (q_near, k_near, v_near, gm_near, q_far, k_far, v_far, gm_far), more = held[:8], held[8:]
    wq, wk, wv = more[:heads], more[heads : 2 * heads], more[2 * heads :]
    (key_t, probs, grads, dkv, terms, far_terms, own_terms, got_near, got_far, got_x), refs = refs[:10], refs[10:]
    bits = len(masks)
    in_kept, refs = refs[0], refs[1:]
    in_got_rs, refs = refs[:bits], refs[bits:]
    out_got_rs, refs = refs[: bits - 1], refs[bits - 1 :]
    go_core_near, go_core_far, go_x, refs = refs[0], refs[1], refs[2], refs[3:]
    (go_sum, go_y_got, go_z_got), refs = refs[:3], refs[3:]
    y_got, z_got, last_got, last_z_got, grad_normed, gain_terms, sems = refs
    head = lax.axis_index("head")
    dp = lax.axis_index("dp")
    lens = (cmem_ref[head], mem_ref[head])
    flags = [jnp.where(jnp.bitwise_and(dp, mask) != 0, 1, 0) for mask in masks]

    def head_device(r):
        return (dp, jnp.bitwise_xor(head, r))

    def dp_device(n):
        return (jnp.bitwise_xor(dp, masks[n]), head)

    barrier = pltpu.get_barrier_semaphore()
    for r in range(1, heads):
        pl.semaphore_signal(barrier, inc=1, device_id=head_device(r), device_id_type=MESH)
    ring = 2 ** (bits - 1)

    def z_device(k):
        return (jnp.bitwise_xor(dp, 2 * k), head)

    pl.semaphore_signal(barrier, inc=1, device_id=dp_device(bits - 1), device_id_type=MESH)
    for k in range(1, ring):
        pl.semaphore_signal(barrier, inc=1, device_id=z_device(k), device_id_type=MESH)
    pl.semaphore_wait(barrier, heads - 1 + ring)

    slots = {}

    def remote(name, source, target, device, part=0):
        if name not in slots:
            slots[name] = 2 * len(slots)
        at = slots[name] + part
        return pltpu.make_async_remote_copy(
            src_ref=source,
            dst_ref=target,
            send_sem=sems.at[0, at],
            recv_sem=sems.at[1, at],
            device_id=device,
            device_id_type=MESH,
        )

    def local(name, source, target):
        if name not in slots:
            slots[name] = 2 * len(slots)
        return pltpu.make_async_copy(source, target, sems.at[0, slots[name]])

    whole = slice(None)

    def rs_copy(name, held, got, n, part=0):
        return remote(
            f"{name}{n}", held.at[(whole,) * n + (1 - flags[n],)], got, dp_device(n), part
        )

    def rs_add(held, got, n):
        for at in range(2**n):
            index = tuple((at >> (n - 1 - b)) & 1 for b in range(n))
            mine = held[index + (flags[n],)]
            got[index] = (got[index].astype(f32) + mine.astype(f32)).astype(bf16)

    fetches = []
    for n, (source, target) in enumerate(zip(sources, held)):
        if n in (3, 7):
            wide = target.shape[1]
            source = source.at[:, pl.ds((n // 4) * wide, wide)]
        fetches.append(local(f"fetch_{n}", source, target))
    for n in (4, 5, 6, 7):
        fetches[n].start()
    load_keys = local("load_keys", key_t_hbm, key_t)
    load_keys.start()
    for n in range(loaded):
        if n not in (4, 5, 6, 7):
            fetches[n].start()
    in_y = remote("in_rs", in_hbm.at[(whole,) * (bits - 1) + (1 - flags[bits - 1],)], in_got_rs[bits - 1], dp_device(bits - 1))
    in_y.start()
    load_in = local("load_in", in_hbm.at[(whole,) * (bits - 1) + (flags[bits - 1],)], in_kept)
    load_in.start()
    out_z = rs_copy("out_rs", out_part, out_got_rs[bits - 2], bits - 2)
    out_z.start()
    rows_o = go_x.shape[0]
    go_core = [
        remote("go_near", go_near.at[pl.ds(rows_o, rows_o)], go_core_near, head_device(1)),
        remote("go_far", go_far.at[pl.ds(rows_o, rows_o)], go_core_far, head_device(1)),
    ]
    for copy in go_core:
        copy.start()
    closing = []
    for name, source, target in (("new", new_ref, new_got), ("conv", conv_ref, conv_got)):
        for r in range(1, heads):
            copy = remote(
                f"{name}_{r}",
                source.at[jnp.bitwise_xor(head, r)],
                target.at[head],
                head_device(r),
            )
            copy.start()
            closing.append(copy)
        target[head] = source[head]
    go_to_x = remote("go_x", go_core_far, go_x, head_device(2))
    out_x = remote("out_x", out_far_hbm, out_x_hbm, head_device(2))

    def in_step(n):
        return rs_copy("in_rs", in_got_rs[n + 1], in_got_rs[n], n)

    def out_step(n):
        return rs_copy("out_rs", out_got_rs[n + 1], out_got_rs[n], n)

    grad_normed[...] = jnp.zeros(grad_normed.shape, f32)
    c = score_scale * log2e

    z_flags, y_flag = tuple(flags[:-1]), flags[-1]
    half_rows = own_terms.shape[1 + bits] // 2
    upper, lower = pl.ds(0, half_rows), pl.ds(half_rows, half_rows)

    parts = (upper, lower)

    def core_copy(r, p):
        return remote(f"core_{r}", terms.at[r // 2], (got_near if r == 1 else got_far).at[p], head_device(1), p)

    def x_copy(p, h=0):
        if p == 0:
            return remote("x_first", far_terms.at[0], got_x.at[0], head_device(2))
        spot = (1,) + (whole,) * bits + (parts[h],)
        return remote(f"x_last{h}", far_terms.at[spot], got_x.at[spot], head_device(2))

    def z_spot(k):
        return tuple(
            jnp.bitwise_xor(flag, (k >> (bits - 2 - b)) & 1) for b, flag in enumerate(z_flags)
        )

    all_z = (whole,) * (bits - 1)

    def plus(*values):
        return sum(value.astype(f32) for value in values).astype(bf16)

    def first_y():
        return remote("first_y", own_terms.at[(0,) + all_z + (1 - y_flag,)], y_got, dp_device(bits - 1))

    def first_z(k):
        return remote(f"first_z{k}", y_got.at[z_spot(k)], z_got.at[k], z_device(k))

    def first_back_z(k):
        spot = sum_rows.at[(0,) + tuple(flags)]
        return remote(f"first_back_z{k}", spot, spot, z_device(k))

    def first_back_y():
        spot = sum_rows.at[(0,) + all_z + (y_flag,)]
        return remote("first_back_y", spot, spot, dp_device(bits - 1))


    def last_y(h):
        source = own_terms.at[(1,) + all_z + (1 - y_flag, parts[h])]
        return remote(f"last_y{h}", source, last_got.at[h], dp_device(bits - 1))

    def last_z(h, k):
        return remote(
            f"last_z{h}_{k}", last_got.at[(h,) + z_spot(k)], last_z_got.at[k, h], z_device(k)
        )

    def last_back_z(h, k):
        spot = sum_rows.at[(1,) + tuple(flags) + (parts[h],)]
        return remote(f"last_back_z{h}_{k}", spot, spot, z_device(k))

    def last_back_y(h):
        spot = sum_rows.at[(1,) + all_z + (y_flag, parts[h])]
        return remote(f"last_back_y{h}", spot, spot, dp_device(bits - 1))

    def go_y():
        return remote("go_y", go_sum.at[all_z + (1 - y_flag,)], go_y_got, dp_device(bits - 1))

    def go_z(k):
        return remote(f"go_z{k}", go_y_got.at[z_spot(k)], go_z_got.at[k], z_device(k))

    def go_back_z(k):
        spot = go_out.at[tuple(flags)]
        return remote(f"go_back_z{k}", spot, spot, z_device(k))

    def go_back_y():
        spot = go_out.at[all_z + (y_flag,)]
        return remote("go_back_y", spot, spot, dp_device(bits - 1))

    def z_index(at):
        return tuple((at >> (bits - 2 - b)) & 1 for b in range(bits - 1))

    def each_block(function):
        def step(at, carry):
            function(tuple(lax.rem(lax.div(at, 2 ** (bits - 1 - b)), 2) for b in range(bits)))
            return carry

        lax.fori_loop(0, 2**bits, step, 0)

    def add_whole(target, source):
        def one(index):
            target[index] = (target[index].astype(f32) + source[index].astype(f32)).astype(bf16)

        each_block(one)

    def attend(r, p):
        half_q, half_k, half_v, half_g, half_l = (
            (q_near, k_near, v_near, gm_near, lse_near)
            if r < 2
            else (q_far, k_far, v_far, gm_far, lse_far)
        )
        cut = pl.ds(pl.multiple_of((r % 2) * 2 * E + p * E, E), E)
        q = half_q[:, cut]
        g = half_g[:, cut]
        q_t = q.T
        g_t = g.T
        k_t = half_k[:, cut].T
        lse = half_l[(r % 2) * 2 + p]
        row_dot = jnp.zeros((1, slot_len), f32)
        for kb in range(6):
            first = BLOCK if kb == 5 else 0
            rows = slice(kb * BLOCK, (kb + 1) * BLOCK)
            s = masked_scores(kb, lens, dot(half_k[rows, cut], q_t[:, first:]))
            pr = jnp.exp2(s * c - lse[:, first:])
            gp = dot(half_v[rows, cut], g_t[:, first:])
            probs[rows, first:] = pr
            grads[rows, first:] = gp
            part = jnp.sum(pr * gp, axis=0, keepdims=True)
            dkv[rows, E:] = dot(pr.astype(bf16), g[first:]).astype(bf16)
            if first:
                row_dot = jnp.concatenate([row_dot[:, :first], row_dot[:, first:] + part], axis=1)
            else:
                row_dot = row_dot + part
        dq = jnp.zeros((E, slot_len), f32)
        for kb in range(6):
            first = BLOCK if kb == 5 else 0
            rows = slice(kb * BLOCK, (kb + 1) * BLOCK)
            ds = (probs[rows, first:] * (grads[rows, first:] - row_dot[:, first:])).astype(bf16)
            dkv[rows, :E] = (dot(ds, q[first:]) * score_scale).astype(bf16)
            out = dot(k_t[:, rows], ds)
            if first:
                dq = jnp.concatenate([dq[:, :first], dq[:, first:] + out], axis=1)
            else:
                dq = dq + out
        return (dq * score_scale).T.astype(bf16)

    per_block = own_terms.shape[1 + bits]

    def weight_terms(dq, target):
        blocks = 2 ** (bits - 1)
        many = blocks * per_block

        def one(at, carry):
            rows = pl.ds(pl.multiple_of(at * many, many), many)
            of_kv = dot(key_t[rows, :], dkv[...]).astype(bf16)
            of_q = dot(key_t[rows, keys - slot_len :], dq).astype(bf16)
            for n in range(blocks):
                index = (at,) + tuple((n >> (bits - 2 - b)) & 1 for b in range(bits - 1))
                cut = slice(n * per_block, (n + 1) * per_block)
                target[index + (whole, slice(0, 2 * E))] = of_kv[cut]
                target[index + (whole, slice(2 * E, 3 * E))] = of_q[cut]
            return carry

        lax.fori_loop(0, 2, one, 0)

    def normed_terms(r, p, dq):
        cut = pl.ds(pl.multiple_of(p * E, E), E)
        dk = dkv[keys - slot_len :, :E]
        dv = dkv[keys - slot_len :, E:]
        columns = 256
        for n in range(grad_normed.shape[1] // columns):
            rows = slice(n * columns, (n + 1) * columns)
            grad_normed[:, rows] += (
                dot_nt(dq, wq[r][rows, cut])
                + dot_nt(dk, wk[r][rows, cut])
                + dot_nt(dv, wv[r][rows, cut])
            )

    def far_parity(p, carry):
        dq = attend(3, p)

        @pl.when(p == 0)
        def _():
            load_keys.wait()

        @pl.when(p == 1)
        def _():
            core_copy(3, 0).wait_send()

        weight_terms(dq, terms.at[1])
        core_copy(3, p).start()

        @pl.when(p == 0)
        def _():
            for n in range(loaded):
                if n not in (4, 5, 6, 7):
                    fetches[n].wait()

        normed_terms(3, p, dq)


        @pl.when(p == 1)
        def _():
            go_to_x.wait_recv()
            for at in range(2**bits):
                rows = slice(at * rows_o // 2**bits, (at + 1) * rows_o // 2**bits)
                index = tuple((at >> (bits - 1 - b)) & 1 for b in range(bits))
                go_sum[index] = plus(go_near[rows], go_core_near[rows], go_x[rows])
            go_y().start()

        dq = attend(2, p)

        weight_terms(dq, far_terms.at[p])
        core_copy(3, p).wait_recv()
        add_whole(far_terms.at[p], got_far.at[p])

        @pl.when(p == 0)
        def _():
            x_copy(0).start()

        @pl.when(p == 1)
        def _():
            x_copy(1, 0).start()
            x_copy(1, 1).start()

        normed_terms(2, p, dq)

        @pl.when(p == 0)
        def _():
            out_z.wait_recv()
            rs_add(out_part, out_got_rs[bits - 2], bits - 2)
            if bits > 2:
                out_step(bits - 3).start()

        @pl.when(p == 1)
        def _():
            in_y.wait_recv()
            load_in.wait()
            held = in_got_rs[bits - 1]
            for at in range(ring):
                index = z_index(at)
                held[index] = plus(held[index], in_kept[index])
            in_step(bits - 2).start()

        return carry

    def near_parity(p, carry):
        dq = attend(1, p)

        @pl.when(p == 1)
        def _():
            core_copy(1, 0).wait_send()

        weight_terms(dq, terms.at[0])
        core_copy(1, p).start()
        normed_terms(1, p, dq)

        @pl.when(p == 0)
        def _():
            for n in reversed(range(bits - 2)):
                out_step(n).wait_recv()
                rs_add(out_got_rs[n + 1], out_got_rs[n], n)
                if n:
                    out_step(n - 1).start()
            grad_out[...] = out_got_rs[0][...]

        @pl.when(p == 1)
        def _():
            pass

        dq = attend(0, p)

        @pl.when(p == 1)
        def _():
            for k in range(1, ring):
                go_z(k).wait_recv()
            go_out[tuple(flags)] = plus(go_y_got[z_flags], *(go_z_got[k] for k in range(1, ring)))
            for k in range(1, ring):
                go_back_z(k).start()

        weight_terms(dq, own_terms.at[p])
        core_copy(1, p).wait_recv()
        add_whole(own_terms.at[p], got_near.at[p])

        @pl.when(p == 0)
        def _():
            in_step(bits - 2).wait_recv()
            rs_add(in_got_rs[bits - 1], in_got_rs[bits - 2], bits - 2)
            for n in reversed(range(bits - 2)):
                in_step(n).start()
                if n:
                    in_step(n).wait_recv()
                    rs_add(in_got_rs[n + 1], in_got_rs[n], n)
            go_y().wait_recv()
            for at in range(ring):
                index = z_index(at)
                go_y_got[index] = plus(go_y_got[index], go_sum[index + (y_flag,)])
            for k in range(1, ring):
                go_z(k).start()
            x_copy(0).wait_recv()
            add_whole(own_terms.at[0], got_x.at[0])
            first_y().start()

        normed_terms(0, p, dq)

        return carry

    for copy in go_core:
        copy.wait_recv()
    go_core_far[...] = plus(go_core_far[...], go_far[:rows_o])
    go_to_x.start()
    for n in (4, 5, 6, 7):
        fetches[n].wait()
    lax.fori_loop(0, 2, far_parity, 0)
    lax.fori_loop(0, 2, near_parity, 0)

    wide = probs.shape[1]

    def half_loads(name, source, target):
        copies = []
        for n in range(2):
            copy = local(
                f"load_{name}{n}",
                source.at[:, pl.ds(n * wide, wide)],
                target.at[pl.ds(n * slot_len, slot_len)],
            )
            copy.start()
            copies.append(copy)
        return copies

    loads = half_loads("inputs", inputs_hbm, probs) + half_loads("hidden", hidden_hbm, grads)
    for copy in loads:
        copy.wait()
    gain_row = gain_ref[...]

    def input_rows(at, carry):
        rows = pl.ds(pl.multiple_of(at * 128, 128), 128)
        lower = pl.ds(pl.multiple_of(slot_len + at * 128, 128), 128)
        values = jnp.concatenate([probs[rows], probs[lower]], axis=1)
        before = jnp.concatenate([grads[rows], grads[lower]], axis=1)
        grad_normed[rows] = before + norm_input_grad(values, gain_row, grad_normed[rows])
        return carry

    lax.fori_loop(0, slot_len // 128, input_rows, 0)
    store_grad = local("store_grad", grad_normed, input_grad_hbm)
    store_grad.start()

    first_y().wait_recv()
    for at in range(ring):
        index = z_index(at)
        y_got[index] = plus(y_got[index], own_terms[(0,) + index + (y_flag,)])
    for k in range(1, ring):
        first_z(k).start()
    def last_bottom(h):
        x_copy(1, h).wait_recv()

        def add(index):
            spot = (1,) + index + (parts[h],)
            own_terms[spot] = plus(own_terms[spot], got_x[spot])

        each_block(add)
        last_y(h).start()

    last_bottom(0)
    for k in range(1, ring):
        go_back_z(k).wait_recv()
    go_back_y().start()
    last_bottom(1)
    out_x.start()
    in_step(0).wait_recv()
    rs_add(in_got_rs[1], in_got_rs[0], 0)
    in_copies = []
    for r in range(1, heads):
        copy = remote(
            f"in_{r}", in_got_rs[0].at[jnp.bitwise_xor(head, r)], in_got.at[head], head_device(r)
        )
        copy.start()
        in_copies.append(copy)
    in_got[head] = in_got_rs[0][head]
    def gain_part(p):
        rows = pl.ds(pl.multiple_of(dp * per_block, per_block), per_block)
        total = jnp.zeros((per_block, 1), f32)
        grad = sum_rows[(p,) + tuple(flags)]
        for n, weight in enumerate((wk[0], wv[0], wq[0])):
            own = weight[rows, p * E : (p + 1) * E].astype(f32)
            total = total + jnp.sum(
                grad[:, n * E : (n + 1) * E].astype(f32) * own, axis=1, keepdims=True
            )
        return total

    def last_middle(h):
        last_y(h).wait_recv()
        for at in range(ring):
            index = z_index(at)
            last_got[(h,) + index] = plus(
                last_got[(h,) + index], own_terms[(1,) + index + (y_flag, parts[h])]
            )
        for k in range(1, ring):
            last_z(h, k).start()

    def last_top(h):
        for k in range(1, ring):
            last_z(h, k).wait_recv()
        sum_rows[(1,) + tuple(flags) + (parts[h],)] = plus(
            last_got[(h,) + z_flags], *(last_z_got[k, h] for k in range(1, ring))
        )
        for k in range(1, ring):
            last_back_z(h, k).start()

    last_middle(0)
    for k in range(1, ring):
        first_z(k).wait_recv()
    sum_rows[(0,) + tuple(flags)] = plus(
        y_got[z_flags], *(z_got[k] for k in range(1, ring))
    )
    for k in range(1, ring):
        first_back_z(k).start()
    last_middle(1)
    gain = gain_part(0)
    for k in range(1, ring):
        first_back_z(k).wait_recv()
    first_back_y().start()
    last_top(0)
    last_top(1)
    gain = gain + gain_part(1)
    gain_terms[head] = jnp.broadcast_to(gain, gain_terms.shape[1:])
    gain_copies = []
    for r in range(1, heads):
        copy = remote(f"gain_{r}", gain_terms.at[head], gain_terms.at[head], head_device(r))
        copy.start()
        gain_copies.append(copy)
    for k in range(1, ring):
        last_back_z(0, k).wait_recv()
    last_back_y(0).start()
    for k in range(1, ring):
        last_back_z(1, k).wait_recv()
    last_back_y(1).start()

    store_grad.wait()
    out_x.wait_recv()
    for copy in gain_copies:
        copy.wait_recv()
    gain_out[...] = sum(gain_terms[h] for h in range(heads))
    for copy in closing + in_copies:
        copy.wait()
    go_back_y().wait_recv()
    first_back_y().wait_recv()
    for h in range(2):
        last_back_y(h).wait_recv()

    for copy in go_core + gain_copies:
        copy.wait_send()
    for copy in (in_y, out_z, go_to_x, out_x, core_copy(1, 1), core_copy(3, 1), x_copy(0), x_copy(1, 0), x_copy(1, 1)):
        copy.wait_send()
    for copy in (first_y(), first_back_y(), go_y(), go_back_y()):
        copy.wait_send()
    for h in range(2):
        last_y(h).wait_send()
        last_back_y(h).wait_send()
    for k in range(1, ring):
        for copy in (first_z, first_back_z, go_z, go_back_z):
            copy(k).wait_send()
        for h in range(2):
            last_z(h, k).wait_send()
            last_back_z(h, k).wait_send()
    for n in range(bits - 1):
        in_step(n).wait_send()
    for n in range(bits - 2):
        out_step(n).wait_send()


def backward(mem_lens, cmem_lens, near, far, grad_mixed, wq, wk, wv, gain, go_near, go_far, out_part, new_cols, conv, key_t, grad_in, inputs, grad_hidden, out_far):
    heads, dps = lax.axis_size("head"), lax.axis_size("dp")
    masks = [1 << b for b in reversed(range(dps.bit_length() - 1))]
    bits = len(masks)
    slot_len, width = inputs.shape
    keys = key_t.shape[1]
    shape = jax.ShapeDtypeStruct
    twos = lambda n: (2,) * n
    in_block = grad_in.shape[bits:]
    out_block = out_part.shape[bits - 1 :]
    rows_o = go_near.shape[0] // 2
    go_block = (rows_o // dps, width)
    sum_block = (width // dps, 3 * E)
    half_block = (width // dps // 2, 3 * E)
    copies = 160 + 16 * bits + 2 * (8 + 3 * heads) + 12 * dps
    q_n, k_n, v_n, l_n = near
    q_f, k_f, v_f, l_f = far
    loaded = (q_n, k_n, v_n, grad_mixed, q_f, k_f, v_f, grad_mixed, *wq, *wk, *wv)
    held = (q_n, k_n, v_n, q_n, q_f, k_f, v_f, q_f, *wq, *wk, *wv)
    scratch = (
        [pltpu.VMEM(value.shape, value.dtype) for value in held]
        + [
            pltpu.VMEM((width, keys), bf16),
            pltpu.VMEM((keys, slot_len), f32),
            pltpu.VMEM((keys, slot_len), f32),
            pltpu.VMEM((keys, 2 * E), bf16),
            pltpu.VMEM((2,) + twos(bits) + sum_block, bf16),
            pltpu.VMEM((2,) + twos(bits) + sum_block, bf16),
            pltpu.VMEM((2,) + twos(bits) + sum_block, bf16),
            pltpu.VMEM((2,) + twos(bits) + sum_block, bf16),
            pltpu.VMEM((2,) + twos(bits) + sum_block, bf16),
            pltpu.VMEM((2,) + twos(bits) + sum_block, bf16),
            pltpu.VMEM(twos(bits - 1) + in_block, bf16),
        ]
        + [pltpu.VMEM(twos(n) + in_block, bf16) for n in range(bits)]
        + [pltpu.VMEM(twos(n) + out_block, bf16) for n in range(bits - 1)]
        + [pltpu.VMEM((rows_o, width), bf16)] * 3
        + [
            pltpu.VMEM(twos(bits) + go_block, bf16),
            pltpu.VMEM(twos(bits - 1) + go_block, bf16),
            pltpu.VMEM((dps // 2,) + go_block, bf16),
        ]
        + [
            pltpu.VMEM(twos(bits - 1) + sum_block, bf16),
            pltpu.VMEM((dps // 2,) + sum_block, bf16),
            pltpu.VMEM((2,) + twos(bits - 1) + half_block, bf16),
            pltpu.VMEM((dps // 2, 2) + half_block, bf16),
        ]
        + [
            pltpu.VMEM((slot_len, width), f32),
            pltpu.VMEM((heads, width // dps, E), f32),
            pltpu.SemaphoreType.DMA((2, copies)),
        ]
    )
    return pl.pallas_call(
        functools.partial(backward_kernel, heads, masks, slot_len, keys),
        in_specs=[pl.BlockSpec(memory_space=pltpu.SMEM)] * 2
        + [vmem()] * 2
        + [anywhere()] * len(loaded)
        + [vmem()] * 6
        + [anywhere()] * 5,
        out_specs=[vmem()] * 2 + [anywhere()] + [vmem()] * 5 + [anywhere()],
        out_shape=[
            shape(out_block, bf16),
            shape((2,) + twos(bits) + sum_block, bf16),
            shape((slot_len, width), f32),
            shape(twos(bits) + go_block, bf16),
            shape((width // dps, E), f32),
            shape(in_block, bf16),
            shape(new_cols.shape, bf16),
            shape(conv.shape, bf16),
            shape(out_far.shape, bf16),
        ],
        scratch_shapes=scratch,
        compiler_params=pltpu.CompilerParams(
            collective_id=1, has_side_effects=True, vmem_limit_bytes=61 * 2**20
        ),
        cost_estimate=pl.CostEstimate(flops=60 * 10**9, bytes_accessed=0, transcendentals=0),
        name="backward",
    )(mem_lens, cmem_lens, l_n, l_f, *loaded, gain, go_near, go_far, out_part, new_cols, conv, key_t, grad_in, inputs, grad_hidden, out_far)


def finish_kernel(
    counts_ref, hidden_ref, own_ref, core_ref, x0_ref, x1_ref, grad_ref, sums_ref, go_ref, out_ref,
    in_ref, new_ref, conv_ref, w_in_ref, outputs, input_grad, grad_q, grad_k, grad_v, grad_o,
    grad_out, grad_in, new, conv, gain
):
    step = pl.program_id(0)
    rows = hidden_ref.shape[0]
    live = lax.broadcasted_iota(jnp.int32, hidden_ref.shape, 0) + step * rows
    live = live < counts_ref[lax.axis_index("head")]

    def whole(x_ref):
        added = own_ref[...] + core_ref[...].astype(f32) + x_ref[...].astype(f32)
        outputs[...] = hidden_ref[...] + jnp.where(live, added, 0.0)

    @pl.when(step < pl.num_programs(0) // 2)
    def _():
        whole(x0_ref)

    @pl.when(step >= pl.num_programs(0) // 2)
    def _():
        whole(x1_ref)

    input_grad[...] = grad_ref[...]
    for p in range(2):
        for n, target in enumerate((grad_k, grad_v, grad_q)):
            target[:, p * E : (p + 1) * E] = sums_ref[p, :, n * E : (n + 1) * E].astype(f32)
    grad_o[...] = go_ref[...].astype(f32)

    @pl.when(step == 0)
    def _():
        grad_out[...] = out_ref[...].astype(f32)
        heads, columns = new_ref.shape[0], new_ref.shape[2]
        for h in range(heads):
            cut = slice(h * columns, (h + 1) * columns)
            new[:, 0, cut] = new_ref[h][: new.shape[0]].astype(f32)
            conv[:, cut] = conv_ref[h].astype(f32)
        total = jnp.zeros((in_ref.shape[1], 1), f32)
        for h in range(heads):
            for n in range(in_ref.shape[2] // E):
                value = in_ref[h, :, n * E : (n + 1) * E].astype(f32)
                cut = slice((n * heads + h) * E, (n * heads + h + 1) * E)
                grad_in[:, cut] = value
                total = total + jnp.sum(
                    value * w_in_ref[:, cut].astype(f32), axis=1, keepdims=True
                )
        gain[...] = jnp.broadcast_to(total, gain.shape)


def finish(counts, hidden, own, core, x0, x1, grad, sums, go, out, grad_in, new, conv, w_in, new_rows):
    slot_len, width = hidden.shape
    steps = 8
    heads = new.shape[0]
    shape = jax.ShapeDtypeStruct
    row = lambda g: (g, 0)
    by_rows = lambda value: pl.BlockSpec((value.shape[0] // steps, value.shape[1]), row)

    def same(value):
        return pl.BlockSpec(value.shape, lambda g: (0,) * len(value.shape))

    half = 2 * E
    outs = [
        shape(hidden.shape, f32),
        shape(hidden.shape, f32),
        *[shape((width, half), f32)] * 3,
        shape(go.shape, f32),
    ]
    fixed = [
        shape(out.shape, f32),
        shape(w_in.shape, f32),
        shape((new_rows, 1, width), f32),
        shape((conv.shape[1], width), f32),
        shape((w_in.shape[0], E), f32),
    ]
    piece = (slot_len // steps, width)
    return pl.pallas_call(
        finish_kernel,
        grid=(steps,),
        in_specs=[pl.BlockSpec(memory_space=pltpu.SMEM)]
        + [by_rows(v) for v in (hidden, own, core)]
        + [
            pl.BlockSpec(piece, lambda g: (jnp.minimum(g, steps // 2 - 1), 0)),
            pl.BlockSpec(piece, lambda g: (jnp.maximum(g - steps // 2, 0), 0)),
            by_rows(grad),
            pl.BlockSpec((2, width // steps, sums.shape[2]), lambda g: (0, g, 0)),
            by_rows(go),
        ]
        + [same(v) for v in (out, grad_in, new, conv, w_in)],
        out_specs=[by_rows(v) for v in outs] + [same(v) for v in fixed],
        out_shape=outs + fixed,
        compiler_params=pltpu.CompilerParams(vmem_limit_bytes=61 * 2**20),
        name="finish",
    )(counts, hidden, own, core, x0, x1, grad, sums, go, out, grad_in, new, conv, w_in)


def swap_head(value, mask):
    size = lax.axis_size("head")
    return lax.ppermute(value, "head", [(i, i ^ mask) for i in range(size)])


def cut_bits(value, masks):
    return value.reshape((2,) * len(masks) + value.shape[1:])


def cut_in_kernel(in_ref, out_ref):
    heads, units = out_ref.shape[0], E
    head = lax.axis_index("head")
    for r in range(heads):
        other = jnp.bitwise_xor(head, r)
        for i in range(out_ref.shape[2] // units):
            source = pl.multiple_of((i * heads + other) * units, units)
            out_ref[r, :, i * units : (i + 1) * units] = in_ref[:, pl.ds(source, units)]


def cut_in(w_in, heads, dps):
    rows, units = w_in.shape[0], w_in.shape[1] // (heads * dps)
    if units == E:
        return pl.pallas_call(
            cut_in_kernel,
            in_specs=[vmem()],
            out_specs=vmem(),
            out_shape=jax.ShapeDtypeStruct((heads, rows, dps * units), bf16),
            name="cut_in",
        )(w_in)
    head = lax.axis_index("head")
    cut = w_in.reshape(rows, dps, heads, units)
    return jnp.stack(
        [
            lax.dynamic_index_in_dim(cut, head ^ r, 2, keepdims=False).reshape(rows, dps * units)
            for r in range(heads)
        ]
    )


def unpack(values, counts):
    parts, at = [], 0
    for count in counts:
        parts.append(values[at : at + count])
        at += count
    return parts


def shards(
    inputs,
    memory,
    compressed,
    counts,
    mem_lens,
    cmem_lens,
    norm_gain,
    w_query,
    w_key,
    w_value,
    w_output,
    ffn_gain,
    w_in,
    w_out,
    w_conv,
    out_grad,
    comp_grad,
):
    slot_len, width = inputs.shape[1:]
    heads, dps = lax.axis_size("head"), lax.axis_size("dp")
    masks = [1 << b for b in reversed(range(dps.bit_length() - 1))]
    bits = len(masks)
    group = memory.shape[0]
    head_at, dp_at = lax.axis_index("head"), lax.axis_index("dp")
    head_width = w_query.shape[1]
    new_rows = comp_grad.shape[1]
    conv_cols = width // heads
    gains = jnp.pad(jnp.stack([norm_gain, ffn_gain]).astype(f32), ((0, 6), (0, 0)))
    units = w_in.shape[1] // (heads * dps)
    (
        (gain_rows, lse_near, lse_far),
        (conv_rows, grad_ffn, q_near, k_near, v_near, q_far, k_far, v_far, mixed_near, mixed_far),
        (key_t, hidden, normed_two),
        weights,
        (grad_conv, w_in_own, w_out_own, gf_rest),
    ) = unpack(
        forward(
            counts,
            mem_lens,
            cmem_lens,
            w_in if units == E else cut_in(w_in, heads, dps),
            w_conv,
            comp_grad.transpose(1, 0, 2),
            gains,
            (w_query, w_key, w_value, w_output),
            w_out,
            out_grad[0],
            inputs[0],
            memory,
            compressed,
        ),
        (3, 10, 3, 12, 4),
    )
    gain_one, gain_two = gain_rows[0:1], gain_rows[1:2]
    wq, wk, wv, wo = (
        [own] + [w.reshape(own.shape) for w in weights[3 * n : 3 * n + 3]]
        for n, own in enumerate((w_query, w_key, w_value, w_output))
    )
    w_in_own = w_in_own.reshape(width, -1)
    w_out_own = w_out_own.reshape(-1, width)
    gf_core, gf_x, gf_diag = (gf_rest[n] for n in range(3))
    pad_rows = (new_rows + 15) // 16 * 16

    (
        (grad_conv, new_cols, out_part, grad_hidden, grad_mixed, go_near, go_far, grad_w_in),
        (out_own, out_core, out_far, out_first),
    ) = unpack(
        middle(
            counts,
            mem_lens,
            gain_rows,
            conv_rows,
            normed_two,
            grad_ffn,
            gf_rest,
            w_in_own,
            w_out_own,
            cut_bits(grad_conv.reshape(dps, -1, conv_cols), masks),
            memory,
            hidden,
            out_grad[0],
            mixed_near,
            mixed_far,
            wo,
        ),
        (8, 4),
    )
    grad_w_out, sum_rows, input_grad, grad_out, gain_terms, grad_w_in, new_all, grad_conv, out_second = backward(
        mem_lens,
        cmem_lens,
        (q_near, k_near, v_near, lse_near),
        (q_far, k_far, v_far, lse_far),
        grad_mixed,
        wq,
        wk,
        wv,
        gain_one,
        go_near,
        go_far,
        out_part,
        new_cols,
        grad_conv,
        key_t,
        cut_bits(grad_w_in.reshape((dps, heads, w_in.shape[0], -1)), masks),
        inputs[0],
        grad_hidden,
        out_far,
    )
    in_source, in_weight = grad_w_in, w_in
    if units != E:
        in_source = (
            grad_w_in.reshape(heads, w_in.shape[0], dps, units)
            .transpose(1, 2, 0, 3)
            .reshape(w_in.shape[0], -1, heads, E)
            .transpose(2, 0, 1, 3)
            .reshape(grad_w_in.shape)
        )
    (
        outputs, input_grad, grad_query, grad_key, grad_value, grad_out, grad_w_out, grad_w_in,
        new_compressed, grad_conv, gain_sums,
    ) = finish(
        counts,
        hidden,
        out_own,
        out_core,
        out_first,
        out_second,
        input_grad,
        sum_rows.reshape(2, width, 3 * E),
        grad_out.reshape(w_output.shape),
        grad_w_out,
        in_source,
        new_all,
        grad_conv,
        w_in,
        new_rows,
    )
    own_gain_two = lax.dynamic_slice_in_dim(
        gain_two[0], (dp_at * heads + head_at) * w_in.shape[0], w_in.shape[0]
    )
    grad_gain_two = gain_sums[:, 0] / own_gain_two
    grad_gain_one = lax.dynamic_slice_in_dim(
        gain_terms[:, 0], head_at * norm_gain.shape[0], norm_gain.shape[0]
    ) / norm_gain.astype(f32)

    return (
        outputs[None],
        input_grad[None],
        new_compressed.transpose(1, 0, 2),
        grad_gain_one,
        grad_query,
        grad_key,
        grad_value,
        grad_out,
        grad_gain_two,
        grad_w_in,
        grad_w_out,
        grad_conv,
    )


def solution(mesh):
    whole = P(("dp", "head"), None, None)
    rows = P(("dp", "head"), None)
    vector = P(("dp", "head"))
    columns = P(None, "head")
    placed = (
        whole,
        P("dp", None, None),
        P("dp", None, None),
        P("dp"),
        P("dp"),
        P("dp"),
        vector,
        columns,
        columns,
        columns,
        P("head", None),
        vector,
        rows,
        rows,
        rows,
        whole,
        whole,
    )
    return jax.shard_map(
        shards,
        mesh=mesh,
        in_specs=placed,
        out_specs=(
            whole,
            whole,
            whole,
            vector,
            columns,
            columns,
            columns,
            P("head", None),
            vector,
            rows,
            rows,
            rows,
        ),
        check_vma=False,
    )
```
